32 devices in a mesh: groups: 2 (over y), labels: 4 (over z), dp: 4 (over x, core).
Axes of the slice: x: 2, y: 2, z: 4, core: 2. Of those that a mesh axis runs over, the one named last changes fastest.
Arguments:
- feats: bfloat16 [4096, 768], P(('groups', 'labels', 'dp')), parts along dimension 0, may hold values from -6 to 6
- enc_weight: bfloat16 [768, 768], P('dp'), may hold values from -0.21875 to 0.21875
- label_weight: bfloat16 [32768, 768], P(('groups', 'labels', 'dp')), parts along dimension 0, may hold values from -0.21875 to 0.21875
- owners: int32 [4096, 4], P(('groups', 'labels', 'dp')), parts along dimension 0, may hold values from 0 to 15, all different within a row; in each aligned block of 128 rows (0 to 127, 128 to 255, ...) at most 64 rows name the same one
- blocks: int32 [4096, 4], P(('groups', 'labels', 'dp')), parts along dimension 0, may hold values from 0 to 7
- positives: int32 [4096, 4], P(('groups', 'labels', 'dp')), parts along dimension 0, may hold values from 0 to 255
Outputs:
- grad_feats: bfloat16 [4096, 768], P(('groups', 'labels', 'dp')), parts along dimension 0
- grad_label: bfloat16 [32768, 768], P(('groups', 'labels', 'dp')), parts along dimension 0
- grad_enc: float32 [1536, 768], P(('groups', 'dp')), parts along dimension 0
The draws below stay inside these ranges and needn't reach their ends.
There are 2 independent parts, one for each index of `groups`. The reference program is written for one: setup_inputs(seed, part) draws one part's arguments, and reference() takes and returns one part's arrays. A program takes and returns all parts, laid end to end along the dimension named above; an argument that names none is the same for every part. Nothing has to cross between parts.
Inputs may be any that keep to these rules, and one draw needn't show every extreme that they name: Each query names 4 different owners; among the 128 queries of one device no owner is named by more than 64 queries, a bound that some block reaches.
All inputs are finite; a program needn't handle non-finite values.
Results may differ from the reference program's by a relative error of at most 0.013.
Values may be sent and summed in bfloat16 or wider, within the bound.
No kernel may reach another device: no remote copies, remote signals or barrier semaphores. Data moves between devices by JAX's collectives and lax.ppermute only.
A program may use at most 64 MiB of HBM per device.

```python
import math
import jax
import jax.numpy as jnp
import numpy as np
from jax import lax

D = 768
BLK = 128
LBL_DEV = 1024
K = 4
QD = 128
QUERIES = 2048
NLAB = 16384
CAP = 64
N_LABELS = 4
N_DP = 4


def touch_ends(result, key, smallest, top_value):
    index_at = [jax.random.randint(jax.random.fold_in(key, axis), (), 0, length) for axis, length in enumerate(result.shape)]
    main_axis = result.shape.index(max(result.shape))
    neighbour = index_at[:main_axis] + [(index_at[main_axis] + 1) % result.shape[main_axis]] + index_at[main_axis + 1:]
    return result.at[tuple(index_at)].set(smallest).at[tuple(neighbour)].set(top_value)


def with_spikes(drawn, key, source, target, parts, factor):
    owner, partner = [(jnp.arange(drawn.shape[axis_at]) // (drawn.shape[axis_at] // parts)).reshape([-1 if axis == axis_at else 1 for axis in range(drawn.ndim)]) for axis_at in (source, target)]
    chosen = jax.random.permutation(key, parts)[partner]
    strong = (owner == chosen) | (owner == (partner + parts // 2) % parts)
    return jnp.where(strong, factor * drawn, drawn)


def steps_of(own_key, dims, split, least, high):
    factor_of = 1.0
    for dim, parts in split:
        steps = jax.random.uniform(jax.random.fold_in(jax.random.fold_in(own_key, 6), dim), (parts,), jnp.float32, least / len(split), high / len(split))
        factor_of = factor_of * jnp.repeat(jnp.exp(steps), dims[dim] // parts).reshape((-1,) + (1,) * (len(dims) - 1 - dim))
    return factor_of


def shared_out(own_key, own, number, rows, count, top, limit, lean):
    ranking = jax.random.permutation(own_key, count)
    heavy_load, usual = portions_of(count, rows * top, limit, lean, True), portions_of(count, rows * top, limit, lean, False)
    places = jnp.arange(count)

    def named(lengths, offset_by):
        used = int((lengths > 0).sum())
        fixed = max(1, used // 4)
        shifted = fixed + (places - fixed + offset_by * (used - fixed)) % max(1, count - fixed)
        return jnp.zeros((count,), jnp.int32).at[ranking[jnp.where(places < fixed, places, shifted)]].set(jnp.asarray(lengths, jnp.int32))

    lengths = jnp.where(number % 4 == 0, named(heavy_load, number // 4), named(usual, number - number // 4 - 1))
    mixed = jax.random.permutation(jax.random.fold_in(own, 3), count)
    source_of, taker = mixed[0:count // 2 * 2:2], mixed[1:count // 2 * 2:2]
    slack = jnp.minimum(lengths[source_of] - 1, limit - lengths[taker]) // 2
    slack = jnp.where((source_of == ranking[0]) | (taker == ranking[0]) | (lengths[taker] == 0), 0, jnp.maximum(slack, 0))
    shifted = jax.random.randint(jax.random.fold_in(own, 4), (count // 2,), 0, 1 << 20) % (slack + 1)
    lengths = lengths.at[source_of].add(-shifted).at[taker].add(shifted)
    labels = jnp.searchsorted(jnp.cumsum(lengths), jnp.arange(rows * top), side="right").astype(jnp.int32)
    grid = labels.reshape(top, rows).T
    grid = grid[jax.random.permutation(jax.random.fold_in(own, 1), rows)]
    offset_by = jax.random.randint(jax.random.fold_in(own, 2), (rows, 1), 0, top)
    return jnp.take_along_axis(grid, (jnp.arange(top)[None, :] + offset_by) % top, axis=1)


def portions_of(number_of, total, reach, slope, full):
    portions = [(1 << 20) // math.isqrt(standing ** slope) + 1 for standing in range(1, number_of + 1)]
    largest = reach if full else min(reach, max(-(-total // number_of), total * portions[0] // sum(portions)))
    least = 1 if total - largest >= number_of - 1 else 0
    counts, surplus = [largest] + [least] * (number_of - 1), total - largest - least * (number_of - 1)
    while surplus > 0:
        movable = [i for i in range(1, number_of) if counts[i] < largest] or [i for i in range(1, number_of) if counts[i] < reach]
        mass, left = sum([portions[i] for i in movable]), surplus
        for i in movable:
            addition = min(reach - counts[i], max(1, left * portions[i] // mass), surplus)
            counts[i] = counts[i] + addition
            surplus = surplus - addition
    return np.array(counts)


def scatter_about(rng, extent, deviation, most, split=(), kind=jnp.bfloat16):
    array = jax.random.normal(rng, extent, jnp.float32) * deviation
    if len(split) > 0:
        array = steps_of(rng, extent, split, -0.22, 0.18) * array
    return jnp.clip(array, min=-most, max=most).astype(kind)


def noise_with(key, shape, spread, most, pieces, heavy, held_as=jnp.bfloat16):
    result = spread * jax.random.normal(key, shape, jnp.float32)
    if pieces:
        result = result * steps_of(key, shape, pieces, -0.22, 0.18)
    return jnp.clip(with_spikes(result, jax.random.fold_in(key, 3), *heavy), -most, most).astype(held_as)


def setup_inputs(seed: int = 0, part: int = 0) -> dict:
    key_of = jax.random.split(jax.random.key(seed), 7)
    part_splits = jax.random.split(jax.random.fold_in(key_of[6], part), 7)
    feats = noise_with(part_splits[0], (QUERIES, D), 1.0, 6.0, ((0, 16),), (0, 1, 16, 2.0))
    enc_weight = scatter_about(key_of[1], (D, D), D ** -0.5, 0.21875, ((0, 4),))
    label_weight = scatter_about(part_splits[2], (NLAB, D), D ** -0.5, 0.21875, ((0, 16),))
    owners_keys = jax.random.split(jax.random.fold_in(part_splits[3], 1), QUERIES // QD)
    owners_turns = jax.random.permutation(jax.random.fold_in(part_splits[3], 3), QUERIES // QD)
    owners = jax.vmap(lambda own, number: shared_out(jax.random.fold_in(part_splits[3], 2), own, number, QD, N_LABELS * N_DP, K, CAP, 2))(owners_keys, owners_turns).reshape((QUERIES, K))
    blocks = touch_ends(jax.random.randint(part_splits[4], (QUERIES, K), 0, LBL_DEV // BLK), jax.random.fold_in(part_splits[4], 1), 0, (LBL_DEV // BLK) - 1).astype(jnp.int32)
    positives = touch_ends(jax.random.randint(part_splits[5], (QUERIES, K), 0, 2 * BLK), jax.random.fold_in(part_splits[5], 1), 0, (2 * BLK) - 1).astype(jnp.int32)
    return dict(feats=feats, enc_weight=enc_weight, label_weight=label_weight, owners=owners, blocks=blocks, positives=positives)


EPSILON = 1e-06

def reference(feats, enc_weight, label_weight, owners, blocks, positives):
    hidden = jnp.dot(feats, enc_weight, preferred_element_type=jnp.float32)
    inv_rms = lax.rsqrt(lax.optimization_barrier(jnp.mean(hidden * hidden, axis=-1, keepdims=True)) + EPSILON)
    embedding = (hidden * inv_rms).astype(jnp.bfloat16)
    table = label_weight.reshape(-1, BLK, D)
    global_block = (owners * (LBL_DEV // BLK) + blocks).astype(jnp.int32)
    block_rows = 64
    steps_count = QUERIES // block_rows

    def one_block(carry, inputs):
        emb_rows, ident, wanted = inputs
        chosen = table[ident].astype(jnp.float32)
        emb_float = emb_rows.astype(jnp.float32)
        scores = jnp.einsum('qd,qkld->qkl', emb_float, chosen)
        target = (jnp.arange(BLK, dtype=jnp.int32)[None, None, :] == wanted[:, :, None]).astype(jnp.float32)
        grad_scores = (jax.nn.sigmoid(scores) - target).astype(jnp.bfloat16).astype(jnp.float32)
        grad_pair = jnp.einsum('qkl,qkld->qkd', grad_scores, chosen).astype(jnp.bfloat16)
        grad_rows = lax.optimization_barrier(jnp.sum(grad_pair.astype(jnp.float32), axis=1))
        contrib = jnp.einsum('qkl,qd->qkld', grad_scores, emb_float).reshape(-1, BLK, D)
        carry = carry.at[ident.reshape(-1)].add(contrib)
        return (carry, grad_rows)
    start_acc = jnp.zeros((NLAB // BLK, BLK, D), jnp.float32)
    label_acc, grad_embedding = lax.scan(one_block, start_acc, (embedding.reshape(steps_count, block_rows, D), global_block.reshape(steps_count, block_rows, K), positives.reshape(steps_count, block_rows, K)))
    grad_embedding = grad_embedding.reshape(QUERIES, D)
    grad_label = label_acc.reshape(NLAB, D).astype(jnp.bfloat16)
    projection = lax.optimization_barrier(jnp.mean(hidden * grad_embedding, axis=-1, keepdims=True))
    grad_hidden = (inv_rms * grad_embedding - hidden * inv_rms ** 3 * projection).astype(jnp.bfloat16)
    grad_feats = jnp.dot(grad_hidden, enc_weight.T, preferred_element_type=jnp.float32).astype(jnp.bfloat16)
    grad_enc = jnp.dot(feats.T, grad_hidden, preferred_element_type=jnp.float32)
    return (grad_feats, grad_label, grad_enc)
```

```python
import functools

import jax
import jax.numpy as jnp
from jax import lax
from jax.experimental import pallas as pl
from jax.experimental.pallas import tpu as pltpu
from jax.sharding import PartitionSpec as P

BLK = 128
EPSILON = 1e-06
STEP_ROWS = 512
F32 = jnp.float32
BF16 = jnp.bfloat16


def dot(a, b, da=1, db=0):
    return lax.dot_general(a, b, (((da,), (db,)), ((), ())), preferred_element_type=F32)


def label_kernel(
    me_ref,
    meta_ref,
    feats_ref,
    enc_ref,
    label_ref,
    back_ref,
    grad_label_ref,
    grad_enc_ref,
    label_acc,
    enc_acc,
    *,
    cap,
):
    step = pl.program_id(0)
    me = me_ref[0]
    sources, rows, width = feats_ref.shape
    n_blocks = label_ref.shape[0] // BLK

    hits, codes = [], []
    for s in range(sources):
        named = meta_ref[s, 0] == me
        hits.append(jnp.sum(named.astype(F32), axis=0, keepdims=True))
        code = (meta_ref[s, 1] * 256 + meta_ref[s, 2] + 1).astype(F32)
        codes.append(jnp.sum(jnp.where(named, code, 0.0), axis=0, keepdims=True))
    hit = jnp.concatenate(hits, axis=0)
    row_id = lax.broadcasted_iota(jnp.int32, (rows, rows), 0)
    col_id = lax.broadcasted_iota(jnp.int32, (rows, rows), 1)
    rank = dot(hit.astype(BF16), (row_id < col_id).astype(BF16))
    slot_id = lax.broadcasted_iota(jnp.int32, (cap, rows), 0).astype(F32)

    picks, picked, slot_codes = [], [], []
    for s in range(sources):
        pick = jnp.where((slot_id == rank[s : s + 1]) & (hits[s] > 0.0), 1.0, 0.0)
        slot_codes.append(jnp.sum(pick * codes[s], axis=1, keepdims=True))
        pick = pick.astype(BF16)
        picks.append(pick)
        picked.append(dot(pick, feats_ref[s]).astype(BF16))
    feats = jnp.concatenate(picked, axis=0)
    code = jnp.concatenate(slot_codes, axis=0).astype(jnp.int32) - 1
    slots = feats.shape[0]

    hidden = dot(feats, enc_ref[...])
    inv_rms = lax.rsqrt(jnp.mean(hidden * hidden, axis=-1, keepdims=True) + EPSILON)
    embedding = (hidden * inv_rms).astype(BF16)

    scores = dot(embedding, label_ref[...], 1, 1)
    block = jnp.broadcast_to(code >> 8, (slots, BLK))
    wanted = jnp.broadcast_to(code & 255, (slots, BLK))
    live = block >= 0
    own_scores = jnp.zeros((slots, BLK), F32)
    for b in range(n_blocks):
        own_scores = jnp.where(block == b, scores[:, b * BLK : (b + 1) * BLK], own_scores)
    column = lax.broadcasted_iota(jnp.int32, (slots, BLK), 1)
    target = jnp.where(column == wanted, 1.0, 0.0)
    grad_scores = jnp.where(live, jax.nn.sigmoid(own_scores) - target, 0.0)

    spread = jnp.concatenate(
        [jnp.where(block == b, grad_scores, 0.0).astype(BF16) for b in range(n_blocks)], axis=1
    )
    grad_pair = dot(spread, label_ref[...]).astype(BF16).astype(F32)

    grad_scores_t = grad_scores.T
    block_t = block.T
    spread_t = jnp.concatenate(
        [jnp.where(block_t == b, grad_scores_t, 0.0).astype(BF16) for b in range(n_blocks)], axis=0
    )
    label_part = dot(spread_t, embedding)

    projection = jnp.mean(hidden * grad_pair, axis=-1, keepdims=True)
    grad_hidden = (inv_rms * grad_pair - hidden * (inv_rms**3 * projection)).astype(BF16)
    enc_part = dot(feats, grad_hidden, 0, 0)
    grad_feats = dot(grad_hidden, enc_ref[...], 1, 1).astype(BF16)
    for s in range(sources):
        back_ref[s] = dot(picks[s], grad_feats[s * cap : (s + 1) * cap], 0, 0).astype(BF16)

    @pl.when(step == 0)
    def _():
        label_acc[...] = label_part
        enc_acc[...] = enc_part

    @pl.when(step > 0)
    def _():
        label_acc[...] += label_part
        enc_acc[...] += enc_part

    @pl.when(step == pl.num_programs(0) - 1)
    def _():
        grad_label_ref[...] = label_acc[...].astype(BF16)
        grad_enc_ref[...] = enc_acc[...].astype(BF16)


def label_work(me, meta, feats, enc_weight, label_weight, cap):
    sources, rows, width = feats.shape
    group = max(1, min(sources, STEP_ROWS // cap))
    while sources % group:
        group -= 1
    labels_here = label_weight.shape[0]
    whole = lambda shape: pl.BlockSpec(shape, lambda i: (0,) * len(shape))
    flops = 2 * sources * cap * width * (3 * labels_here + 3 * width + 2 * rows)
    return pl.pallas_call(
        functools.partial(label_kernel, cap=cap),
        grid=(sources // group,),
        in_specs=[
            pl.BlockSpec(memory_space=pltpu.SMEM),
            pl.BlockSpec((group,) + meta.shape[1:], lambda i: (i, 0, 0, 0)),
            pl.BlockSpec((group, rows, width), lambda i: (i, 0, 0)),
            whole(enc_weight.shape),
            whole(label_weight.shape),
        ],
        out_specs=[
            pl.BlockSpec((group, rows, width), lambda i: (i, 0, 0)),
            whole(label_weight.shape),
            whole(enc_weight.shape),
        ],
        out_shape=[
            jax.ShapeDtypeStruct(feats.shape, BF16),
            jax.ShapeDtypeStruct(label_weight.shape, BF16),
            jax.ShapeDtypeStruct(enc_weight.shape, BF16),
        ],
        scratch_shapes=[
            pltpu.VMEM(label_weight.shape, F32),
            pltpu.VMEM(enc_weight.shape, F32),
        ],
        compiler_params=pltpu.CompilerParams(vmem_limit_bytes=56 << 20),
        cost_estimate=pl.CostEstimate(flops=flops, bytes_accessed=12 << 20, transcendentals=0),
        name="label_work",
    )(me, meta, feats, enc_weight, label_weight)


def swap(x):
    x = lax.all_to_all(x, "labels", split_axis=0, concat_axis=0, tiled=True)
    return lax.all_to_all(x, "dp", split_axis=1, concat_axis=1, tiled=True)


def local(feats, enc_weight, label_weight, owners, blocks, positives):
    n_labels = lax.axis_size("labels")
    n_data = lax.axis_size("dp")
    n_owner = n_labels * n_data
    row_count, width = feats.shape
    pick_count = owners.shape[1]
    cap = max(2, 2 * row_count * pick_count // n_owner)
    me = (lax.axis_index("labels") * n_data + lax.axis_index("dp")).astype(jnp.int32)
    full_weight = lax.all_gather(enc_weight, "dp", axis=0, tiled=True)

    if row_count <= n_data * cap:
        meta = jnp.stack([owners.T, blocks.T, positives.T])
        all_feats = lax.all_gather(feats, ("labels", "dp"))
        all_meta = lax.all_gather(meta, ("labels", "dp"))
        back, grad_label, enc_part = label_work(
            me.reshape(1), all_meta, all_feats, full_weight, label_weight, cap
        )
        grad_feats = lax.psum_scatter(back, ("labels", "dp"), scatter_dimension=0)
    else:
        flat = owners.reshape(-1)
        onehot = (flat[:, None] == jnp.arange(n_owner, dtype=jnp.int32)[None, :]).astype(jnp.int32)
        rank = jnp.sum((jnp.cumsum(onehot, axis=0) - onehot) * onehot, axis=1)
        slot = (flat * cap + rank).reshape(row_count, pick_count)
        slot_total = n_owner * cap
        slots = jnp.arange(slot_total, dtype=jnp.int32)
        place = slots[:, None, None] == slot[None]
        pick = jnp.any(place, axis=2).astype(BF16)
        live = jnp.any(place, axis=(1, 2))
        block_of = jnp.sum(jnp.where(place, blocks[None], 0), axis=(1, 2))
        wanted = jnp.sum(jnp.where(place, positives[None], 0), axis=(1, 2))
        owner_of = jnp.where(live, slots // cap, -1)
        out = dot(pick, feats).astype(BF16).reshape(n_labels, n_data, cap, width)
        meta = jnp.stack([owner_of, block_of, wanted], axis=1).reshape(n_labels, n_data, cap, 3)
        tile = 128
        got = swap(out).reshape(slot_total // tile, tile, width)
        got_meta = swap(meta).reshape(slot_total // tile, tile, 3)
        got_meta = got_meta.transpose(0, 2, 1)[:, :, None, :]
        back, grad_label, enc_part = label_work(
            me.reshape(1), got_meta, got, full_weight, label_weight, tile
        )
        back = swap(back.reshape(n_labels, n_data, cap, width)).reshape(slot_total, width)
        grad_feats = dot(pick, back, 0, 0).astype(BF16)

    share = lax.psum_scatter(enc_part, "dp", scatter_dimension=0, tiled=True)
    grad_enc = lax.psum(share.astype(F32), "labels")
    return (grad_feats, grad_label, grad_enc)


def solution(mesh):
    rows = P(("groups", "labels", "dp"), None)
    return jax.shard_map(
        local,
        mesh=mesh,
        in_specs=(rows, P("dp", None), rows, rows, rows, rows),
        out_specs=(rows, rows, P(("groups", "dp"), None)),
        check_vma=False,
    )
```

```python
import functools

import jax
import jax.numpy as jnp
from jax import lax
from jax.experimental import pallas as pl
from jax.experimental.pallas import tpu as pltpu
from jax.sharding import PartitionSpec as P

BLK = 128
EPSILON = 1e-06
STEP_ROWS = 512
META_ROWS = 16
F32 = jnp.float32
BF16 = jnp.bfloat16


def dot(a, b, da=1, db=0):
    return lax.dot_general(a, b, (((da,), (db,)), ((), ())), preferred_element_type=F32)


def label_kernel(where_ref, *refs, cap, sources, n_data, pick_count):
    it = iter(refs)
    take = lambda n: [next(it) for _ in range(n)]
    source_refs = take(sources)
    shard_refs = take(n_data)
    label_ref = next(it)
    back_refs = take(2 * sources // n_data)
    grad_label_ref = next(it)
    share_refs = take(2)
    src, back, enc, label_acc, enc_acc, in_sem, out_sem = it

    me = where_ref[0].astype(F32)
    my_data = where_ref[1]
    rows, width = src.shape[1] - META_ROWS, src.shape[2]
    shard_rows = shard_refs[0].shape[0]
    n_blocks = label_ref.shape[0] // BLK
    group = max(1, min(sources, STEP_ROWS // cap))
    while sources % group:
        group -= 1
    slots = group * cap

    for i in range(sources):
        pltpu.make_async_copy(source_refs[i], src.at[i], in_sem.at[i]).start()

    def shard(m):
        at = jnp.bitwise_xor(my_data, m) * shard_rows
        return pl.ds(pl.multiple_of(at, 16), shard_rows)

    for m in range(n_data):
        enc[shard(m), :] = shard_refs[m][...]
    label_acc[...] = jnp.zeros_like(label_acc)
    enc_acc[...] = jnp.zeros_like(enc_acc)

    row_id = lax.broadcasted_iota(jnp.int32, (rows, rows), 0)
    col_id = lax.broadcasted_iota(jnp.int32, (rows, rows), 1)
    before = (row_id < col_id).astype(BF16)
    slot_id = lax.broadcasted_iota(jnp.int32, (cap, rows), 0).astype(F32)
    column = lax.broadcasted_iota(jnp.int32, (slots, BLK), 1)

    def chunk(g, carry):
        first = g * group
        for s in range(group):
            at = first + s
            pltpu.make_async_copy(src.at[at], src.at[at], in_sem.at[at]).wait()

        hits, codes = [], []
        for s in range(group):
            meta = src[first + s, pl.ds(rows, META_ROWS), 0 : 3 * rows].astype(F32)[:pick_count]
            named = meta[:, :rows] == me
            hits.append(jnp.sum(named.astype(F32), axis=0, keepdims=True))
            code = meta[:, rows : 2 * rows] * 256.0 + meta[:, 2 * rows :] + 1.0
            codes.append(jnp.sum(jnp.where(named, code, 0.0), axis=0, keepdims=True))
        rank = dot(jnp.concatenate(hits, axis=0).astype(BF16), before)

        picks, picked, slot_codes = [], [], []
        for s in range(group):
            pick = jnp.where((slot_id == rank[s : s + 1]) & (hits[s] > 0.0), 1.0, 0.0)
            slot_codes.append(jnp.sum(pick * codes[s], axis=1, keepdims=True))
            pick = pick.astype(BF16)
            picks.append(pick)
            picked.append(dot(pick, src[first + s, pl.ds(0, rows), :]).astype(BF16))
        feats = jnp.concatenate(picked, axis=0)
        code = jnp.concatenate(slot_codes, axis=0).astype(jnp.int32) - 1

        hidden = dot(feats, enc[...])
        inv_rms = lax.rsqrt(jnp.mean(hidden * hidden, axis=-1, keepdims=True) + EPSILON)
        embedding = (hidden * inv_rms).astype(BF16)

        scores = dot(embedding, label_ref[...], 1, 1)
        block = jnp.broadcast_to(code >> 8, (slots, BLK))
        wanted = jnp.broadcast_to(code & 255, (slots, BLK))
        own_scores = jnp.zeros((slots, BLK), F32)
        for b in range(n_blocks):
            own_scores = jnp.where(block == b, scores[:, b * BLK : (b + 1) * BLK], own_scores)
        target = jnp.where(column == wanted, 1.0, 0.0)
        grad_scores = jnp.where(block >= 0, jax.nn.sigmoid(own_scores) - target, 0.0)

        spread = jnp.concatenate(
            [jnp.where(block == b, grad_scores, 0.0).astype(BF16) for b in range(n_blocks)], axis=1
        )
        grad_pair = dot(spread, label_ref[...]).astype(BF16).astype(F32)

        grad_scores_t = grad_scores.T
        block_t = block.T
        spread_t = jnp.concatenate(
            [jnp.where(block_t == b, grad_scores_t, 0.0).astype(BF16) for b in range(n_blocks)],
            axis=0,
        )
        label_acc[...] += dot(spread_t, embedding)

        projection = jnp.mean(hidden * grad_pair, axis=-1, keepdims=True)
        grad_hidden = (inv_rms * grad_pair - hidden * (inv_rms**3 * projection)).astype(BF16)
        enc_acc[...] += dot(feats, grad_hidden, 0, 0)
        grad_feats = dot(grad_hidden, enc[...], 1, 1).astype(BF16)
        for s in range(group):
            part = dot(picks[s], grad_feats[s * cap : (s + 1) * cap], 0, 0)
            back[first + s] = part.astype(BF16)
        return carry

    lax.fori_loop(0, sources // group, chunk, 0)

    copies = []
    for i in range(sources):
        s, m = divmod(i, n_data)
        copy = pltpu.make_async_copy(
            back.at[i], back_refs[2 * s + m % 2].at[m // 2], out_sem.at[i]
        )
        copy.start()
        copies.append(copy)
    grad_label_ref[...] = label_acc[...].astype(BF16)
    for m in range(n_data):
        share_refs[m % 2][m // 2] = enc_acc[shard(m), :].astype(BF16)
    for copy in copies:
        copy.wait()


def label_work(where, blocks, shards, label_weight, cap, pick_count):
    sources, n_data = len(blocks), len(shards)
    block_rows, width = blocks[0].shape
    rows = block_rows - META_ROWS
    labels_here = label_weight.shape[0]
    shard_rows = shards[0].shape[0]
    half = n_data // 2
    hbm = pl.BlockSpec(memory_space=pl.ANY)
    vmem = pl.BlockSpec(memory_space=pltpu.VMEM)
    flops = 2 * sources * cap * width * (3 * labels_here + 3 * width + 2 * rows)
    runs = 2 * sources // n_data
    return pl.pallas_call(
        functools.partial(
            label_kernel, cap=cap, sources=sources, n_data=n_data, pick_count=pick_count
        ),
        in_specs=[pl.BlockSpec(memory_space=pltpu.SMEM)] + [hbm] * sources + [vmem] * (n_data + 1),
        out_specs=[hbm] * runs + [vmem] * 3,
        out_shape=[jax.ShapeDtypeStruct((half, rows, width), BF16)] * runs
        + [jax.ShapeDtypeStruct(label_weight.shape, BF16)]
        + [jax.ShapeDtypeStruct((half, shard_rows, width), BF16)] * 2,
        scratch_shapes=[
            pltpu.VMEM((sources, block_rows, width), BF16),
            pltpu.VMEM((sources, rows, width), BF16),
            pltpu.VMEM((n_data * shard_rows, width), BF16),
            pltpu.VMEM(label_weight.shape, F32),
            pltpu.VMEM((n_data * shard_rows, width), F32),
            pltpu.SemaphoreType.DMA((sources,)),
            pltpu.SemaphoreType.DMA((sources,)),
        ],
        compiler_params=pltpu.CompilerParams(vmem_limit_bytes=56 << 20),
        cost_estimate=pl.CostEstimate(flops=flops, bytes_accessed=12 << 20, transcendentals=0),
        name="label_work",
    )(where, *blocks, *shards, label_weight)


def swap(x):
    x = lax.all_to_all(x, "labels", split_axis=0, concat_axis=0, tiled=True)
    return lax.all_to_all(x, "dp", split_axis=1, concat_axis=1, tiled=True)


def partner(x, axis, mask):
    return lax.ppermute(x, axis, [(i, i ^ mask) for i in range(lax.axis_size(axis))])


def shifted(x, axis, by):
    n = lax.axis_size(axis)
    return lax.ppermute(x, axis, [(i, (i + by) % n) for i in range(n)])


def masks(n):
    return [1 << i for i in range(n.bit_length() - 1)]


def gather_dp(x):
    got = {0: x}
    for mask in reversed(masks(lax.axis_size("dp"))):
        got.update({m | mask: partner(v, "dp", mask) for m, v in list(got.items())})
    return [got[m] for m in range(len(got))]


def add(*terms):
    return sum(t.astype(F32) for t in terms)


def reduce_dp(even, odd):
    got = partner(odd, "dp", 1)
    terms = [[even[i], got[i]] for i in range(even.shape[0])]
    for mask in masks(len(terms)):
        for i in range(len(terms)):
            if i & mask == 0 and i % mask == 0:
                terms[i].append(partner(add(*terms[i | mask]).astype(BF16), "dp", 2 * mask))
    return add(*terms[0])


def with_meta(feats, owner_rows, block_rows, positive_rows):
    meta = jnp.concatenate([owner_rows, block_rows, positive_rows], axis=1).astype(BF16)
    meta = jnp.pad(meta, ((0, META_ROWS - meta.shape[0]), (0, feats.shape[1] - meta.shape[1])))
    return jnp.concatenate([feats, meta], axis=0)


def local(feats, enc_weight, label_weight, owners, blocks, positives):
    n_labels = lax.axis_size("labels")
    n_data = lax.axis_size("dp")
    n_owner = n_labels * n_data
    row_count, width = feats.shape
    pick_count = owners.shape[1]
    cap = max(2, 2 * row_count * pick_count // n_owner)
    my_data = lax.axis_index("dp")
    where = jnp.stack([lax.axis_index("labels") * n_data + my_data, my_data]).astype(jnp.int32)
    shards = gather_dp(enc_weight)

    if row_count <= n_data * cap:
        own = with_meta(feats, owners.T, blocks.T, positives.T)
        sources = []
        for by in range(n_labels):
            sources += gather_dp(own if by == 0 else shifted(own, "labels", by))
        *back, grad_label, even, odd = label_work(
            where, sources, shards, label_weight, cap, pick_count
        )
        total = []
        for by in range(n_labels):
            part = reduce_dp(back[2 * by], back[2 * by + 1])
            total.append(part if by == 0 else shifted(part.astype(BF16), "labels", -by))
        grad_feats = add(*total).astype(BF16)
    else:
        flat = owners.reshape(-1)
        onehot = (flat[:, None] == jnp.arange(n_owner, dtype=jnp.int32)[None, :]).astype(jnp.int32)
        rank = jnp.sum((jnp.cumsum(onehot, axis=0) - onehot) * onehot, axis=1)
        slot = (flat * cap + rank).reshape(row_count, pick_count)
        slot_total = n_owner * cap
        slots = jnp.arange(slot_total, dtype=jnp.int32)
        place = slots[:, None, None] == slot[None]
        pick = jnp.any(place, axis=2).astype(BF16)
        live = jnp.any(place, axis=(1, 2))
        block_of = jnp.sum(jnp.where(place, blocks[None], 0), axis=(1, 2))
        wanted = jnp.sum(jnp.where(place, positives[None], 0), axis=(1, 2))
        owner_of = jnp.where(live, slots // cap, -1)
        out = dot(pick, feats).astype(BF16).reshape(n_labels, n_data, cap, width)
        meta = jnp.stack([owner_of, block_of, wanted], axis=1).reshape(n_labels, n_data, cap, 3)
        tile = 128
        got = swap(out).reshape(slot_total // tile, tile, width)
        got_meta = swap(meta).reshape(slot_total // tile, tile, 3).transpose(0, 2, 1)
        sources = [
            with_meta(got[i], got_meta[i, 0:1], got_meta[i, 1:2], got_meta[i, 2:3])
            for i in range(slot_total // tile)
        ]
        *back, grad_label, even, odd = label_work(where, sources, shards, label_weight, tile, 1)
        back = jnp.stack(back).reshape(-1, 2, n_data // 2, tile, width).transpose(0, 2, 1, 3, 4)
        back = swap(back.reshape(n_labels, n_data, cap, width)).reshape(slot_total, width)
        grad_feats = dot(pick, back, 0, 0).astype(BF16)

    grad_enc = reduce_dp(even, odd)
    for mask in masks(n_labels):
        grad_enc = add(grad_enc, partner(grad_enc.astype(BF16), "labels", mask))
    return (grad_feats, grad_label, grad_enc)


def solution(mesh):
    rows = P(("groups", "labels", "dp"), None)
    return jax.shard_map(
        local,
        mesh=mesh,
        in_specs=(rows, P("dp", None), rows, rows, rows, rows),
        out_specs=(rows, rows, P(("groups", "dp"), None)),
        check_vma=False,
    )
```

```python
import functools

import jax
import jax.numpy as jnp
from jax import lax
from jax.experimental import pallas as pl
from jax.experimental.pallas import tpu as pltpu
from jax.sharding import PartitionSpec as P

BLK = 128
EPSILON = 1e-06
META_ROWS = 16
F32 = jnp.float32
BF16 = jnp.bfloat16


def dot(a, b, da=1, db=0):
    return lax.dot_general(a, b, (((da,), (db,)), ((), ())), preferred_element_type=F32)


def pair_kernel(where_ref, *refs, cap, pick_count):
    n_data = (len(refs) - 9) // 2
    sources, shards, label_ref = refs[:n_data], refs[n_data : 2 * n_data], refs[2 * n_data]
    even_ref, odd_ref, grad_scores_ref, block_ref, embedding_ref, feats_ref, grad_hidden_ref, enc = (
        refs[2 * n_data + 1 :]
    )
    me = where_ref[0].astype(F32)
    my_data = where_ref[1]
    rows = sources[0].shape[0] - META_ROWS
    shard_rows = shards[0].shape[0]
    n_blocks = label_ref.shape[0] // BLK
    slots = n_data * cap

    for m in range(n_data):
        enc[shard_at(my_data, m, shard_rows), :] = shards[m][...]

    row_id = lax.broadcasted_iota(jnp.int32, (rows, rows), 0)
    col_id = lax.broadcasted_iota(jnp.int32, (rows, rows), 1)
    before = (row_id < col_id).astype(BF16)
    slot_id = lax.broadcasted_iota(jnp.int32, (cap, rows), 0).astype(F32)
    column = lax.broadcasted_iota(jnp.int32, (slots, BLK), 1)

    hits, codes = [], []
    for source in sources:
        meta = source[rows:, 0 : 3 * rows].astype(F32)[:pick_count]
        named = meta[:, :rows] == me
        hits.append(jnp.sum(named.astype(F32), axis=0, keepdims=True))
        code = meta[:, rows : 2 * rows] * 256.0 + meta[:, 2 * rows :] + 1.0
        codes.append(jnp.sum(jnp.where(named, code, 0.0), axis=0, keepdims=True))
    rank = dot(jnp.concatenate(hits, axis=0).astype(BF16), before)

    picks, picked, slot_codes = [], [], []
    for s, source in enumerate(sources):
        pick = jnp.where((slot_id == rank[s : s + 1]) & (hits[s] > 0.0), 1.0, 0.0)
        slot_codes.append(jnp.sum(pick * codes[s], axis=1, keepdims=True))
        pick = pick.astype(BF16)
        picks.append(pick)
        picked.append(dot(pick, source[:rows, :]).astype(BF16))
    feats = jnp.concatenate(picked, axis=0)
    feats_ref[...] = feats
    code = jnp.concatenate(slot_codes, axis=0).astype(jnp.int32) - 1

    hidden = dot(feats, enc[...])
    inv_rms = lax.rsqrt(jnp.mean(hidden * hidden, axis=-1, keepdims=True) + EPSILON)
    embedding = (hidden * inv_rms).astype(BF16)
    embedding_ref[...] = embedding

    scores = dot(embedding, label_ref[...], 1, 1)
    block = jnp.broadcast_to(code >> 8, (slots, BLK))
    block_ref[...] = block
    wanted = jnp.broadcast_to(code & 255, (slots, BLK))
    own_scores = jnp.zeros((slots, BLK), F32)
    for b in range(n_blocks):
        own_scores = jnp.where(block == b, scores[:, b * BLK : (b + 1) * BLK], own_scores)
    target = jnp.where(column == wanted, 1.0, 0.0)
    grad_scores = jnp.where(block >= 0, jax.nn.sigmoid(own_scores) - target, 0.0)
    grad_scores_ref[...] = grad_scores

    spread = jnp.concatenate(
        [jnp.where(block == b, grad_scores, 0.0).astype(BF16) for b in range(n_blocks)], axis=1
    )
    grad_pair = dot(spread, label_ref[...]).astype(BF16).astype(F32)
    projection = jnp.mean(hidden * grad_pair, axis=-1, keepdims=True)
    grad_hidden = (inv_rms * grad_pair - hidden * (inv_rms**3 * projection)).astype(BF16)
    grad_hidden_ref[...] = grad_hidden
    grad_feats = dot(grad_hidden, enc[...], 1, 1).astype(BF16)
    for m in range(n_data):
        part = dot(picks[m], grad_feats[m * cap : (m + 1) * cap], 0, 0)
        (odd_ref if m % 2 else even_ref)[m // 2] = part.astype(BF16)


def enc_kernel(where_ref, *refs):
    runs = (len(refs) - 3) // 2
    even_ref, odd_ref, total = refs[2 * runs :]
    feats = jnp.concatenate([r[...] for r in refs[:runs]], axis=0)
    grad_hidden = jnp.concatenate([r[...] for r in refs[runs : 2 * runs]], axis=0)
    total[...] = dot(feats, grad_hidden, 0, 0)
    half, shard_rows, _ = even_ref.shape
    for m in range(2 * half):
        part = total[shard_at(where_ref[1], m, shard_rows), :]
        (odd_ref if m % 2 else even_ref)[m // 2] = part.astype(BF16)


def grad_label_kernel(*refs):
    runs = (len(refs) - 1) // 3
    grad_scores, blocks, embeddings = refs[:runs], refs[runs : 2 * runs], refs[2 * runs : 3 * runs]
    out_ref = refs[-1]
    grad_scores_t = jnp.concatenate([r[...].T for r in grad_scores], axis=1)
    block_t = jnp.concatenate([r[...].T for r in blocks], axis=1)
    embedding = jnp.concatenate([r[...] for r in embeddings], axis=0)
    for b in range(out_ref.shape[0] // BLK):
        spread_t = jnp.where(block_t == b, grad_scores_t, 0.0).astype(BF16)
        out_ref[b * BLK : (b + 1) * BLK, :] = dot(spread_t, embedding).astype(BF16)


def shard_at(my_data, m, shard_rows):
    at = jnp.bitwise_xor(my_data, m) * shard_rows
    return pl.ds(pl.multiple_of(at, 16), shard_rows)


def call(kernel, name, out_shape, scratch, flops, megabytes, *args):
    smem = pl.BlockSpec(memory_space=pltpu.SMEM)
    vmem = pl.BlockSpec(memory_space=pltpu.VMEM)
    return pl.pallas_call(
        kernel,
        in_specs=[smem if a.ndim == 1 else vmem for a in args],
        out_specs=jax.tree.map(lambda _: vmem, out_shape),
        out_shape=out_shape,
        scratch_shapes=scratch,
        compiler_params=pltpu.CompilerParams(vmem_limit_bytes=24 << 20),
        cost_estimate=pl.CostEstimate(
            flops=flops, bytes_accessed=megabytes << 20, transcendentals=0
        ),
        name=name,
    )(*args)


def pair_work(where, sources, shards, label_weight, cap, pick_count):
    n_data = len(sources)
    rows, width = sources[0].shape[0] - META_ROWS, sources[0].shape[1]
    slots = n_data * cap
    return call(
        functools.partial(pair_kernel, cap=cap, pick_count=pick_count),
        "pair_work",
        [jax.ShapeDtypeStruct((n_data // 2, rows, width), BF16)] * 2
        + [
            jax.ShapeDtypeStruct((slots, BLK), F32),
            jax.ShapeDtypeStruct((slots, BLK), jnp.int32),
        ]
        + [jax.ShapeDtypeStruct((slots, width), BF16)] * 3,
        [pltpu.VMEM((n_data * shards[0].shape[0], width), BF16)],
        2 * slots * width * (2 * label_weight.shape[0] + 2 * width + 2 * rows),
        8,
        where,
        *sources,
        *shards,
        label_weight,
    )


def enc_work(where, feats, grad_hidden, shard, n_data):
    shard_rows, width = shard.shape
    return call(
        enc_kernel,
        "enc_work",
        [jax.ShapeDtypeStruct((n_data // 2, shard_rows, width), BF16)] * 2,
        [pltpu.VMEM((n_data * shard_rows, width), F32)],
        2 * len(feats) * feats[0].shape[0] * width * width,
        4,
        where,
        *feats,
        *grad_hidden,
    )


def grad_label_work(grad_scores, blocks, embeddings, label_weight):
    return call(
        grad_label_kernel,
        "grad_label_work",
        jax.ShapeDtypeStruct(label_weight.shape, BF16),
        [],
        2 * len(blocks) * blocks[0].shape[0] * label_weight.size,
        4,
        *grad_scores,
        *blocks,
        *embeddings,
    )


def swap(x):
    x = lax.all_to_all(x, "labels", split_axis=0, concat_axis=0, tiled=True)
    return lax.all_to_all(x, "dp", split_axis=1, concat_axis=1, tiled=True)


def partner(x, axis, mask):
    return lax.ppermute(x, axis, [(i, i ^ mask) for i in range(lax.axis_size(axis))])


def shifted(x, axis, by):
    n = lax.axis_size(axis)
    return lax.ppermute(x, axis, [(i, (i + by) % n) for i in range(n)])


def masks(n):
    return [1 << i for i in range(n.bit_length() - 1)]


def gather_dp(x):
    got = {0: x}
    for mask in reversed(masks(lax.axis_size("dp"))):
        got.update({m | mask: partner(v, "dp", mask) for m, v in list(got.items())})
    return [got[m] for m in range(len(got))]


def add(*terms):
    return sum(t.astype(F32) for t in terms)


def reduce_dp(even, odd):
    got = partner(odd, "dp", 1)
    terms = [[even[i], got[i]] for i in range(even.shape[0])]
    for mask in masks(len(terms)):
        for i in range(len(terms)):
            if i & mask == 0 and i % mask == 0:
                terms[i].append(partner(add(*terms[i | mask]).astype(BF16), "dp", 2 * mask))
    return add(*terms[0])


def with_meta(feats, owner_rows, block_rows, positive_rows):
    meta = jnp.concatenate([owner_rows, block_rows, positive_rows], axis=1).astype(BF16)
    meta = jnp.pad(meta, ((0, META_ROWS - meta.shape[0]), (0, feats.shape[1] - meta.shape[1])))
    return jnp.concatenate([feats, meta], axis=0)


def local(feats, enc_weight, label_weight, owners, blocks, positives):
    n_labels = lax.axis_size("labels")
    n_data = lax.axis_size("dp")
    n_owner = n_labels * n_data
    row_count, width = feats.shape
    pick_count = owners.shape[1]
    cap = max(2, 2 * row_count * pick_count // n_owner)
    my_data = lax.axis_index("dp")
    where = jnp.stack([lax.axis_index("labels") * n_data + my_data, my_data]).astype(jnp.int32)
    shards = gather_dp(enc_weight)

    if row_count <= n_data * cap:
        own = with_meta(feats, owners.T, blocks.T, positives.T)
        runs = []
        block = own
        for by in range(n_labels):
            if by:
                block = shifted(block, "labels", 1)
            runs.append(gather_dp(block))
        work = [
            pair_work(where, sources, shards, label_weight, cap, pick_count) for sources in runs
        ]
        total = []
        for by in range(n_labels):
            part = reduce_dp(work[by][0], work[by][1])
            total.append(part if by == 0 else shifted(part.astype(BF16), "labels", -by))
        grad_feats = add(*total).astype(BF16)
    else:
        flat = owners.reshape(-1)
        onehot = (flat[:, None] == jnp.arange(n_owner, dtype=jnp.int32)[None, :]).astype(jnp.int32)
        rank = jnp.sum((jnp.cumsum(onehot, axis=0) - onehot) * onehot, axis=1)
        slot = (flat * cap + rank).reshape(row_count, pick_count)
        slot_total = n_owner * cap
        slots = jnp.arange(slot_total, dtype=jnp.int32)
        place = slots[:, None, None] == slot[None]
        pick = jnp.any(place, axis=2).astype(BF16)
        live = jnp.any(place, axis=(1, 2))
        block_of = jnp.sum(jnp.where(place, blocks[None], 0), axis=(1, 2))
        wanted = jnp.sum(jnp.where(place, positives[None], 0), axis=(1, 2))
        owner_of = jnp.where(live, slots // cap, -1)
        out = dot(pick, feats).astype(BF16).reshape(n_labels, n_data, cap, width)
        meta = jnp.stack([owner_of, block_of, wanted], axis=1).reshape(n_labels, n_data, cap, 3)
        tile = 128
        got = swap(out).reshape(slot_total // tile, tile, width)
        got_meta = swap(meta).reshape(slot_total // tile, tile, 3).transpose(0, 2, 1)
        sources = [
            with_meta(got[i], got_meta[i, 0:1], got_meta[i, 1:2], got_meta[i, 2:3])
            for i in range(slot_total // tile)
        ]
        work = [
            pair_work(where, sources[i : i + n_data], shards, label_weight, tile, 1)
            for i in range(0, len(sources), n_data)
        ]
        back = jnp.stack([part for run in work for part in run[:2]])
        back = back.reshape(-1, 2, n_data // 2, tile, width).transpose(0, 2, 1, 3, 4)
        back = swap(back.reshape(n_labels, n_data, cap, width)).reshape(slot_total, width)
        grad_feats = dot(pick, back, 0, 0).astype(BF16)

    _, _, grad_scores, block_of, embedding, picked, grad_hidden = zip(*work)
    even, odd = enc_work(where, picked, grad_hidden, enc_weight, n_data)
    grad_label = grad_label_work(grad_scores, block_of, embedding, label_weight)
    grad_enc = reduce_dp(even, odd)
    for mask in masks(n_labels):
        grad_enc = add(grad_enc, partner(grad_enc.astype(BF16), "labels", mask))
    return (grad_feats, grad_label, grad_enc)


def solution(mesh):
    rows = P(("groups", "labels", "dp"), None)
    return jax.shard_map(
        local,
        mesh=mesh,
        in_specs=(rows, P("dp", None), rows, rows, rows, rows),
        out_specs=(rows, rows, P(("groups", "dp"), None)),
        check_vma=False,
    )
```

```python
import functools

import jax
import jax.numpy as jnp
from jax import lax
from jax.experimental import pallas as pl
from jax.experimental.pallas import tpu as pltpu
from jax.sharding import PartitionSpec as P

BLK = 128
EPSILON = 1e-06
META_ROWS = 8
F32 = jnp.float32
BF16 = jnp.bfloat16


def dot(a, b, da=1, db=0):
    return lax.dot_general(a, b, (((da,), (db,)), ((), ())), preferred_element_type=F32)


def pair_kernel(where_ref, *refs, cap, pick_count):
    n_data = (len(refs) - 9) // 2
    sources, shards, label_ref = refs[:n_data], refs[n_data : 2 * n_data], refs[2 * n_data]
    even_ref, odd_ref, grad_scores_ref, block_ref, embedding_ref, feats_ref, grad_hidden_ref, enc = (
        refs[2 * n_data + 1 :]
    )
    me = where_ref[0].astype(F32)
    my_data = where_ref[1]
    rows = sources[0].shape[0] - META_ROWS
    shard_rows = shards[0].shape[0]
    n_blocks = label_ref.shape[0] // BLK
    slots = n_data * cap

    for m in range(n_data):
        enc[shard_at(my_data, m, shard_rows), :] = shards[m][...]

    row_id = lax.broadcasted_iota(jnp.int32, (rows, rows), 0)
    col_id = lax.broadcasted_iota(jnp.int32, (rows, rows), 1)
    before = (row_id < col_id).astype(BF16)
    slot_id = lax.broadcasted_iota(jnp.int32, (cap, rows), 0).astype(F32)
    column = lax.broadcasted_iota(jnp.int32, (slots, BLK), 1)

    hits, codes = [], []
    for source in sources:
        meta = source[rows:, 0 : 3 * rows].astype(F32)[:pick_count]
        named = meta[:, :rows] == me
        hits.append(jnp.sum(named.astype(F32), axis=0, keepdims=True))
        code = meta[:, rows : 2 * rows] * 256.0 + meta[:, 2 * rows :] + 1.0
        codes.append(jnp.sum(jnp.where(named, code, 0.0), axis=0, keepdims=True))
    rank = dot(jnp.concatenate(hits, axis=0).astype(BF16), before)

    picks, picked, slot_codes = [], [], []
    for s, source in enumerate(sources):
        pick = jnp.where((slot_id == rank[s : s + 1]) & (hits[s] > 0.0), 1.0, 0.0)
        slot_codes.append(jnp.sum(pick * codes[s], axis=1, keepdims=True))
        pick = pick.astype(BF16)
        picks.append(pick)
        picked.append(dot(pick, source[:rows, :]).astype(BF16))
    feats = jnp.concatenate(picked, axis=0)
    feats_ref[...] = feats
    code = jnp.concatenate(slot_codes, axis=0).astype(jnp.int32) - 1

    hidden = dot(feats, enc[...])
    inv_rms = lax.rsqrt(jnp.mean(hidden * hidden, axis=-1, keepdims=True) + EPSILON)
    embedding = (hidden * inv_rms).astype(BF16)
    embedding_ref[...] = embedding

    scores = dot(embedding, label_ref[...], 1, 1)
    block = jnp.broadcast_to(code >> 8, (slots, BLK))
    block_ref[...] = block
    wanted = jnp.broadcast_to(code & 255, (slots, BLK))
    own_scores = jnp.zeros((slots, BLK), F32)
    for b in range(n_blocks):
        own_scores = jnp.where(block == b, scores[:, b * BLK : (b + 1) * BLK], own_scores)
    target = jnp.where(column == wanted, 1.0, 0.0)
    grad_scores = jnp.where(block >= 0, jax.nn.sigmoid(own_scores) - target, 0.0)
    grad_scores_ref[...] = grad_scores

    spread = jnp.concatenate(
        [jnp.where(block == b, grad_scores, 0.0).astype(BF16) for b in range(n_blocks)], axis=1
    )
    grad_pair = dot(spread, label_ref[...]).astype(BF16).astype(F32)
    projection = jnp.mean(hidden * grad_pair, axis=-1, keepdims=True)
    grad_hidden = (inv_rms * grad_pair - hidden * (inv_rms**3 * projection)).astype(BF16)
    grad_hidden_ref[...] = grad_hidden
    grad_feats = dot(grad_hidden, enc[...], 1, 1).astype(BF16)
    for m in range(n_data):
        part = dot(picks[m], grad_feats[m * cap : (m + 1) * cap], 0, 0)
        (odd_ref if m % 2 else even_ref)[m // 2] = part.astype(BF16)


def enc_kernel(where_ref, *refs):
    runs = (len(refs) - 3) // 2
    even_ref, odd_ref, total = refs[2 * runs :]
    feats = jnp.concatenate([r[...] for r in refs[:runs]], axis=0)
    grad_hidden = jnp.concatenate([r[...] for r in refs[runs : 2 * runs]], axis=0)
    total[...] = dot(feats, grad_hidden, 0, 0)
    half, shard_rows, _ = even_ref.shape
    for m in range(2 * half):
        part = total[shard_at(where_ref[1], m, shard_rows), :]
        (odd_ref if m % 2 else even_ref)[m // 2] = part.astype(BF16)


def grad_label_kernel(*refs):
    runs = (len(refs) - 1) // 3
    grad_scores, blocks, embeddings = refs[:runs], refs[runs : 2 * runs], refs[2 * runs : 3 * runs]
    out_ref = refs[-1]
    grad_scores_t = jnp.concatenate([r[...].T for r in grad_scores], axis=1)
    block_t = jnp.concatenate([r[...].T for r in blocks], axis=1)
    embedding = jnp.concatenate([r[...] for r in embeddings], axis=0)
    for b in range(out_ref.shape[0] // BLK):
        spread_t = jnp.where(block_t == b, grad_scores_t, 0.0).astype(BF16)
        out_ref[b * BLK : (b + 1) * BLK, :] = dot(spread_t, embedding).astype(BF16)


def shard_at(my_data, m, shard_rows):
    at = jnp.bitwise_xor(my_data, m) * shard_rows
    return pl.ds(pl.multiple_of(at, 16), shard_rows)


def call(kernel, name, out_shape, scratch, flops, megabytes, *args):
    smem = pl.BlockSpec(memory_space=pltpu.SMEM)
    vmem = pl.BlockSpec(memory_space=pltpu.VMEM)
    return pl.pallas_call(
        kernel,
        in_specs=[smem if a.ndim == 1 else vmem for a in args],
        out_specs=jax.tree.map(lambda _: vmem, out_shape),
        out_shape=out_shape,
        scratch_shapes=scratch,
        compiler_params=pltpu.CompilerParams(vmem_limit_bytes=24 << 20),
        cost_estimate=pl.CostEstimate(
            flops=flops, bytes_accessed=megabytes << 20, transcendentals=0
        ),
        name=name,
    )(*args)


def pair_work(where, sources, shards, label_weight, cap, pick_count):
    n_data = len(sources)
    rows, width = sources[0].shape[0] - META_ROWS, sources[0].shape[1]
    slots = n_data * cap
    return call(
        functools.partial(pair_kernel, cap=cap, pick_count=pick_count),
        "pair_work",
        [jax.ShapeDtypeStruct((n_data // 2, rows, width), BF16)] * 2
        + [
            jax.ShapeDtypeStruct((slots, BLK), F32),
            jax.ShapeDtypeStruct((slots, BLK), jnp.int32),
        ]
        + [jax.ShapeDtypeStruct((slots, width), BF16)] * 3,
        [pltpu.VMEM((n_data * shards[0].shape[0], width), BF16)],
        2 * slots * width * (2 * label_weight.shape[0] + 2 * width + 2 * rows),
        8,
        where,
        *sources,
        *shards,
        label_weight,
    )


def enc_work(where, feats, grad_hidden, shard, n_data):
    shard_rows, width = shard.shape
    return call(
        enc_kernel,
        "enc_work",
        [jax.ShapeDtypeStruct((n_data // 2, shard_rows, width), BF16)] * 2,
        [pltpu.VMEM((n_data * shard_rows, width), F32)],
        2 * len(feats) * feats[0].shape[0] * width * width,
        4,
        where,
        *feats,
        *grad_hidden,
    )


def grad_label_work(grad_scores, blocks, embeddings, label_weight):
    return call(
        grad_label_kernel,
        "grad_label_work",
        jax.ShapeDtypeStruct(label_weight.shape, BF16),
        [],
        2 * len(blocks) * blocks[0].shape[0] * label_weight.size,
        4,
        *grad_scores,
        *blocks,
        *embeddings,
    )


def swap(x):
    x = lax.all_to_all(x, "labels", split_axis=0, concat_axis=0, tiled=True)
    return lax.all_to_all(x, "dp", split_axis=1, concat_axis=1, tiled=True)


def partner(x, axis, mask):
    return lax.ppermute(x, axis, [(i, i ^ mask) for i in range(lax.axis_size(axis))])


def shifted(x, axis, by):
    n = lax.axis_size(axis)
    return lax.ppermute(x, axis, [(i, (i + by) % n) for i in range(n)])


def masks(n):
    return [1 << i for i in range(n.bit_length() - 1)]


def after(x, *others):
    return lax.optimization_barrier((x, *others))[0]


def gather_dp(x, first=None):
    got = {0: x}
    for mask in reversed(masks(lax.axis_size("dp"))):
        for m, v in list(got.items()):
            if first is not None and mask == 1 and m:
                v = after(v, first)
            got[m | mask] = partner(v, "dp", mask)
    return [got[m] for m in range(len(got))]


def add(*terms):
    return sum(t.astype(F32) for t in terms)


def reduce_dp(even, odd):
    got = partner(odd, "dp", 1)
    terms = [[even[i], got[i]] for i in range(even.shape[0])]
    for mask in masks(len(terms)):
        for i in range(len(terms)):
            if i & mask == 0 and i % mask == 0:
                terms[i].append(partner(add(*terms[i | mask]).astype(BF16), "dp", 2 * mask))
    return add(*terms[0])


def sum_labels(x):
    half = x.shape[0] // 2
    odd = lax.axis_index("labels") & 1
    cut = lambda p: lax.dynamic_slice_in_dim(x, p * half, half, 0)
    x = add(cut(odd), partner(cut(1 - odd).astype(BF16), "labels", 1)).astype(BF16)
    for mask in masks(lax.axis_size("labels"))[1:]:
        x = add(x, partner(x, "labels", mask)).astype(BF16)
    other = partner(x, "labels", 1)
    low, high = jnp.where(odd == 0, x, other), jnp.where(odd == 0, other, x)
    return jnp.concatenate([low, high], axis=0).astype(F32)


def with_meta(feats, owner_rows, block_rows, positive_rows):
    meta = jnp.concatenate([owner_rows, block_rows, positive_rows], axis=1).astype(BF16)
    meta = jnp.pad(meta, ((0, META_ROWS - meta.shape[0]), (0, feats.shape[1] - meta.shape[1])))
    return jnp.concatenate([feats, meta], axis=0)


def local(feats, enc_weight, label_weight, owners, blocks, positives):
    n_labels = lax.axis_size("labels")
    n_data = lax.axis_size("dp")
    n_owner = n_labels * n_data
    row_count, width = feats.shape
    pick_count = owners.shape[1]
    cap = max(2, 2 * row_count * pick_count // n_owner)
    my_data = lax.axis_index("dp")
    where = jnp.stack([lax.axis_index("labels") * n_data + my_data, my_data]).astype(jnp.int32)
    shards = gather_dp(enc_weight)

    if row_count <= n_data * cap:
        own = with_meta(feats, owners.T, blocks.T, positives.T)
        rows_of = [own]
        for _ in range(1, n_labels):
            rows_of.append(shifted(rows_of[-1], "labels", 1))
        work = []
        for by in range(n_labels):
            run = gather_dp(rows_of[by], work[-1][0] if work else None)
            if by + 2 < n_labels:
                run[0] = after(run[0], rows_of[by + 2])
            work.append(pair_work(where, run, shards, label_weight, cap, pick_count))
        total = []
        for by in range(n_labels):
            part = reduce_dp(work[by][0], work[by][1])
            total.append(part if by == 0 else shifted(part.astype(BF16), "labels", -by))
        grad_feats = add(*total).astype(BF16)
    else:
        flat = owners.reshape(-1)
        onehot = (flat[:, None] == jnp.arange(n_owner, dtype=jnp.int32)[None, :]).astype(jnp.int32)
        rank = jnp.sum((jnp.cumsum(onehot, axis=0) - onehot) * onehot, axis=1)
        slot = (flat * cap + rank).reshape(row_count, pick_count)
        slot_total = n_owner * cap
        slots = jnp.arange(slot_total, dtype=jnp.int32)
        place = slots[:, None, None] == slot[None]
        pick = jnp.any(place, axis=2).astype(BF16)
        live = jnp.any(place, axis=(1, 2))
        block_of = jnp.sum(jnp.where(place, blocks[None], 0), axis=(1, 2))
        wanted = jnp.sum(jnp.where(place, positives[None], 0), axis=(1, 2))
        owner_of = jnp.where(live, slots // cap, -1)
        out = dot(pick, feats).astype(BF16).reshape(n_labels, n_data, cap, width)
        meta = jnp.stack([owner_of, block_of, wanted], axis=1).reshape(n_labels, n_data, cap, 3)
        tile = 128
        got = swap(out).reshape(slot_total // tile, tile, width)
        got_meta = swap(meta).reshape(slot_total // tile, tile, 3).transpose(0, 2, 1)
        sources = [
            with_meta(got[i], got_meta[i, 0:1], got_meta[i, 1:2], got_meta[i, 2:3])
            for i in range(slot_total // tile)
        ]
        work = [
            pair_work(where, sources[i : i + n_data], shards, label_weight, tile, 1)
            for i in range(0, len(sources), n_data)
        ]
        back = jnp.stack([part for run in work for part in run[:2]])
        back = back.reshape(-1, 2, n_data // 2, tile, width).transpose(0, 2, 1, 3, 4)
        back = swap(back.reshape(n_labels, n_data, cap, width)).reshape(slot_total, width)
        grad_feats = dot(pick, back, 0, 0).astype(BF16)

    _, _, grad_scores, block_of, embedding, picked, grad_hidden = zip(*work)
    even, odd = enc_work(where, picked, grad_hidden, enc_weight, n_data)
    share = reduce_dp(even, odd)
    embedding = (after(embedding[0], share),) + embedding[1:]
    grad_label = grad_label_work(grad_scores, block_of, embedding, label_weight)
    grad_enc = sum_labels(share)
    return (grad_feats, grad_label, grad_enc)


def solution(mesh):
    rows = P(("groups", "labels", "dp"), None)
    return jax.shard_map(
        local,
        mesh=mesh,
        in_specs=(rows, P("dp", None), rows, rows, rows, rows),
        out_specs=(rows, rows, P(("groups", "dp"), None)),
        check_vma=False,
    )
```

```python
import functools

import jax
import jax.numpy as jnp
from jax import lax
from jax.experimental import pallas as pl
from jax.experimental.pallas import tpu as pltpu
from jax.sharding import PartitionSpec as P

BLK = 128
EPSILON = 1e-06
META_ROWS = 8
F32 = jnp.float32
BF16 = jnp.bfloat16


def dot(a, b, da=1, db=0):
    return lax.dot_general(a, b, (((da,), (db,)), ((), ())), preferred_element_type=F32)


def pair_kernel(where_ref, *refs, cap, pick_count, n_data, prior):
    it = iter(refs)
    take = lambda n: [next(it) for _ in range(n)]
    last = prior is not None
    source_in, shard_in, label_in = take(n_data), take(n_data), next(it)
    prior_in = take(2 * prior if last else 0)
    outs = take(9 if last else 7)
    src, enc, label = take(3)
    results = take(9 if last else 7)
    in_sem, out_sem = take(2)
    all_feats, all_grad_hidden, total = take(3) if last else [None] * 3
    even, odd, grad_scores_v, block_v, embedding_v, feats_v, grad_hidden_v = results[:7]

    me = where_ref[0].astype(F32)
    my_data = where_ref[1]
    rows = src.shape[1] - META_ROWS
    shard_rows = shard_in[0].shape[0]
    n_blocks = label.shape[0] // BLK
    slots = n_data * cap

    pairs = [(ref, src.at[m]) for m, ref in enumerate(source_in)]
    pairs += [(ref, enc.at[shard_at(my_data, m, shard_rows)]) for m, ref in enumerate(shard_in)]
    pairs += [(label_in, label)]
    for i in range(len(prior_in) // 2):
        at = pl.ds(i * slots, slots)
        pairs += [(prior_in[i], all_feats.at[at]), (prior_in[prior + i], all_grad_hidden.at[at])]
    fetch = [pltpu.make_async_copy(a, b, in_sem.at[i]) for i, (a, b) in enumerate(pairs)]
    for copy in fetch:
        copy.start()
    store = [pltpu.make_async_copy(a, b, out_sem.at[i]) for i, (a, b) in enumerate(zip(results, outs))]

    row_id = lax.broadcasted_iota(jnp.int32, (rows, rows), 0)
    col_id = lax.broadcasted_iota(jnp.int32, (rows, rows), 1)
    before = (row_id < col_id).astype(BF16)
    slot_id = lax.broadcasted_iota(jnp.int32, (cap, rows), 0).astype(F32)
    column = lax.broadcasted_iota(jnp.int32, (slots, BLK), 1)

    hits, codes = [], []
    for m in range(n_data):
        fetch[m].wait()
        meta = src[m, rows:, 0 : 3 * rows].astype(F32)[:pick_count]
        named = meta[:, :rows] == me
        hits.append(jnp.sum(named.astype(F32), axis=0, keepdims=True))
        code = meta[:, rows : 2 * rows] * 256.0 + meta[:, 2 * rows :] + 1.0
        codes.append(jnp.sum(jnp.where(named, code, 0.0), axis=0, keepdims=True))
    rank = dot(jnp.concatenate(hits, axis=0).astype(BF16), before)

    picks, picked, slot_codes = [], [], []
    for m in range(n_data):
        pick = jnp.where((slot_id == rank[m : m + 1]) & (hits[m] > 0.0), 1.0, 0.0)
        slot_codes.append(jnp.sum(pick * codes[m], axis=1, keepdims=True))
        pick = pick.astype(BF16)
        picks.append(pick)
        picked.append(dot(pick, src[m, :rows, :]).astype(BF16))
    feats = jnp.concatenate(picked, axis=0)
    feats_v[...] = feats
    store[5].start()
    code = jnp.concatenate(slot_codes, axis=0).astype(jnp.int32) - 1

    for m in range(n_data):
        fetch[n_data + m].wait()
    hidden = dot(feats, enc[...])
    inv_rms = lax.rsqrt(jnp.mean(hidden * hidden, axis=-1, keepdims=True) + EPSILON)
    embedding = (hidden * inv_rms).astype(BF16)
    embedding_v[...] = embedding
    store[4].start()

    fetch[2 * n_data].wait()
    scores = dot(embedding, label[...], 1, 1)
    block = jnp.broadcast_to(code >> 8, (slots, BLK))
    block_v[...] = block
    store[3].start()
    wanted = jnp.broadcast_to(code & 255, (slots, BLK))
    own_scores = jnp.zeros((slots, BLK), F32)
    for b in range(n_blocks):
        own_scores = jnp.where(block == b, scores[:, b * BLK : (b + 1) * BLK], own_scores)
    target = jnp.where(column == wanted, 1.0, 0.0)
    grad_scores = jnp.where(block >= 0, jax.nn.sigmoid(own_scores) - target, 0.0)
    grad_scores_v[...] = grad_scores
    store[2].start()

    spread = jnp.concatenate(
        [jnp.where(block == b, grad_scores, 0.0).astype(BF16) for b in range(n_blocks)], axis=1
    )
    grad_pair = dot(spread, label[...]).astype(BF16).astype(F32)
    projection = jnp.mean(hidden * grad_pair, axis=-1, keepdims=True)
    grad_hidden = (inv_rms * grad_pair - hidden * (inv_rms**3 * projection)).astype(BF16)
    grad_hidden_v[...] = grad_hidden
    store[6].start()

    if last:
        at = pl.ds(prior * slots, slots)
        all_feats[at, :] = feats
        all_grad_hidden[at, :] = grad_hidden
        for copy in fetch[2 * n_data + 1 :]:
            copy.wait()
        total[...] = dot(all_feats[...], all_grad_hidden[...], 0, 0)
        for m in range(n_data):
            part = total[shard_at(my_data, m, shard_rows), :]
            results[7 + m % 2][m // 2] = part.astype(BF16)
        store[7].start()
        store[8].start()

    grad_feats = dot(grad_hidden, enc[...], 1, 1).astype(BF16)
    for m in range(n_data):
        part = dot(picks[m], grad_feats[m * cap : (m + 1) * cap], 0, 0)
        results[m % 2][m // 2] = part.astype(BF16)
    store[0].start()
    store[1].start()
    for copy in store:
        copy.wait()


def grad_label_kernel(*refs, runs):
    ins, out_ref, scratch, sem = refs[: 3 * runs], refs[3 * runs], refs[3 * runs + 1 : -1], refs[-1]
    slots = ins[0].shape[0]
    fetch = []
    for i, ref in enumerate(ins):
        target = scratch[i // runs].at[pl.ds(i % runs * slots, slots)]
        fetch.append(pltpu.make_async_copy(ref, target, sem.at[i]))
        fetch[-1].start()
    for copy in fetch:
        copy.wait()
    grad_scores_t, block_t, embedding = scratch[0][...].T, scratch[1][...].T, scratch[2][...]
    for b in range(out_ref.shape[0] // BLK):
        spread_t = jnp.where(block_t == b, grad_scores_t, 0.0).astype(BF16)
        out_ref[b * BLK : (b + 1) * BLK, :] = dot(spread_t, embedding).astype(BF16)


def shard_at(my_data, m, shard_rows):
    at = jnp.bitwise_xor(my_data, m) * shard_rows
    return pl.ds(pl.multiple_of(at, 16), shard_rows)


def call(kernel, name, out_spec, out_shape, scratch, flops, megabytes, *args):
    smem = pl.BlockSpec(memory_space=pltpu.SMEM)
    anywhere = pl.BlockSpec(memory_space=pl.ANY)
    return pl.pallas_call(
        kernel,
        in_specs=[smem if a.ndim == 1 else anywhere for a in args],
        out_specs=jax.tree.map(lambda _: pl.BlockSpec(memory_space=out_spec), out_shape),
        out_shape=out_shape,
        scratch_shapes=scratch,
        compiler_params=pltpu.CompilerParams(vmem_limit_bytes=32 << 20),
        cost_estimate=pl.CostEstimate(
            flops=flops, bytes_accessed=megabytes << 20, transcendentals=0
        ),
        name=name,
    )(*args)


def pair_work(where, sources, shards, label_weight, cap, pick_count, prior=None):
    n_data = len(sources)
    block_rows, width = sources[0].shape
    rows = block_rows - META_ROWS
    slots = n_data * cap
    shard_rows = shards[0].shape[0]
    shapes = [((n_data // 2, rows, width), BF16)] * 2 + [((slots, BLK), F32)]
    shapes += [((slots, BLK), jnp.int32)] + [((slots, width), BF16)] * 3
    scratch, more = [], []
    if prior is not None:
        shapes += [((n_data // 2, shard_rows, width), BF16)] * 2
        more = [run[5] for run in prior] + [run[6] for run in prior]
        scratch = [pltpu.VMEM(((len(prior) + 1) * slots, width), BF16)] * 2
        scratch += [pltpu.VMEM((n_data * shard_rows, width), F32)]
    return call(
        functools.partial(
            pair_kernel,
            cap=cap,
            pick_count=pick_count,
            n_data=n_data,
            prior=None if prior is None else len(prior),
        ),
        "pair_work",
        pl.ANY,
        [jax.ShapeDtypeStruct(*shape) for shape in shapes],
        [
            pltpu.VMEM((n_data, block_rows, width), BF16),
            pltpu.VMEM((n_data * shard_rows, width), BF16),
            pltpu.VMEM(label_weight.shape, BF16),
        ]
        + [pltpu.VMEM(*shape) for shape in shapes]
        + [
            pltpu.SemaphoreType.DMA((2 * n_data + 1 + len(more),)),
            pltpu.SemaphoreType.DMA((len(shapes),)),
        ]
        + scratch,
        2 * slots * width * (2 * label_weight.shape[0] + 2 * width + 2 * rows),
        6,
        where,
        *sources,
        *shards,
        label_weight,
        *more,
    )


def grad_label_work(grad_scores, blocks, embeddings, label_weight):
    runs, slots = len(blocks), blocks[0].shape[0]
    return call(
        functools.partial(grad_label_kernel, runs=runs),
        "grad_label_work",
        pltpu.VMEM,
        jax.ShapeDtypeStruct(label_weight.shape, BF16),
        [
            pltpu.VMEM((runs * slots, BLK), F32),
            pltpu.VMEM((runs * slots, BLK), jnp.int32),
            pltpu.VMEM((runs * slots, label_weight.shape[1]), BF16),
            pltpu.SemaphoreType.DMA((3 * runs,)),
        ],
        2 * runs * slots * label_weight.size,
        4,
        *grad_scores,
        *blocks,
        *embeddings,
    )


def swap(x):
    x = lax.all_to_all(x, "labels", split_axis=0, concat_axis=0, tiled=True)
    return lax.all_to_all(x, "dp", split_axis=1, concat_axis=1, tiled=True)


def partner(x, axis, mask):
    return lax.ppermute(x, axis, [(i, i ^ mask) for i in range(lax.axis_size(axis))])


def masks(n):
    return [1 << i for i in range(n.bit_length() - 1)]


def after(x, *others):
    return lax.optimization_barrier((x, *others))[0]


def gather_dp(x, first=None):
    got = {0: x}
    *far, near = reversed(masks(lax.axis_size("dp")))
    for mask in far:
        got.update({m | mask: partner(v, "dp", mask) for m, v in list(got.items())})
    for m, v in sorted(got.items(), reverse=True):
        if m:
            v = v if first is None else after(v, first)
        elif len(got) > 1:
            v = after(v, got[max(i for i in got if i & near == 0)])
        got[m | near] = partner(v, "dp", near)
    return [got[m] for m in range(len(got))]


def gather_labels(x):
    got = {0: x}
    for mask in reversed(masks(lax.axis_size("labels"))):
        got.update({m | mask: partner(v, "labels", mask) for m, v in list(got.items())})
    return [got[m] for m in range(len(got))]


def add(*terms):
    return sum(t.astype(F32) for t in terms)


def reduce_dp(even, odd):
    got = partner(odd, "dp", 1)
    terms = [[even[i], got[i]] for i in range(even.shape[0])]
    for mask in masks(len(terms)):
        for i in range(len(terms)):
            if i & mask == 0 and i % mask == 0:
                terms[i].append(partner(add(*terms[i | mask]).astype(BF16), "dp", 2 * mask))
    return add(*terms[0])


def sum_labels(x):
    half = x.shape[0] // 2
    odd = lax.axis_index("labels") & 1
    cut = lambda p: lax.dynamic_slice_in_dim(x, p * half, half, 0)
    x = add(cut(odd), partner(cut(1 - odd).astype(BF16), "labels", 1)).astype(BF16)
    for mask in masks(lax.axis_size("labels"))[1:]:
        x = add(x, partner(x, "labels", mask)).astype(BF16)
    other = partner(x, "labels", 1)
    low, high = jnp.where(odd == 0, x, other), jnp.where(odd == 0, other, x)
    return jnp.concatenate([low, high], axis=0).astype(F32)


def reduce_labels(parts):
    terms = [[part] for part in parts]
    for mask in masks(len(terms)):
        for i in range(len(terms)):
            if i & mask == 0 and i % mask == 0:
                terms[i].append(partner(add(*terms[i | mask]).astype(BF16), "labels", mask))
    return add(*terms[0])


def with_meta(feats, owner_rows, block_rows, positive_rows):
    meta = jnp.concatenate([owner_rows, block_rows, positive_rows], axis=1).astype(BF16)
    meta = jnp.pad(meta, ((0, META_ROWS - meta.shape[0]), (0, feats.shape[1] - meta.shape[1])))
    return jnp.concatenate([feats, meta], axis=0)


def local(feats, enc_weight, label_weight, owners, blocks, positives):
    n_labels = lax.axis_size("labels")
    n_data = lax.axis_size("dp")
    n_owner = n_labels * n_data
    row_count, width = feats.shape
    pick_count = owners.shape[1]
    cap = max(2, 2 * row_count * pick_count // n_owner)
    my_data = lax.axis_index("dp")
    where = jnp.stack([lax.axis_index("labels") * n_data + my_data, my_data]).astype(jnp.int32)
    shards = gather_dp(enc_weight)

    if row_count <= n_data * cap:
        own = with_meta(feats, owners.T, blocks.T, positives.T)
        rows_of = gather_labels(own)
        work = []
        for by in range(n_labels):
            run = gather_dp(rows_of[by], work[-1][0] if work else None)
            if by + 1 < n_labels:
                run[0] = after(run[0], *rows_of[by + 1 : by + 3])
            prior = work if by == n_labels - 1 else None
            work.append(pair_work(where, run, shards, label_weight, cap, pick_count, prior))
        grad_feats = reduce_labels([reduce_dp(*run[:2]) for run in work]).astype(BF16)
    else:
        flat = owners.reshape(-1)
        onehot = (flat[:, None] == jnp.arange(n_owner, dtype=jnp.int32)[None, :]).astype(jnp.int32)
        rank = jnp.sum((jnp.cumsum(onehot, axis=0) - onehot) * onehot, axis=1)
        slot = (flat * cap + rank).reshape(row_count, pick_count)
        slot_total = n_owner * cap
        slots = jnp.arange(slot_total, dtype=jnp.int32)
        place = slots[:, None, None] == slot[None]
        pick = jnp.any(place, axis=2).astype(BF16)
        live = jnp.any(place, axis=(1, 2))
        block_of = jnp.sum(jnp.where(place, blocks[None], 0), axis=(1, 2))
        wanted = jnp.sum(jnp.where(place, positives[None], 0), axis=(1, 2))
        owner_of = jnp.where(live, slots // cap, -1)
        out = dot(pick, feats).astype(BF16).reshape(n_labels, n_data, cap, width)
        meta = jnp.stack([owner_of, block_of, wanted], axis=1).reshape(n_labels, n_data, cap, 3)
        tile = 128
        got = swap(out).reshape(slot_total // tile, tile, width)
        got_meta = swap(meta).reshape(slot_total // tile, tile, 3).transpose(0, 2, 1)
        sources = [
            with_meta(got[i], got_meta[i, 0:1], got_meta[i, 1:2], got_meta[i, 2:3])
            for i in range(slot_total // tile)
        ]
        work = []
        for i in range(0, len(sources), n_data):
            prior = work if i + n_data == len(sources) else None
            run = sources[i : i + n_data]
            work.append(pair_work(where, run, shards, label_weight, tile, 1, prior))
        back = jnp.stack([part for run in work for part in run[:2]])
        back = back.reshape(-1, 2, n_data // 2, tile, width).transpose(0, 2, 1, 3, 4)
        back = swap(back.reshape(n_labels, n_data, cap, width)).reshape(slot_total, width)
        grad_feats = dot(pick, back, 0, 0).astype(BF16)

    _, _, grad_scores, block_of, embedding, _, _ = zip(*(run[:7] for run in work))
    share = reduce_dp(*work[-1][7:])
    embedding = (after(embedding[0], share),) + embedding[1:]
    grad_label = grad_label_work(grad_scores, block_of, embedding, label_weight)
    grad_enc = sum_labels(share)
    return (grad_feats, grad_label, grad_enc)


def solution(mesh):
    rows = P(("groups", "labels", "dp"), None)
    return jax.shard_map(
        local,
        mesh=mesh,
        in_specs=(rows, P("dp", None), rows, rows, rows, rows),
        out_specs=(rows, rows, P(("groups", "dp"), None)),
        check_vma=False,
    )
```

```python
import functools

import jax
import jax.numpy as jnp
from jax import lax
from jax.experimental import pallas as pl
from jax.experimental.pallas import tpu as pltpu
from jax.sharding import PartitionSpec as P

BLK = 128
EPSILON = 1e-06
META_ROWS = 8
F32 = jnp.float32
BF16 = jnp.bfloat16


def dot(a, b, da=1, db=0):
    return lax.dot_general(a, b, (((da,), (db,)), ((), ())), preferred_element_type=F32)


def pair_kernel(*refs, cap, pick_count, n_data, prior):
    it = iter(refs)
    take = lambda n: [next(it) for _ in range(n)]
    last = prior is not None
    sources, shards, label = take(n_data), take(n_data), next(it)
    prior_refs = take(2 * prior if last else 0)
    even_ref, odd_ref, grad_scores_ref, block_ref, embedding_ref, feats_ref, grad_hidden_ref = take(7)
    share_refs = take(2 if last else 0)
    enc = next(it)

    my_data = lax.axis_index("dp")
    me = (lax.axis_index("labels") * n_data + my_data).astype(F32)
    rows = sources[0].shape[0] - META_ROWS
    shard_rows = shards[0].shape[0]
    n_blocks = label.shape[0] // BLK
    slots = n_data * cap

    for m in range(n_data):
        enc[shard_at(my_data, m, shard_rows), :] = shards[m][...]

    row_id = lax.broadcasted_iota(jnp.int32, (rows, rows), 0)
    col_id = lax.broadcasted_iota(jnp.int32, (rows, rows), 1)
    before = (row_id < col_id).astype(BF16)
    slot_id = lax.broadcasted_iota(jnp.int32, (cap, rows), 0).astype(F32)
    column = lax.broadcasted_iota(jnp.int32, (slots, BLK), 1)

    hits, codes = [], []
    for source in sources:
        meta = source[rows:, 0 : 3 * rows].astype(F32)[:pick_count]
        named = meta[:, :rows] == me
        hits.append(jnp.sum(named.astype(F32), axis=0, keepdims=True))
        code = meta[:, rows : 2 * rows] * 256.0 + meta[:, 2 * rows :] + 1.0
        codes.append(jnp.sum(jnp.where(named, code, 0.0), axis=0, keepdims=True))
    rank = dot(jnp.concatenate(hits, axis=0).astype(BF16), before)

    picks, picked, slot_codes = [], [], []
    for m, source in enumerate(sources):
        pick = jnp.where((slot_id == rank[m : m + 1]) & (hits[m] > 0.0), 1.0, 0.0)
        slot_codes.append(jnp.sum(pick * codes[m], axis=1, keepdims=True))
        pick = pick.astype(BF16)
        picks.append(pick)
        picked.append(dot(pick, source[:rows, :]).astype(BF16))
    feats = jnp.concatenate(picked, axis=0)
    feats_ref[...] = feats
    code = jnp.concatenate(slot_codes, axis=0).astype(jnp.int32) - 1

    hidden = dot(feats, enc[...])
    inv_rms = lax.rsqrt(jnp.mean(hidden * hidden, axis=-1, keepdims=True) + EPSILON)
    embedding = (hidden * inv_rms).astype(BF16)
    embedding_ref[...] = embedding

    scores = dot(embedding, label[...], 1, 1)
    block = jnp.broadcast_to(code >> 8, (slots, BLK))
    block_ref[...] = block
    wanted = jnp.broadcast_to(code & 255, (slots, BLK))
    own_scores = jnp.zeros((slots, BLK), F32)
    for b in range(n_blocks):
        own_scores = jnp.where(block == b, scores[:, b * BLK : (b + 1) * BLK], own_scores)
    target = jnp.where(column == wanted, 1.0, 0.0)
    grad_scores = jnp.where(block >= 0, jax.nn.sigmoid(own_scores) - target, 0.0)
    grad_scores_ref[...] = grad_scores

    spread = jnp.concatenate(
        [jnp.where(block == b, grad_scores, 0.0).astype(BF16) for b in range(n_blocks)], axis=1
    )
    grad_pair = dot(spread, label[...]).astype(BF16).astype(F32)
    projection = jnp.mean(hidden * grad_pair, axis=-1, keepdims=True)
    grad_hidden = (inv_rms * grad_pair - hidden * (inv_rms**3 * projection)).astype(BF16)
    grad_hidden_ref[...] = grad_hidden

    if last:
        total = next(it)
        all_feats = jnp.concatenate([r[...] for r in prior_refs[:prior]] + [feats], axis=0)
        all_grads = jnp.concatenate([r[...] for r in prior_refs[prior:]] + [grad_hidden], axis=0)
        total[...] = dot(all_feats, all_grads, 0, 0)
        for m in range(n_data):
            part = total[shard_at(my_data, m, shard_rows), :]
            share_refs[m % 2][m // 2] = part.astype(BF16)

    grad_feats = dot(grad_hidden, enc[...], 1, 1).astype(BF16)
    for m in range(n_data):
        part = dot(picks[m], grad_feats[m * cap : (m + 1) * cap], 0, 0)
        (odd_ref if m % 2 else even_ref)[m // 2] = part.astype(BF16)


def grad_label_kernel(*refs):
    runs = (len(refs) - 1) // 3
    grad_scores, blocks, embeddings = refs[:runs], refs[runs : 2 * runs], refs[2 * runs : 3 * runs]
    out_ref = refs[-1]
    grad_scores_t = jnp.concatenate([r[...].T for r in grad_scores], axis=1)
    block_t = jnp.concatenate([r[...].T for r in blocks], axis=1)
    embedding = jnp.concatenate([r[...] for r in embeddings], axis=0)
    for b in range(out_ref.shape[0] // BLK):
        spread_t = jnp.where(block_t == b, grad_scores_t, 0.0).astype(BF16)
        out_ref[b * BLK : (b + 1) * BLK, :] = dot(spread_t, embedding).astype(BF16)


def half_at(mine, half):
    odd = jnp.bitwise_and(lax.axis_index("labels"), 1)
    return pl.ds(pl.multiple_of((odd if mine else 1 - odd) * half, 16), half)


def split_kernel(even_ref, got_ref, *refs):
    *more, keep_ref, send_ref, total = refs
    share = even_ref[0].astype(F32) + got_ref[0].astype(F32)
    for ref in more:
        share = share + ref[...].astype(F32)
    total[...] = share
    half = keep_ref.shape[0]
    keep_ref[...] = total[half_at(True, half), :]
    send_ref[...] = total[half_at(False, half), :].astype(BF16)


def merge_kernel(mine_ref, other_ref, out_ref):
    half = mine_ref.shape[0]
    out_ref[half_at(True, half), :] = mine_ref[...].astype(F32)
    out_ref[half_at(False, half), :] = other_ref[...].astype(F32)


def shard_at(my_data, m, shard_rows):
    at = jnp.bitwise_xor(my_data, m) * shard_rows
    return pl.ds(pl.multiple_of(at, 16), shard_rows)


def call(kernel, name, out_shape, scratch, flops, megabytes, *args):
    vmem = pl.BlockSpec(memory_space=pltpu.VMEM)
    return pl.pallas_call(
        kernel,
        in_specs=[vmem] * len(args),
        out_specs=jax.tree.map(lambda _: vmem, out_shape),
        out_shape=out_shape,
        scratch_shapes=scratch,
        compiler_params=pltpu.CompilerParams(vmem_limit_bytes=24 << 20),
        cost_estimate=pl.CostEstimate(
            flops=flops, bytes_accessed=megabytes << 20, transcendentals=0
        ),
        name=name,
    )(*args)


def pair_work(sources, shards, label_weight, cap, pick_count, prior=None):
    n_data = len(sources)
    block_rows, width = sources[0].shape
    rows = block_rows - META_ROWS
    slots = n_data * cap
    shard_rows = shards[0].shape[0]
    shapes = [((n_data // 2, rows, width), BF16)] * 2 + [((slots, BLK), F32)]
    shapes += [((slots, BLK), jnp.int32)] + [((slots, width), BF16)] * 3
    scratch = [pltpu.VMEM((n_data * shard_rows, width), BF16)]
    more = []
    if prior is not None:
        shapes += [((n_data // 2, shard_rows, width), BF16)] * 2
        more = [run[5] for run in prior] + [run[6] for run in prior]
        scratch += [pltpu.VMEM((n_data * shard_rows, width), F32)]
    return call(
        functools.partial(
            pair_kernel,
            cap=cap,
            pick_count=pick_count,
            n_data=n_data,
            prior=None if prior is None else len(prior),
        ),
        "pair_work",
        [jax.ShapeDtypeStruct(*shape) for shape in shapes],
        scratch,
        2 * slots * width * (2 * label_weight.shape[0] + 2 * width + 2 * rows),
        6,
        *sources,
        *shards,
        label_weight,
        *more,
    )


def grad_label_work(grad_scores, blocks, embeddings, label_weight):
    return call(
        grad_label_kernel,
        "grad_label_work",
        jax.ShapeDtypeStruct(label_weight.shape, BF16),
        [],
        2 * len(blocks) * blocks[0].shape[0] * label_weight.size,
        4,
        *grad_scores,
        *blocks,
        *embeddings,
    )


def swap(x):
    x = lax.all_to_all(x, "labels", split_axis=0, concat_axis=0, tiled=True)
    return lax.all_to_all(x, "dp", split_axis=1, concat_axis=1, tiled=True)


def partner(x, axis, mask):
    return lax.ppermute(x, axis, [(i, i ^ mask) for i in range(lax.axis_size(axis))])


def masks(n):
    return [1 << i for i in range(n.bit_length() - 1)]


def after(x, *others):
    return lax.optimization_barrier((x, *others))[0]


def gather_dp(x, first=None):
    got = {0: x}
    *far, near = reversed(masks(lax.axis_size("dp")))
    for mask in far:
        got.update({m | mask: partner(v, "dp", mask) for m, v in list(got.items())})
    for m, v in sorted(got.items(), reverse=True):
        if m:
            v = v if first is None else after(v, first)
        elif len(got) > 1:
            v = after(v, got[max(i for i in got if i & near == 0)])
        got[m | near] = partner(v, "dp", near)
    return [got[m] for m in range(len(got))]


def gather_labels(x):
    got = {0: x}
    for mask in reversed(masks(lax.axis_size("labels"))):
        got.update({m | mask: partner(v, "labels", mask) for m, v in list(got.items())})
    return [got[m] for m in range(len(got))]


def add(*terms):
    return sum(t.astype(F32) for t in terms)


def dp_terms(even, odd):
    got = partner(odd, "dp", 1)
    terms = [[even[i], got[i]] for i in range(even.shape[0])]
    for mask in masks(len(terms)):
        for i in range(len(terms)):
            if i & mask == 0 and i % mask == 0:
                terms[i].append(partner(add(*terms[i | mask]).astype(BF16), "dp", 2 * mask))
    return got, terms[0]


def reduce_dp(even, odd):
    return add(*dp_terms(even, odd)[1])


def sum_shares(even, odd):
    got, terms = dp_terms(even, odd)
    rows, width = even.shape[1:]
    half = rows // 2
    keep, send = call(
        split_kernel,
        "split_share",
        [jax.ShapeDtypeStruct((half, width), F32), jax.ShapeDtypeStruct((half, width), BF16)],
        [pltpu.VMEM((rows, width), F32)],
        0,
        1,
        even,
        got,
        *terms[2:],
    )
    x = add(keep, partner(send, "labels", 1)).astype(BF16)
    for mask in masks(lax.axis_size("labels"))[1:]:
        x = add(x, partner(x, "labels", mask)).astype(BF16)
    other = partner(x, "labels", 1)
    out = jax.ShapeDtypeStruct((rows, width), F32)
    return keep, call(merge_kernel, "merge_share", out, [], 0, 1, x, other)


def reduce_labels(parts):
    terms = [[part] for part in parts]
    for mask in masks(len(terms)):
        for i in range(len(terms)):
            if i & mask == 0 and i % mask == 0:
                terms[i].append(partner(add(*terms[i | mask]).astype(BF16), "labels", mask))
    return add(*terms[0])


def with_meta(feats, owner_rows, block_rows, positive_rows):
    meta = jnp.concatenate([owner_rows, block_rows, positive_rows], axis=1).astype(BF16)
    meta = jnp.pad(meta, ((0, META_ROWS - meta.shape[0]), (0, feats.shape[1] - meta.shape[1])))
    return jnp.concatenate([feats, meta], axis=0)


def local(feats, enc_weight, label_weight, owners, blocks, positives):
    n_labels = lax.axis_size("labels")
    n_data = lax.axis_size("dp")
    n_owner = n_labels * n_data
    row_count, width = feats.shape
    pick_count = owners.shape[1]
    cap = max(2, 2 * row_count * pick_count // n_owner)
    shards = gather_dp(enc_weight)

    if row_count <= n_data * cap:
        own = with_meta(feats, owners.T, blocks.T, positives.T)
        rows_of = gather_labels(own)
        work = []
        for by in range(n_labels):
            run = gather_dp(rows_of[by], work[-1][0] if work else None)
            if by + 1 < n_labels:
                run[0] = after(run[0], *rows_of[by + 1 : by + 3])
            prior = work if by == n_labels - 1 else None
            work.append(pair_work(run, shards, label_weight, cap, pick_count, prior))
        grad_feats = reduce_labels([reduce_dp(*run[:2]) for run in work]).astype(BF16)
    else:
        flat = owners.reshape(-1)
        onehot = (flat[:, None] == jnp.arange(n_owner, dtype=jnp.int32)[None, :]).astype(jnp.int32)
        rank = jnp.sum((jnp.cumsum(onehot, axis=0) - onehot) * onehot, axis=1)
        slot = (flat * cap + rank).reshape(row_count, pick_count)
        slot_total = n_owner * cap
        slots = jnp.arange(slot_total, dtype=jnp.int32)
        place = slots[:, None, None] == slot[None]
        pick = jnp.any(place, axis=2).astype(BF16)
        live = jnp.any(place, axis=(1, 2))
        block_of = jnp.sum(jnp.where(place, blocks[None], 0), axis=(1, 2))
        wanted = jnp.sum(jnp.where(place, positives[None], 0), axis=(1, 2))
        owner_of = jnp.where(live, slots // cap, -1)
        out = dot(pick, feats).astype(BF16).reshape(n_labels, n_data, cap, width)
        meta = jnp.stack([owner_of, block_of, wanted], axis=1).reshape(n_labels, n_data, cap, 3)
        tile = 128
        got = swap(out).reshape(slot_total // tile, tile, width)
        got_meta = swap(meta).reshape(slot_total // tile, tile, 3).transpose(0, 2, 1)
        sources = [
            with_meta(got[i], got_meta[i, 0:1], got_meta[i, 1:2], got_meta[i, 2:3])
            for i in range(slot_total // tile)
        ]
        work = []
        for i in range(0, len(sources), n_data):
            prior = work if i + n_data == len(sources) else None
            run = sources[i : i + n_data]
            work.append(pair_work(run, shards, label_weight, tile, 1, prior))
        back = jnp.stack([part for run in work for part in run[:2]])
        back = back.reshape(-1, 2, n_data // 2, tile, width).transpose(0, 2, 1, 3, 4)
        back = swap(back.reshape(n_labels, n_data, cap, width)).reshape(slot_total, width)
        grad_feats = dot(pick, back, 0, 0).astype(BF16)

    _, _, grad_scores, block_of, embedding, _, _ = zip(*(run[:7] for run in work))
    keep, grad_enc = sum_shares(*work[-1][7:])
    embedding = (after(embedding[0], keep),) + embedding[1:]
    grad_label = grad_label_work(grad_scores, block_of, embedding, label_weight)
    return (grad_feats, grad_label, grad_enc)


def solution(mesh):
    rows = P(("groups", "labels", "dp"), None)
    return jax.shard_map(
        local,
        mesh=mesh,
        in_specs=(rows, P("dp", None), rows, rows, rows, rows),
        out_specs=(rows, rows, P(("groups", "dp"), None)),
        check_vma=False,
    )
```

```python
import functools

import jax
import jax.numpy as jnp
from jax import lax
from jax.experimental import pallas as pl
from jax.experimental.pallas import tpu as pltpu
from jax.sharding import PartitionSpec as P

BLK = 128
EPSILON = 1e-06
META_ROWS = 8
F32 = jnp.float32
BF16 = jnp.bfloat16


def dot(a, b, da=1, db=0):
    return lax.dot_general(a, b, (((da,), (db,)), ((), ())), preferred_element_type=F32)


def pair_kernel(*refs, cap, pick_count, n_data, first, prior):
    it = iter(refs)
    take = lambda n: [next(it) for _ in range(n)]
    last = prior is not None
    sources, shards, label = take(n_data), take(n_data if first else 1), next(it)
    prior_refs = take(2 * prior if last else 0)
    even_ref, odd_ref, grad_scores_ref, block_ref, embedding_ref, feats_ref, grad_hidden_ref = take(7)
    enc = next(it) if first else shards[0]
    share_refs = take(2 if last else 0)

    my_data = lax.axis_index("dp")
    me = (lax.axis_index("labels") * n_data + my_data).astype(F32)
    rows = sources[0].shape[0] - META_ROWS
    shard_rows = enc.shape[0] // n_data
    n_blocks = label.shape[0] // BLK
    slots = n_data * cap

    for m in range(n_data if first else 0):
        enc[shard_at(my_data, m, shard_rows), :] = shards[m][...]

    row_id = lax.broadcasted_iota(jnp.int32, (rows, rows), 0)
    col_id = lax.broadcasted_iota(jnp.int32, (rows, rows), 1)
    before = (row_id < col_id).astype(BF16)
    slot_id = lax.broadcasted_iota(jnp.int32, (cap, rows), 0).astype(F32)
    column = lax.broadcasted_iota(jnp.int32, (slots, BLK), 1)

    hits, codes = [], []
    for source in sources:
        meta = source[rows:, 0 : 3 * rows].astype(F32)[:pick_count]
        named = meta[:, :rows] == me
        hits.append(jnp.sum(named.astype(F32), axis=0, keepdims=True))
        code = meta[:, rows : 2 * rows] * 256.0 + meta[:, 2 * rows :] + 1.0
        codes.append(jnp.sum(jnp.where(named, code, 0.0), axis=0, keepdims=True))
    rank = dot(jnp.concatenate(hits, axis=0).astype(BF16), before)

    picks, picked, slot_codes = [], [], []
    for m, source in enumerate(sources):
        pick = jnp.where((slot_id == rank[m : m + 1]) & (hits[m] > 0.0), 1.0, 0.0)
        slot_codes.append(jnp.sum(pick * codes[m], axis=1, keepdims=True))
        pick = pick.astype(BF16)
        picks.append(pick)
        picked.append(dot(pick, source[:rows, :]).astype(BF16))
    feats = jnp.concatenate(picked, axis=0)
    feats_ref[...] = feats
    code = jnp.concatenate(slot_codes, axis=0).astype(jnp.int32) - 1

    hidden = dot(feats, enc[...])
    inv_rms = lax.rsqrt(jnp.mean(hidden * hidden, axis=-1, keepdims=True) + EPSILON)
    embedding = (hidden * inv_rms).astype(BF16)
    embedding_ref[...] = embedding

    scores = dot(embedding, label[...], 1, 1)
    block = jnp.broadcast_to(code >> 8, (slots, BLK))
    block_ref[...] = block
    wanted = jnp.broadcast_to(code & 255, (slots, BLK))
    own_scores = jnp.zeros((slots, BLK), F32)
    for b in range(n_blocks):
        own_scores = jnp.where(block == b, scores[:, b * BLK : (b + 1) * BLK], own_scores)
    target = jnp.where(column == wanted, 1.0, 0.0)
    grad_scores = jnp.where(block >= 0, jax.nn.sigmoid(own_scores) - target, 0.0)
    grad_scores_ref[...] = grad_scores

    spread = jnp.concatenate(
        [jnp.where(block == b, grad_scores, 0.0).astype(BF16) for b in range(n_blocks)], axis=1
    )
    grad_pair = dot(spread, label[...]).astype(BF16).astype(F32)
    projection = jnp.mean(hidden * grad_pair, axis=-1, keepdims=True)
    grad_hidden = (inv_rms * grad_pair - hidden * (inv_rms**3 * projection)).astype(BF16)
    grad_hidden_ref[...] = grad_hidden

    if last:
        total = next(it)
        all_feats = jnp.concatenate([r[...] for r in prior_refs[:prior]] + [feats], axis=0)
        all_grads = jnp.concatenate([r[...] for r in prior_refs[prior:]] + [grad_hidden], axis=0)
        total[...] = dot(all_feats, all_grads, 0, 0)
        for m in range(n_data):
            part = total[shard_at(my_data, m, shard_rows), :]
            share_refs[m % 2][m // 2] = part.astype(BF16)

    grad_feats = dot(grad_hidden, enc[...], 1, 1).astype(BF16)
    for m in range(n_data):
        part = dot(picks[m], grad_feats[m * cap : (m + 1) * cap], 0, 0)
        (odd_ref if m % 2 else even_ref)[m // 2] = part.astype(BF16)


def grad_label_kernel(*refs):
    runs = (len(refs) - 1) // 3
    grad_scores, blocks, embeddings = refs[:runs], refs[runs : 2 * runs], refs[2 * runs : 3 * runs]
    out_ref = refs[-1]
    grad_scores_t = jnp.concatenate([r[...].T for r in grad_scores], axis=1)
    block_t = jnp.concatenate([r[...].T for r in blocks], axis=1)
    embedding = jnp.concatenate([r[...] for r in embeddings], axis=0)
    for b in range(out_ref.shape[0] // BLK):
        spread_t = jnp.where(block_t == b, grad_scores_t, 0.0).astype(BF16)
        out_ref[b * BLK : (b + 1) * BLK, :] = dot(spread_t, embedding).astype(BF16)


def own_block_kernel(feats_ref, owners_ref, blocks_ref, positives_ref, out_ref):
    rows, width = feats_ref.shape
    out_ref[:rows, :] = feats_ref[...]
    meta = [r[...].astype(F32) for r in (owners_ref, blocks_ref, positives_ref)]
    meta += [jnp.zeros((meta[0].shape[0], width - 3 * rows), F32)]
    meta = jnp.concatenate(meta, axis=1)
    rest = jnp.zeros((META_ROWS - meta.shape[0], width), F32)
    out_ref[rows:, :] = jnp.concatenate([meta, rest], axis=0).astype(BF16)


def load_kernel(label_ref, shard_ref, label_out, shard_out):
    label_out[...] = label_ref[...]
    shard_out[...] = shard_ref[...]


def half_at(mine, half):
    odd = jnp.bitwise_and(lax.axis_index("labels"), 1)
    return pl.ds(pl.multiple_of((odd if mine else 1 - odd) * half, 16), half)


def split_kernel(even_ref, got_ref, *refs):
    *more, keep_ref, send_ref, total = refs
    share = even_ref[0].astype(F32) + got_ref[0].astype(F32)
    for ref in more:
        share = share + ref[...].astype(F32)
    total[...] = share
    half = keep_ref.shape[0]
    keep_ref[...] = total[half_at(True, half), :]
    send_ref[...] = total[half_at(False, half), :].astype(BF16)


def merge_kernel(mine_ref, other_ref, out_ref):
    half = mine_ref.shape[0]
    out_ref[half_at(True, half), :] = mine_ref[...].astype(F32)
    out_ref[half_at(False, half), :] = other_ref[...].astype(F32)


def shard_at(my_data, m, shard_rows):
    at = jnp.bitwise_xor(my_data, m) * shard_rows
    return pl.ds(pl.multiple_of(at, 16), shard_rows)


def call(kernel, name, out_shape, scratch, flops, megabytes, *args):
    vmem = pl.BlockSpec(memory_space=pltpu.VMEM)
    return pl.pallas_call(
        kernel,
        in_specs=[vmem] * len(args),
        out_specs=jax.tree.map(lambda _: vmem, out_shape),
        out_shape=out_shape,
        scratch_shapes=scratch,
        compiler_params=pltpu.CompilerParams(vmem_limit_bytes=24 << 20),
        cost_estimate=pl.CostEstimate(
            flops=flops, bytes_accessed=megabytes << 20, transcendentals=0
        ),
        name=name,
    )(*args)


def pair_work(sources, shards, label_weight, cap, pick_count, before, last):
    n_data = len(sources)
    block_rows, width = sources[0].shape
    rows = block_rows - META_ROWS
    slots = n_data * cap
    shard_rows = shards[0].shape[0]
    full = (n_data * shard_rows, width)
    shapes = [((n_data // 2, rows, width), BF16)] * 2 + [((slots, BLK), F32)]
    shapes += [((slots, BLK), jnp.int32)] + [((slots, width), BF16)] * 3
    scratch, more = [], []
    if before:
        shards = before[0][7:8]
    else:
        shapes += [(full, BF16)]
    if last:
        shapes += [((n_data // 2, shard_rows, width), BF16)] * 2
        more = [run[5] for run in before] + [run[6] for run in before]
        scratch = [pltpu.VMEM(full, F32)]
    return call(
        functools.partial(
            pair_kernel,
            cap=cap,
            pick_count=pick_count,
            n_data=n_data,
            first=not before,
            prior=len(before) if last else None,
        ),
        "pair_work",
        [jax.ShapeDtypeStruct(*shape) for shape in shapes],
        scratch,
        2 * slots * width * (2 * label_weight.shape[0] + 2 * width + 2 * rows),
        6,
        *sources,
        *shards,
        label_weight,
        *more,
    )


def grad_label_work(grad_scores, blocks, embeddings, label_weight):
    return call(
        grad_label_kernel,
        "grad_label_work",
        jax.ShapeDtypeStruct(label_weight.shape, BF16),
        [],
        2 * len(blocks) * blocks[0].shape[0] * label_weight.size,
        4,
        *grad_scores,
        *blocks,
        *embeddings,
    )


def swap(x):
    x = lax.all_to_all(x, "labels", split_axis=0, concat_axis=0, tiled=True)
    return lax.all_to_all(x, "dp", split_axis=1, concat_axis=1, tiled=True)


def partner(x, axis, mask):
    return lax.ppermute(x, axis, [(i, i ^ mask) for i in range(lax.axis_size(axis))])


def masks(n):
    return [1 << i for i in range(n.bit_length() - 1)]


def after(x, *others):
    return lax.optimization_barrier((x, *others))[0]


def gather_far(x):
    got = {0: x}
    for mask in reversed(masks(lax.axis_size("dp"))[1:]):
        got.update({m | mask: partner(v, "dp", mask) for m, v in list(got.items())})
    return [got[m] for m in sorted(got)]


def gather_near(far, *first):
    near = [partner(after(v, *first, *far[1:]), "dp", 1) for v in far]
    return [v for pair in zip(far, near) for v in pair]


def gather_labels(x):
    got = {0: x}
    for mask in reversed(masks(lax.axis_size("labels"))):
        got.update({m | mask: partner(v, "labels", mask) for m, v in list(got.items())})
    return [got[m] for m in range(len(got))]


def add(*terms):
    return sum(t.astype(F32) for t in terms)


def dp_terms(even, odd):
    got = partner(odd, "dp", 1)
    terms = [[even[i], got[i]] for i in range(even.shape[0])]
    for mask in masks(len(terms)):
        for i in range(len(terms)):
            if i & mask == 0 and i % mask == 0:
                terms[i].append(partner(add(*terms[i | mask]).astype(BF16), "dp", 2 * mask))
    return got, terms[0]


def sum_shares(even, odd):
    got, terms = dp_terms(even, odd)
    rows, width = even.shape[1:]
    half = rows // 2
    keep, send = call(
        split_kernel,
        "split_share",
        [jax.ShapeDtypeStruct((half, width), F32), jax.ShapeDtypeStruct((half, width), BF16)],
        [pltpu.VMEM((rows, width), F32)],
        0,
        1,
        even,
        got,
        *terms[2:],
    )
    x = add(keep, partner(send, "labels", 1)).astype(BF16)
    for mask in masks(lax.axis_size("labels"))[1:]:
        x = add(x, partner(x, "labels", mask)).astype(BF16)
    other = partner(x, "labels", 1)
    out = jax.ShapeDtypeStruct((rows, width), F32)
    return keep, call(merge_kernel, "merge_share", out, [], 0, 1, x, other)


def both_cores(run):
    return [run[0], partner(run[1], "dp", 1)]


def reduce_runs(terms):
    n = len(terms)
    held = ()
    for i in reversed(range(0, n, 2)):
        sent = after(add(*terms[i + 1]).astype(BF16), *held)
        held = (partner(sent, "labels", 1),)
        terms[i].append(*held)
    sums = {}
    for i in range(0, n, 2):
        parts = [[t[h] for t in terms[i]] for h in range(terms[i][0].shape[0])]
        for mask in masks(len(parts)):
            for h in range(0, len(parts), 2 * mask):
                sent = add(*parts[h + mask]).astype(BF16)
                parts[h].append(partner(sent, "dp", 2 * mask))
        sums[i] = parts[0]
    for mask in masks(n)[1:]:
        for i in range(0, n, 2 * mask):
            sums[i].append(partner(add(*sums[i + mask]).astype(BF16), "labels", mask))
    return add(*sums[0]).astype(BF16)


def with_meta(feats, owner_rows, block_rows, positive_rows):
    meta = jnp.concatenate([owner_rows, block_rows, positive_rows], axis=1).astype(BF16)
    meta = jnp.pad(meta, ((0, META_ROWS - meta.shape[0]), (0, feats.shape[1] - meta.shape[1])))
    return jnp.concatenate([feats, meta], axis=0)


def local(feats, enc_weight, label_weight, owners, blocks, positives):
    n_labels = lax.axis_size("labels")
    n_data = lax.axis_size("dp")
    n_owner = n_labels * n_data
    row_count, width = feats.shape
    pick_count = owners.shape[1]
    cap = max(2, 2 * row_count * pick_count // n_owner)

    if row_count <= n_data * cap:
        own = call(
            own_block_kernel,
            "own_block",
            jax.ShapeDtypeStruct((row_count + META_ROWS, width), BF16),
            [],
            0,
            1,
            feats,
            owners.T,
            blocks.T,
            positives.T,
        )
        near = gather_labels(own)
        far = [gather_far(block) for block in near]
        shards = gather_near(gather_far(after(enc_weight, own)))
        label_weight, shards[0] = call(
            load_kernel,
            "load",
            [jax.ShapeDtypeStruct(x.shape, BF16) for x in (label_weight, enc_weight)],
            [],
            0,
            4,
            after(label_weight, near[1]),
            enc_weight,
        )
        waits = {0: [near[-1]] + [x for blocks in far[1:-1] for x in blocks[1:]], 1: far[-1][1:]}
        work, terms = [], []
        for by in range(n_labels):
            run = gather_near(far[by])
            run[0] = after(run[0], *waits.get(by, []))
            run_work = pair_work(
                run, shards, label_weight, cap, pick_count, work, by == n_labels - 1
            )
            work.append(run_work)
            terms.append(both_cores(run_work))
        grad_feats = reduce_runs(terms)
    else:
        flat = owners.reshape(-1)
        onehot = (flat[:, None] == jnp.arange(n_owner, dtype=jnp.int32)[None, :]).astype(jnp.int32)
        rank = jnp.sum((jnp.cumsum(onehot, axis=0) - onehot) * onehot, axis=1)
        slot = (flat * cap + rank).reshape(row_count, pick_count)
        slot_total = n_owner * cap
        slots = jnp.arange(slot_total, dtype=jnp.int32)
        place = slots[:, None, None] == slot[None]
        pick = jnp.any(place, axis=2).astype(BF16)
        live = jnp.any(place, axis=(1, 2))
        block_of = jnp.sum(jnp.where(place, blocks[None], 0), axis=(1, 2))
        wanted = jnp.sum(jnp.where(place, positives[None], 0), axis=(1, 2))
        owner_of = jnp.where(live, slots // cap, -1)
        shards = gather_near(gather_far(enc_weight))
        out = dot(pick, feats).astype(BF16).reshape(n_labels, n_data, cap, width)
        meta = jnp.stack([owner_of, block_of, wanted], axis=1).reshape(n_labels, n_data, cap, 3)
        tile = 128
        got = swap(out).reshape(slot_total // tile, tile, width)
        got_meta = swap(meta).reshape(slot_total // tile, tile, 3).transpose(0, 2, 1)
        sources = [
            with_meta(got[i], got_meta[i, 0:1], got_meta[i, 1:2], got_meta[i, 2:3])
            for i in range(slot_total // tile)
        ]
        work = []
        for i in range(0, len(sources), n_data):
            last = i + n_data == len(sources)
            run = sources[i : i + n_data]
            work.append(pair_work(run, shards, label_weight, tile, 1, work, last))
        back = jnp.stack([part for run in work for part in run[:2]])
        back = back.reshape(-1, 2, n_data // 2, tile, width).transpose(0, 2, 1, 3, 4)
        back = swap(back.reshape(n_labels, n_data, cap, width)).reshape(slot_total, width)
        grad_feats = dot(pick, back, 0, 0).astype(BF16)

    _, _, grad_scores, block_of, embedding, _, _ = zip(*(run[:7] for run in work))
    keep, grad_enc = sum_shares(*work[-1][-2:])
    embedding = (after(embedding[0], keep),) + embedding[1:]
    grad_label = grad_label_work(grad_scores, block_of, embedding, label_weight)
    return (grad_feats, grad_label, grad_enc)


def solution(mesh):
    rows = P(("groups", "labels", "dp"), None)
    return jax.shard_map(
        local,
        mesh=mesh,
        in_specs=(rows, P("dp", None), rows, rows, rows, rows),
        out_specs=(rows, rows, P(("groups", "dp"), None)),
        check_vma=False,
    )
```

```python
import functools

import jax
import jax.numpy as jnp
from jax import lax
from jax.experimental import pallas as pl
from jax.experimental.pallas import tpu as pltpu
from jax.sharding import PartitionSpec as P

BLK = 128
EPSILON = 1e-06
META_ROWS = 8
TILE = 128
F32 = jnp.float32
BF16 = jnp.bfloat16
VMEM = pl.BlockSpec(memory_space=pltpu.VMEM)
HBM = pl.BlockSpec(memory_space=pltpu.HBM)


def dot(a, b, da=1, db=0):
    return lax.dot_general(a, b, (((da,), (db,)), ((), ())), preferred_element_type=F32)


def shard_at(m, shard_rows):
    at = jnp.bitwise_xor(lax.axis_index("dp"), m) * shard_rows
    return pl.ds(pl.multiple_of(at, 16), shard_rows)


def pair_kernel(*refs, cap, pick_count, n_sources, n_sets, n_data, first, last):
    it = iter(refs)
    take = lambda n: [next(it) for _ in range(n)]
    sources, labels = take(n_sources), take(n_sets)
    shards = take(n_data if first else 0)
    enc, total_in = (None, None) if first else take(2)
    backs, grad_scores_ref, block_ref, embedding_ref = take(n_sources // 2), *take(3)
    enc = next(it) if first else enc
    shares = take(2 if last else 0)
    total_ref = next(it)

    n_owner_data = lax.axis_size("dp")
    me = lax.axis_index("labels") * n_owner_data + lax.axis_index("dp")
    rows = sources[0].shape[0] - META_ROWS
    shard_rows = enc.shape[0] // n_data
    n_blocks = labels[0].shape[0] // BLK
    part = n_sources * cap
    slots = n_sets * part

    for m, shard in enumerate(shards):
        enc[shard_at(m, shard_rows), :] = shard[...]

    row_id = lax.broadcasted_iota(jnp.int32, (rows, rows), 0)
    col_id = lax.broadcasted_iota(jnp.int32, (rows, rows), 1)
    before = (row_id < col_id).astype(BF16)
    slot_id = lax.broadcasted_iota(jnp.int32, (cap, rows), 0).astype(F32)
    column = lax.broadcasted_iota(jnp.int32, (slots, BLK), 1)

    hits, codes = [], []
    for source in sources:
        meta = source[rows:, 0 : 3 * rows].astype(F32)[:pick_count]
        code = meta[:, rows : 2 * rows] * 256.0 + meta[:, 2 * rows :] + 1.0
        for j in range(n_sets):
            named = meta[:, :rows] == jnp.bitwise_xor(me, j).astype(F32)
            hits.append(jnp.sum(named.astype(F32), axis=0, keepdims=True))
            codes.append(jnp.sum(jnp.where(named, code, 0.0), axis=0, keepdims=True))
    rank = dot(jnp.concatenate(hits, axis=0).astype(BF16), before)

    picks, picked, slot_codes = [], {}, {}
    for s, source in enumerate(sources):
        pick = []
        for j in range(n_sets):
            i = s * n_sets + j
            pick.append(jnp.where((slot_id == rank[i : i + 1]) & (hits[i] > 0.0), 1.0, 0.0))
            slot_codes[j, s] = jnp.sum(pick[j] * codes[i], axis=1, keepdims=True)
        picks.append(jnp.concatenate(pick, axis=0).astype(BF16))
        found = dot(picks[s], source[:rows, :]).astype(BF16)
        for j in range(n_sets):
            picked[j, s] = found[j * cap : (j + 1) * cap]
    order = [(j, s) for j in range(n_sets) for s in range(n_sources)]
    feats = jnp.concatenate([picked[i] for i in order], axis=0)
    code = jnp.concatenate([slot_codes[i] for i in order], axis=0).astype(jnp.int32) - 1

    hidden = dot(feats, enc[...])
    inv_rms = lax.rsqrt(jnp.mean(hidden * hidden, axis=-1, keepdims=True) + EPSILON)
    embedding = (hidden * inv_rms).astype(BF16)
    embedding_ref[...] = embedding

    block = jnp.broadcast_to(code >> 8, (slots, BLK))
    block_ref[...] = block
    wanted = jnp.broadcast_to(code & 255, (slots, BLK))
    target = jnp.where(column == wanted, 1.0, 0.0)
    grad_pairs = []
    for j in range(n_sets):
        at = slice(j * part, (j + 1) * part)
        scores = dot(embedding[at], labels[j][...], 1, 1)
        mine = block[at]
        own_scores = jnp.zeros((part, BLK), F32)
        for b in range(n_blocks):
            own_scores = jnp.where(mine == b, scores[:, b * BLK : (b + 1) * BLK], own_scores)
        grad_scores = jnp.where(mine >= 0, jax.nn.sigmoid(own_scores) - target[at], 0.0)
        grad_scores_ref[at, :] = grad_scores
        spread = jnp.concatenate(
            [jnp.where(mine == b, grad_scores, 0.0).astype(BF16) for b in range(n_blocks)], axis=1
        )
        grad_pairs.append(dot(spread, labels[j][...]))
    grad_pair = jnp.concatenate(grad_pairs, axis=0).astype(BF16).astype(F32)

    projection = jnp.mean(hidden * grad_pair, axis=-1, keepdims=True)
    grad_hidden = (inv_rms * grad_pair - hidden * (inv_rms**3 * projection)).astype(BF16)
    total = dot(feats, grad_hidden, 0, 0)
    total_ref[...] = total if first else total + total_in[...]
    for m in range(n_data if last else 0):
        shares[m % 2][m // 2] = total_ref[shard_at(m, shard_rows), :].astype(BF16)

    grad_feats = dot(grad_hidden, enc[...], 1, 1).astype(BF16)
    for s in range(n_sources):
        parts = [
            grad_feats[(j * n_sources + s) * cap : (j * n_sources + s + 1) * cap]
            for j in range(n_sets)
        ]
        back = dot(picks[s], jnp.concatenate(parts, axis=0), 0, 0)
        backs[s // 2][s % 2] = back.astype(BF16)


def grad_label_kernel(*refs, calls, n_sets, j):
    grad_scores, blocks, embeddings = refs[:calls], refs[calls : 2 * calls], refs[2 * calls : 3 * calls]
    more, out_ref = refs[3 * calls : -1], refs[-1]
    part = blocks[0].shape[0] // n_sets
    at = slice(j * part, (j + 1) * part)
    grad_scores_t = jnp.concatenate([r[at, :].T for r in grad_scores], axis=1)
    block_t = jnp.concatenate([r[at, :].T for r in blocks], axis=1)
    embedding = jnp.concatenate([r[at, :] for r in embeddings], axis=0)
    for b in range(out_ref.shape[0] // BLK):
        rows = slice(b * BLK, (b + 1) * BLK)
        spread_t = jnp.where(block_t == b, grad_scores_t, 0.0).astype(BF16)
        total = dot(spread_t, embedding)
        for ref in more:
            total = total + ref[rows, :].astype(F32)
        out_ref[rows, :] = total.astype(BF16)


def own_block_kernel(feats_ref, owners_ref, blocks_ref, positives_ref, out_ref, ints, sem):
    rows, width = feats_ref.shape
    feats = pltpu.make_async_copy(feats_ref, out_ref.at[pl.ds(0, rows)], sem.at[0])
    feats.start()
    copies = []
    for i, ref in enumerate((owners_ref, blocks_ref, positives_ref)):
        copies.append(pltpu.make_async_copy(ref, ints.at[i], sem.at[i + 1]))
        copies[i].start()
    for copy in copies:
        copy.wait()
    meta = [ints[i].astype(F32) for i in range(3)]
    meta += [jnp.zeros((meta[0].shape[0], width - 3 * rows), F32)]
    meta = jnp.concatenate(meta, axis=1)
    rest = jnp.zeros((META_ROWS - meta.shape[0], width), F32)
    out_ref[rows:, :] = jnp.concatenate([meta, rest], axis=0).astype(BF16)
    feats.wait()


def load_kernel(label_ref, shard_ref, label_out, shard_out, sem):
    copies = [pltpu.make_async_copy(shard_ref, shard_out, sem.at[0])]
    pieces = sem.shape[0] - 1
    rows = label_ref.shape[0] // pieces
    for i in range(pieces):
        at = pl.ds(i * rows, rows)
        copies.append(pltpu.make_async_copy(label_ref.at[at], label_out.at[at], sem.at[i + 1]))
    for copy in copies:
        copy.start()
    for copy in copies:
        copy.wait()


def half_at(mine, half):
    odd = jnp.bitwise_and(lax.axis_index("labels"), 1)
    return pl.ds(pl.multiple_of((odd if mine else 1 - odd) * half, 16), half)


def split_kernel(even_ref, got_ref, *refs):
    *more, keep_ref, send_ref, total = refs
    share = even_ref[0].astype(F32) + got_ref[0].astype(F32)
    for ref in more:
        share = share + ref[...].astype(F32)
    total[...] = share
    half = keep_ref.shape[0]
    keep_ref[...] = total[half_at(True, half), :]
    send_ref[...] = total[half_at(False, half), :].astype(BF16)


def merge_kernel(mine_ref, other_ref, out_ref):
    half = mine_ref.shape[0]
    out_ref[half_at(True, half), :] = mine_ref[...].astype(F32)
    out_ref[half_at(False, half), :] = other_ref[...].astype(F32)


def call(kernel, name, out_shape, scratch, flops, megabytes, *args, space=VMEM, limit=24):
    return pl.pallas_call(
        kernel,
        in_specs=[space] * len(args),
        out_specs=jax.tree.map(lambda _: VMEM, out_shape),
        out_shape=out_shape,
        scratch_shapes=scratch,
        compiler_params=pltpu.CompilerParams(vmem_limit_bytes=limit << 20),
        cost_estimate=pl.CostEstimate(
            flops=flops, bytes_accessed=megabytes << 20, transcendentals=0
        ),
        name=name,
    )(*args)


def shaped(shape, dtype=BF16):
    return jax.ShapeDtypeStruct(shape, dtype)


def pair_work(sources, labels, shards, cap, pick_count, before, last):
    n_data, n_sets = len(shards), len(labels)
    block_rows, width = sources[0].shape
    rows = block_rows - META_ROWS
    slots = n_sets * len(sources) * cap
    shard_rows = shards[0].shape[0]
    full = (n_data * shard_rows, width)
    backs = len(sources) // 2
    shapes = [shaped((2, rows, width))] * backs
    shapes += [shaped((slots, BLK), F32), shaped((slots, BLK), jnp.int32), shaped((slots, width))]
    more = [before["enc"], before["total"]] if before else shards
    scratch = []
    if not before:
        shapes += [shaped(full)]
    if last:
        shapes += [shaped((n_data // 2, shard_rows, width))] * 2
        scratch = [pltpu.VMEM(full, F32)]
    else:
        shapes += [shaped(full, F32)]
    out = call(
        functools.partial(
            pair_kernel,
            cap=cap,
            pick_count=pick_count,
            n_sources=len(sources),
            n_sets=n_sets,
            n_data=n_data,
            first=not before,
            last=last,
        ),
        "pair_work",
        shapes,
        scratch,
        2 * slots * width * (2 * labels[0].shape[0] + 3 * width + 2 * rows),
        8,
        *sources,
        *labels,
        *more,
    )
    result = {"back": out[:backs], "slots": list(out[backs : backs + 3])}
    rest = list(out[backs + 3 :])
    result["enc"] = before["enc"] if before else rest.pop(0)
    result["shares" if last else "total"] = rest if last else rest[0]
    return result


def grad_label_work(works, n_sets, j, labels_shape, *more):
    slots = list(zip(*(work["slots"] for work in works)))
    return call(
        functools.partial(grad_label_kernel, calls=len(works), n_sets=n_sets, j=j),
        "grad_label_work",
        shaped(labels_shape),
        [],
        2 * sum(x.shape[0] for x in slots[0]) // n_sets * labels_shape[0] * labels_shape[1],
        4,
        *slots[0],
        *slots[1],
        *slots[2],
        *more,
    )


def swap(x):
    x = lax.all_to_all(x, "labels", split_axis=0, concat_axis=0, tiled=True)
    return lax.all_to_all(x, "dp", split_axis=1, concat_axis=1, tiled=True)


def partner(x, axis, mask):
    return lax.ppermute(x, axis, [(i, i ^ mask) for i in range(lax.axis_size(axis))])


def masks(n):
    return [1 << i for i in range(n.bit_length() - 1)]


def after(x, *others):
    return lax.optimization_barrier((x, *others))[0]


def gather_far(x):
    got = {0: x}
    for mask in reversed(masks(lax.axis_size("dp"))[1:]):
        got.update({m | mask: partner(v, "dp", mask) for m, v in list(got.items())})
    return [got[m] for m in sorted(got)]


def gather_near(far):
    near = [partner(after(v, *far[1:]), "dp", 1) for v in far]
    return [v for pair in zip(far, near) for v in pair]


def gather_labels(x):
    got = {0: x}
    for mask in reversed(masks(lax.axis_size("labels"))):
        got.update({m | mask: partner(v, "labels", mask) for m, v in list(got.items())})
    return [got[m] for m in range(len(got))]


def add(*terms):
    return sum(t.astype(F32) for t in terms)


def dp_terms(even, odd):
    got = sent = partner(odd, "dp", 1)
    terms = [[even[i], got[i]] for i in range(even.shape[0])]
    for mask in masks(len(terms)):
        for i in range(len(terms)):
            if i & mask == 0 and i % mask == 0:
                sent = add(*terms[i | mask]).astype(BF16)
                terms[i].append(partner(sent, "dp", 2 * mask))
    return got, terms[0], sent


def sum_shares(even, odd):
    got, terms, sent = dp_terms(even, odd)
    rows, width = even.shape[1:]
    half = rows // 2
    keep, send = call(
        split_kernel,
        "split_share",
        [shaped((half, width), F32), shaped((half, width))],
        [pltpu.VMEM((rows, width), F32)],
        0,
        1,
        even,
        got,
        *terms[2:],
    )
    x = add(keep, partner(send, "labels", 1)).astype(BF16)
    for mask in masks(lax.axis_size("labels"))[1:]:
        x = add(x, partner(x, "labels", mask)).astype(BF16)
    other = partner(x, "labels", 1)
    total = call(merge_kernel, "merge_share", shaped((rows, width), F32), [], 0, 1, x, other)
    return sent, keep, total


def reduce_runs(runs, hold):
    n = len(runs)
    sums = {}
    for i in range(0, n, 2):
        got = partner(runs[i + 1] if i else after(runs[i + 1], hold), "labels", 1)
        parts = [[runs[i][h], got[h]] for h in range(got.shape[0])]
        for mask in masks(len(parts)):
            for h in range(0, len(parts), 2 * mask):
                sent = add(*parts[h + mask]).astype(BF16)
                parts[h].append(partner(sent, "dp", 2 * mask))
        sums[i] = parts[0]
    for mask in masks(n)[1:]:
        for i in range(0, n, 2 * mask):
            sums[i].append(partner(add(*sums[i + mask]).astype(BF16), "labels", mask))
    return add(*sums[0]).astype(BF16)


def with_meta(feats, owner_rows, block_rows, positive_rows):
    meta = jnp.concatenate([owner_rows, block_rows, positive_rows], axis=1).astype(BF16)
    meta = jnp.pad(meta, ((0, META_ROWS - meta.shape[0]), (0, feats.shape[1] - meta.shape[1])))
    return jnp.concatenate([feats, meta], axis=0)


def local(feats, enc_weight, label_weight, owners, blocks, positives):
    n_labels = lax.axis_size("labels")
    n_data = lax.axis_size("dp")
    n_owner = n_labels * n_data
    row_count, width = feats.shape
    pick_count = owners.shape[1]
    cap = max(2, 2 * row_count * pick_count // n_owner)

    if row_count <= n_data * cap:
        own = call(
            own_block_kernel,
            "own_block",
            shaped((row_count + META_ROWS, width)),
            [
                pltpu.VMEM((3, pick_count, row_count), jnp.int32),
                pltpu.SemaphoreType.DMA((4,)),
            ],
            0,
            1,
            feats,
            owners.T,
            blocks.T,
            positives.T,
            space=HBM,
            limit=60,
        )
        near = gather_labels(own)
        far = [gather_far(block) for block in near]
        labels = [label_weight, partner(label_weight, "dp", 1)]
        shards = gather_near(gather_far(after(enc_weight, own)))
        labels[0], shards[0] = call(
            load_kernel,
            "load",
            [shaped(label_weight.shape), shaped(enc_weight.shape)],
            [pltpu.SemaphoreType.DMA((9,))],
            0,
            4,
            after(label_weight, near[1]),
            enc_weight,
            space=HBM,
        )
        works = []
        for by in range(0, n_labels, 2):
            sources = far[by] + far[by + 1]
            if by == 0:
                sources[0] = after(sources[0], near[3 % n_labels])
            before = works[-1] if works else None
            last = by + 2 >= n_labels
            works.append(pair_work(sources, labels, shards, cap, pick_count, before, last))
        sent, keep, grad_enc = sum_shares(*works[-1]["shares"])
        grad_feats = reduce_runs([back for work in works for back in work["back"]], keep)
        works[0]["slots"][2] = after(works[0]["slots"][2], sent)
        other = grad_label_work(works, 2, 1, label_weight.shape)
        other = partner(other, "dp", 1)
        grad_label = grad_label_work(works, 2, 0, label_weight.shape, other)
    else:
        shards = gather_near(gather_far(enc_weight))
        flat = owners.reshape(-1)
        onehot = (flat[:, None] == jnp.arange(n_owner, dtype=jnp.int32)[None, :]).astype(jnp.int32)
        rank = jnp.sum((jnp.cumsum(onehot, axis=0) - onehot) * onehot, axis=1)
        slot = (flat * cap + rank).reshape(row_count, pick_count)
        slot_total = n_owner * cap
        slots = jnp.arange(slot_total, dtype=jnp.int32)
        place = slots[:, None, None] == slot[None]
        pick = jnp.any(place, axis=2).astype(BF16)
        live = jnp.any(place, axis=(1, 2))
        block_of = jnp.sum(jnp.where(place, blocks[None], 0), axis=(1, 2))
        wanted = jnp.sum(jnp.where(place, positives[None], 0), axis=(1, 2))
        owner_of = jnp.where(live, slots // cap, -1)
        out = dot(pick, feats).astype(BF16).reshape(n_labels, n_data, cap, width)
        meta = jnp.stack([owner_of, block_of, wanted], axis=1).reshape(n_labels, n_data, cap, 3)
        tiles = slot_total // TILE
        got = swap(out).reshape(tiles, TILE, width)
        got_meta = swap(meta).reshape(tiles, TILE, 3).transpose(0, 2, 1)
        sources = [
            with_meta(got[i], got_meta[i, 0:1], got_meta[i, 1:2], got_meta[i, 2:3])
            for i in range(tiles)
        ]
        works = []
        for i in range(0, tiles, 4):
            before = works[-1] if works else None
            last = i + 4 >= tiles
            works.append(pair_work(sources[i : i + 4], [label_weight], shards, TILE, 1, before, last))
        back = jnp.concatenate([back for work in works for back in work["back"]], axis=0)
        back = swap(back.reshape(n_labels, n_data, cap, width)).reshape(slot_total, width)
        grad_feats = dot(pick, back, 0, 0).astype(BF16)
        _, _, grad_enc = sum_shares(*works[-1]["shares"])
        grad_label = grad_label_work(works, 1, 0, label_weight.shape)

    return (grad_feats, grad_label, grad_enc)


def solution(mesh):
    rows = P(("groups", "labels", "dp"), None)
    return jax.shard_map(
        local,
        mesh=mesh,
        in_specs=(rows, P("dp", None), rows, rows, rows, rows),
        out_specs=(rows, rows, P(("groups", "dp"), None)),
        check_vma=False,
    )
```

```python
import functools

import jax
import jax.numpy as jnp
from jax import lax
from jax.experimental import pallas as pl
from jax.experimental.pallas import tpu as pltpu
from jax.sharding import PartitionSpec as P

BLK = 128
EPSILON = 1e-06
META_ROWS = 8
TILE = 128
F32 = jnp.float32
BF16 = jnp.bfloat16
VMEM = pl.BlockSpec(memory_space=pltpu.VMEM)
HBM = pl.BlockSpec(memory_space=pltpu.HBM)


def dot(a, b, da=1, db=0):
    return lax.dot_general(a, b, (((da,), (db,)), ((), ())), preferred_element_type=F32)


def shard_at(m, shard_rows):
    at = jnp.bitwise_xor(lax.axis_index("dp"), m) * shard_rows
    return pl.ds(pl.multiple_of(at, 16), shard_rows)


def pair_kernel(*refs, cap, pick_count, n_sources, n_sets, n_data, first, last):
    it = iter(refs)
    take = lambda n: [next(it) for _ in range(n)]
    sources, labels = take(n_sources), take(n_sets)
    shards = take(n_data if first else 0)
    enc, total_in = (None, None) if first else take(2)
    backs, grad_scores_ref, block_ref, embedding_ref = take(n_sources // 2), *take(3)
    enc = next(it) if first else enc
    shares = take(2 if last else 0)
    total_ref = next(it)

    n_owner_data = lax.axis_size("dp")
    me = lax.axis_index("labels") * n_owner_data + lax.axis_index("dp")
    rows = sources[0].shape[0] - META_ROWS
    shard_rows = enc.shape[0] // n_data
    n_blocks = labels[0].shape[0] // BLK
    part = n_sources * cap
    slots = n_sets * part

    for m, shard in enumerate(shards):
        enc[shard_at(m, shard_rows), :] = shard[...]

    row_id = lax.broadcasted_iota(jnp.int32, (rows, rows), 0)
    col_id = lax.broadcasted_iota(jnp.int32, (rows, rows), 1)
    before = (row_id < col_id).astype(BF16)
    slot_id = lax.broadcasted_iota(jnp.int32, (cap, rows), 0).astype(F32)
    column = lax.broadcasted_iota(jnp.int32, (slots, BLK), 1)

    hits, codes = [], []
    for source in sources:
        meta = source[rows:, 0 : 3 * rows].astype(F32)[:pick_count]
        code = meta[:, rows : 2 * rows] * 256.0 + meta[:, 2 * rows :] + 1.0
        for j in range(n_sets):
            named = meta[:, :rows] == jnp.bitwise_xor(me, j).astype(F32)
            hits.append(jnp.sum(named.astype(F32), axis=0, keepdims=True))
            codes.append(jnp.sum(jnp.where(named, code, 0.0), axis=0, keepdims=True))
    rank = dot(jnp.concatenate(hits, axis=0).astype(BF16), before)

    picks, picked, slot_codes = [], {}, {}
    for s, source in enumerate(sources):
        pick = []
        for j in range(n_sets):
            i = s * n_sets + j
            pick.append(jnp.where((slot_id == rank[i : i + 1]) & (hits[i] > 0.0), 1.0, 0.0))
            slot_codes[j, s] = jnp.sum(pick[j] * codes[i], axis=1, keepdims=True)
        picks.append(jnp.concatenate(pick, axis=0).astype(BF16))
        found = dot(picks[s], source[:rows, :]).astype(BF16)
        for j in range(n_sets):
            picked[j, s] = found[j * cap : (j + 1) * cap]
    order = [(j, s) for j in range(n_sets) for s in range(n_sources)]
    feats = jnp.concatenate([picked[i] for i in order], axis=0)
    code = jnp.concatenate([slot_codes[i] for i in order], axis=0).astype(jnp.int32) - 1

    hidden = dot(feats, enc[...])
    inv_rms = lax.rsqrt(jnp.mean(hidden * hidden, axis=-1, keepdims=True) + EPSILON)
    embedding = (hidden * inv_rms).astype(BF16)
    embedding_ref[...] = embedding

    block = jnp.broadcast_to(code >> 8, (slots, BLK))
    block_ref[...] = block
    wanted = jnp.broadcast_to(code & 255, (slots, BLK))
    target = jnp.where(column == wanted, 1.0, 0.0)
    grad_pairs = []
    for j in range(n_sets):
        at = slice(j * part, (j + 1) * part)
        scores = dot(embedding[at], labels[j][...], 1, 1)
        mine = block[at]
        own_scores = jnp.zeros((part, BLK), F32)
        for b in range(n_blocks):
            own_scores = jnp.where(mine == b, scores[:, b * BLK : (b + 1) * BLK], own_scores)
        grad_scores = jnp.where(mine >= 0, jax.nn.sigmoid(own_scores) - target[at], 0.0)
        grad_scores_ref[at, :] = grad_scores
        spread = jnp.concatenate(
            [jnp.where(mine == b, grad_scores, 0.0).astype(BF16) for b in range(n_blocks)], axis=1
        )
        grad_pairs.append(dot(spread, labels[j][...]))
    grad_pair = jnp.concatenate(grad_pairs, axis=0).astype(BF16).astype(F32)

    projection = jnp.mean(hidden * grad_pair, axis=-1, keepdims=True)
    grad_hidden = (inv_rms * grad_pair - hidden * (inv_rms**3 * projection)).astype(BF16)
    total = dot(feats, grad_hidden, 0, 0)
    total_ref[...] = total if first else total + total_in[...]
    for m in range(n_data if last else 0):
        shares[m % 2][m // 2] = total_ref[shard_at(m, shard_rows), :].astype(BF16)

    grad_feats = dot(grad_hidden, enc[...], 1, 1).astype(BF16)
    for s in range(n_sources):
        parts = [
            grad_feats[(j * n_sources + s) * cap : (j * n_sources + s + 1) * cap]
            for j in range(n_sets)
        ]
        back = dot(picks[s], jnp.concatenate(parts, axis=0), 0, 0)
        backs[s // 2][s % 2] = back.astype(BF16)


def grad_label_kernel(*refs, calls, n_sets, j):
    grad_scores, blocks, embeddings = refs[:calls], refs[calls : 2 * calls], refs[2 * calls : 3 * calls]
    more, out_ref = refs[3 * calls : -1], refs[-1]
    part = blocks[0].shape[0] // n_sets
    at = slice(j * part, (j + 1) * part)
    grad_scores_t = jnp.concatenate([r[at, :].T for r in grad_scores], axis=1)
    block_t = jnp.concatenate([r[at, :].T for r in blocks], axis=1)
    embedding = jnp.concatenate([r[at, :] for r in embeddings], axis=0)
    for b in range(out_ref.shape[0] // BLK):
        rows = slice(b * BLK, (b + 1) * BLK)
        spread_t = jnp.where(block_t == b, grad_scores_t, 0.0).astype(BF16)
        total = dot(spread_t, embedding)
        for ref in more:
            total = total + ref[rows, :].astype(F32)
        out_ref[rows, :] = total.astype(BF16)


def own_block_kernel(feats_ref, owners_ref, blocks_ref, positives_ref, out_ref, ints, sem):
    rows, width = feats_ref.shape
    feats = pltpu.make_async_copy(feats_ref, out_ref.at[pl.ds(0, rows)], sem.at[0])
    feats.start()
    copies = []
    for i, ref in enumerate((owners_ref, blocks_ref, positives_ref)):
        copies.append(pltpu.make_async_copy(ref, ints.at[i], sem.at[i + 1]))
        copies[i].start()
    for copy in copies:
        copy.wait()
    meta = [ints[i].astype(F32) for i in range(3)]
    meta += [jnp.zeros((meta[0].shape[0], width - 3 * rows), F32)]
    meta = jnp.concatenate(meta, axis=1)
    rest = jnp.zeros((META_ROWS - meta.shape[0], width), F32)
    out_ref[rows:, :] = jnp.concatenate([meta, rest], axis=0).astype(BF16)
    feats.wait()


def load_kernel(label_ref, shard_ref, label_out, shard_out):
    label_out[...] = label_ref[...]
    shard_out[...] = shard_ref[...]


def half_at(mine, half):
    odd = jnp.bitwise_and(lax.axis_index("labels"), 1)
    return pl.ds(pl.multiple_of((odd if mine else 1 - odd) * half, 16), half)


def split_kernel(even_ref, got_ref, *refs):
    *more, keep_ref, send_ref, total = refs
    share = even_ref[0].astype(F32) + got_ref[0].astype(F32)
    for ref in more:
        share = share + ref[...].astype(F32)
    total[...] = share
    half = keep_ref.shape[0]
    keep_ref[...] = total[half_at(True, half), :]
    send_ref[...] = total[half_at(False, half), :].astype(BF16)


def merge_kernel(mine_ref, other_ref, out_ref):
    half = mine_ref.shape[0]
    out_ref[half_at(True, half), :] = mine_ref[...].astype(F32)
    out_ref[half_at(False, half), :] = other_ref[...].astype(F32)


def call(kernel, name, out_shape, scratch, flops, megabytes, *args, space=VMEM, limit=24):
    return pl.pallas_call(
        kernel,
        in_specs=[space] * len(args),
        out_specs=jax.tree.map(lambda _: VMEM, out_shape),
        out_shape=out_shape,
        scratch_shapes=scratch,
        compiler_params=pltpu.CompilerParams(vmem_limit_bytes=limit << 20),
        cost_estimate=pl.CostEstimate(
            flops=flops, bytes_accessed=megabytes << 20, transcendentals=0
        ),
        name=name,
    )(*args)


def shaped(shape, dtype=BF16):
    return jax.ShapeDtypeStruct(shape, dtype)


def pair_work(sources, labels, shards, cap, pick_count, before, last):
    n_data, n_sets = len(shards), len(labels)
    block_rows, width = sources[0].shape
    rows = block_rows - META_ROWS
    slots = n_sets * len(sources) * cap
    shard_rows = shards[0].shape[0]
    full = (n_data * shard_rows, width)
    backs = len(sources) // 2
    shapes = [shaped((2, rows, width))] * backs
    shapes += [shaped((slots, BLK), F32), shaped((slots, BLK), jnp.int32), shaped((slots, width))]
    more = [before["enc"], before["total"]] if before else shards
    scratch = []
    if not before:
        shapes += [shaped(full)]
    if last:
        shapes += [shaped((n_data // 2, shard_rows, width))] * 2
        scratch = [pltpu.VMEM(full, F32)]
    else:
        shapes += [shaped(full, F32)]
    out = call(
        functools.partial(
            pair_kernel,
            cap=cap,
            pick_count=pick_count,
            n_sources=len(sources),
            n_sets=n_sets,
            n_data=n_data,
            first=not before,
            last=last,
        ),
        "pair_work",
        shapes,
        scratch,
        2 * slots * width * (2 * labels[0].shape[0] + 3 * width + 2 * rows),
        8,
        *sources,
        *labels,
        *more,
    )
    result = {"back": out[:backs], "slots": list(out[backs : backs + 3])}
    rest = list(out[backs + 3 :])
    result["enc"] = before["enc"] if before else rest.pop(0)
    result["shares" if last else "total"] = rest if last else rest[0]
    return result


def grad_label_work(works, n_sets, j, labels_shape, *more):
    slots = list(zip(*(work["slots"] for work in works)))
    return call(
        functools.partial(grad_label_kernel, calls=len(works), n_sets=n_sets, j=j),
        "grad_label_work",
        shaped(labels_shape),
        [],
        2 * sum(x.shape[0] for x in slots[0]) // n_sets * labels_shape[0] * labels_shape[1],
        4,
        *slots[0],
        *slots[1],
        *slots[2],
        *more,
    )


def swap(x):
    x = lax.all_to_all(x, "labels", split_axis=0, concat_axis=0, tiled=True)
    return lax.all_to_all(x, "dp", split_axis=1, concat_axis=1, tiled=True)


def partner(x, axis, mask):
    return lax.ppermute(x, axis, [(i, i ^ mask) for i in range(lax.axis_size(axis))])


def masks(n):
    return [1 << i for i in range(n.bit_length() - 1)]


def after(x, *others):
    return lax.optimization_barrier((x, *others))[0]


def gather_far(x):
    got = {0: x}
    for mask in reversed(masks(lax.axis_size("dp"))[1:]):
        got.update({m | mask: partner(v, "dp", mask) for m, v in list(got.items())})
    return [got[m] for m in sorted(got)]


def gather_near(far, *first):
    near = [partner(after(v, *far[1:], *first), "dp", 1) for v in far]
    return [v for pair in zip(far, near) for v in pair]


def gather_labels(x, first):
    got = {0: x}
    for mask in reversed(masks(lax.axis_size("labels"))):
        for m, v in list(got.items()):
            got[m | mask] = partner(after(v, first) if m else v, "labels", mask)
    return [got[m] for m in range(len(got))]


def add(*terms):
    return sum(t.astype(F32) for t in terms)


def dp_terms(even, odd):
    got = sent = partner(odd, "dp", 1)
    terms = [[even[i], got[i]] for i in range(even.shape[0])]
    for mask in masks(len(terms)):
        for i in range(len(terms)):
            if i & mask == 0 and i % mask == 0:
                sent = add(*terms[i | mask]).astype(BF16)
                terms[i].append(partner(sent, "dp", 2 * mask))
    return got, terms[0], sent


def sum_shares(even, odd):
    got, terms, sent = dp_terms(even, odd)
    rows, width = even.shape[1:]
    half = rows // 2
    keep, send = call(
        split_kernel,
        "split_share",
        [shaped((half, width), F32), shaped((half, width))],
        [pltpu.VMEM((rows, width), F32)],
        0,
        1,
        even,
        got,
        *terms[2:],
    )
    x = add(keep, partner(send, "labels", 1)).astype(BF16)
    first = x
    for mask in masks(lax.axis_size("labels"))[1:]:
        x = add(x, partner(x, "labels", mask)).astype(BF16)
    return sent, first, x


def join_halves(x, *first):
    other = partner(x, "labels", 1)
    out = shaped((2 * x.shape[0], x.shape[1]), F32)
    return call(merge_kernel, "merge_share", out, [], 0, 1, after(x, *first), other)


def reduce_runs(runs):
    n = len(runs)
    gots = []
    for i in reversed(range(0, n, 2)):
        gots.append(partner(after(runs[i + 1], *gots[-1:]), "labels", 1))
    sums = {}
    held = []
    for i, got in zip(reversed(range(0, n, 2)), gots):
        parts = [[runs[i][h], got[h]] for h in range(got.shape[0])]
        for mask in masks(len(parts)):
            for h in range(0, len(parts), 2 * mask):
                sent = after(add(*parts[h + mask]).astype(BF16), *held)
                parts[h].append(partner(sent, "dp", 2 * mask))
        sums[i] = parts[0]
        held = parts[0][-1:]
    for mask in masks(n)[1:]:
        for i in range(0, n, 2 * mask):
            sums[i].append(partner(add(*sums[i + mask]).astype(BF16), "labels", mask))
    return add(*sums[0]).astype(BF16)


def with_meta(feats, owner_rows, block_rows, positive_rows):
    meta = jnp.concatenate([owner_rows, block_rows, positive_rows], axis=1).astype(BF16)
    meta = jnp.pad(meta, ((0, META_ROWS - meta.shape[0]), (0, feats.shape[1] - meta.shape[1])))
    return jnp.concatenate([feats, meta], axis=0)


def local(feats, enc_weight, label_weight, owners, blocks, positives):
    n_labels = lax.axis_size("labels")
    n_data = lax.axis_size("dp")
    n_owner = n_labels * n_data
    row_count, width = feats.shape
    pick_count = owners.shape[1]
    cap = max(2, 2 * row_count * pick_count // n_owner)

    if row_count <= n_data * cap:
        own = call(
            own_block_kernel,
            "own_block",
            shaped((row_count + META_ROWS, width)),
            [
                pltpu.VMEM((3, pick_count, row_count), jnp.int32),
                pltpu.SemaphoreType.DMA((4,)),
            ],
            0,
            1,
            feats,
            owners.T,
            blocks.T,
            positives.T,
            space=HBM,
            limit=60,
        )
        labels = [label_weight, partner(label_weight, "dp", 1)]
        labels[0], own_shard = call(
            load_kernel,
            "load",
            [shaped(label_weight.shape), shaped(enc_weight.shape)],
            [],
            0,
            4,
            after(label_weight, labels[1]),
            enc_weight,
        )
        near = gather_labels(own, labels[0])
        far, works = [], []
        for by in range(n_labels):
            last = by == n_labels - 1
            held = far[0][1:] if by else []
            if last and works:
                held = held + far[-1][1:] + works[0]["slots"][:1]
            far.append(gather_far(after(near[by], *held)))
            if by == 0:
                shards = gather_near(
                    gather_far(after(enc_weight, own)), *far[0][1:], *near[1:3], labels[0]
                )
                shards[0] = own_shard
                far[0][0] = after(far[0][0], near[2 % n_labels])
            if by == 0 or last:
                for run in range(len(works), by + 1):
                    sources = [near[run] if run else far[0][0]] + far[run][1:]
                    before = works[-1] if works else None
                    final = run == n_labels - 1
                    works.append(pair_work(sources, labels, shards, cap, pick_count, before, final))
        sent, first, share = sum_shares(*works[-1]["shares"])
        grad_feats = reduce_runs([back for work in works for back in work["back"]])
        works[0]["slots"][2] = after(works[0]["slots"][2], sent)
        other = partner(grad_label_work(works, 2, 1, label_weight.shape), "dp", 1)
        works[0]["slots"][2] = after(works[0]["slots"][2], first)
        grad_label = grad_label_work(works, 2, 0, label_weight.shape, other)
        grad_enc = join_halves(share, grad_label, grad_feats)
    else:
        shards = gather_near(gather_far(enc_weight))
        flat = owners.reshape(-1)
        onehot = (flat[:, None] == jnp.arange(n_owner, dtype=jnp.int32)[None, :]).astype(jnp.int32)
        rank = jnp.sum((jnp.cumsum(onehot, axis=0) - onehot) * onehot, axis=1)
        slot = (flat * cap + rank).reshape(row_count, pick_count)
        slot_total = n_owner * cap
        slots = jnp.arange(slot_total, dtype=jnp.int32)
        place = slots[:, None, None] == slot[None]
        pick = jnp.any(place, axis=2).astype(BF16)
        live = jnp.any(place, axis=(1, 2))
        block_of = jnp.sum(jnp.where(place, blocks[None], 0), axis=(1, 2))
        wanted = jnp.sum(jnp.where(place, positives[None], 0), axis=(1, 2))
        owner_of = jnp.where(live, slots // cap, -1)
        out = dot(pick, feats).astype(BF16).reshape(n_labels, n_data, cap, width)
        meta = jnp.stack([owner_of, block_of, wanted], axis=1).reshape(n_labels, n_data, cap, 3)
        tiles = slot_total // TILE
        got = swap(out).reshape(tiles, TILE, width)
        got_meta = swap(meta).reshape(tiles, TILE, 3).transpose(0, 2, 1)
        sources = [
            with_meta(got[i], got_meta[i, 0:1], got_meta[i, 1:2], got_meta[i, 2:3])
            for i in range(tiles)
        ]
        works = []
        for i in range(0, tiles, 4):
            before = works[-1] if works else None
            last = i + 4 >= tiles
            works.append(pair_work(sources[i : i + 4], [label_weight], shards, TILE, 1, before, last))
        back = jnp.concatenate([back for work in works for back in work["back"]], axis=0)
        back = swap(back.reshape(n_labels, n_data, cap, width)).reshape(slot_total, width)
        grad_feats = dot(pick, back, 0, 0).astype(BF16)
        _, _, share = sum_shares(*works[-1]["shares"])
        grad_label = grad_label_work(works, 1, 0, label_weight.shape)
        grad_enc = join_halves(share, grad_label, grad_feats)

    return (grad_feats, grad_label, grad_enc)


def solution(mesh):
    rows = P(("groups", "labels", "dp"), None)
    return jax.shard_map(
        local,
        mesh=mesh,
        in_specs=(rows, P("dp", None), rows, rows, rows, rows),
        out_specs=(rows, rows, P(("groups", "dp"), None)),
        check_vma=False,
    )
```

```python
import functools

import jax
import jax.numpy as jnp
from jax import lax
from jax.experimental import pallas as pl
from jax.experimental.pallas import tpu as pltpu
from jax.sharding import PartitionSpec as P

BLK = 128
EPSILON = 1e-06
META_ROWS = 8
TILE = 128
F32 = jnp.float32
BF16 = jnp.bfloat16
VMEM = pl.BlockSpec(memory_space=pltpu.VMEM)
HBM = pl.BlockSpec(memory_space=pltpu.HBM)


def dot(a, b, da=1, db=0):
    return lax.dot_general(a, b, (((da,), (db,)), ((), ())), preferred_element_type=F32)


def shard_at(m, shard_rows):
    at = jnp.bitwise_xor(lax.axis_index("dp"), m) * shard_rows
    return pl.ds(pl.multiple_of(at, 16), shard_rows)


def pair_kernel(*refs, cap, pick_count, n_sources, n_sets, n_data, first, last):
    it = iter(refs)
    take = lambda n: [next(it) for _ in range(n)]
    sources, labels = take(n_sources), take(n_sets)
    shards = take(n_data if first else 0)
    enc, total_in = (None, None) if first else take(2)
    backs, grad_scores_ref, block_ref, embedding_ref = take(n_sources), *take(3)
    enc = next(it) if first else enc
    shares = take(2 if last else 0)
    total_ref = next(it)

    n_owner_data = lax.axis_size("dp")
    me = lax.axis_index("labels") * n_owner_data + lax.axis_index("dp")
    rows = sources[0].shape[0] - META_ROWS
    shard_rows = enc.shape[0] // n_data
    n_blocks = labels[0].shape[0] // BLK
    part = n_sources * cap
    slots = n_sets * part

    for m, shard in enumerate(shards):
        enc[shard_at(m, shard_rows), :] = shard[...]

    row_id = lax.broadcasted_iota(jnp.int32, (rows, rows), 0)
    col_id = lax.broadcasted_iota(jnp.int32, (rows, rows), 1)
    before = (row_id < col_id).astype(BF16)
    slot_id = lax.broadcasted_iota(jnp.int32, (cap, rows), 0).astype(F32)
    column = lax.broadcasted_iota(jnp.int32, (slots, BLK), 1)

    hits, codes = [], []
    for source in sources:
        meta = source[rows:, 0 : 3 * rows].astype(F32)[:pick_count]
        code = meta[:, rows : 2 * rows] * 256.0 + meta[:, 2 * rows :] + 1.0
        for j in range(n_sets):
            named = meta[:, :rows] == jnp.bitwise_xor(me, j).astype(F32)
            hits.append(jnp.sum(named.astype(F32), axis=0, keepdims=True))
            codes.append(jnp.sum(jnp.where(named, code, 0.0), axis=0, keepdims=True))
    rank = dot(jnp.concatenate(hits, axis=0).astype(BF16), before)

    picks, picked, slot_codes = [], {}, {}
    for s, source in enumerate(sources):
        pick = []
        for j in range(n_sets):
            i = s * n_sets + j
            pick.append(jnp.where((slot_id == rank[i : i + 1]) & (hits[i] > 0.0), 1.0, 0.0))
            slot_codes[j, s] = jnp.sum(pick[j] * codes[i], axis=1, keepdims=True)
        picks.append(jnp.concatenate(pick, axis=0).astype(BF16))
        found = dot(picks[s], source[:rows, :]).astype(BF16)
        for j in range(n_sets):
            picked[j, s] = found[j * cap : (j + 1) * cap]
    order = [(j, s) for j in range(n_sets) for s in range(n_sources)]
    feats = jnp.concatenate([picked[i] for i in order], axis=0)
    code = jnp.concatenate([slot_codes[i] for i in order], axis=0).astype(jnp.int32) - 1

    hidden = dot(feats, enc[...])
    inv_rms = lax.rsqrt(jnp.mean(hidden * hidden, axis=-1, keepdims=True) + EPSILON)
    embedding = (hidden * inv_rms).astype(BF16)
    embedding_ref[...] = embedding

    block = jnp.broadcast_to(code >> 8, (slots, BLK))
    block_ref[...] = block
    wanted = jnp.broadcast_to(code & 255, (slots, BLK))
    target = jnp.where(column == wanted, 1.0, 0.0)
    grad_pairs = []
    for j in range(n_sets):
        at = slice(j * part, (j + 1) * part)
        scores = dot(embedding[at], labels[j][...], 1, 1)
        mine = block[at]
        own_scores = jnp.zeros((part, BLK), F32)
        for b in range(n_blocks):
            own_scores = jnp.where(mine == b, scores[:, b * BLK : (b + 1) * BLK], own_scores)
        grad_scores = jnp.where(mine >= 0, jax.nn.sigmoid(own_scores) - target[at], 0.0)
        grad_scores_ref[at, :] = grad_scores
        spread = jnp.concatenate(
            [jnp.where(mine == b, grad_scores, 0.0).astype(BF16) for b in range(n_blocks)], axis=1
        )
        grad_pairs.append(dot(spread, labels[j][...]))
    grad_pair = jnp.concatenate(grad_pairs, axis=0).astype(BF16).astype(F32)

    projection = jnp.mean(hidden * grad_pair, axis=-1, keepdims=True)
    grad_hidden = (inv_rms * grad_pair - hidden * (inv_rms**3 * projection)).astype(BF16)
    total = dot(feats, grad_hidden, 0, 0)
    total_ref[...] = total if first else total + total_in[...]
    for m in range(n_data if last else 0):
        shares[m % 2][m // 2] = total_ref[shard_at(m, shard_rows), :].astype(BF16)

    grad_feats = dot(grad_hidden, enc[...], 1, 1).astype(BF16)
    for s in range(n_sources):
        parts = [
            grad_feats[(j * n_sources + s) * cap : (j * n_sources + s + 1) * cap]
            for j in range(n_sets)
        ]
        backs[s][...] = dot(picks[s], jnp.concatenate(parts, axis=0), 0, 0).astype(BF16)


def grad_label_kernel(*refs, calls, n_sets, j):
    grad_scores, blocks, embeddings = refs[:calls], refs[calls : 2 * calls], refs[2 * calls : 3 * calls]
    more, out_ref = refs[3 * calls : -1], refs[-1]
    part = blocks[0].shape[0] // n_sets
    at = slice(j * part, (j + 1) * part)
    grad_scores_t = jnp.concatenate([r[at, :].T for r in grad_scores], axis=1)
    block_t = jnp.concatenate([r[at, :].T for r in blocks], axis=1)
    embedding = jnp.concatenate([r[at, :] for r in embeddings], axis=0)
    for b in range(out_ref.shape[0] // BLK):
        rows = slice(b * BLK, (b + 1) * BLK)
        spread_t = jnp.where(block_t == b, grad_scores_t, 0.0).astype(BF16)
        total = dot(spread_t, embedding)
        for ref in more:
            total = total + ref[rows, :].astype(F32)
        out_ref[rows, :] = total.astype(BF16)


def own_block_kernel(feats_ref, owners_ref, blocks_ref, positives_ref, out_ref, ints, sem):
    rows, width = feats_ref.shape
    feats = pltpu.make_async_copy(feats_ref, out_ref.at[pl.ds(0, rows)], sem.at[0])
    feats.start()
    copies = []
    for i, ref in enumerate((owners_ref, blocks_ref, positives_ref)):
        copies.append(pltpu.make_async_copy(ref, ints.at[i], sem.at[i + 1]))
        copies[i].start()
    for copy in copies:
        copy.wait()
    meta = [ints[i].astype(F32) for i in range(3)]
    meta += [jnp.zeros((meta[0].shape[0], width - 3 * rows), F32)]
    meta = jnp.concatenate(meta, axis=1)
    rest = jnp.zeros((META_ROWS - meta.shape[0], width), F32)
    out_ref[rows:, :] = jnp.concatenate([meta, rest], axis=0).astype(BF16)
    feats.wait()


def load_kernel(label_ref, shard_ref, label_out, shard_out):
    label_out[...] = label_ref[...]
    shard_out[...] = shard_ref[...]


def half_at(mine, half):
    odd = jnp.bitwise_and(lax.axis_index("labels"), 1)
    return pl.ds(pl.multiple_of((odd if mine else 1 - odd) * half, 16), half)


def split_kernel(even_ref, got_ref, *refs):
    *more, keep_ref, send_ref, total = refs
    share = even_ref[0].astype(F32) + got_ref[0].astype(F32)
    for ref in more:
        share = share + ref[...].astype(F32)
    total[...] = share
    half = keep_ref.shape[0]
    keep_ref[...] = total[half_at(True, half), :]
    send_ref[...] = total[half_at(False, half), :].astype(BF16)


def merge_kernel(mine_ref, other_ref, out_ref):
    half = mine_ref.shape[0]
    out_ref[half_at(True, half), :] = mine_ref[...].astype(F32)
    out_ref[half_at(False, half), :] = other_ref[...].astype(F32)


def call(kernel, name, out_shape, scratch, flops, megabytes, *args, space=VMEM, limit=24):
    return pl.pallas_call(
        kernel,
        in_specs=[space] * len(args),
        out_specs=jax.tree.map(lambda _: VMEM, out_shape),
        out_shape=out_shape,
        scratch_shapes=scratch,
        compiler_params=pltpu.CompilerParams(vmem_limit_bytes=limit << 20),
        cost_estimate=pl.CostEstimate(
            flops=flops, bytes_accessed=megabytes << 20, transcendentals=0
        ),
        name=name,
    )(*args)


def shaped(shape, dtype=BF16):
    return jax.ShapeDtypeStruct(shape, dtype)


def pair_work(sources, labels, shards, cap, pick_count, before, last):
    n_data, n_sets = len(shards), len(labels)
    block_rows, width = sources[0].shape
    rows = block_rows - META_ROWS
    slots = n_sets * len(sources) * cap
    shard_rows = shards[0].shape[0]
    full = (n_data * shard_rows, width)
    backs = len(sources)
    shapes = [shaped((rows, width))] * backs
    shapes += [shaped((slots, BLK), F32), shaped((slots, BLK), jnp.int32), shaped((slots, width))]
    more = [before["enc"], before["total"]] if before else shards
    scratch = []
    if not before:
        shapes += [shaped(full)]
    if last:
        shapes += [shaped((n_data // 2, shard_rows, width))] * 2
        scratch = [pltpu.VMEM(full, F32)]
    else:
        shapes += [shaped(full, F32)]
    out = call(
        functools.partial(
            pair_kernel,
            cap=cap,
            pick_count=pick_count,
            n_sources=len(sources),
            n_sets=n_sets,
            n_data=n_data,
            first=not before,
            last=last,
        ),
        "pair_work",
        shapes,
        scratch,
        2 * slots * width * (2 * labels[0].shape[0] + 3 * width + 2 * rows),
        8,
        *sources,
        *labels,
        *more,
    )
    result = {"back": list(out[:backs]), "slots": list(out[backs : backs + 3])}
    rest = list(out[backs + 3 :])
    result["enc"] = before["enc"] if before else rest.pop(0)
    result["shares" if last else "total"] = rest if last else rest[0]
    return result


def grad_label_work(works, n_sets, j, labels_shape, *more):
    slots = list(zip(*(work["slots"] for work in works)))
    return call(
        functools.partial(grad_label_kernel, calls=len(works), n_sets=n_sets, j=j),
        "grad_label_work",
        shaped(labels_shape),
        [],
        2 * sum(x.shape[0] for x in slots[0]) // n_sets * labels_shape[0] * labels_shape[1],
        4,
        *slots[0],
        *slots[1],
        *slots[2],
        *more,
    )


def swap(x):
    x = lax.all_to_all(x, "labels", split_axis=0, concat_axis=0, tiled=True)
    return lax.all_to_all(x, "dp", split_axis=1, concat_axis=1, tiled=True)


def partner(x, axis, mask):
    return lax.ppermute(x, axis, [(i, i ^ mask) for i in range(lax.axis_size(axis))])


def masks(n):
    return [1 << i for i in range(n.bit_length() - 1)]


def after(x, *others):
    return lax.optimization_barrier((x, *others))[0]


def gather_far(x):
    got = {0: x}
    for mask in reversed(masks(lax.axis_size("dp"))[1:]):
        got.update({m | mask: partner(v, "dp", mask) for m, v in list(got.items())})
    return [got[m] for m in sorted(got)]


def gather_near(far, *first):
    near = [partner(after(v, *far[1:], *first), "dp", 1) for v in far]
    return [v for pair in zip(far, near) for v in pair]


def gather_labels(x, first):
    got = {0: x}
    for mask in reversed(masks(lax.axis_size("labels"))):
        for m, v in list(got.items()):
            got[m | mask] = partner(after(v, first) if m else v, "labels", mask)
    return [got[m] for m in range(len(got))]


def add(*terms):
    return sum(t.astype(F32) for t in terms)


def dp_terms(even, odd):
    got = partner(odd, "dp", 1)
    terms = [[even[i], got[i]] for i in range(even.shape[0])]
    for mask in masks(len(terms)):
        for i in range(len(terms)):
            if i & mask == 0 and i % mask == 0:
                terms[i].append(partner(add(*terms[i | mask]).astype(BF16), "dp", 2 * mask))
    return got, terms[0]


def sum_shares(even, odd, *first):
    got, terms = dp_terms(even, odd)
    rows, width = even.shape[1:]
    half = rows // 2
    keep, send = call(
        split_kernel,
        "split_share",
        [shaped((half, width), F32), shaped((half, width))],
        [pltpu.VMEM((rows, width), F32)],
        0,
        1,
        even,
        after(got, *first),
        *terms[2:],
    )
    x = add(keep, partner(send, "labels", 1)).astype(BF16)
    first = x
    for mask in masks(lax.axis_size("labels"))[1:]:
        x = add(x, partner(x, "labels", mask)).astype(BF16)
    return keep, first, x


def join_halves(x, *first):
    other = partner(x, "labels", 1)
    out = shaped((2 * x.shape[0], x.shape[1]), F32)
    return call(merge_kernel, "merge_share", out, [], 0, 1, after(x, *first), other)


def reduce_runs(runs, got_last, keep, first):
    n = len(runs)
    sums = {}
    held = [keep]
    for i in reversed(range(0, n, 2)):
        got = got_last
        if i + 2 < n:
            holds = [[first]] + [held] * (len(runs[i]) - 1)
            got = [partner(after(x, *hold), "labels", 1) for x, hold in zip(runs[i + 1], holds)]
        parts = [[part, got[h]] for h, part in enumerate(runs[i])]
        for mask in masks(len(parts)):
            for h in range(0, len(parts), 2 * mask):
                sent = after(add(*parts[h + mask]).astype(BF16), *held)
                parts[h].append(partner(sent, "dp", 2 * mask))
        sums[i] = parts[0]
        held = parts[0][-1:]
    for mask in masks(n)[1:]:
        for i in range(0, n, 2 * mask):
            sent = after(add(*sums[i + mask]).astype(BF16), first)
            sums[i].append(partner(sent, "labels", mask))
    return add(*sums[0]).astype(BF16)


def with_meta(feats, owner_rows, block_rows, positive_rows):
    meta = jnp.concatenate([owner_rows, block_rows, positive_rows], axis=1).astype(BF16)
    meta = jnp.pad(meta, ((0, META_ROWS - meta.shape[0]), (0, feats.shape[1] - meta.shape[1])))
    return jnp.concatenate([feats, meta], axis=0)


def local(feats, enc_weight, label_weight, owners, blocks, positives):
    n_labels = lax.axis_size("labels")
    n_data = lax.axis_size("dp")
    n_owner = n_labels * n_data
    row_count, width = feats.shape
    pick_count = owners.shape[1]
    cap = max(2, 2 * row_count * pick_count // n_owner)

    if row_count <= n_data * cap:
        own = call(
            own_block_kernel,
            "own_block",
            shaped((row_count + META_ROWS, width)),
            [
                pltpu.VMEM((3, pick_count, row_count), jnp.int32),
                pltpu.SemaphoreType.DMA((4,)),
            ],
            0,
            1,
            feats,
            owners.T,
            blocks.T,
            positives.T,
            space=HBM,
            limit=60,
        )
        labels = [label_weight, partner(label_weight, "dp", 1)]
        labels[0], own_shard = call(
            load_kernel,
            "load",
            [shaped(label_weight.shape), shaped(enc_weight.shape)],
            [],
            0,
            4,
            after(label_weight, labels[1]),
            enc_weight,
        )
        near = gather_labels(own, labels[0])
        far = {0: gather_far(near[0])}
        shards = gather_near(gather_far(enc_weight), *far[0][1:], *near[1:3], labels[0])
        shards[0] = own_shard
        works, backs = [], {}
        for run in [*range(0, n_labels, 2), *range(1, n_labels, 2)]:
            last = run == n_labels - 1
            if last:
                far[run] = gather_far(after(near[run], *far[run - 1][1:]))
            elif run % 2:
                sent = [after(x, works[0]["slots"][0]) for x in far[run - 1][1:]]
                far[run] = near[run : run + 1] + [partner(x, "labels", 1) for x in sent]
            elif run:
                far[run] = gather_far(after(near[run], *far[0][1:]))
            sources = [after(near[run], *([] if run else near[1:3]))] + far[run][1:]
            before = works[-1] if works else None
            works.append(pair_work(sources, labels, shards, cap, pick_count, before, last))
            backs[run] = works[-1]["back"]
        got_last = [partner(x, "labels", 1) for x in works[-1]["back"]]
        keep, first, share = sum_shares(*works[-1]["shares"], *got_last[1:])
        grad_feats = reduce_runs(backs, got_last, keep, first)
        works[0]["slots"][2] = after(works[0]["slots"][2], *got_last[1:])
        other = partner(grad_label_work(works, 2, 1, label_weight.shape), "dp", 1)
        grad_label = grad_label_work(works, 2, 0, label_weight.shape, other)
        grad_enc = join_halves(share, grad_label, grad_feats)
    else:
        shards = gather_near(gather_far(enc_weight))
        flat = owners.reshape(-1)
        onehot = (flat[:, None] == jnp.arange(n_owner, dtype=jnp.int32)[None, :]).astype(jnp.int32)
        rank = jnp.sum((jnp.cumsum(onehot, axis=0) - onehot) * onehot, axis=1)
        slot = (flat * cap + rank).reshape(row_count, pick_count)
        slot_total = n_owner * cap
        slots = jnp.arange(slot_total, dtype=jnp.int32)
        place = slots[:, None, None] == slot[None]
        pick = jnp.any(place, axis=2).astype(BF16)
        live = jnp.any(place, axis=(1, 2))
        block_of = jnp.sum(jnp.where(place, blocks[None], 0), axis=(1, 2))
        wanted = jnp.sum(jnp.where(place, positives[None], 0), axis=(1, 2))
        owner_of = jnp.where(live, slots // cap, -1)
        out = dot(pick, feats).astype(BF16).reshape(n_labels, n_data, cap, width)
        meta = jnp.stack([owner_of, block_of, wanted], axis=1).reshape(n_labels, n_data, cap, 3)
        tiles = slot_total // TILE
        got = swap(out).reshape(tiles, TILE, width)
        got_meta = swap(meta).reshape(tiles, TILE, 3).transpose(0, 2, 1)
        sources = [
            with_meta(got[i], got_meta[i, 0:1], got_meta[i, 1:2], got_meta[i, 2:3])
            for i in range(tiles)
        ]
        works = []
        for i in range(0, tiles, 4):
            before = works[-1] if works else None
            last = i + 4 >= tiles
            works.append(pair_work(sources[i : i + 4], [label_weight], shards, TILE, 1, before, last))
        back = jnp.concatenate([back for work in works for back in work["back"]], axis=0)
        back = swap(back.reshape(n_labels, n_data, cap, width)).reshape(slot_total, width)
        grad_feats = dot(pick, back, 0, 0).astype(BF16)
        *_, share = sum_shares(*works[-1]["shares"])
        grad_label = grad_label_work(works, 1, 0, label_weight.shape)
        grad_enc = join_halves(share, grad_label, grad_feats)

    return (grad_feats, grad_label, grad_enc)


def solution(mesh):
    rows = P(("groups", "labels", "dp"), None)
    return jax.shard_map(
        local,
        mesh=mesh,
        in_specs=(rows, P("dp", None), rows, rows, rows, rows),
        out_specs=(rows, rows, P(("groups", "dp"), None)),
        check_vma=False,
    )
```

```python
import functools

import jax
import jax.numpy as jnp
from jax import lax
from jax.experimental import pallas as pl
from jax.experimental.pallas import tpu as pltpu
from jax.sharding import PartitionSpec as P

BLK = 128
EPSILON = 1e-06
META_ROWS = 8
TILE = 128
F32 = jnp.float32
BF16 = jnp.bfloat16
VMEM = pl.BlockSpec(memory_space=pltpu.VMEM)
HBM = pl.BlockSpec(memory_space=pltpu.HBM)


def dot(a, b, da=1, db=0):
    return lax.dot_general(a, b, (((da,), (db,)), ((), ())), preferred_element_type=F32)


def shard_at(m, shard_rows):
    at = jnp.bitwise_xor(lax.axis_index("dp"), m) * shard_rows
    return pl.ds(pl.multiple_of(at, 16), shard_rows)


def pair_kernel(*refs, cap, pick_count, n_sources, n_sets, n_data, first, last):
    it = iter(refs)
    take = lambda n: [next(it) for _ in range(n)]
    sources, labels = take(n_sources), take(n_sets)
    shards = take(n_data if first else 0)
    enc, total_in = (None, None) if first else take(2)
    backs, grad_scores_ref, block_ref, embedding_ref = take(n_sources), *take(3)
    enc = next(it) if first else enc
    shares = take(2 if last else 0)
    total_ref = next(it)

    n_owner_data = lax.axis_size("dp")
    me = lax.axis_index("labels") * n_owner_data + lax.axis_index("dp")
    rows = sources[0].shape[0] - META_ROWS
    shard_rows = enc.shape[0] // n_data
    n_blocks = labels[0].shape[0] // BLK
    part = n_sources * cap
    slots = n_sets * part

    for m, shard in enumerate(shards):
        enc[shard_at(m, shard_rows), :] = shard[...]

    row_id = lax.broadcasted_iota(jnp.int32, (rows, rows), 0)
    col_id = lax.broadcasted_iota(jnp.int32, (rows, rows), 1)
    before = (row_id < col_id).astype(BF16)
    slot_id = lax.broadcasted_iota(jnp.int32, (cap, rows), 0).astype(F32)
    column = lax.broadcasted_iota(jnp.int32, (slots, BLK), 1)

    hits, codes = [], []
    for source in sources:
        meta = source[rows:, 0 : 3 * rows].astype(F32)[:pick_count]
        code = meta[:, rows : 2 * rows] * 256.0 + meta[:, 2 * rows :] + 1.0
        for j in range(n_sets):
            named = meta[:, :rows] == jnp.bitwise_xor(me, j).astype(F32)
            hits.append(jnp.sum(named.astype(F32), axis=0, keepdims=True))
            codes.append(jnp.sum(jnp.where(named, code, 0.0), axis=0, keepdims=True))
    rank = dot(jnp.concatenate(hits, axis=0).astype(BF16), before)

    picks, picked, slot_codes = [], {}, {}
    for s, source in enumerate(sources):
        pick = []
        for j in range(n_sets):
            i = s * n_sets + j
            pick.append(jnp.where((slot_id == rank[i : i + 1]) & (hits[i] > 0.0), 1.0, 0.0))
            slot_codes[j, s] = jnp.sum(pick[j] * codes[i], axis=1, keepdims=True)
        picks.append(jnp.concatenate(pick, axis=0).astype(BF16))
        found = dot(picks[s], source[:rows, :]).astype(BF16)
        for j in range(n_sets):
            picked[j, s] = found[j * cap : (j + 1) * cap]
    order = [(j, s) for j in range(n_sets) for s in range(n_sources)]
    feats = jnp.concatenate([picked[i] for i in order], axis=0)
    code = jnp.concatenate([slot_codes[i] for i in order], axis=0).astype(jnp.int32) - 1

    hidden = dot(feats, enc[...])
    inv_rms = lax.rsqrt(jnp.mean(hidden * hidden, axis=-1, keepdims=True) + EPSILON)
    embedding = (hidden * inv_rms).astype(BF16)
    embedding_ref[...] = embedding

    block = jnp.broadcast_to(code >> 8, (slots, BLK))
    block_ref[...] = block
    wanted = jnp.broadcast_to(code & 255, (slots, BLK))
    target = jnp.where(column == wanted, 1.0, 0.0)
    grad_pairs = []
    for j in range(n_sets):
        at = slice(j * part, (j + 1) * part)
        scores = dot(embedding[at], labels[j][...], 1, 1)
        mine = block[at]
        own_scores = jnp.zeros((part, BLK), F32)
        for b in range(n_blocks):
            own_scores = jnp.where(mine == b, scores[:, b * BLK : (b + 1) * BLK], own_scores)
        grad_scores = jnp.where(mine >= 0, jax.nn.sigmoid(own_scores) - target[at], 0.0)
        grad_scores_ref[at, :] = grad_scores
        spread = jnp.concatenate(
            [jnp.where(mine == b, grad_scores, 0.0).astype(BF16) for b in range(n_blocks)], axis=1
        )
        grad_pairs.append(dot(spread, labels[j][...]))
    grad_pair = jnp.concatenate(grad_pairs, axis=0).astype(BF16).astype(F32)

    projection = jnp.mean(hidden * grad_pair, axis=-1, keepdims=True)
    grad_hidden = (inv_rms * grad_pair - hidden * (inv_rms**3 * projection)).astype(BF16)
    total = dot(feats, grad_hidden, 0, 0)
    total_ref[...] = total if first else total + total_in[...]
    for m in range(n_data if last else 0):
        shares[m % 2][m // 2] = total_ref[shard_at(m, shard_rows), :].astype(BF16)

    grad_feats = dot(grad_hidden, enc[...], 1, 1).astype(BF16)
    for s in range(n_sources):
        parts = [
            grad_feats[(j * n_sources + s) * cap : (j * n_sources + s + 1) * cap]
            for j in range(n_sets)
        ]
        backs[s][...] = dot(picks[s], jnp.concatenate(parts, axis=0), 0, 0).astype(BF16)


def grad_label_kernel(*refs, calls, n_sets, j):
    grad_scores, blocks, embeddings = refs[:calls], refs[calls : 2 * calls], refs[2 * calls : 3 * calls]
    more, out_ref = refs[3 * calls : -1], refs[-1]
    part = blocks[0].shape[0] // n_sets
    at = slice(j * part, (j + 1) * part)
    grad_scores_t = jnp.concatenate([r[at, :].T for r in grad_scores], axis=1)
    block_t = jnp.concatenate([r[at, :].T for r in blocks], axis=1)
    embedding = jnp.concatenate([r[at, :] for r in embeddings], axis=0)
    for b in range(out_ref.shape[0] // BLK):
        rows = slice(b * BLK, (b + 1) * BLK)
        spread_t = jnp.where(block_t == b, grad_scores_t, 0.0).astype(BF16)
        total = dot(spread_t, embedding)
        for ref in more:
            total = total + ref[rows, :].astype(F32)
        out_ref[rows, :] = total.astype(BF16)


def own_block_kernel(feats_ref, owners_ref, blocks_ref, positives_ref, out_ref, ints, sem):
    rows, width = feats_ref.shape
    feats = pltpu.make_async_copy(feats_ref, out_ref.at[pl.ds(0, rows)], sem.at[0])
    feats.start()
    copies = []
    for i, ref in enumerate((owners_ref, blocks_ref, positives_ref)):
        copies.append(pltpu.make_async_copy(ref, ints.at[i], sem.at[i + 1]))
        copies[i].start()
    for copy in copies:
        copy.wait()
    meta = [ints[i].astype(F32) for i in range(3)]
    meta += [jnp.zeros((meta[0].shape[0], width - 3 * rows), F32)]
    meta = jnp.concatenate(meta, axis=1)
    rest = jnp.zeros((META_ROWS - meta.shape[0], width), F32)
    out_ref[rows:, :] = jnp.concatenate([meta, rest], axis=0).astype(BF16)
    feats.wait()


def load_kernel(label_ref, shard_ref, label_out, shard_out):
    label_out[...] = label_ref[...]
    shard_out[...] = shard_ref[...]


def half_at(mine, half):
    odd = jnp.bitwise_and(lax.axis_index("labels"), 1)
    return pl.ds(pl.multiple_of((odd if mine else 1 - odd) * half, 16), half)


def split_kernel(even_ref, got_ref, *refs):
    *more, keep_ref, send_ref, total = refs
    share = even_ref[0].astype(F32) + got_ref[0].astype(F32)
    for ref in more:
        share = share + ref[...].astype(F32)
    total[...] = share
    half = keep_ref.shape[0]
    keep_ref[...] = total[half_at(True, half), :]
    send_ref[...] = total[half_at(False, half), :].astype(BF16)


def merge_kernel(mine_ref, other_ref, out_ref):
    half = mine_ref.shape[0]
    out_ref[half_at(True, half), :] = mine_ref[...].astype(F32)
    out_ref[half_at(False, half), :] = other_ref[...].astype(F32)


def call(kernel, name, out_shape, scratch, flops, megabytes, *args, space=VMEM, limit=24):
    return pl.pallas_call(
        kernel,
        in_specs=[space] * len(args),
        out_specs=jax.tree.map(lambda _: VMEM, out_shape),
        out_shape=out_shape,
        scratch_shapes=scratch,
        compiler_params=pltpu.CompilerParams(vmem_limit_bytes=limit << 20),
        cost_estimate=pl.CostEstimate(
            flops=flops, bytes_accessed=megabytes << 20, transcendentals=0
        ),
        name=name,
    )(*args)


def shaped(shape, dtype=BF16):
    return jax.ShapeDtypeStruct(shape, dtype)


def pair_work(sources, labels, shards, cap, pick_count, before, last):
    n_data, n_sets = len(shards), len(labels)
    block_rows, width = sources[0].shape
    rows = block_rows - META_ROWS
    slots = n_sets * len(sources) * cap
    shard_rows = shards[0].shape[0]
    full = (n_data * shard_rows, width)
    backs = len(sources)
    shapes = [shaped((rows, width))] * backs
    shapes += [shaped((slots, BLK), F32), shaped((slots, BLK), jnp.int32), shaped((slots, width))]
    more = [before["enc"], before["total"]] if before else shards
    scratch = []
    if not before:
        shapes += [shaped(full)]
    if last:
        shapes += [shaped((n_data // 2, shard_rows, width))] * 2
        scratch = [pltpu.VMEM(full, F32)]
    else:
        shapes += [shaped(full, F32)]
    out = call(
        functools.partial(
            pair_kernel,
            cap=cap,
            pick_count=pick_count,
            n_sources=len(sources),
            n_sets=n_sets,
            n_data=n_data,
            first=not before,
            last=last,
        ),
        "pair_work",
        shapes,
        scratch,
        2 * slots * width * (2 * labels[0].shape[0] + 3 * width + 2 * rows),
        8,
        *sources,
        *labels,
        *more,
    )
    result = {"back": list(out[:backs]), "slots": list(out[backs : backs + 3])}
    rest = list(out[backs + 3 :])
    result["enc"] = before["enc"] if before else rest.pop(0)
    result["shares" if last else "total"] = rest if last else rest[0]
    return result


def grad_label_work(works, n_sets, j, labels_shape, *more):
    slots = list(zip(*(work["slots"] for work in works)))
    return call(
        functools.partial(grad_label_kernel, calls=len(works), n_sets=n_sets, j=j),
        "grad_label_work",
        shaped(labels_shape),
        [],
        2 * sum(x.shape[0] for x in slots[0]) // n_sets * labels_shape[0] * labels_shape[1],
        4,
        *slots[0],
        *slots[1],
        *slots[2],
        *more,
    )


def swap(x):
    x = lax.all_to_all(x, "labels", split_axis=0, concat_axis=0, tiled=True)
    return lax.all_to_all(x, "dp", split_axis=1, concat_axis=1, tiled=True)


def partner(x, axis, mask):
    return lax.ppermute(x, axis, [(i, i ^ mask) for i in range(lax.axis_size(axis))])


def masks(n):
    return [1 << i for i in range(n.bit_length() - 1)]


def after(x, *others):
    return lax.optimization_barrier((x, *others))[0]


def gather_far(x):
    got = {0: x}
    for mask in reversed(masks(lax.axis_size("dp"))[1:]):
        got.update({m | mask: partner(v, "dp", mask) for m, v in list(got.items())})
    return [got[m] for m in sorted(got)]


def gather_near(far, *first):
    near = [partner(after(v, *far[1:], *first), "dp", 1) for v in far]
    return [v for pair in zip(far, near) for v in pair]


def gather_labels(x, first):
    got = {0: x}
    for mask in reversed(masks(lax.axis_size("labels"))):
        for m, v in list(got.items()):
            got[m | mask] = partner(after(v, first) if m else v, "labels", mask)
    return [got[m] for m in range(len(got))]


def add(*terms):
    return sum(t.astype(F32) for t in terms)


def dp_terms(even, odd):
    got = partner(odd, "dp", 1)
    terms = [[even[i], got[i]] for i in range(even.shape[0])]
    for mask in masks(len(terms)):
        for i in range(len(terms)):
            if i & mask == 0 and i % mask == 0:
                terms[i].append(partner(add(*terms[i | mask]).astype(BF16), "dp", 2 * mask))
    return got, terms[0]


def sum_shares(even, odd, *first):
    got, terms = dp_terms(even, odd)
    rows, width = even.shape[1:]
    half = rows // 2
    keep, send = call(
        split_kernel,
        "split_share",
        [shaped((half, width), F32), shaped((half, width))],
        [pltpu.VMEM((rows, width), F32)],
        0,
        1,
        even,
        after(got, *first),
        *terms[2:],
    )
    x = add(keep, partner(send, "labels", 1)).astype(BF16)
    first = x
    for mask in masks(lax.axis_size("labels"))[1:]:
        x = add(x, partner(x, "labels", mask)).astype(BF16)
    return keep, first, x


def join_halves(x, *first):
    other = partner(x, "labels", 1)
    out = shaped((2 * x.shape[0], x.shape[1]), F32)
    return call(merge_kernel, "merge_share", out, [], 0, 1, after(x, *first), other)


def reduce_runs(runs, got_last, keep, first):
    def over_dp(parts, *hold):
        parts = [list(part) for part in parts]
        for mask in masks(len(parts)):
            for h in range(0, len(parts), 2 * mask):
                sent = after(add(*parts[h + mask]).astype(BF16), *hold)
                parts[h].append(partner(sent, "dp", 2 * mask))
        return parts[0]

    n = len(runs)
    sums = {n - 2: over_dp(list(zip(runs[n - 2], got_last)), keep)}
    held = sums[n - 2][-1:]
    for i in reversed(range(0, n - 2, 2)):
        near = after(add(*over_dp([[x] for x in runs[i + 1]], *held)).astype(BF16), first)
        sums[i] = over_dp([[x] for x in runs[i]], *held) + [partner(near, "labels", 1)]
    for mask in masks(n)[1:]:
        for i in range(0, n, 2 * mask):
            sent = after(add(*sums[i + mask]).astype(BF16), first)
            sums[i].append(partner(sent, "labels", mask))
    return sums[0]


def with_meta(feats, owner_rows, block_rows, positive_rows):
    meta = jnp.concatenate([owner_rows, block_rows, positive_rows], axis=1).astype(BF16)
    meta = jnp.pad(meta, ((0, META_ROWS - meta.shape[0]), (0, feats.shape[1] - meta.shape[1])))
    return jnp.concatenate([feats, meta], axis=0)


def local(feats, enc_weight, label_weight, owners, blocks, positives):
    n_labels = lax.axis_size("labels")
    n_data = lax.axis_size("dp")
    n_owner = n_labels * n_data
    row_count, width = feats.shape
    pick_count = owners.shape[1]
    cap = max(2, 2 * row_count * pick_count // n_owner)

    if row_count <= n_data * cap:
        own = call(
            own_block_kernel,
            "own_block",
            shaped((row_count + META_ROWS, width)),
            [
                pltpu.VMEM((3, pick_count, row_count), jnp.int32),
                pltpu.SemaphoreType.DMA((4,)),
            ],
            0,
            1,
            feats,
            owners.T,
            blocks.T,
            positives.T,
            space=HBM,
            limit=60,
        )
        labels = [label_weight, partner(label_weight, "dp", 1)]
        labels[0], own_shard = call(
            load_kernel,
            "load",
            [shaped(label_weight.shape), shaped(enc_weight.shape)],
            [],
            0,
            4,
            after(label_weight, labels[1]),
            enc_weight,
        )
        near = gather_labels(own, labels[0])
        far = {0: gather_far(near[0])}
        shards = gather_near(gather_far(enc_weight), *far[0][1:], *near[1:3], labels[0])
        shards[0] = own_shard
        works, backs = [], {}
        for run in [*range(0, n_labels, 2), *range(1, n_labels, 2)]:
            last = run == n_labels - 1
            if last:
                far[run] = gather_far(after(near[run], *far[run - 1][1:]))
            elif run % 2:
                sent = [after(x, works[0]["slots"][0]) for x in far[run - 1][1:]]
                far[run] = near[run : run + 1] + [partner(x, "labels", 1) for x in sent]
            elif run:
                far[run] = gather_far(after(near[run], *far[0][1:]))
            sources = [after(near[run], *([] if run else near[1:3]))] + far[run][1:]
            before = works[-1] if works else None
            works.append(pair_work(sources, labels, shards, cap, pick_count, before, last))
            backs[run] = works[-1]["back"]
        got_last = [partner(x, "labels", 1) for x in works[-1]["back"]]
        keep, first, share = sum_shares(*works[-1]["shares"], *got_last[1:])
        terms = reduce_runs(backs, got_last, keep, first)
        works[0]["slots"][2] = after(works[0]["slots"][2], *got_last[1:])
        other = partner(grad_label_work(works, 2, 1, label_weight.shape), "dp", 1)
        grad_label = grad_label_work(works, 2, 0, label_weight.shape, other)
        grad_feats = add(after(terms[0], grad_label), *terms[1:]).astype(BF16)
        grad_enc = join_halves(share, grad_label, grad_feats)
    else:
        shards = gather_near(gather_far(enc_weight))
        flat = owners.reshape(-1)
        onehot = (flat[:, None] == jnp.arange(n_owner, dtype=jnp.int32)[None, :]).astype(jnp.int32)
        rank = jnp.sum((jnp.cumsum(onehot, axis=0) - onehot) * onehot, axis=1)
        slot = (flat * cap + rank).reshape(row_count, pick_count)
        slot_total = n_owner * cap
        slots = jnp.arange(slot_total, dtype=jnp.int32)
        place = slots[:, None, None] == slot[None]
        pick = jnp.any(place, axis=2).astype(BF16)
        live = jnp.any(place, axis=(1, 2))
        block_of = jnp.sum(jnp.where(place, blocks[None], 0), axis=(1, 2))
        wanted = jnp.sum(jnp.where(place, positives[None], 0), axis=(1, 2))
        owner_of = jnp.where(live, slots // cap, -1)
        out = dot(pick, feats).astype(BF16).reshape(n_labels, n_data, cap, width)
        meta = jnp.stack([owner_of, block_of, wanted], axis=1).reshape(n_labels, n_data, cap, 3)
        tiles = slot_total // TILE
        got = swap(out).reshape(tiles, TILE, width)
        got_meta = swap(meta).reshape(tiles, TILE, 3).transpose(0, 2, 1)
        sources = [
            with_meta(got[i], got_meta[i, 0:1], got_meta[i, 1:2], got_meta[i, 2:3])
            for i in range(tiles)
        ]
        works = []
        for i in range(0, tiles, 4):
            before = works[-1] if works else None
            last = i + 4 >= tiles
            works.append(pair_work(sources[i : i + 4], [label_weight], shards, TILE, 1, before, last))
        back = jnp.concatenate([back for work in works for back in work["back"]], axis=0)
        back = swap(back.reshape(n_labels, n_data, cap, width)).reshape(slot_total, width)
        grad_feats = dot(pick, back, 0, 0).astype(BF16)
        *_, share = sum_shares(*works[-1]["shares"])
        grad_label = grad_label_work(works, 1, 0, label_weight.shape)
        grad_enc = join_halves(share, grad_label, grad_feats)

    return (grad_feats, grad_label, grad_enc)


def solution(mesh):
    rows = P(("groups", "labels", "dp"), None)
    return jax.shard_map(
        local,
        mesh=mesh,
        in_specs=(rows, P("dp", None), rows, rows, rows, rows),
        out_specs=(rows, rows, P(("groups", "dp"), None)),
        check_vma=False,
    )
```

```python
import functools

import jax
import jax.numpy as jnp
from jax import lax
from jax.experimental import pallas as pl
from jax.experimental.pallas import tpu as pltpu
from jax.sharding import PartitionSpec as P

BLK = 128
EPSILON = 1e-06
META_ROWS = 8
TILE = 128
F32 = jnp.float32
BF16 = jnp.bfloat16
VMEM = pl.BlockSpec(memory_space=pltpu.VMEM)
HBM = pl.BlockSpec(memory_space=pltpu.HBM)


def dot(a, b, da=1, db=0):
    return lax.dot_general(a, b, (((da,), (db,)), ((), ())), preferred_element_type=F32)


def shard_at(m, shard_rows):
    at = jnp.bitwise_xor(lax.axis_index("dp"), m) * shard_rows
    return pl.ds(pl.multiple_of(at, 16), shard_rows)


def pair_kernel(*refs, cap, pick_count, n_sources, n_sets, n_data, first, last):
    it = iter(refs)
    take = lambda n: [next(it) for _ in range(n)]
    sources, labels = take(n_sources), take(n_sets)
    shards = take(n_data if first else 0)
    enc, total_in = (None, None) if first else take(2)
    backs, grad_scores_ref, block_ref, embedding_ref = take(n_sources), *take(3)
    enc = next(it) if first else enc
    shares = take(2 if last else 0)
    total_ref = next(it)

    n_owner_data = lax.axis_size("dp")
    me = lax.axis_index("labels") * n_owner_data + lax.axis_index("dp")
    rows = sources[0].shape[0] - META_ROWS
    shard_rows = enc.shape[0] // n_data
    n_blocks = labels[0].shape[0] // BLK
    part = n_sources * cap
    slots = n_sets * part

    for m, shard in enumerate(shards):
        enc[shard_at(m, shard_rows), :] = shard[...]

    row_id = lax.broadcasted_iota(jnp.int32, (rows, rows), 0)
    col_id = lax.broadcasted_iota(jnp.int32, (rows, rows), 1)
    before = (row_id < col_id).astype(BF16)
    slot_id = lax.broadcasted_iota(jnp.int32, (cap, rows), 0).astype(F32)
    column = lax.broadcasted_iota(jnp.int32, (slots, BLK), 1)

    hits, codes = [], []
    for source in sources:
        meta = source[rows:, 0 : 3 * rows].astype(F32)[:pick_count]
        code = meta[:, rows : 2 * rows] * 256.0 + meta[:, 2 * rows :] + 1.0
        for j in range(n_sets):
            named = meta[:, :rows] == jnp.bitwise_xor(me, j).astype(F32)
            hits.append(jnp.sum(named.astype(F32), axis=0, keepdims=True))
            codes.append(jnp.sum(jnp.where(named, code, 0.0), axis=0, keepdims=True))
    rank = dot(jnp.concatenate(hits, axis=0).astype(BF16), before)

    picks, picked, slot_codes = [], {}, {}
    for s, source in enumerate(sources):
        pick = []
        for j in range(n_sets):
            i = s * n_sets + j
            pick.append(jnp.where((slot_id == rank[i : i + 1]) & (hits[i] > 0.0), 1.0, 0.0))
            slot_codes[j, s] = jnp.sum(pick[j] * codes[i], axis=1, keepdims=True)
        picks.append(jnp.concatenate(pick, axis=0).astype(BF16))
        found = dot(picks[s], source[:rows, :]).astype(BF16)
        for j in range(n_sets):
            picked[j, s] = found[j * cap : (j + 1) * cap]
    order = [(j, s) for j in range(n_sets) for s in range(n_sources)]
    feats = jnp.concatenate([picked[i] for i in order], axis=0)
    code = jnp.concatenate([slot_codes[i] for i in order], axis=0).astype(jnp.int32) - 1

    hidden = dot(feats, enc[...])
    inv_rms = lax.rsqrt(jnp.mean(hidden * hidden, axis=-1, keepdims=True) + EPSILON)
    embedding = (hidden * inv_rms).astype(BF16)
    embedding_ref[...] = embedding

    block = jnp.broadcast_to(code >> 8, (slots, BLK))
    block_ref[...] = block
    wanted = jnp.broadcast_to(code & 255, (slots, BLK))
    target = jnp.where(column == wanted, 1.0, 0.0)
    grad_pairs = []
    for j in range(n_sets):
        at = slice(j * part, (j + 1) * part)
        scores = dot(embedding[at], labels[j][...], 1, 1)
        mine = block[at]
        own_scores = jnp.zeros((part, BLK), F32)
        for b in range(n_blocks):
            own_scores = jnp.where(mine == b, scores[:, b * BLK : (b + 1) * BLK], own_scores)
        grad_scores = jnp.where(mine >= 0, jax.nn.sigmoid(own_scores) - target[at], 0.0)
        grad_scores_ref[at, :] = grad_scores
        spread = jnp.concatenate(
            [jnp.where(mine == b, grad_scores, 0.0).astype(BF16) for b in range(n_blocks)], axis=1
        )
        grad_pairs.append(dot(spread, labels[j][...]))
    grad_pair = jnp.concatenate(grad_pairs, axis=0).astype(BF16).astype(F32)

    projection = jnp.mean(hidden * grad_pair, axis=-1, keepdims=True)
    grad_hidden = (inv_rms * grad_pair - hidden * (inv_rms**3 * projection)).astype(BF16)
    total = dot(feats, grad_hidden, 0, 0)
    total_ref[...] = total if first else total + total_in[...]
    for m in range(n_data if last else 0):
        shares[m % 2][m // 2] = total_ref[shard_at(m, shard_rows), :].astype(BF16)

    grad_feats = dot(grad_hidden, enc[...], 1, 1).astype(BF16)
    for s in range(n_sources):
        parts = [
            grad_feats[(j * n_sources + s) * cap : (j * n_sources + s + 1) * cap]
            for j in range(n_sets)
        ]
        backs[s][...] = dot(picks[s], jnp.concatenate(parts, axis=0), 0, 0).astype(BF16)


def grad_label_kernel(*refs, calls, n_sets, j):
    grad_scores, blocks, embeddings = refs[:calls], refs[calls : 2 * calls], refs[2 * calls : 3 * calls]
    more, out_ref = refs[3 * calls : -1], refs[-1]
    part = blocks[0].shape[0] // n_sets
    at = slice(j * part, (j + 1) * part)
    grad_scores_t = jnp.concatenate([r[at, :].T for r in grad_scores], axis=1)
    block_t = jnp.concatenate([r[at, :].T for r in blocks], axis=1)
    embedding = jnp.concatenate([r[at, :] for r in embeddings], axis=0)
    for b in range(out_ref.shape[0] // BLK):
        rows = slice(b * BLK, (b + 1) * BLK)
        spread_t = jnp.where(block_t == b, grad_scores_t, 0.0).astype(BF16)
        total = dot(spread_t, embedding)
        for ref in more:
            total = total + ref[rows, :].astype(F32)
        out_ref[rows, :] = total.astype(BF16)


def own_block_kernel(feats_ref, owners_ref, blocks_ref, positives_ref, out_ref, ints, sem):
    rows, width = feats_ref.shape
    feats = pltpu.make_async_copy(feats_ref, out_ref.at[pl.ds(0, rows)], sem.at[0])
    feats.start()
    copies = []
    for i, ref in enumerate((owners_ref, blocks_ref, positives_ref)):
        copies.append(pltpu.make_async_copy(ref, ints.at[i], sem.at[i + 1]))
        copies[i].start()
    for copy in copies:
        copy.wait()
    meta = [ints[i].astype(F32) for i in range(3)]
    meta += [jnp.zeros((meta[0].shape[0], width - 3 * rows), F32)]
    meta = jnp.concatenate(meta, axis=1)
    rest = jnp.zeros((META_ROWS - meta.shape[0], width), F32)
    out_ref[rows:, :] = jnp.concatenate([meta, rest], axis=0).astype(BF16)
    feats.wait()


def load_kernel(label_ref, shard_ref, label_out, shard_out):
    label_out[...] = label_ref[...]
    shard_out[...] = shard_ref[...]


def half_at(mine, half):
    odd = jnp.bitwise_and(lax.axis_index("labels"), 1)
    return pl.ds(pl.multiple_of((odd if mine else 1 - odd) * half, 16), half)


def split_kernel(even_ref, got_ref, *refs):
    *more, keep_ref, send_ref, total = refs
    share = even_ref[0].astype(F32) + got_ref[0].astype(F32)
    for ref in more:
        share = share + ref[...].astype(F32)
    total[...] = share
    half = keep_ref.shape[0]
    keep_ref[...] = total[half_at(True, half), :]
    send_ref[...] = total[half_at(False, half), :].astype(BF16)


def merge_kernel(mine_ref, other_ref, out_ref):
    half = mine_ref.shape[0]
    out_ref[half_at(True, half), :] = mine_ref[...].astype(F32)
    out_ref[half_at(False, half), :] = other_ref[...].astype(F32)


def call(kernel, name, out_shape, scratch, flops, megabytes, *args, space=VMEM, limit=24):
    return pl.pallas_call(
        kernel,
        in_specs=[space] * len(args),
        out_specs=jax.tree.map(lambda _: VMEM, out_shape),
        out_shape=out_shape,
        scratch_shapes=scratch,
        compiler_params=pltpu.CompilerParams(vmem_limit_bytes=limit << 20),
        cost_estimate=pl.CostEstimate(
            flops=flops, bytes_accessed=megabytes << 20, transcendentals=0
        ),
        name=name,
    )(*args)


def shaped(shape, dtype=BF16):
    return jax.ShapeDtypeStruct(shape, dtype)


def pair_work(sources, labels, shards, cap, pick_count, before, last):
    n_data, n_sets = len(shards), len(labels)
    block_rows, width = sources[0].shape
    rows = block_rows - META_ROWS
    slots = n_sets * len(sources) * cap
    shard_rows = shards[0].shape[0]
    full = (n_data * shard_rows, width)
    backs = len(sources)
    shapes = [shaped((rows, width))] * backs
    shapes += [shaped((slots, BLK), F32), shaped((slots, BLK), jnp.int32), shaped((slots, width))]
    more = [before["enc"], before["total"]] if before else shards
    scratch = []
    if not before:
        shapes += [shaped(full)]
    if last:
        shapes += [shaped((n_data // 2, shard_rows, width))] * 2
        scratch = [pltpu.VMEM(full, F32)]
    else:
        shapes += [shaped(full, F32)]
    out = call(
        functools.partial(
            pair_kernel,
            cap=cap,
            pick_count=pick_count,
            n_sources=len(sources),
            n_sets=n_sets,
            n_data=n_data,
            first=not before,
            last=last,
        ),
        "pair_work",
        shapes,
        scratch,
        2 * slots * width * (2 * labels[0].shape[0] + 3 * width + 2 * rows),
        8,
        *sources,
        *labels,
        *more,
    )
    result = {"back": list(out[:backs]), "slots": list(out[backs : backs + 3])}
    rest = list(out[backs + 3 :])
    result["enc"] = before["enc"] if before else rest.pop(0)
    result["shares" if last else "total"] = rest if last else rest[0]
    return result


def grad_label_work(works, n_sets, j, labels_shape, *more):
    slots = list(zip(*(work["slots"] for work in works)))
    return call(
        functools.partial(grad_label_kernel, calls=len(works), n_sets=n_sets, j=j),
        "grad_label_work",
        shaped(labels_shape),
        [],
        2 * sum(x.shape[0] for x in slots[0]) // n_sets * labels_shape[0] * labels_shape[1],
        4,
        *slots[0],
        *slots[1],
        *slots[2],
        *more,
    )


def swap(x):
    x = lax.all_to_all(x, "labels", split_axis=0, concat_axis=0, tiled=True)
    return lax.all_to_all(x, "dp", split_axis=1, concat_axis=1, tiled=True)


def partner(x, axis, mask):
    return lax.ppermute(x, axis, [(i, i ^ mask) for i in range(lax.axis_size(axis))])


def masks(n):
    return [1 << i for i in range(n.bit_length() - 1)]


def after(x, *others):
    return lax.optimization_barrier((x, *others))[0]


def gather_far(x):
    got = {0: x}
    for mask in reversed(masks(lax.axis_size("dp"))[1:]):
        got.update({m | mask: partner(v, "dp", mask) for m, v in list(got.items())})
    return [got[m] for m in sorted(got)]


def gather_near(far, *first):
    near = [partner(after(v, *far[1:], *first), "dp", 1) for v in far]
    return [v for pair in zip(far, near) for v in pair]


def gather_labels(x, first):
    got = {0: x}
    for mask in reversed(masks(lax.axis_size("labels"))):
        for m, v in list(got.items()):
            got[m | mask] = partner(after(v, first) if m else v, "labels", mask)
    return [got[m] for m in range(len(got))]


def add(*terms):
    return sum(t.astype(F32) for t in terms)


def dp_terms(even, odd):
    got = partner(odd, "dp", 1)
    terms = [[even[i], got[i]] for i in range(even.shape[0])]
    for mask in masks(len(terms)):
        for i in range(len(terms)):
            if i & mask == 0 and i % mask == 0:
                terms[i].append(partner(add(*terms[i | mask]).astype(BF16), "dp", 2 * mask))
    return got, terms[0]


def sum_shares(even, odd, *first):
    got, terms = dp_terms(even, odd)
    rows, width = even.shape[1:]
    half = rows // 2
    keep, send = call(
        split_kernel,
        "split_share",
        [shaped((half, width), F32), shaped((half, width))],
        [pltpu.VMEM((rows, width), F32)],
        0,
        1,
        even,
        after(got, *first),
        *terms[2:],
    )
    x = add(keep, partner(send, "labels", 1)).astype(BF16)
    first = x
    for mask in masks(lax.axis_size("labels"))[1:]:
        x = add(x, partner(x, "labels", mask)).astype(BF16)
    return keep, first, x


def join_halves(x, *first):
    other = partner(x, "labels", 1)
    out = shaped((2 * x.shape[0], x.shape[1]), F32)
    return call(merge_kernel, "merge_share", out, [], 0, 1, after(x, *first), other)


def reduce_runs(runs, got_last, keep, first):
    def over_dp(parts, *hold):
        parts = [list(part) for part in parts]
        for mask in masks(len(parts)):
            for h in range(0, len(parts), 2 * mask):
                sent = after(add(*parts[h + mask]).astype(BF16), *hold)
                parts[h].append(partner(sent, "dp", 2 * mask))
        return parts[0]

    n = len(runs)
    sums = {n - 2: over_dp(list(zip(runs[n - 2], got_last)), keep)}
    held = sums[n - 2][-1:]
    for i in reversed(range(0, n - 2, 2)):
        near = after(add(*over_dp([[x] for x in runs[i + 1]], keep)).astype(BF16), first)
        sums[i] = over_dp([[x] for x in runs[i]], *held) + [partner(near, "labels", 1)]
    for mask in masks(n)[1:]:
        for i in range(0, n, 2 * mask):
            sent = after(add(*sums[i + mask]).astype(BF16), first)
            sums[i].append(partner(sent, "labels", mask))
    return sums[0]


def with_meta(feats, owner_rows, block_rows, positive_rows):
    meta = jnp.concatenate([owner_rows, block_rows, positive_rows], axis=1).astype(BF16)
    meta = jnp.pad(meta, ((0, META_ROWS - meta.shape[0]), (0, feats.shape[1] - meta.shape[1])))
    return jnp.concatenate([feats, meta], axis=0)


def local(feats, enc_weight, label_weight, owners, blocks, positives):
    n_labels = lax.axis_size("labels")
    n_data = lax.axis_size("dp")
    n_owner = n_labels * n_data
    row_count, width = feats.shape
    pick_count = owners.shape[1]
    cap = max(2, 2 * row_count * pick_count // n_owner)

    if row_count <= n_data * cap:
        own = call(
            own_block_kernel,
            "own_block",
            shaped((row_count + META_ROWS, width)),
            [
                pltpu.VMEM((3, pick_count, row_count), jnp.int32),
                pltpu.SemaphoreType.DMA((4,)),
            ],
            0,
            1,
            feats,
            owners.T,
            blocks.T,
            positives.T,
            space=HBM,
            limit=60,
        )
        labels = [label_weight, partner(label_weight, "dp", 1)]
        labels[0], own_shard = call(
            load_kernel,
            "load",
            [shaped(label_weight.shape), shaped(enc_weight.shape)],
            [],
            0,
            4,
            after(label_weight, labels[1]),
            enc_weight,
        )
        near = gather_labels(own, labels[0])
        far = {0: gather_far(near[0])}
        shards = gather_near(gather_far(enc_weight), *far[0][1:], *near[1:3], labels[0])
        shards[0] = own_shard
        works, backs = [], {}
        for run in [*range(0, n_labels, 2), *range(1, n_labels, 2)]:
            last = run == n_labels - 1
            if last:
                far[run] = gather_far(after(near[run], *far[run - 1][1:]))
            elif run % 2:
                sent = [after(x, works[0]["slots"][0]) for x in far[run - 1][1:]]
                far[run] = near[run : run + 1] + [partner(x, "labels", 1) for x in sent]
            elif run:
                far[run] = gather_far(after(near[run], *far[0][1:]))
            sources = [after(near[run], *([] if run else near[1:3]))] + far[run][1:]
            before = works[-1] if works else None
            works.append(pair_work(sources, labels, shards, cap, pick_count, before, last))
            backs[run] = works[-1]["back"]
        got_last = [partner(x, "labels", 1) for x in works[-1]["back"]]
        keep, first, share = sum_shares(*works[-1]["shares"], *got_last[1:])
        terms = reduce_runs(backs, got_last, keep, first)
        works[0]["slots"][2] = after(works[0]["slots"][2], *got_last[1:])
        other = partner(grad_label_work(works, 2, 1, label_weight.shape), "dp", 1)
        grad_label = grad_label_work(works, 2, 0, label_weight.shape, other)
        grad_feats = add(*terms).astype(BF16)
        grad_enc = join_halves(share, grad_label, grad_feats)
    else:
        shards = gather_near(gather_far(enc_weight))
        flat = owners.reshape(-1)
        onehot = (flat[:, None] == jnp.arange(n_owner, dtype=jnp.int32)[None, :]).astype(jnp.int32)
        rank = jnp.sum((jnp.cumsum(onehot, axis=0) - onehot) * onehot, axis=1)
        slot = (flat * cap + rank).reshape(row_count, pick_count)
        slot_total = n_owner * cap
        slots = jnp.arange(slot_total, dtype=jnp.int32)
        place = slots[:, None, None] == slot[None]
        pick = jnp.any(place, axis=2).astype(BF16)
        live = jnp.any(place, axis=(1, 2))
        block_of = jnp.sum(jnp.where(place, blocks[None], 0), axis=(1, 2))
        wanted = jnp.sum(jnp.where(place, positives[None], 0), axis=(1, 2))
        owner_of = jnp.where(live, slots // cap, -1)
        out = dot(pick, feats).astype(BF16).reshape(n_labels, n_data, cap, width)
        meta = jnp.stack([owner_of, block_of, wanted], axis=1).reshape(n_labels, n_data, cap, 3)
        tiles = slot_total // TILE
        got = swap(out).reshape(tiles, TILE, width)
        got_meta = swap(meta).reshape(tiles, TILE, 3).transpose(0, 2, 1)
        sources = [
            with_meta(got[i], got_meta[i, 0:1], got_meta[i, 1:2], got_meta[i, 2:3])
            for i in range(tiles)
        ]
        works = []
        for i in range(0, tiles, 4):
            before = works[-1] if works else None
            last = i + 4 >= tiles
            works.append(pair_work(sources[i : i + 4], [label_weight], shards, TILE, 1, before, last))
        back = jnp.concatenate([back for work in works for back in work["back"]], axis=0)
        back = swap(back.reshape(n_labels, n_data, cap, width)).reshape(slot_total, width)
        grad_feats = dot(pick, back, 0, 0).astype(BF16)
        *_, share = sum_shares(*works[-1]["shares"])
        grad_label = grad_label_work(works, 1, 0, label_weight.shape)
        grad_enc = join_halves(share, grad_label, grad_feats)

    return (grad_feats, grad_label, grad_enc)


def solution(mesh):
    rows = P(("groups", "labels", "dp"), None)
    return jax.shard_map(
        local,
        mesh=mesh,
        in_specs=(rows, P("dp", None), rows, rows, rows, rows),
        out_specs=(rows, rows, P(("groups", "dp"), None)),
        check_vma=False,
    )
```

```python
import functools

import jax
import jax.numpy as jnp
from jax import lax
from jax.experimental import pallas as pl
from jax.experimental.pallas import tpu as pltpu
from jax.sharding import PartitionSpec as P

BLK = 128
EPSILON = 1e-06
META_ROWS = 8
TILE = 128
F32 = jnp.float32
BF16 = jnp.bfloat16
VMEM = pl.BlockSpec(memory_space=pltpu.VMEM)
HBM = pl.BlockSpec(memory_space=pltpu.HBM)


def dot(a, b, da=1, db=0):
    return lax.dot_general(a, b, (((da,), (db,)), ((), ())), preferred_element_type=F32)


def shard_at(m, shard_rows):
    at = jnp.bitwise_xor(lax.axis_index("dp"), m) * shard_rows
    return pl.ds(pl.multiple_of(at, 16), shard_rows)


def pair_kernel(*refs, cap, pick_count, n_sources, n_sets, n_data, first, last):
    it = iter(refs)
    take = lambda n: [next(it) for _ in range(n)]
    sources, labels = take(n_sources), take(n_sets)
    shards = take(n_data if first else 0)
    enc, total_in = (None, None) if first else take(2)
    backs, grad_scores_ref, block_ref, embedding_ref = take(n_sources), *take(3)
    enc = next(it) if first else enc
    shares = take(2 if last else 0)
    total_ref = next(it)

    n_owner_data = lax.axis_size("dp")
    me = lax.axis_index("labels") * n_owner_data + lax.axis_index("dp")
    rows = sources[0].shape[0] - META_ROWS
    shard_rows = enc.shape[0] // n_data
    n_blocks = labels[0].shape[0] // BLK
    part = n_sources * cap
    slots = n_sets * part

    for m, shard in enumerate(shards):
        enc[shard_at(m, shard_rows), :] = shard[...]

    row_id = lax.broadcasted_iota(jnp.int32, (rows, rows), 0)
    col_id = lax.broadcasted_iota(jnp.int32, (rows, rows), 1)
    before = (row_id < col_id).astype(BF16)
    slot_id = lax.broadcasted_iota(jnp.int32, (cap, rows), 0).astype(F32)
    column = lax.broadcasted_iota(jnp.int32, (slots, BLK), 1)

    hits, codes = [], []
    for source in sources:
        meta = source[rows:, 0 : 3 * rows].astype(F32)[:pick_count]
        code = meta[:, rows : 2 * rows] * 256.0 + meta[:, 2 * rows :] + 1.0
        for j in range(n_sets):
            named = meta[:, :rows] == jnp.bitwise_xor(me, j).astype(F32)
            hits.append(jnp.sum(named.astype(F32), axis=0, keepdims=True))
            codes.append(jnp.sum(jnp.where(named, code, 0.0), axis=0, keepdims=True))
    rank = dot(jnp.concatenate(hits, axis=0).astype(BF16), before)

    picks, picked, slot_codes = [], {}, {}
    for s, source in enumerate(sources):
        pick = []
        for j in range(n_sets):
            i = s * n_sets + j
            pick.append(jnp.where((slot_id == rank[i : i + 1]) & (hits[i] > 0.0), 1.0, 0.0))
            slot_codes[j, s] = jnp.sum(pick[j] * codes[i], axis=1, keepdims=True)
        picks.append(jnp.concatenate(pick, axis=0).astype(BF16))
        found = dot(picks[s], source[:rows, :]).astype(BF16)
        for j in range(n_sets):
            picked[j, s] = found[j * cap : (j + 1) * cap]
    order = [(j, s) for j in range(n_sets) for s in range(n_sources)]
    feats = jnp.concatenate([picked[i] for i in order], axis=0)
    code = jnp.concatenate([slot_codes[i] for i in order], axis=0).astype(jnp.int32) - 1

    hidden = dot(feats, enc[...])
    inv_rms = lax.rsqrt(jnp.mean(hidden * hidden, axis=-1, keepdims=True) + EPSILON)
    embedding = (hidden * inv_rms).astype(BF16)
    embedding_ref[...] = embedding

    block = jnp.broadcast_to(code >> 8, (slots, BLK))
    block_ref[...] = block
    wanted = jnp.broadcast_to(code & 255, (slots, BLK))
    target = jnp.where(column == wanted, 1.0, 0.0)
    grad_pairs = []
    for j in range(n_sets):
        at = slice(j * part, (j + 1) * part)
        scores = dot(embedding[at], labels[j][...], 1, 1)
        mine = block[at]
        own_scores = jnp.zeros((part, BLK), F32)
        for b in range(n_blocks):
            own_scores = jnp.where(mine == b, scores[:, b * BLK : (b + 1) * BLK], own_scores)
        grad_scores = jnp.where(mine >= 0, jax.nn.sigmoid(own_scores) - target[at], 0.0)
        grad_scores_ref[at, :] = grad_scores
        spread = jnp.concatenate(
            [jnp.where(mine == b, grad_scores, 0.0).astype(BF16) for b in range(n_blocks)], axis=1
        )
        grad_pairs.append(dot(spread, labels[j][...]))
    grad_pair = jnp.concatenate(grad_pairs, axis=0).astype(BF16).astype(F32)

    projection = jnp.mean(hidden * grad_pair, axis=-1, keepdims=True)
    grad_hidden = (inv_rms * grad_pair - hidden * (inv_rms**3 * projection)).astype(BF16)
    total = dot(feats, grad_hidden, 0, 0)
    total_ref[...] = total if first else total + total_in[...]
    for m in range(n_data if last else 0):
        shares[m % 2][m // 2] = total_ref[shard_at(m, shard_rows), :].astype(BF16)

    grad_feats = dot(grad_hidden, enc[...], 1, 1).astype(BF16)
    for s in range(n_sources):
        parts = [
            grad_feats[(j * n_sources + s) * cap : (j * n_sources + s + 1) * cap]
            for j in range(n_sets)
        ]
        backs[s][...] = dot(picks[s], jnp.concatenate(parts, axis=0), 0, 0).astype(BF16)


def grad_label_kernel(*refs, calls, n_sets, j):
    grad_scores, blocks, embeddings = refs[:calls], refs[calls : 2 * calls], refs[2 * calls : 3 * calls]
    *more, out_ref, result, sem = refs[3 * calls :]
    rows_of = [slice(j * r.shape[0] // n_sets, (j + 1) * r.shape[0] // n_sets) for r in blocks]
    grad_scores_t = jnp.concatenate([r[at, :].T for r, at in zip(grad_scores, rows_of)], axis=1)
    block_t = jnp.concatenate([r[at, :].T for r, at in zip(blocks, rows_of)], axis=1)
    embedding = jnp.concatenate([r[at, :] for r, at in zip(embeddings, rows_of)], axis=0)
    copies = []
    for b in range(out_ref.shape[0] // BLK):
        rows = pl.ds(b * BLK, BLK)
        spread_t = jnp.where(block_t == b, grad_scores_t, 0.0).astype(BF16)
        total = dot(spread_t, embedding)
        for ref in more:
            total = total + ref[rows, :].astype(F32)
        result[rows, :] = total.astype(BF16)
        copies.append(pltpu.make_async_copy(result.at[rows], out_ref.at[rows], sem.at[b]))
        copies[b].start()
    for copy in copies:
        copy.wait()


def own_block_kernel(feats_ref, owners_ref, blocks_ref, positives_ref, out_ref, ints, sem):
    rows, width = feats_ref.shape
    feats = pltpu.make_async_copy(feats_ref, out_ref.at[pl.ds(0, rows)], sem.at[0])
    feats.start()
    copies = []
    for i, ref in enumerate((owners_ref, blocks_ref, positives_ref)):
        copies.append(pltpu.make_async_copy(ref, ints.at[i], sem.at[i + 1]))
        copies[i].start()
    for copy in copies:
        copy.wait()
    meta = [ints[i].astype(F32) for i in range(3)]
    meta += [jnp.zeros((meta[0].shape[0], width - 3 * rows), F32)]
    meta = jnp.concatenate(meta, axis=1)
    rest = jnp.zeros((META_ROWS - meta.shape[0], width), F32)
    out_ref[rows:, :] = jnp.concatenate([meta, rest], axis=0).astype(BF16)
    feats.wait()


def load_kernel(label_ref, shard_ref, label_out, shard_out):
    label_out[...] = label_ref[...]
    shard_out[...] = shard_ref[...]


def half_at(mine, half):
    odd = jnp.bitwise_and(lax.axis_index("labels"), 1)
    return pl.ds(pl.multiple_of((odd if mine else 1 - odd) * half, 16), half)


def split_kernel(even_ref, got_ref, *refs):
    *more, keep_ref, send_ref, total = refs
    share = even_ref[0].astype(F32) + got_ref[0].astype(F32)
    for ref in more:
        share = share + ref[...].astype(F32)
    total[...] = share
    half = keep_ref.shape[0]
    keep_ref[...] = total[half_at(True, half), :]
    send_ref[...] = total[half_at(False, half), :].astype(BF16)


def merge_kernel(mine_ref, other_ref, out_ref):
    half = mine_ref.shape[0]
    out_ref[half_at(True, half), :] = mine_ref[...].astype(F32)
    out_ref[half_at(False, half), :] = other_ref[...].astype(F32)


def call(kernel, name, out_shape, scratch, flops, megabytes, *args, space=VMEM, out_space=VMEM, limit=24):
    return pl.pallas_call(
        kernel,
        in_specs=[space] * len(args),
        out_specs=jax.tree.map(lambda _: out_space, out_shape),
        out_shape=out_shape,
        scratch_shapes=scratch,
        compiler_params=pltpu.CompilerParams(vmem_limit_bytes=limit << 20),
        cost_estimate=pl.CostEstimate(
            flops=flops, bytes_accessed=megabytes << 20, transcendentals=0
        ),
        name=name,
    )(*args)


def shaped(shape, dtype=BF16):
    return jax.ShapeDtypeStruct(shape, dtype)


def pair_work(sources, labels, shards, cap, pick_count, before, last):
    n_data, n_sets = len(shards), len(labels)
    block_rows, width = sources[0].shape
    rows = block_rows - META_ROWS
    slots = n_sets * len(sources) * cap
    shard_rows = shards[0].shape[0]
    full = (n_data * shard_rows, width)
    backs = len(sources)
    shapes = [shaped((rows, width))] * backs
    shapes += [shaped((slots, BLK), F32), shaped((slots, BLK), jnp.int32), shaped((slots, width))]
    more = [before["enc"], before["total"]] if before else shards
    scratch = []
    if not before:
        shapes += [shaped(full)]
    if last:
        shapes += [shaped((n_data // 2, shard_rows, width))] * 2
        scratch = [pltpu.VMEM(full, F32)]
    else:
        shapes += [shaped(full, F32)]
    out = call(
        functools.partial(
            pair_kernel,
            cap=cap,
            pick_count=pick_count,
            n_sources=len(sources),
            n_sets=n_sets,
            n_data=n_data,
            first=not before,
            last=last,
        ),
        "pair_work",
        shapes,
        scratch,
        2 * slots * width * (2 * labels[0].shape[0] + 3 * width + 2 * rows),
        8,
        *sources,
        *labels,
        *more,
    )
    result = {"back": list(out[:backs]), "slots": list(out[backs : backs + 3])}
    rest = list(out[backs + 3 :])
    result["enc"] = before["enc"] if before else rest.pop(0)
    result["shares" if last else "total"] = rest if last else rest[0]
    return result


def grad_label_work(works, n_sets, j, labels_shape, *more):
    slots = list(zip(*(work["slots"] for work in works)))
    return call(
        functools.partial(grad_label_kernel, calls=len(works), n_sets=n_sets, j=j),
        "grad_label_work",
        shaped(labels_shape),
        [pltpu.VMEM(labels_shape, BF16), pltpu.SemaphoreType.DMA((labels_shape[0] // BLK,))],
        2 * sum(x.shape[0] for x in slots[0]) // n_sets * labels_shape[0] * labels_shape[1],
        4,
        *slots[0],
        *slots[1],
        *slots[2],
        *more,
        out_space=pl.BlockSpec(memory_space=pl.ANY),
    )


def swap(x):
    x = lax.all_to_all(x, "labels", split_axis=0, concat_axis=0, tiled=True)
    return lax.all_to_all(x, "dp", split_axis=1, concat_axis=1, tiled=True)


def partner(x, axis, mask):
    return lax.ppermute(x, axis, [(i, i ^ mask) for i in range(lax.axis_size(axis))])


def masks(n):
    return [1 << i for i in range(n.bit_length() - 1)]


def after(x, *others):
    return lax.optimization_barrier((x, *others))[0]


def gather_far(x):
    got = {0: x}
    for mask in reversed(masks(lax.axis_size("dp"))[1:]):
        got.update({m | mask: partner(v, "dp", mask) for m, v in list(got.items())})
    return [got[m] for m in sorted(got)]


def gather_near(far, *first):
    near = [partner(after(v, *far[1:], *first), "dp", 1) for v in far]
    return [v for pair in zip(far, near) for v in pair]


def gather_labels(x, first):
    got = {0: x}
    for mask in reversed(masks(lax.axis_size("labels"))):
        for m, v in list(got.items()):
            got[m | mask] = partner(after(v, first) if m else v, "labels", mask)
    return [got[m] for m in range(len(got))]


def add(*terms):
    return sum(t.astype(F32) for t in terms)


def dp_terms(even, odd):
    got = partner(odd, "dp", 1)
    terms = [[even[i], got[i]] for i in range(even.shape[0])]
    for mask in masks(len(terms)):
        for i in range(len(terms)):
            if i & mask == 0 and i % mask == 0:
                terms[i].append(partner(add(*terms[i | mask]).astype(BF16), "dp", 2 * mask))
    return got, terms[0]


def sum_shares(even, odd, *first):
    got, terms = dp_terms(even, odd)
    rows, width = even.shape[1:]
    half = rows // 2
    keep, send = call(
        split_kernel,
        "split_share",
        [shaped((half, width), F32), shaped((half, width))],
        [pltpu.VMEM((rows, width), F32)],
        0,
        1,
        even,
        after(got, *first),
        *terms[2:],
    )
    x = add(keep, partner(send, "labels", 1)).astype(BF16)
    first = x
    for mask in masks(lax.axis_size("labels"))[1:]:
        x = add(x, partner(x, "labels", mask)).astype(BF16)
    return keep, first, x


def join_halves(x, *first):
    other = partner(x, "labels", 1)
    out = shaped((2 * x.shape[0], x.shape[1]), F32)
    return call(merge_kernel, "merge_share", out, [], 0, 1, after(x, *first), other)


def reduce_runs(runs, got_last, keep, first):
    def over_dp(parts, *hold):
        parts = [list(part) for part in parts]
        for mask in masks(len(parts)):
            for h in range(0, len(parts), 2 * mask):
                sent = after(add(*parts[h + mask]).astype(BF16), *hold)
                parts[h].append(partner(sent, "dp", 2 * mask))
        return parts[0]

    n = len(runs)
    sums = {n - 2: over_dp(list(zip(runs[n - 2], got_last)), keep)}
    held = sums[n - 2][-1:]
    for i in reversed(range(0, n - 2, 2)):
        near = after(add(*over_dp([[x] for x in runs[i + 1]], keep)).astype(BF16), first)
        sums[i] = over_dp([[x] for x in runs[i]], *held) + [partner(near, "labels", 1)]
    for mask in masks(n)[1:]:
        for i in range(0, n, 2 * mask):
            sent = after(add(*sums[i + mask]).astype(BF16), first)
            sums[i].append(partner(sent, "labels", mask))
    return sums[0]


def with_meta(feats, owner_rows, block_rows, positive_rows):
    meta = jnp.concatenate([owner_rows, block_rows, positive_rows], axis=1).astype(BF16)
    meta = jnp.pad(meta, ((0, META_ROWS - meta.shape[0]), (0, feats.shape[1] - meta.shape[1])))
    return jnp.concatenate([feats, meta], axis=0)


def local(feats, enc_weight, label_weight, owners, blocks, positives):
    n_labels = lax.axis_size("labels")
    n_data = lax.axis_size("dp")
    n_owner = n_labels * n_data
    row_count, width = feats.shape
    pick_count = owners.shape[1]
    cap = max(2, 2 * row_count * pick_count // n_owner)

    if row_count <= n_data * cap:
        own = call(
            own_block_kernel,
            "own_block",
            shaped((row_count + META_ROWS, width)),
            [
                pltpu.VMEM((3, pick_count, row_count), jnp.int32),
                pltpu.SemaphoreType.DMA((4,)),
            ],
            0,
            1,
            feats,
            owners.T,
            blocks.T,
            positives.T,
            space=HBM,
            limit=60,
        )
        labels = [label_weight, partner(label_weight, "dp", 1)]
        labels[0], own_shard = call(
            load_kernel,
            "load",
            [shaped(label_weight.shape), shaped(enc_weight.shape)],
            [],
            0,
            4,
            after(label_weight, labels[1]),
            enc_weight,
        )
        near = gather_labels(own, labels[0])
        far = {0: gather_far(near[0])}
        shards = gather_near(
            gather_far(enc_weight), *far[0][1:], *near[1:3], labels[0]
        )
        shards[0] = own_shard
        works, backs = [], {}
        last_call = list(range(1, n_labels, 2))
        for call_runs in [[run] for run in range(0, n_labels, 2)] + [last_call]:
            sources = []
            for run in call_runs:
                if run == n_labels - 1:
                    held = far[run - 1][1:] + works[0]["slots"][:1]
                    far[run] = gather_far(after(near[run], *held))
                elif run % 2:
                    sent = [after(x, *shards[1:]) for x in far[run - 1][1:]]
                    far[run] = near[run : run + 1] + [partner(x, "labels", 1) for x in sent]
                elif run:
                    far[run] = gather_far(after(near[run], *far[0][1:]))
                sources += [after(near[run], *([] if run else near[1:3]))] + far[run][1:]
            before, last = works[-1] if works else None, call_runs is last_call
            works.append(pair_work(sources, labels, shards, cap, pick_count, before, last))
            parts = len(sources) // len(call_runs)
            for i, run in enumerate(call_runs):
                backs[run] = works[-1]["back"][i * parts : (i + 1) * parts]
        got_last = [partner(x, "labels", 1) for x in backs[n_labels - 1]]
        keep, first, share = sum_shares(*works[-1]["shares"], *got_last)
        terms = reduce_runs(backs, got_last, keep, first)
        works[0]["slots"][2] = after(works[0]["slots"][2], *got_last[1:])
        other = partner(grad_label_work(works, 2, 1, label_weight.shape), "dp", 1)
        grad_label = grad_label_work(works, 2, 0, label_weight.shape, other)
        grad_feats = add(*terms).astype(BF16)
        grad_enc = join_halves(share, grad_label, grad_feats)
    else:
        shards = gather_near(gather_far(enc_weight))
        flat = owners.reshape(-1)
        onehot = (flat[:, None] == jnp.arange(n_owner, dtype=jnp.int32)[None, :]).astype(jnp.int32)
        rank = jnp.sum((jnp.cumsum(onehot, axis=0) - onehot) * onehot, axis=1)
        slot = (flat * cap + rank).reshape(row_count, pick_count)
        slot_total = n_owner * cap
        slots = jnp.arange(slot_total, dtype=jnp.int32)
        place = slots[:, None, None] == slot[None]
        pick = jnp.any(place, axis=2).astype(BF16)
        live = jnp.any(place, axis=(1, 2))
        block_of = jnp.sum(jnp.where(place, blocks[None], 0), axis=(1, 2))
        wanted = jnp.sum(jnp.where(place, positives[None], 0), axis=(1, 2))
        owner_of = jnp.where(live, slots // cap, -1)
        out = dot(pick, feats).astype(BF16).reshape(n_labels, n_data, cap, width)
        meta = jnp.stack([owner_of, block_of, wanted], axis=1).reshape(n_labels, n_data, cap, 3)
        tiles = slot_total // TILE
        got = swap(out).reshape(tiles, TILE, width)
        got_meta = swap(meta).reshape(tiles, TILE, 3).transpose(0, 2, 1)
        sources = [
            with_meta(got[i], got_meta[i, 0:1], got_meta[i, 1:2], got_meta[i, 2:3])
            for i in range(tiles)
        ]
        works = []
        for i in range(0, tiles, 4):
            before = works[-1] if works else None
            last = i + 4 >= tiles
            works.append(pair_work(sources[i : i + 4], [label_weight], shards, TILE, 1, before, last))
        back = jnp.concatenate([back for work in works for back in work["back"]], axis=0)
        back = swap(back.reshape(n_labels, n_data, cap, width)).reshape(slot_total, width)
        grad_feats = dot(pick, back, 0, 0).astype(BF16)
        *_, share = sum_shares(*works[-1]["shares"])
        grad_label = grad_label_work(works, 1, 0, label_weight.shape)
        grad_enc = join_halves(share, grad_label, grad_feats)

    return (grad_feats, grad_label, grad_enc)


def solution(mesh):
    rows = P(("groups", "labels", "dp"), None)
    return jax.shard_map(
        local,
        mesh=mesh,
        in_specs=(rows, P("dp", None), rows, rows, rows, rows),
        out_specs=(rows, rows, P(("groups", "dp"), None)),
        check_vma=False,
    )
```

```python
import functools

import jax
import jax.numpy as jnp
from jax import lax
from jax.experimental import pallas as pl
from jax.experimental.pallas import tpu as pltpu
from jax.sharding import PartitionSpec as P

BLK = 128
EPSILON = 1e-06
META_ROWS = 8
TILE = 128
F32 = jnp.float32
BF16 = jnp.bfloat16
VMEM = pl.BlockSpec(memory_space=pltpu.VMEM)
HBM = pl.BlockSpec(memory_space=pltpu.HBM)


def dot(a, b, da=1, db=0):
    return lax.dot_general(a, b, (((da,), (db,)), ((), ())), preferred_element_type=F32)


def shard_at(m, shard_rows):
    at = jnp.bitwise_xor(lax.axis_index("dp"), m) * shard_rows
    return pl.ds(pl.multiple_of(at, 16), shard_rows)


def pair_kernel(*refs, cap, pick_count, n_sources, n_sets, n_data, first, last):
    it = iter(refs)
    take = lambda n: [next(it) for _ in range(n)]
    sources, labels = take(n_sources), take(n_sets)
    shards = take(n_data if first else 0)
    enc, total_in = (None, None) if first else take(2)
    backs, grad_scores_ref, block_ref, embedding_ref = take(n_sources), *take(3)
    enc = next(it) if first else enc
    shares = take(2 if last else 0)
    total_ref = next(it)

    n_owner_data = lax.axis_size("dp")
    me = lax.axis_index("labels") * n_owner_data + lax.axis_index("dp")
    rows = sources[0].shape[0] - META_ROWS
    shard_rows = enc.shape[0] // n_data
    n_blocks = labels[0].shape[0] // BLK
    part = n_sources * cap
    slots = n_sets * part

    for m, shard in enumerate(shards):
        enc[shard_at(m, shard_rows), :] = shard[...]

    row_id = lax.broadcasted_iota(jnp.int32, (rows, rows), 0)
    col_id = lax.broadcasted_iota(jnp.int32, (rows, rows), 1)
    before = (row_id < col_id).astype(BF16)
    slot_id = lax.broadcasted_iota(jnp.int32, (cap, rows), 0).astype(F32)
    column = lax.broadcasted_iota(jnp.int32, (slots, BLK), 1)

    hits, codes = [], []
    for source in sources:
        meta = source[rows:, 0 : 3 * rows].astype(F32)[:pick_count]
        code = meta[:, rows : 2 * rows] * 256.0 + meta[:, 2 * rows :] + 1.0
        for j in range(n_sets):
            named = meta[:, :rows] == jnp.bitwise_xor(me, j).astype(F32)
            hits.append(jnp.sum(named.astype(F32), axis=0, keepdims=True))
            codes.append(jnp.sum(jnp.where(named, code, 0.0), axis=0, keepdims=True))
    rank = dot(jnp.concatenate(hits, axis=0).astype(BF16), before)

    picks, picked, slot_codes = [], {}, {}
    for s, source in enumerate(sources):
        pick = []
        for j in range(n_sets):
            i = s * n_sets + j
            pick.append(jnp.where((slot_id == rank[i : i + 1]) & (hits[i] > 0.0), 1.0, 0.0))
            slot_codes[j, s] = jnp.sum(pick[j] * codes[i], axis=1, keepdims=True)
        picks.append(jnp.concatenate(pick, axis=0).astype(BF16))
        found = dot(picks[s], source[:rows, :]).astype(BF16)
        for j in range(n_sets):
            picked[j, s] = found[j * cap : (j + 1) * cap]
    order = [(j, s) for j in range(n_sets) for s in range(n_sources)]
    feats = jnp.concatenate([picked[i] for i in order], axis=0)
    code = jnp.concatenate([slot_codes[i] for i in order], axis=0).astype(jnp.int32) - 1

    hidden = dot(feats, enc[...])
    inv_rms = lax.rsqrt(jnp.mean(hidden * hidden, axis=-1, keepdims=True) + EPSILON)
    embedding = (hidden * inv_rms).astype(BF16)
    embedding_ref[...] = embedding

    block = jnp.broadcast_to(code >> 8, (slots, BLK))
    block_ref[...] = block
    wanted = jnp.broadcast_to(code & 255, (slots, BLK))
    target = jnp.where(column == wanted, 1.0, 0.0)
    grad_pairs = []
    for j in range(n_sets):
        at = slice(j * part, (j + 1) * part)
        scores = dot(embedding[at], labels[j][...], 1, 1)
        mine = block[at]
        own_scores = jnp.zeros((part, BLK), F32)
        for b in range(n_blocks):
            own_scores = jnp.where(mine == b, scores[:, b * BLK : (b + 1) * BLK], own_scores)
        grad_scores = jnp.where(mine >= 0, jax.nn.sigmoid(own_scores) - target[at], 0.0)
        grad_scores_ref[at, :] = grad_scores
        spread = jnp.concatenate(
            [jnp.where(mine == b, grad_scores, 0.0).astype(BF16) for b in range(n_blocks)], axis=1
        )
        grad_pairs.append(dot(spread, labels[j][...]))
    grad_pair = jnp.concatenate(grad_pairs, axis=0).astype(BF16).astype(F32)

    projection = jnp.mean(hidden * grad_pair, axis=-1, keepdims=True)
    grad_hidden = (inv_rms * grad_pair - hidden * (inv_rms**3 * projection)).astype(BF16)
    total = dot(feats, grad_hidden, 0, 0)
    total_ref[...] = total if first else total + total_in[...]
    for m in range(n_data if last else 0):
        shares[m % 2][m // 2] = total_ref[shard_at(m, shard_rows), :].astype(BF16)

    grad_feats = dot(grad_hidden, enc[...], 1, 1).astype(BF16)
    for s in range(n_sources):
        parts = [
            grad_feats[(j * n_sources + s) * cap : (j * n_sources + s + 1) * cap]
            for j in range(n_sets)
        ]
        backs[s][...] = dot(picks[s], jnp.concatenate(parts, axis=0), 0, 0).astype(BF16)


def grad_label_kernel(*refs, calls, n_sets, j, n_more):
    grad_scores, blocks, embeddings = refs[:calls], refs[calls : 2 * calls], refs[2 * calls : 3 * calls]
    more, rest = refs[3 * calls : 3 * calls + n_more], refs[3 * calls + n_more :]
    out_ref, (result, *sem) = rest[0], rest[-2:] if len(rest) > 1 else rest
    rows_of = [slice(j * r.shape[0] // n_sets, (j + 1) * r.shape[0] // n_sets) for r in blocks]
    grad_scores_t = jnp.concatenate([r[at, :].T for r, at in zip(grad_scores, rows_of)], axis=1)
    block_t = jnp.concatenate([r[at, :].T for r, at in zip(blocks, rows_of)], axis=1)
    embedding = jnp.concatenate([r[at, :] for r, at in zip(embeddings, rows_of)], axis=0)
    copies = []
    for b in range(out_ref.shape[0] // BLK):
        rows = pl.ds(b * BLK, BLK)
        spread_t = jnp.where(block_t == b, grad_scores_t, 0.0).astype(BF16)
        total = dot(spread_t, embedding)
        for ref in more:
            total = total + ref[rows, :].astype(F32)
        result[rows, :] = total.astype(BF16)
        if sem:
            copies.append(pltpu.make_async_copy(result.at[rows], out_ref.at[rows], sem[0].at[b]))
            copies[b].start()
    for copy in copies:
        copy.wait()


def own_block_kernel(feats_ref, owners_ref, blocks_ref, positives_ref, out_ref, ints, sem):
    rows, width = feats_ref.shape
    feats = pltpu.make_async_copy(feats_ref, out_ref.at[pl.ds(0, rows)], sem.at[0])
    feats.start()
    copies = []
    for i, ref in enumerate((owners_ref, blocks_ref, positives_ref)):
        copies.append(pltpu.make_async_copy(ref, ints.at[i], sem.at[i + 1]))
        copies[i].start()
    for copy in copies:
        copy.wait()
    meta = [ints[i].astype(F32) for i in range(3)]
    meta += [jnp.zeros((meta[0].shape[0], width - 3 * rows), F32)]
    meta = jnp.concatenate(meta, axis=1)
    rest = jnp.zeros((META_ROWS - meta.shape[0], width), F32)
    out_ref[rows:, :] = jnp.concatenate([meta, rest], axis=0).astype(BF16)
    feats.wait()


def load_kernel(label_ref, shard_ref, label_out, shard_out):
    label_out[...] = label_ref[...]
    shard_out[...] = shard_ref[...]


def half_at(mine, half):
    odd = jnp.bitwise_and(lax.axis_index("labels"), 1)
    return pl.ds(pl.multiple_of((odd if mine else 1 - odd) * half, 16), half)


def split_kernel(even_ref, got_ref, *refs):
    *more, keep_ref, send_ref, total = refs
    share = even_ref[0].astype(F32) + got_ref[0].astype(F32)
    for ref in more:
        share = share + ref[...].astype(F32)
    total[...] = share
    half = keep_ref.shape[0]
    keep_ref[...] = total[half_at(True, half), :]
    send_ref[...] = total[half_at(False, half), :].astype(BF16)


def merge_kernel(mine_ref, other_ref, out_ref):
    half = mine_ref.shape[0]
    out_ref[half_at(True, half), :] = mine_ref[...].astype(F32)
    out_ref[half_at(False, half), :] = other_ref[...].astype(F32)


def call(kernel, name, out_shape, scratch, flops, megabytes, *args, space=VMEM, out_space=VMEM, limit=24):
    return pl.pallas_call(
        kernel,
        in_specs=[space] * len(args),
        out_specs=jax.tree.map(lambda _: out_space, out_shape),
        out_shape=out_shape,
        scratch_shapes=scratch,
        compiler_params=pltpu.CompilerParams(vmem_limit_bytes=limit << 20),
        cost_estimate=pl.CostEstimate(
            flops=flops, bytes_accessed=megabytes << 20, transcendentals=0
        ),
        name=name,
    )(*args)


def shaped(shape, dtype=BF16):
    return jax.ShapeDtypeStruct(shape, dtype)


def pair_work(sources, labels, shards, cap, pick_count, before, last):
    n_data, n_sets = len(shards), len(labels)
    block_rows, width = sources[0].shape
    rows = block_rows - META_ROWS
    slots = n_sets * len(sources) * cap
    shard_rows = shards[0].shape[0]
    full = (n_data * shard_rows, width)
    backs = len(sources)
    shapes = [shaped((rows, width))] * backs
    shapes += [shaped((slots, BLK), F32), shaped((slots, BLK), jnp.int32), shaped((slots, width))]
    more = [before["enc"], before["total"]] if before else shards
    scratch = []
    if not before:
        shapes += [shaped(full)]
    if last:
        shapes += [shaped((n_data // 2, shard_rows, width))] * 2
        scratch = [pltpu.VMEM(full, F32)]
    else:
        shapes += [shaped(full, F32)]
    out = call(
        functools.partial(
            pair_kernel,
            cap=cap,
            pick_count=pick_count,
            n_sources=len(sources),
            n_sets=n_sets,
            n_data=n_data,
            first=not before,
            last=last,
        ),
        "pair_work",
        shapes,
        scratch,
        2 * slots * width * (2 * labels[0].shape[0] + 3 * width + 2 * rows),
        8,
        *sources,
        *labels,
        *more,
    )
    result = {"back": list(out[:backs]), "slots": list(out[backs : backs + 3])}
    rest = list(out[backs + 3 :])
    result["enc"] = before["enc"] if before else rest.pop(0)
    result["shares" if last else "total"] = rest if last else rest[0]
    return result


def grad_label_work(works, n_sets, j, labels_shape, *more):
    slots = list(zip(*(work["slots"] for work in works)))
    scratch = []
    if j == 0:
        sem = pltpu.SemaphoreType.DMA((labels_shape[0] // BLK,))
        scratch = [pltpu.VMEM(labels_shape, BF16), sem]
    return call(
        functools.partial(
            grad_label_kernel, calls=len(works), n_sets=n_sets, j=j, n_more=len(more)
        ),
        "grad_label_work",
        shaped(labels_shape),
        scratch,
        2 * sum(x.shape[0] for x in slots[0]) // n_sets * labels_shape[0] * labels_shape[1],
        4,
        *slots[0],
        *slots[1],
        *slots[2],
        *more,
        out_space=pl.BlockSpec(memory_space=pl.ANY) if scratch else VMEM,
    )


def swap(x):
    x = lax.all_to_all(x, "labels", split_axis=0, concat_axis=0, tiled=True)
    return lax.all_to_all(x, "dp", split_axis=1, concat_axis=1, tiled=True)


def partner(x, axis, mask):
    return lax.ppermute(x, axis, [(i, i ^ mask) for i in range(lax.axis_size(axis))])


def masks(n):
    return [1 << i for i in range(n.bit_length() - 1)]


def after(x, *others):
    return lax.optimization_barrier((x, *others))[0]


def gather_far(x):
    got = {0: x}
    for mask in reversed(masks(lax.axis_size("dp"))[1:]):
        got.update({m | mask: partner(v, "dp", mask) for m, v in list(got.items())})
    return [got[m] for m in sorted(got)]


def gather_near(far, *first):
    near = [partner(after(v, *far[1:], *first), "dp", 1) for v in far]
    return [v for pair in zip(far, near) for v in pair]


def gather_labels(x, first):
    got = {0: x}
    for mask in reversed(masks(lax.axis_size("labels"))):
        for m, v in list(got.items()):
            got[m | mask] = partner(after(v, first) if m else v, "labels", mask)
    return [got[m] for m in range(len(got))]


def add(*terms):
    return sum(t.astype(F32) for t in terms)


def dp_terms(even, odd):
    got = sent = partner(odd, "dp", 1)
    terms = [[even[i], got[i]] for i in range(even.shape[0])]
    for mask in masks(len(terms)):
        for i in range(len(terms)):
            if i & mask == 0 and i % mask == 0:
                sent = add(*terms[i | mask]).astype(BF16)
                terms[i].append(partner(sent, "dp", 2 * mask))
    return got, terms[0], sent


def sum_shares(even, got, terms, *first):
    rows, width = even.shape[1:]
    half = rows // 2
    keep, send = call(
        split_kernel,
        "split_share",
        [shaped((half, width), F32), shaped((half, width))],
        [pltpu.VMEM((rows, width), F32)],
        0,
        1,
        even,
        after(got, *first),
        *terms[2:],
    )
    x = add(keep, partner(send, "labels", 1)).astype(BF16)
    first = x
    for mask in masks(lax.axis_size("labels"))[1:]:
        x = add(x, partner(x, "labels", mask)).astype(BF16)
    return keep, first, x


def join_halves(x, *first):
    other = partner(x, "labels", 1)
    out = shaped((2 * x.shape[0], x.shape[1]), F32)
    return call(merge_kernel, "merge_share", out, [], 0, 1, after(x, *first), other)


def reduce_runs(runs, got_last, ahead, keep, first):
    def over_dp(parts, *hold):
        parts = [list(part) for part in parts]
        for mask in masks(len(parts)):
            for h in range(0, len(parts), 2 * mask):
                sent = after(add(*parts[h + mask]).astype(BF16), *hold)
                parts[h].append(partner(sent, "dp", 2 * mask))
        return parts[0]

    n = len(runs)
    sums = {n - 2: over_dp(list(zip(runs[n - 2], got_last)), ahead)}
    for i in reversed(range(0, n - 2, 2)):
        near = after(add(*over_dp([[x] for x in runs[i + 1]], keep)).astype(BF16), first)
        sums[i] = over_dp([[x] for x in runs[i]], keep) + [partner(near, "labels", 1)]
    for mask in masks(n)[1:]:
        for i in range(0, n, 2 * mask):
            sent = after(add(*sums[i + mask]).astype(BF16), first)
            sums[i].append(partner(sent, "labels", mask))
    return sums[0]


def with_meta(feats, owner_rows, block_rows, positive_rows):
    meta = jnp.concatenate([owner_rows, block_rows, positive_rows], axis=1).astype(BF16)
    meta = jnp.pad(meta, ((0, META_ROWS - meta.shape[0]), (0, feats.shape[1] - meta.shape[1])))
    return jnp.concatenate([feats, meta], axis=0)


def local(feats, enc_weight, label_weight, owners, blocks, positives):
    n_labels = lax.axis_size("labels")
    n_data = lax.axis_size("dp")
    n_owner = n_labels * n_data
    row_count, width = feats.shape
    pick_count = owners.shape[1]
    cap = max(2, 2 * row_count * pick_count // n_owner)

    if row_count <= n_data * cap:
        own = call(
            own_block_kernel,
            "own_block",
            shaped((row_count + META_ROWS, width)),
            [
                pltpu.VMEM((3, pick_count, row_count), jnp.int32),
                pltpu.SemaphoreType.DMA((4,)),
            ],
            0,
            1,
            feats,
            owners.T,
            blocks.T,
            positives.T,
            space=HBM,
            limit=60,
        )
        labels = [label_weight, partner(label_weight, "dp", 1)]
        labels[0], own_shard = call(
            load_kernel,
            "load",
            [shaped(label_weight.shape), shaped(enc_weight.shape)],
            [],
            0,
            4,
            after(label_weight, labels[1]),
            enc_weight,
        )
        near = gather_labels(own, labels[0])
        far = {0: gather_far(near[0])}
        shards = gather_near(
            gather_far(enc_weight), *far[0][1:], *near[1:3], labels[0]
        )
        shards[0] = own_shard
        works, backs = [], {}
        last_call = list(range(1, n_labels, 2))
        for call_runs in (list(range(0, n_labels, 2)), last_call):
            sources = []
            for run in call_runs:
                if run == n_labels - 1:
                    far[run] = gather_far(after(near[run], *far[run - 1][1:]))
                elif run % 2:
                    sent = [after(x, *shards[1:]) for x in far[run - 1][1:]]
                    far[run] = near[run : run + 1] + [partner(x, "labels", 1) for x in sent]
                elif run:
                    far[run] = gather_far(after(near[run], *far[0][1:]))
                sources += [after(near[run], *([] if run else near[1:3]))] + far[run][1:]
            before, last = works[-1] if works else None, call_runs is last_call
            works.append(pair_work(sources, labels, shards, cap, pick_count, before, last))
            parts = len(sources) // len(call_runs)
            for i, run in enumerate(call_runs):
                backs[run] = works[-1]["back"][i * parts : (i + 1) * parts]
        even, odd = works[-1]["shares"]
        got, share_terms, sent = dp_terms(even, odd)
        near_last, *far_last = backs[n_labels - 1]
        got_last = [partner(x, "labels", 1) for x in (after(near_last, sent), *far_last)]
        keep, first, share = sum_shares(even, got, share_terms, *got_last)
        terms = reduce_runs(backs, got_last, sent, keep, first)
        works[0]["slots"][2] = after(works[0]["slots"][2], sent)
        other = partner(grad_label_work(works, 2, 1, label_weight.shape), "dp", 1)
        grad_label = grad_label_work(works, 2, 0, label_weight.shape, other)
        grad_feats = add(*terms).astype(BF16)
        grad_enc = join_halves(share, grad_label, grad_feats)
    else:
        shards = gather_near(gather_far(enc_weight))
        flat = owners.reshape(-1)
        onehot = (flat[:, None] == jnp.arange(n_owner, dtype=jnp.int32)[None, :]).astype(jnp.int32)
        rank = jnp.sum((jnp.cumsum(onehot, axis=0) - onehot) * onehot, axis=1)
        slot = (flat * cap + rank).reshape(row_count, pick_count)
        slot_total = n_owner * cap
        slots = jnp.arange(slot_total, dtype=jnp.int32)
        place = slots[:, None, None] == slot[None]
        pick = jnp.any(place, axis=2).astype(BF16)
        live = jnp.any(place, axis=(1, 2))
        block_of = jnp.sum(jnp.where(place, blocks[None], 0), axis=(1, 2))
        wanted = jnp.sum(jnp.where(place, positives[None], 0), axis=(1, 2))
        owner_of = jnp.where(live, slots // cap, -1)
        out = dot(pick, feats).astype(BF16).reshape(n_labels, n_data, cap, width)
        meta = jnp.stack([owner_of, block_of, wanted], axis=1).reshape(n_labels, n_data, cap, 3)
        tiles = slot_total // TILE
        got = swap(out).reshape(tiles, TILE, width)
        got_meta = swap(meta).reshape(tiles, TILE, 3).transpose(0, 2, 1)
        sources = [
            with_meta(got[i], got_meta[i, 0:1], got_meta[i, 1:2], got_meta[i, 2:3])
            for i in range(tiles)
        ]
        works = []
        for i in range(0, tiles, 4):
            before = works[-1] if works else None
            last = i + 4 >= tiles
            works.append(pair_work(sources[i : i + 4], [label_weight], shards, TILE, 1, before, last))
        back = jnp.concatenate([back for work in works for back in work["back"]], axis=0)
        back = swap(back.reshape(n_labels, n_data, cap, width)).reshape(slot_total, width)
        grad_feats = dot(pick, back, 0, 0).astype(BF16)
        even, odd = works[-1]["shares"]
        got, share_terms, _ = dp_terms(even, odd)
        *_, share = sum_shares(even, got, share_terms)
        grad_label = grad_label_work(works, 1, 0, label_weight.shape)
        grad_enc = join_halves(share, grad_label, grad_feats)

    return (grad_feats, grad_label, grad_enc)


def solution(mesh):
    rows = P(("groups", "labels", "dp"), None)
    return jax.shard_map(
        local,
        mesh=mesh,
        in_specs=(rows, P("dp", None), rows, rows, rows, rows),
        out_specs=(rows, rows, P(("groups", "dp"), None)),
        check_vma=False,
    )
```

```python
import functools

import jax
import jax.numpy as jnp
from jax import lax
from jax.experimental import pallas as pl
from jax.experimental.pallas import tpu as pltpu
from jax.sharding import PartitionSpec as P

BLK = 128
EPSILON = 1e-06
META_ROWS = 8
TILE = 128
F32 = jnp.float32
BF16 = jnp.bfloat16
VMEM = pl.BlockSpec(memory_space=pltpu.VMEM)
HBM = pl.BlockSpec(memory_space=pltpu.HBM)


def dot(a, b, da=1, db=0):
    return lax.dot_general(a, b, (((da,), (db,)), ((), ())), preferred_element_type=F32)


def shard_at(m, shard_rows):
    at = jnp.bitwise_xor(lax.axis_index("dp"), m) * shard_rows
    return pl.ds(pl.multiple_of(at, 16), shard_rows)


def pair_kernel(*refs, cap, pick_count, n_sources, n_sets, n_data, first, last):
    it = iter(refs)
    take = lambda n: [next(it) for _ in range(n)]
    sources, labels = take(n_sources), take(n_sets)
    shards = take(n_data if first else 0)
    enc, total_in = (None, None) if first else take(2)
    backs, grad_scores_ref, block_ref, embedding_ref = take(n_sources), *take(3)
    enc = next(it) if first else enc
    shares = take(2 if last else 0)
    total_ref = next(it)

    n_owner_data = lax.axis_size("dp")
    me = lax.axis_index("labels") * n_owner_data + lax.axis_index("dp")
    rows = sources[0].shape[0] - META_ROWS
    shard_rows = enc.shape[0] // n_data
    n_blocks = labels[0].shape[0] // BLK
    part = n_sources * cap
    slots = n_sets * part

    for m, shard in enumerate(shards):
        enc[shard_at(m, shard_rows), :] = shard[...]

    row_id = lax.broadcasted_iota(jnp.int32, (rows, rows), 0)
    col_id = lax.broadcasted_iota(jnp.int32, (rows, rows), 1)
    before = (row_id < col_id).astype(BF16)
    slot_id = lax.broadcasted_iota(jnp.int32, (cap, rows), 0).astype(F32)
    column = lax.broadcasted_iota(jnp.int32, (slots, BLK), 1)

    hits, codes = [], []
    for source in sources:
        meta = source[rows:, 0 : 3 * rows].astype(F32)[:pick_count]
        code = meta[:, rows : 2 * rows] * 256.0 + meta[:, 2 * rows :] + 1.0
        for j in range(n_sets):
            named = meta[:, :rows] == jnp.bitwise_xor(me, j).astype(F32)
            hits.append(jnp.sum(named.astype(F32), axis=0, keepdims=True))
            codes.append(jnp.sum(jnp.where(named, code, 0.0), axis=0, keepdims=True))
    rank = dot(jnp.concatenate(hits, axis=0).astype(BF16), before)

    picks, picked, slot_codes = [], {}, {}
    for s, source in enumerate(sources):
        pick = []
        for j in range(n_sets):
            i = s * n_sets + j
            pick.append(jnp.where((slot_id == rank[i : i + 1]) & (hits[i] > 0.0), 1.0, 0.0))
            slot_codes[j, s] = jnp.sum(pick[j] * codes[i], axis=1, keepdims=True)
        picks.append(jnp.concatenate(pick, axis=0).astype(BF16))
        found = dot(picks[s], source[:rows, :]).astype(BF16)
        for j in range(n_sets):
            picked[j, s] = found[j * cap : (j + 1) * cap]
    order = [(j, s) for j in range(n_sets) for s in range(n_sources)]
    feats = jnp.concatenate([picked[i] for i in order], axis=0)
    code = jnp.concatenate([slot_codes[i] for i in order], axis=0).astype(jnp.int32) - 1

    hidden = dot(feats, enc[...])
    inv_rms = lax.rsqrt(jnp.mean(hidden * hidden, axis=-1, keepdims=True) + EPSILON)
    embedding = (hidden * inv_rms).astype(BF16)
    embedding_ref[...] = embedding

    block = jnp.broadcast_to(code >> 8, (slots, BLK))
    block_ref[...] = block
    wanted = jnp.broadcast_to(code & 255, (slots, BLK))
    target = jnp.where(column == wanted, 1.0, 0.0)
    grad_pairs = []
    for j in range(n_sets):
        at = slice(j * part, (j + 1) * part)
        scores = dot(embedding[at], labels[j][...], 1, 1)
        mine = block[at]
        own_scores = jnp.zeros((part, BLK), F32)
        for b in range(n_blocks):
            own_scores = jnp.where(mine == b, scores[:, b * BLK : (b + 1) * BLK], own_scores)
        grad_scores = jnp.where(mine >= 0, jax.nn.sigmoid(own_scores) - target[at], 0.0)
        grad_scores_ref[at, :] = grad_scores
        spread = jnp.concatenate(
            [jnp.where(mine == b, grad_scores, 0.0).astype(BF16) for b in range(n_blocks)], axis=1
        )
        grad_pairs.append(dot(spread, labels[j][...]))
    grad_pair = jnp.concatenate(grad_pairs, axis=0).astype(BF16).astype(F32)

    projection = jnp.mean(hidden * grad_pair, axis=-1, keepdims=True)
    grad_hidden = (inv_rms * grad_pair - hidden * (inv_rms**3 * projection)).astype(BF16)
    total = dot(feats, grad_hidden, 0, 0)
    total_ref[...] = total if first else total + total_in[...]
    for m in range(n_data if last else 0):
        shares[m % 2][m // 2] = total_ref[shard_at(m, shard_rows), :].astype(BF16)

    grad_feats = dot(grad_hidden, enc[...], 1, 1).astype(BF16)
    for s in range(n_sources):
        parts = [
            grad_feats[(j * n_sources + s) * cap : (j * n_sources + s + 1) * cap]
            for j in range(n_sets)
        ]
        backs[s][...] = dot(picks[s], jnp.concatenate(parts, axis=0), 0, 0).astype(BF16)


def grad_label_kernel(*refs, calls, n_sets, j, n_more):
    grad_scores, blocks, embeddings = refs[:calls], refs[calls : 2 * calls], refs[2 * calls : 3 * calls]
    more, rest = refs[3 * calls : 3 * calls + n_more], refs[3 * calls + n_more :]
    out_ref, (result, *sem) = rest[0], rest[-2:] if len(rest) > 1 else rest
    rows_of = [slice(j * r.shape[0] // n_sets, (j + 1) * r.shape[0] // n_sets) for r in blocks]
    grad_scores_t = jnp.concatenate([r[at, :].T for r, at in zip(grad_scores, rows_of)], axis=1)
    block_t = jnp.concatenate([r[at, :].T for r, at in zip(blocks, rows_of)], axis=1)
    embedding = jnp.concatenate([r[at, :] for r, at in zip(embeddings, rows_of)], axis=0)
    copies = []
    for b in range(out_ref.shape[0] // BLK):
        rows = pl.ds(b * BLK, BLK)
        spread_t = jnp.where(block_t == b, grad_scores_t, 0.0).astype(BF16)
        total = dot(spread_t, embedding)
        for ref in more:
            total = total + ref[rows, :].astype(F32)
        result[rows, :] = total.astype(BF16)
        if sem:
            copies.append(pltpu.make_async_copy(result.at[rows], out_ref.at[rows], sem[0].at[b]))
            copies[b].start()
    for copy in copies:
        copy.wait()


def own_block_kernel(feats_ref, owners_ref, blocks_ref, positives_ref, out_ref, ints, sem):
    rows, width = feats_ref.shape
    feats = pltpu.make_async_copy(feats_ref, out_ref.at[pl.ds(0, rows)], sem.at[0])
    feats.start()
    copies = []
    for i, ref in enumerate((owners_ref, blocks_ref, positives_ref)):
        copies.append(pltpu.make_async_copy(ref, ints.at[i], sem.at[i + 1]))
        copies[i].start()
    for copy in copies:
        copy.wait()
    meta = [ints[i].astype(F32) for i in range(3)]
    meta += [jnp.zeros((meta[0].shape[0], width - 3 * rows), F32)]
    meta = jnp.concatenate(meta, axis=1)
    rest = jnp.zeros((META_ROWS - meta.shape[0], width), F32)
    out_ref[rows:, :] = jnp.concatenate([meta, rest], axis=0).astype(BF16)
    feats.wait()


def load_kernel(label_ref, shard_ref, label_out, shard_out):
    label_out[...] = label_ref[...]
    shard_out[...] = shard_ref[...]


def half_at(mine, half):
    odd = jnp.bitwise_and(lax.axis_index("labels"), 1)
    return pl.ds(pl.multiple_of((odd if mine else 1 - odd) * half, 16), half)


def split_kernel(even_ref, got_ref, *refs):
    *more, keep_ref, send_ref, total = refs
    share = even_ref[0].astype(F32) + got_ref[0].astype(F32)
    for ref in more:
        share = share + ref[...].astype(F32)
    total[...] = share
    half = keep_ref.shape[0]
    keep_ref[...] = total[half_at(True, half), :]
    send_ref[...] = total[half_at(False, half), :].astype(BF16)


def merge_kernel(mine_ref, other_ref, out_ref):
    half = mine_ref.shape[0]
    out_ref[half_at(True, half), :] = mine_ref[...].astype(F32)
    out_ref[half_at(False, half), :] = other_ref[...].astype(F32)


def call(kernel, name, out_shape, scratch, flops, megabytes, *args, space=VMEM, out_space=VMEM, limit=24):
    return pl.pallas_call(
        kernel,
        in_specs=[space] * len(args),
        out_specs=jax.tree.map(lambda _: out_space, out_shape),
        out_shape=out_shape,
        scratch_shapes=scratch,
        compiler_params=pltpu.CompilerParams(vmem_limit_bytes=limit << 20),
        cost_estimate=pl.CostEstimate(
            flops=flops, bytes_accessed=megabytes << 20, transcendentals=0
        ),
        name=name,
    )(*args)


def shaped(shape, dtype=BF16):
    return jax.ShapeDtypeStruct(shape, dtype)


def pair_work(sources, labels, shards, cap, pick_count, before, last):
    n_data, n_sets = len(shards), len(labels)
    block_rows, width = sources[0].shape
    rows = block_rows - META_ROWS
    slots = n_sets * len(sources) * cap
    shard_rows = shards[0].shape[0]
    full = (n_data * shard_rows, width)
    backs = len(sources)
    shapes = [shaped((rows, width))] * backs
    shapes += [shaped((slots, BLK), F32), shaped((slots, BLK), jnp.int32), shaped((slots, width))]
    more = [before["enc"], before["total"]] if before else shards
    scratch = []
    if not before:
        shapes += [shaped(full)]
    if last:
        shapes += [shaped((n_data // 2, shard_rows, width))] * 2
        scratch = [pltpu.VMEM(full, F32)]
    else:
        shapes += [shaped(full, F32)]
    out = call(
        functools.partial(
            pair_kernel,
            cap=cap,
            pick_count=pick_count,
            n_sources=len(sources),
            n_sets=n_sets,
            n_data=n_data,
            first=not before,
            last=last,
        ),
        "pair_work",
        shapes,
        scratch,
        2 * slots * width * (2 * labels[0].shape[0] + 3 * width + 2 * rows),
        8,
        *sources,
        *labels,
        *more,
    )
    result = {"back": list(out[:backs]), "slots": list(out[backs : backs + 3])}
    rest = list(out[backs + 3 :])
    result["enc"] = before["enc"] if before else rest.pop(0)
    result["shares" if last else "total"] = rest if last else rest[0]
    return result


def grad_label_work(works, n_sets, j, labels_shape, *more):
    slots = list(zip(*(work["slots"] for work in works)))
    scratch = []
    if j == 0:
        sem = pltpu.SemaphoreType.DMA((labels_shape[0] // BLK,))
        scratch = [pltpu.VMEM(labels_shape, BF16), sem]
    return call(
        functools.partial(
            grad_label_kernel, calls=len(works), n_sets=n_sets, j=j, n_more=len(more)
        ),
        "grad_label_work",
        shaped(labels_shape),
        scratch,
        2 * sum(x.shape[0] for x in slots[0]) // n_sets * labels_shape[0] * labels_shape[1],
        4,
        *slots[0],
        *slots[1],
        *slots[2],
        *more,
        out_space=pl.BlockSpec(memory_space=pl.ANY) if scratch else VMEM,
    )


def swap(x):
    x = lax.all_to_all(x, "labels", split_axis=0, concat_axis=0, tiled=True)
    return lax.all_to_all(x, "dp", split_axis=1, concat_axis=1, tiled=True)


def partner(x, axis, mask):
    return lax.ppermute(x, axis, [(i, i ^ mask) for i in range(lax.axis_size(axis))])


def masks(n):
    return [1 << i for i in range(n.bit_length() - 1)]


def after(x, *others):
    return lax.optimization_barrier((x, *others))[0]


def gather_far(x):
    got = {0: x}
    for mask in reversed(masks(lax.axis_size("dp"))[1:]):
        got.update({m | mask: partner(v, "dp", mask) for m, v in list(got.items())})
    return [got[m] for m in sorted(got)]


def gather_near(far, *first):
    near = [partner(after(v, *far[1:], *first), "dp", 1) for v in far]
    return [v for pair in zip(far, near) for v in pair]


def gather_labels(x, first):
    got = {0: x}
    for mask in reversed(masks(lax.axis_size("labels"))):
        for m, v in list(got.items()):
            got[m | mask] = partner(after(v, first) if m else v, "labels", mask)
    return [got[m] for m in range(len(got))]


def add(*terms):
    return sum(t.astype(F32) for t in terms)


def dp_terms(even, odd):
    got = sent = partner(odd, "dp", 1)
    terms = [[even[i], got[i]] for i in range(even.shape[0])]
    for mask in masks(len(terms)):
        for i in range(len(terms)):
            if i & mask == 0 and i % mask == 0:
                sent = add(*terms[i | mask]).astype(BF16)
                terms[i].append(partner(sent, "dp", 2 * mask))
    return got, terms[0], sent


def sum_shares(even, got, terms, *first):
    rows, width = even.shape[1:]
    half = rows // 2
    keep, send = call(
        split_kernel,
        "split_share",
        [shaped((half, width), F32), shaped((half, width))],
        [pltpu.VMEM((rows, width), F32)],
        0,
        1,
        even,
        after(got, *first),
        *terms[2:],
    )
    x = add(keep, partner(send, "labels", 1)).astype(BF16)
    first = x
    for mask in masks(lax.axis_size("labels"))[1:]:
        x = add(x, partner(x, "labels", mask)).astype(BF16)
    return keep, first, x


def join_halves(x, *first):
    other = partner(x, "labels", 1)
    out = shaped((2 * x.shape[0], x.shape[1]), F32)
    return call(merge_kernel, "merge_share", out, [], 0, 1, after(x, *first), other)


def reduce_runs(runs, got_last, ahead, keep, first):
    def over_dp(parts, *hold):
        parts = [list(part) for part in parts]
        for mask in masks(len(parts)):
            for h in range(0, len(parts), 2 * mask):
                sent = after(add(*parts[h + mask]).astype(BF16), *hold)
                parts[h].append(partner(sent, "dp", 2 * mask))
        return parts[0]

    n = len(runs)
    sums, sent_near = {n - 2: over_dp(list(zip(runs[n - 2], got_last)), ahead)}, []
    for i in reversed(range(0, n - 2, 2)):
        near = add(*over_dp([[x] for x in runs[i + 1]], ahead)).astype(BF16)
        sent_near.append(partner(near, "labels", 1))
        sums[i] = over_dp([[x] for x in runs[i]], keep) + sent_near[-1:]
    for mask in masks(n)[1:]:
        for i in range(0, n, 2 * mask):
            sent = after(add(*sums[i + mask]).astype(BF16), first, *sent_near)
            sums[i].append(partner(sent, "labels", mask))
    return sums[0]


def with_meta(feats, owner_rows, block_rows, positive_rows):
    meta = jnp.concatenate([owner_rows, block_rows, positive_rows], axis=1).astype(BF16)
    meta = jnp.pad(meta, ((0, META_ROWS - meta.shape[0]), (0, feats.shape[1] - meta.shape[1])))
    return jnp.concatenate([feats, meta], axis=0)


def local(feats, enc_weight, label_weight, owners, blocks, positives):
    n_labels = lax.axis_size("labels")
    n_data = lax.axis_size("dp")
    n_owner = n_labels * n_data
    row_count, width = feats.shape
    pick_count = owners.shape[1]
    cap = max(2, 2 * row_count * pick_count // n_owner)

    if row_count <= n_data * cap:
        own = call(
            own_block_kernel,
            "own_block",
            shaped((row_count + META_ROWS, width)),
            [
                pltpu.VMEM((3, pick_count, row_count), jnp.int32),
                pltpu.SemaphoreType.DMA((4,)),
            ],
            0,
            1,
            feats,
            owners.T,
            blocks.T,
            positives.T,
            space=HBM,
            limit=60,
        )
        labels = [label_weight, partner(label_weight, "dp", 1)]
        labels[0], own_shard = call(
            load_kernel,
            "load",
            [shaped(label_weight.shape), shaped(enc_weight.shape)],
            [],
            0,
            4,
            after(label_weight, labels[1]),
            enc_weight,
        )
        near = gather_labels(own, labels[0])
        far = {0: gather_far(own)}
        shards = gather_near(gather_far(enc_weight))
        shards[0] = own_shard
        works, backs = [], {}
        last_call = list(range(1, n_labels, 2))
        for call_runs in (list(range(0, n_labels, 2)), last_call):
            sources = []
            for run in call_runs:
                if run == n_labels - 1:
                    far[run] = gather_far(after(near[run], *far[run - 1][1:]))
                elif run % 2:
                    sent = [after(x, *shards[1:]) for x in far[run - 1][1:]]
                    far[run] = near[run : run + 1] + [partner(x, "labels", 1) for x in sent]
                elif run:
                    far[run] = gather_far(after(near[run], *far[0][1:], *near[1:3], labels[0]))
                sources += [after(near[run], *([] if run else near[1:3]))] + far[run][1:]
            before, last = works[-1] if works else None, call_runs is last_call
            works.append(pair_work(sources, labels, shards, cap, pick_count, before, last))
            parts = len(sources) // len(call_runs)
            for i, run in enumerate(call_runs):
                backs[run] = works[-1]["back"][i * parts : (i + 1) * parts]
        even, odd = works[-1]["shares"]
        got, share_terms, sent = dp_terms(even, odd)
        near_last, *far_last = backs[n_labels - 1]
        got_last = [partner(x, "labels", 1) for x in (after(near_last, sent), *far_last)]
        keep, first, share = sum_shares(even, got, share_terms, *got_last)
        terms = reduce_runs(backs, got_last, sent, keep, first)
        other = partner(grad_label_work(works, 2, 1, label_weight.shape), "dp", 1)
        grad_label = grad_label_work(works, 2, 0, label_weight.shape, other)
        grad_feats = add(*terms).astype(BF16)
        grad_enc = join_halves(share, grad_label, grad_feats)
    else:
        shards = gather_near(gather_far(enc_weight))
        flat = owners.reshape(-1)
        onehot = (flat[:, None] == jnp.arange(n_owner, dtype=jnp.int32)[None, :]).astype(jnp.int32)
        rank = jnp.sum((jnp.cumsum(onehot, axis=0) - onehot) * onehot, axis=1)
        slot = (flat * cap + rank).reshape(row_count, pick_count)
        slot_total = n_owner * cap
        slots = jnp.arange(slot_total, dtype=jnp.int32)
        place = slots[:, None, None] == slot[None]
        pick = jnp.any(place, axis=2).astype(BF16)
        live = jnp.any(place, axis=(1, 2))
        block_of = jnp.sum(jnp.where(place, blocks[None], 0), axis=(1, 2))
        wanted = jnp.sum(jnp.where(place, positives[None], 0), axis=(1, 2))
        owner_of = jnp.where(live, slots // cap, -1)
        out = dot(pick, feats).astype(BF16).reshape(n_labels, n_data, cap, width)
        meta = jnp.stack([owner_of, block_of, wanted], axis=1).reshape(n_labels, n_data, cap, 3)
        tiles = slot_total // TILE
        got = swap(out).reshape(tiles, TILE, width)
        got_meta = swap(meta).reshape(tiles, TILE, 3).transpose(0, 2, 1)
        sources = [
            with_meta(got[i], got_meta[i, 0:1], got_meta[i, 1:2], got_meta[i, 2:3])
            for i in range(tiles)
        ]
        works = []
        for i in range(0, tiles, 4):
            before = works[-1] if works else None
            last = i + 4 >= tiles
            works.append(pair_work(sources[i : i + 4], [label_weight], shards, TILE, 1, before, last))
        back = jnp.concatenate([back for work in works for back in work["back"]], axis=0)
        back = swap(back.reshape(n_labels, n_data, cap, width)).reshape(slot_total, width)
        grad_feats = dot(pick, back, 0, 0).astype(BF16)
        even, odd = works[-1]["shares"]
        got, share_terms, _ = dp_terms(even, odd)
        *_, share = sum_shares(even, got, share_terms)
        grad_label = grad_label_work(works, 1, 0, label_weight.shape)
        grad_enc = join_halves(share, grad_label, grad_feats)

    return (grad_feats, grad_label, grad_enc)


def solution(mesh):
    rows = P(("groups", "labels", "dp"), None)
    return jax.shard_map(
        local,
        mesh=mesh,
        in_specs=(rows, P("dp", None), rows, rows, rows, rows),
        out_specs=(rows, rows, P(("groups", "dp"), None)),
        check_vma=False,
    )
```

```python
import functools

import jax
import jax.numpy as jnp
from jax import lax
from jax.experimental import pallas as pl
from jax.experimental.pallas import tpu as pltpu
from jax.sharding import PartitionSpec as P

BLK = 128
EPSILON = 1e-06
META_ROWS = 8
TILE = 128
F32 = jnp.float32
BF16 = jnp.bfloat16
VMEM = pl.BlockSpec(memory_space=pltpu.VMEM)
HBM = pl.BlockSpec(memory_space=pltpu.HBM)


def dot(a, b, da=1, db=0):
    return lax.dot_general(a, b, (((da,), (db,)), ((), ())), preferred_element_type=F32)


def shard_at(m, shard_rows):
    at = jnp.bitwise_xor(lax.axis_index("dp"), m) * shard_rows
    return pl.ds(pl.multiple_of(at, 16), shard_rows)


def pair_kernel(*refs, cap, pick_count, n_sources, n_sets, n_data, first, last):
    it = iter(refs)
    take = lambda n: [next(it) for _ in range(n)]
    sources, labels = take(n_sources), take(n_sets)
    shards = take(n_data if first else 0)
    enc, total_in = (None, None) if first else take(2)
    backs, grad_scores_ref, block_ref, embedding_ref = take(n_sources), *take(3)
    enc = next(it) if first else enc
    shares = take(2 if last else 0)
    total_ref = next(it)

    n_owner_data = lax.axis_size("dp")
    me = lax.axis_index("labels") * n_owner_data + lax.axis_index("dp")
    rows = sources[0].shape[0] - META_ROWS
    shard_rows = enc.shape[0] // n_data
    n_blocks = labels[0].shape[0] // BLK
    part = n_sources * cap
    slots = n_sets * part

    for m, shard in enumerate(shards):
        enc[shard_at(m, shard_rows), :] = shard[...]

    row_id = lax.broadcasted_iota(jnp.int32, (rows, rows), 0)
    col_id = lax.broadcasted_iota(jnp.int32, (rows, rows), 1)
    before = (row_id < col_id).astype(BF16)
    slot_id = lax.broadcasted_iota(jnp.int32, (cap, rows), 0).astype(F32)
    column = lax.broadcasted_iota(jnp.int32, (slots, BLK), 1)

    hits, codes = [], []
    for source in sources:
        meta = source[rows:, 0 : 3 * rows].astype(F32)[:pick_count]
        code = meta[:, rows : 2 * rows] * 256.0 + meta[:, 2 * rows :] + 1.0
        for j in range(n_sets):
            named = meta[:, :rows] == jnp.bitwise_xor(me, j).astype(F32)
            hits.append(jnp.sum(named.astype(F32), axis=0, keepdims=True))
            codes.append(jnp.sum(jnp.where(named, code, 0.0), axis=0, keepdims=True))
    rank = dot(jnp.concatenate(hits, axis=0).astype(BF16), before)

    picks, picked, slot_codes = [], {}, {}
    for s, source in enumerate(sources):
        pick = []
        for j in range(n_sets):
            i = s * n_sets + j
            pick.append(jnp.where((slot_id == rank[i : i + 1]) & (hits[i] > 0.0), 1.0, 0.0))
            slot_codes[j, s] = jnp.sum(pick[j] * codes[i], axis=1, keepdims=True)
        picks.append(jnp.concatenate(pick, axis=0).astype(BF16))
        found = dot(picks[s], source[:rows, :]).astype(BF16)
        for j in range(n_sets):
            picked[j, s] = found[j * cap : (j + 1) * cap]
    order = [(j, s) for j in range(n_sets) for s in range(n_sources)]
    feats = jnp.concatenate([picked[i] for i in order], axis=0)
    code = jnp.concatenate([slot_codes[i] for i in order], axis=0).astype(jnp.int32) - 1

    hidden = dot(feats, enc[...])
    inv_rms = lax.rsqrt(jnp.mean(hidden * hidden, axis=-1, keepdims=True) + EPSILON)
    embedding = (hidden * inv_rms).astype(BF16)
    embedding_ref[...] = embedding

    block = jnp.broadcast_to(code >> 8, (slots, BLK))
    block_ref[...] = block
    wanted = jnp.broadcast_to(code & 255, (slots, BLK))
    target = jnp.where(column == wanted, 1.0, 0.0)
    grad_pairs = []
    for j in range(n_sets):
        at = slice(j * part, (j + 1) * part)
        scores = dot(embedding[at], labels[j][...], 1, 1)
        mine = block[at]
        own_scores = jnp.zeros((part, BLK), F32)
        for b in range(n_blocks):
            own_scores = jnp.where(mine == b, scores[:, b * BLK : (b + 1) * BLK], own_scores)
        grad_scores = jnp.where(mine >= 0, jax.nn.sigmoid(own_scores) - target[at], 0.0)
        grad_scores_ref[at, :] = grad_scores
        spread = jnp.concatenate(
            [jnp.where(mine == b, grad_scores, 0.0).astype(BF16) for b in range(n_blocks)], axis=1
        )
        grad_pairs.append(dot(spread, labels[j][...]))
    grad_pair = jnp.concatenate(grad_pairs, axis=0).astype(BF16).astype(F32)

    projection = jnp.mean(hidden * grad_pair, axis=-1, keepdims=True)
    grad_hidden = (inv_rms * grad_pair - hidden * (inv_rms**3 * projection)).astype(BF16)
    total = dot(feats, grad_hidden, 0, 0)
    total_ref[...] = total if first else total + total_in[...]
    for m in range(n_data if last else 0):
        shares[m % 2][m // 2] = total_ref[shard_at(m, shard_rows), :].astype(BF16)

    grad_feats = dot(grad_hidden, enc[...], 1, 1).astype(BF16)
    for s in range(n_sources):
        parts = [
            grad_feats[(j * n_sources + s) * cap : (j * n_sources + s + 1) * cap]
            for j in range(n_sets)
        ]
        backs[s][...] = dot(picks[s], jnp.concatenate(parts, axis=0), 0, 0).astype(BF16)


def grad_label_kernel(*refs, calls, n_sets, j, n_more):
    grad_scores, blocks, embeddings = refs[:calls], refs[calls : 2 * calls], refs[2 * calls : 3 * calls]
    more, rest = refs[3 * calls : 3 * calls + n_more], refs[3 * calls + n_more :]
    out_ref, (result, *sem) = rest[0], rest[-2:] if len(rest) > 1 else rest
    rows_of = [slice(j * r.shape[0] // n_sets, (j + 1) * r.shape[0] // n_sets) for r in blocks]
    grad_scores_t = jnp.concatenate([r[at, :].T for r, at in zip(grad_scores, rows_of)], axis=1)
    block_t = jnp.concatenate([r[at, :].T for r, at in zip(blocks, rows_of)], axis=1)
    embedding = jnp.concatenate([r[at, :] for r, at in zip(embeddings, rows_of)], axis=0)
    copies = []
    for b in range(out_ref.shape[0] // BLK):
        rows = pl.ds(b * BLK, BLK)
        spread_t = jnp.where(block_t == b, grad_scores_t, 0.0).astype(BF16)
        total = dot(spread_t, embedding)
        for ref in more:
            total = total + ref[rows, :].astype(F32)
        result[rows, :] = total.astype(BF16)
        if sem:
            copies.append(pltpu.make_async_copy(result.at[rows], out_ref.at[rows], sem[0].at[b]))
            copies[b].start()
    for copy in copies:
        copy.wait()


def own_block_kernel(feats_ref, owners_ref, blocks_ref, positives_ref, out_ref, ints, sem):
    rows, width = feats_ref.shape
    feats = pltpu.make_async_copy(feats_ref, out_ref.at[pl.ds(0, rows)], sem.at[0])
    feats.start()
    copies = []
    for i, ref in enumerate((owners_ref, blocks_ref, positives_ref)):
        copies.append(pltpu.make_async_copy(ref, ints.at[i], sem.at[i + 1]))
        copies[i].start()
    for copy in copies:
        copy.wait()
    meta = [ints[i].astype(F32) for i in range(3)]
    meta += [jnp.zeros((meta[0].shape[0], width - 3 * rows), F32)]
    meta = jnp.concatenate(meta, axis=1)
    rest = jnp.zeros((META_ROWS - meta.shape[0], width), F32)
    out_ref[rows:, :] = jnp.concatenate([meta, rest], axis=0).astype(BF16)
    feats.wait()


def load_kernel(label_ref, shard_ref, label_out, shard_out):
    label_out[...] = label_ref[...]
    shard_out[...] = shard_ref[...]


def half_at(mine, half):
    odd = jnp.bitwise_and(lax.axis_index("labels"), 1)
    return pl.ds(pl.multiple_of((odd if mine else 1 - odd) * half, 16), half)


def split_kernel(even_ref, got_ref, *refs):
    *more, keep_ref, send_ref, total = refs
    share = even_ref[0].astype(F32) + got_ref[0].astype(F32)
    for ref in more:
        share = share + ref[...].astype(F32)
    total[...] = share
    half = keep_ref.shape[0]
    keep_ref[...] = total[half_at(True, half), :]
    send_ref[...] = total[half_at(False, half), :].astype(BF16)


def merge_kernel(mine_ref, other_ref, out_ref):
    half = mine_ref.shape[0]
    out_ref[half_at(True, half), :] = mine_ref[...].astype(F32)
    out_ref[half_at(False, half), :] = other_ref[...].astype(F32)


def call(kernel, name, out_shape, scratch, flops, megabytes, *args, space=VMEM, out_space=VMEM, limit=24):
    return pl.pallas_call(
        kernel,
        in_specs=[space] * len(args),
        out_specs=jax.tree.map(lambda _: out_space, out_shape),
        out_shape=out_shape,
        scratch_shapes=scratch,
        compiler_params=pltpu.CompilerParams(vmem_limit_bytes=limit << 20),
        cost_estimate=pl.CostEstimate(
            flops=flops, bytes_accessed=megabytes << 20, transcendentals=0
        ),
        name=name,
    )(*args)


def shaped(shape, dtype=BF16):
    return jax.ShapeDtypeStruct(shape, dtype)


def pair_work(sources, labels, shards, cap, pick_count, before, last):
    n_data, n_sets = len(shards), len(labels)
    block_rows, width = sources[0].shape
    rows = block_rows - META_ROWS
    slots = n_sets * len(sources) * cap
    shard_rows = shards[0].shape[0]
    full = (n_data * shard_rows, width)
    backs = len(sources)
    shapes = [shaped((rows, width))] * backs
    shapes += [shaped((slots, BLK), F32), shaped((slots, BLK), jnp.int32), shaped((slots, width))]
    more = [before["enc"], before["total"]] if before else shards
    scratch = []
    if not before:
        shapes += [shaped(full)]
    if last:
        shapes += [shaped((n_data // 2, shard_rows, width))] * 2
        scratch = [pltpu.VMEM(full, F32)]
    else:
        shapes += [shaped(full, F32)]
    out = call(
        functools.partial(
            pair_kernel,
            cap=cap,
            pick_count=pick_count,
            n_sources=len(sources),
            n_sets=n_sets,
            n_data=n_data,
            first=not before,
            last=last,
        ),
        "pair_work",
        shapes,
        scratch,
        2 * slots * width * (2 * labels[0].shape[0] + 3 * width + 2 * rows),
        8,
        *sources,
        *labels,
        *more,
    )
    result = {"back": list(out[:backs]), "slots": list(out[backs : backs + 3])}
    rest = list(out[backs + 3 :])
    result["enc"] = before["enc"] if before else rest.pop(0)
    result["shares" if last else "total"] = rest if last else rest[0]
    return result


def grad_label_work(works, n_sets, j, labels_shape, *more):
    slots = list(zip(*(work["slots"] for work in works)))
    scratch = []
    if j == 0:
        sem = pltpu.SemaphoreType.DMA((labels_shape[0] // BLK,))
        scratch = [pltpu.VMEM(labels_shape, BF16), sem]
    return call(
        functools.partial(
            grad_label_kernel, calls=len(works), n_sets=n_sets, j=j, n_more=len(more)
        ),
        "grad_label_work",
        shaped(labels_shape),
        scratch,
        2 * sum(x.shape[0] for x in slots[0]) // n_sets * labels_shape[0] * labels_shape[1],
        4,
        *slots[0],
        *slots[1],
        *slots[2],
        *more,
        out_space=pl.BlockSpec(memory_space=pl.ANY) if scratch else VMEM,
    )


def swap(x):
    x = lax.all_to_all(x, "labels", split_axis=0, concat_axis=0, tiled=True)
    return lax.all_to_all(x, "dp", split_axis=1, concat_axis=1, tiled=True)


def partner(x, axis, mask):
    return lax.ppermute(x, axis, [(i, i ^ mask) for i in range(lax.axis_size(axis))])


def masks(n):
    return [1 << i for i in range(n.bit_length() - 1)]


def after(x, *others):
    return lax.optimization_barrier((x, *others))[0]


def gather_far(x):
    got = {0: x}
    for mask in reversed(masks(lax.axis_size("dp"))[1:]):
        got.update({m | mask: partner(v, "dp", mask) for m, v in list(got.items())})
    return [got[m] for m in sorted(got)]


def gather_near(far, *first):
    near = [partner(after(v, *far[1:], *first), "dp", 1) for v in far]
    return [v for pair in zip(far, near) for v in pair]


def gather_labels(x, first):
    got = {0: x}
    for mask in reversed(masks(lax.axis_size("labels"))):
        for m, v in list(got.items()):
            got[m | mask] = partner(after(v, first) if m else v, "labels", mask)
    return [got[m] for m in range(len(got))]


def add(*terms):
    return sum(t.astype(F32) for t in terms)


def dp_terms(even, odd):
    got = sent = partner(odd, "dp", 1)
    terms = [[even[i], got[i]] for i in range(even.shape[0])]
    for mask in masks(len(terms)):
        for i in range(len(terms)):
            if i & mask == 0 and i % mask == 0:
                sent = add(*terms[i | mask]).astype(BF16)
                terms[i].append(partner(sent, "dp", 2 * mask))
    return got, terms[0], sent


def sum_shares(even, got, terms, *first):
    rows, width = even.shape[1:]
    half = rows // 2
    keep, send = call(
        split_kernel,
        "split_share",
        [shaped((half, width), F32), shaped((half, width))],
        [pltpu.VMEM((rows, width), F32)],
        0,
        1,
        even,
        after(got, *first),
        *terms[2:],
    )
    x = add(keep, partner(send, "labels", 1)).astype(BF16)
    first = x
    for mask in masks(lax.axis_size("labels"))[1:]:
        x = add(x, partner(x, "labels", mask)).astype(BF16)
    return keep, first, x


def join_halves(x, *first):
    other = partner(x, "labels", 1)
    out = shaped((2 * x.shape[0], x.shape[1]), F32)
    return call(merge_kernel, "merge_share", out, [], 0, 1, after(x, *first), other)


def reduce_runs(runs, got_last, ahead, keep, first):
    def over_dp(parts, *hold):
        parts = [list(part) for part in parts]
        for mask in masks(len(parts)):
            for h in range(0, len(parts), 2 * mask):
                sent = after(add(*parts[h + mask]).astype(BF16), *hold)
                parts[h].append(partner(sent, "dp", 2 * mask))
        return parts[0]

    n = len(runs)
    sums, sent_near = {n - 2: over_dp(list(zip(runs[n - 2], got_last)), ahead)}, []
    for i in reversed(range(0, n - 2, 2)):
        near = add(*over_dp([[x] for x in runs[i + 1]], ahead)).astype(BF16)
        sent_near.append(partner(near, "labels", 1))
        sums[i] = over_dp([[x] for x in runs[i]], keep) + sent_near[-1:]
    for mask in masks(n)[1:]:
        for i in range(0, n, 2 * mask):
            sent = after(add(*sums[i + mask]).astype(BF16), first, *sent_near)
            sums[i].append(partner(sent, "labels", mask))
    return sums[0]


def with_meta(feats, owner_rows, block_rows, positive_rows):
    meta = jnp.concatenate([owner_rows, block_rows, positive_rows], axis=1).astype(BF16)
    meta = jnp.pad(meta, ((0, META_ROWS - meta.shape[0]), (0, feats.shape[1] - meta.shape[1])))
    return jnp.concatenate([feats, meta], axis=0)


def local(feats, enc_weight, label_weight, owners, blocks, positives):
    n_labels = lax.axis_size("labels")
    n_data = lax.axis_size("dp")
    n_owner = n_labels * n_data
    row_count, width = feats.shape
    pick_count = owners.shape[1]
    cap = max(2, 2 * row_count * pick_count // n_owner)

    if row_count <= n_data * cap:
        own = call(
            own_block_kernel,
            "own_block",
            shaped((row_count + META_ROWS, width)),
            [
                pltpu.VMEM((3, pick_count, row_count), jnp.int32),
                pltpu.SemaphoreType.DMA((4,)),
            ],
            0,
            1,
            feats,
            owners.T,
            blocks.T,
            positives.T,
            space=HBM,
            limit=60,
        )
        labels = [label_weight, partner(label_weight, "dp", 1)]
        labels[0], own_shard = call(
            load_kernel,
            "load",
            [shaped(label_weight.shape), shaped(enc_weight.shape)],
            [],
            0,
            4,
            after(label_weight, labels[1]),
            enc_weight,
        )
        near = gather_labels(own, labels[0])
        far = {0: gather_far(own)}
        shards = gather_near(gather_far(enc_weight))
        shards[0] = own_shard
        works, backs = [], {}
        last_call = list(range(1, n_labels, 2))
        for call_runs in (list(range(0, n_labels, 2)), last_call):
            sources = []
            for run in call_runs:
                if run == n_labels - 1:
                    far[run] = gather_far(after(near[run], *far[run - 1][1:]))
                elif run % 2:
                    sent = [after(x, *shards[1:]) for x in far[run - 1][1:]]
                    far[run] = near[run : run + 1] + [partner(x, "labels", 1) for x in sent]
                elif run:
                    far[run] = gather_far(after(near[run], *far[0][1:], *near[1:3], labels[0]))
                sources += [after(near[run], *([] if run else near[1:3]))] + far[run][1:]
            before, last = works[-1] if works else None, call_runs is last_call
            works.append(pair_work(sources, labels, shards, cap, pick_count, before, last))
            parts = len(sources) // len(call_runs)
            for i, run in enumerate(call_runs):
                backs[run] = works[-1]["back"][i * parts : (i + 1) * parts]
        even, odd = works[-1]["shares"]
        got, share_terms, sent = dp_terms(even, odd)
        near_last, *far_last = backs[n_labels - 1]
        got_last = [partner(x, "labels", 1) for x in (after(near_last, sent), *far_last)]
        keep, first, share = sum_shares(even, got, share_terms, *got_last)
        terms = reduce_runs(backs, got_last, sent, keep, first)
        other = partner(grad_label_work(works, 2, 1, label_weight.shape), "dp", 1)
        grad_label = grad_label_work(works, 2, 0, label_weight.shape, other)
        grad_enc = join_halves(share, grad_label)
        grad_feats = add(after(terms[0], grad_enc), *terms[1:]).astype(BF16)
    else:
        shards = gather_near(gather_far(enc_weight))
        flat = owners.reshape(-1)
        onehot = (flat[:, None] == jnp.arange(n_owner, dtype=jnp.int32)[None, :]).astype(jnp.int32)
        rank = jnp.sum((jnp.cumsum(onehot, axis=0) - onehot) * onehot, axis=1)
        slot = (flat * cap + rank).reshape(row_count, pick_count)
        slot_total = n_owner * cap
        slots = jnp.arange(slot_total, dtype=jnp.int32)
        place = slots[:, None, None] == slot[None]
        pick = jnp.any(place, axis=2).astype(BF16)
        live = jnp.any(place, axis=(1, 2))
        block_of = jnp.sum(jnp.where(place, blocks[None], 0), axis=(1, 2))
        wanted = jnp.sum(jnp.where(place, positives[None], 0), axis=(1, 2))
        owner_of = jnp.where(live, slots // cap, -1)
        out = dot(pick, feats).astype(BF16).reshape(n_labels, n_data, cap, width)
        meta = jnp.stack([owner_of, block_of, wanted], axis=1).reshape(n_labels, n_data, cap, 3)
        tiles = slot_total // TILE
        got = swap(out).reshape(tiles, TILE, width)
        got_meta = swap(meta).reshape(tiles, TILE, 3).transpose(0, 2, 1)
        sources = [
            with_meta(got[i], got_meta[i, 0:1], got_meta[i, 1:2], got_meta[i, 2:3])
            for i in range(tiles)
        ]
        works = []
        for i in range(0, tiles, 4):
            before = works[-1] if works else None
            last = i + 4 >= tiles
            works.append(pair_work(sources[i : i + 4], [label_weight], shards, TILE, 1, before, last))
        back = jnp.concatenate([back for work in works for back in work["back"]], axis=0)
        back = swap(back.reshape(n_labels, n_data, cap, width)).reshape(slot_total, width)
        grad_feats = dot(pick, back, 0, 0).astype(BF16)
        even, odd = works[-1]["shares"]
        got, share_terms, _ = dp_terms(even, odd)
        *_, share = sum_shares(even, got, share_terms)
        grad_label = grad_label_work(works, 1, 0, label_weight.shape)
        grad_enc = join_halves(share, grad_label, grad_feats)

    return (grad_feats, grad_label, grad_enc)


def solution(mesh):
    rows = P(("groups", "labels", "dp"), None)
    return jax.shard_map(
        local,
        mesh=mesh,
        in_specs=(rows, P("dp", None), rows, rows, rows, rows),
        out_specs=(rows, rows, P(("groups", "dp"), None)),
        check_vma=False,
    )
```

```python
import functools

import jax
import jax.numpy as jnp
from jax import lax
from jax.experimental import pallas as pl
from jax.experimental.pallas import tpu as pltpu
from jax.sharding import PartitionSpec as P

BLK = 128
EPSILON = 1e-06
META_ROWS = 8
TILE = 128
F32 = jnp.float32
BF16 = jnp.bfloat16
VMEM = pl.BlockSpec(memory_space=pltpu.VMEM)
HBM = pl.BlockSpec(memory_space=pltpu.HBM)


def dot(a, b, da=1, db=0):
    return lax.dot_general(a, b, (((da,), (db,)), ((), ())), preferred_element_type=F32)


def shard_at(m, shard_rows):
    at = jnp.bitwise_xor(lax.axis_index("dp"), m) * shard_rows
    return pl.ds(pl.multiple_of(at, 16), shard_rows)


def pair_kernel(*refs, cap, pick_count, n_sources, n_sets, n_data, first, last):
    it = iter(refs)
    take = lambda n: [next(it) for _ in range(n)]
    sources, labels = take(n_sources), take(n_sets)
    shards = take(n_data if first else 0)
    enc, total_in = (None, None) if first else take(2)
    backs, grad_scores_ref, block_ref, embedding_ref = take(n_sources), *take(3)
    enc = next(it) if first else enc
    shares = take(2 if last else 0)
    total_ref = next(it)

    n_owner_data = lax.axis_size("dp")
    me = lax.axis_index("labels") * n_owner_data + lax.axis_index("dp")
    rows = sources[0].shape[0] - META_ROWS
    shard_rows = enc.shape[0] // n_data
    n_blocks = labels[0].shape[0] // BLK
    part = n_sources * cap
    slots = n_sets * part

    for m, shard in enumerate(shards):
        enc[shard_at(m, shard_rows), :] = shard[...]

    row_id = lax.broadcasted_iota(jnp.int32, (rows, rows), 0)
    col_id = lax.broadcasted_iota(jnp.int32, (rows, rows), 1)
    before = (row_id < col_id).astype(BF16)
    slot_id = lax.broadcasted_iota(jnp.int32, (cap, rows), 0).astype(F32)
    column = lax.broadcasted_iota(jnp.int32, (slots, BLK), 1)

    hits, codes = [], []
    for source in sources:
        meta = source[rows:, 0 : 3 * rows].astype(F32)[:pick_count]
        code = meta[:, rows : 2 * rows] * 256.0 + meta[:, 2 * rows :] + 1.0
        for j in range(n_sets):
            named = meta[:, :rows] == jnp.bitwise_xor(me, j).astype(F32)
            hits.append(jnp.sum(named.astype(F32), axis=0, keepdims=True))
            codes.append(jnp.sum(jnp.where(named, code, 0.0), axis=0, keepdims=True))
    rank = dot(jnp.concatenate(hits, axis=0).astype(BF16), before)

    picks, picked, slot_codes = [], {}, {}
    for s, source in enumerate(sources):
        pick = []
        for j in range(n_sets):
            i = s * n_sets + j
            pick.append(jnp.where((slot_id == rank[i : i + 1]) & (hits[i] > 0.0), 1.0, 0.0))
            slot_codes[j, s] = jnp.sum(pick[j] * codes[i], axis=1, keepdims=True)
        picks.append(jnp.concatenate(pick, axis=0).astype(BF16))
        found = dot(picks[s], source[:rows, :]).astype(BF16)
        for j in range(n_sets):
            picked[j, s] = found[j * cap : (j + 1) * cap]
    order = [(j, s) for j in range(n_sets) for s in range(n_sources)]
    feats = jnp.concatenate([picked[i] for i in order], axis=0)
    code = jnp.concatenate([slot_codes[i] for i in order], axis=0).astype(jnp.int32) - 1

    hidden = dot(feats, enc[...])
    inv_rms = lax.rsqrt(jnp.mean(hidden * hidden, axis=-1, keepdims=True) + EPSILON)
    embedding = (hidden * inv_rms).astype(BF16)
    embedding_ref[...] = embedding

    block = jnp.broadcast_to(code >> 8, (slots, BLK))
    block_ref[...] = block
    wanted = jnp.broadcast_to(code & 255, (slots, BLK))
    target = jnp.where(column == wanted, 1.0, 0.0)
    grad_pairs = []
    for j in range(n_sets):
        at = slice(j * part, (j + 1) * part)
        scores = dot(embedding[at], labels[j][...], 1, 1)
        mine = block[at]
        own_scores = jnp.zeros((part, BLK), F32)
        for b in range(n_blocks):
            own_scores = jnp.where(mine == b, scores[:, b * BLK : (b + 1) * BLK], own_scores)
        grad_scores = jnp.where(mine >= 0, jax.nn.sigmoid(own_scores) - target[at], 0.0)
        grad_scores_ref[at, :] = grad_scores
        spread = jnp.concatenate(
            [jnp.where(mine == b, grad_scores, 0.0).astype(BF16) for b in range(n_blocks)], axis=1
        )
        grad_pairs.append(dot(spread, labels[j][...]))
    grad_pair = jnp.concatenate(grad_pairs, axis=0).astype(BF16).astype(F32)

    projection = jnp.mean(hidden * grad_pair, axis=-1, keepdims=True)
    grad_hidden = (inv_rms * grad_pair - hidden * (inv_rms**3 * projection)).astype(BF16)
    total = dot(feats, grad_hidden, 0, 0)
    total_ref[...] = total if first else total + total_in[...]
    for m in range(n_data if last else 0):
        shares[m % 2][m // 2] = total_ref[shard_at(m, shard_rows), :].astype(BF16)

    grad_feats = dot(grad_hidden, enc[...], 1, 1).astype(BF16)
    for s in range(n_sources):
        parts = [
            grad_feats[(j * n_sources + s) * cap : (j * n_sources + s + 1) * cap]
            for j in range(n_sets)
        ]
        backs[s][...] = dot(picks[s], jnp.concatenate(parts, axis=0), 0, 0).astype(BF16)


def grad_label_kernel(*refs, calls, n_sets, j, n_more):
    grad_scores, blocks, embeddings = refs[:calls], refs[calls : 2 * calls], refs[2 * calls : 3 * calls]
    more, rest = refs[3 * calls : 3 * calls + n_more], refs[3 * calls + n_more :]
    out_ref, (result, *sem) = rest[0], rest[-2:] if len(rest) > 1 else rest
    rows_of = [slice(j * r.shape[0] // n_sets, (j + 1) * r.shape[0] // n_sets) for r in blocks]
    grad_scores_t = jnp.concatenate([r[at, :].T for r, at in zip(grad_scores, rows_of)], axis=1)
    block_t = jnp.concatenate([r[at, :].T for r, at in zip(blocks, rows_of)], axis=1)
    embedding = jnp.concatenate([r[at, :] for r, at in zip(embeddings, rows_of)], axis=0)
    copies = []
    for b in range(out_ref.shape[0] // BLK):
        rows = pl.ds(b * BLK, BLK)
        spread_t = jnp.where(block_t == b, grad_scores_t, 0.0).astype(BF16)
        total = dot(spread_t, embedding)
        for ref in more:
            total = total + ref[rows, :].astype(F32)
        result[rows, :] = total.astype(BF16)
        if sem:
            copies.append(pltpu.make_async_copy(result.at[rows], out_ref.at[rows], sem[0].at[b]))
            copies[b].start()
    for copy in copies:
        copy.wait()


def own_block_kernel(feats_ref, owners_ref, blocks_ref, positives_ref, out_ref, ints, sem):
    rows, width = feats_ref.shape
    feats = pltpu.make_async_copy(feats_ref, out_ref.at[pl.ds(0, rows)], sem.at[0])
    feats.start()
    copies = []
    for i, ref in enumerate((owners_ref, blocks_ref, positives_ref)):
        copies.append(pltpu.make_async_copy(ref, ints.at[i], sem.at[i + 1]))
        copies[i].start()
    for copy in copies:
        copy.wait()
    meta = [ints[i].astype(F32) for i in range(3)]
    meta += [jnp.zeros((meta[0].shape[0], width - 3 * rows), F32)]
    meta = jnp.concatenate(meta, axis=1)
    rest = jnp.zeros((META_ROWS - meta.shape[0], width), F32)
    out_ref[rows:, :] = jnp.concatenate([meta, rest], axis=0).astype(BF16)
    feats.wait()


def load_kernel(label_ref, shard_ref, label_out, shard_out):
    label_out[...] = label_ref[...]
    shard_out[...] = shard_ref[...]


def half_at(mine, half):
    odd = jnp.bitwise_and(lax.axis_index("labels"), 1)
    return pl.ds(pl.multiple_of((odd if mine else 1 - odd) * half, 16), half)


def split_kernel(even_ref, got_ref, *refs):
    *more, keep_ref, send_ref, total = refs
    share = even_ref[0].astype(F32) + got_ref[0].astype(F32)
    for ref in more:
        share = share + ref[...].astype(F32)
    total[...] = share
    half = keep_ref.shape[0]
    keep_ref[...] = total[half_at(True, half), :]
    send_ref[...] = total[half_at(False, half), :].astype(BF16)


def merge_kernel(mine_ref, other_ref, out_ref):
    half = mine_ref.shape[0]
    out_ref[half_at(True, half), :] = mine_ref[...].astype(F32)
    out_ref[half_at(False, half), :] = other_ref[...].astype(F32)


def call(kernel, name, out_shape, scratch, flops, megabytes, *args, space=VMEM, out_space=VMEM, limit=24):
    return pl.pallas_call(
        kernel,
        in_specs=[space] * len(args),
        out_specs=jax.tree.map(lambda _: out_space, out_shape),
        out_shape=out_shape,
        scratch_shapes=scratch,
        compiler_params=pltpu.CompilerParams(vmem_limit_bytes=limit << 20),
        cost_estimate=pl.CostEstimate(
            flops=flops, bytes_accessed=megabytes << 20, transcendentals=0
        ),
        name=name,
    )(*args)


def shaped(shape, dtype=BF16):
    return jax.ShapeDtypeStruct(shape, dtype)


def pair_work(sources, labels, shards, cap, pick_count, before, last):
    n_data, n_sets = len(shards), len(labels)
    block_rows, width = sources[0].shape
    rows = block_rows - META_ROWS
    slots = n_sets * len(sources) * cap
    shard_rows = shards[0].shape[0]
    full = (n_data * shard_rows, width)
    backs = len(sources)
    shapes = [shaped((rows, width))] * backs
    shapes += [shaped((slots, BLK), F32), shaped((slots, BLK), jnp.int32), shaped((slots, width))]
    more = [before["enc"], before["total"]] if before else shards
    scratch = []
    if not before:
        shapes += [shaped(full)]
    if last:
        shapes += [shaped((n_data // 2, shard_rows, width))] * 2
        scratch = [pltpu.VMEM(full, F32)]
    else:
        shapes += [shaped(full, F32)]
    out = call(
        functools.partial(
            pair_kernel,
            cap=cap,
            pick_count=pick_count,
            n_sources=len(sources),
            n_sets=n_sets,
            n_data=n_data,
            first=not before,
            last=last,
        ),
        "pair_work",
        shapes,
        scratch,
        2 * slots * width * (2 * labels[0].shape[0] + 3 * width + 2 * rows),
        8,
        *sources,
        *labels,
        *more,
    )
    result = {"back": list(out[:backs]), "slots": list(out[backs : backs + 3])}
    rest = list(out[backs + 3 :])
    result["enc"] = before["enc"] if before else rest.pop(0)
    result["shares" if last else "total"] = rest if last else rest[0]
    return result


def grad_label_work(works, n_sets, j, labels_shape, *more):
    slots = list(zip(*(work["slots"] for work in works)))
    scratch = []
    if j == 0:
        sem = pltpu.SemaphoreType.DMA((labels_shape[0] // BLK,))
        scratch = [pltpu.VMEM(labels_shape, BF16), sem]
    return call(
        functools.partial(
            grad_label_kernel, calls=len(works), n_sets=n_sets, j=j, n_more=len(more)
        ),
        "grad_label_work",
        shaped(labels_shape),
        scratch,
        2 * sum(x.shape[0] for x in slots[0]) // n_sets * labels_shape[0] * labels_shape[1],
        4,
        *slots[0],
        *slots[1],
        *slots[2],
        *more,
        out_space=pl.BlockSpec(memory_space=pl.ANY) if scratch else VMEM,
    )


def swap(x):
    x = lax.all_to_all(x, "labels", split_axis=0, concat_axis=0, tiled=True)
    return lax.all_to_all(x, "dp", split_axis=1, concat_axis=1, tiled=True)


def partner(x, axis, mask):
    return lax.ppermute(x, axis, [(i, i ^ mask) for i in range(lax.axis_size(axis))])


def masks(n):
    return [1 << i for i in range(n.bit_length() - 1)]


def after(x, *others):
    return lax.optimization_barrier((x, *others))[0]


def gather_far(x):
    got = {0: x}
    for mask in reversed(masks(lax.axis_size("dp"))[1:]):
        got.update({m | mask: partner(v, "dp", mask) for m, v in list(got.items())})
    return [got[m] for m in sorted(got)]


def gather_near(far, *first):
    near = [partner(after(v, *far[1:], *first), "dp", 1) for v in far]
    return [v for pair in zip(far, near) for v in pair]


def gather_labels(x, first):
    got = {0: x}
    for mask in reversed(masks(lax.axis_size("labels"))):
        for m, v in list(got.items()):
            got[m | mask] = partner(after(v, first) if m else v, "labels", mask)
    return [got[m] for m in range(len(got))]


def add(*terms):
    return sum(t.astype(F32) for t in terms)


def dp_terms(even, odd):
    got = sent = partner(odd, "dp", 1)
    terms = [[even[i], got[i]] for i in range(even.shape[0])]
    for mask in masks(len(terms)):
        for i in range(len(terms)):
            if i & mask == 0 and i % mask == 0:
                sent = add(*terms[i | mask]).astype(BF16)
                terms[i].append(partner(sent, "dp", 2 * mask))
    return got, terms[0], sent


def sum_shares(even, got, terms, *first):
    rows, width = even.shape[1:]
    half = rows // 2
    keep, send = call(
        split_kernel,
        "split_share",
        [shaped((half, width), F32), shaped((half, width))],
        [pltpu.VMEM((rows, width), F32)],
        0,
        1,
        even,
        after(got, *first),
        *terms[2:],
    )
    x = add(keep, partner(send, "labels", 1)).astype(BF16)
    first = x
    for mask in masks(lax.axis_size("labels"))[1:]:
        x = add(x, partner(x, "labels", mask)).astype(BF16)
    return keep, first, x


def join_halves(x, *first):
    other = partner(x, "labels", 1)
    out = shaped((2 * x.shape[0], x.shape[1]), F32)
    return call(merge_kernel, "merge_share", out, [], 0, 1, after(x, *first), other)


def reduce_runs(runs, got_last, ahead, keep, first):
    def over_dp(parts, *hold):
        parts = [list(part) for part in parts]
        for mask in masks(len(parts)):
            for h in range(0, len(parts), 2 * mask):
                sent = after(add(*parts[h + mask]).astype(BF16), *hold)
                parts[h].append(partner(sent, "dp", 2 * mask))
        return parts[0]

    n = len(runs)
    sums, sent_near = {n - 2: over_dp(list(zip(runs[n - 2], got_last)), ahead)}, []
    for i in reversed(range(0, n - 2, 2)):
        odd = over_dp([[x] for x in runs[i + 1]], keep)
        sent_near.append(odd[-1])
        got = partner(add(*odd).astype(BF16), "labels", 1)
        sums[i] = over_dp([[x] for x in runs[i]], odd[-1]) + [got]
    for mask in masks(n)[1:]:
        for i in range(0, n, 2 * mask):
            sent = after(add(*sums[i + mask]).astype(BF16), first, *sent_near)
            sums[i].append(partner(sent, "labels", mask))
    return sums[0]


def with_meta(feats, owner_rows, block_rows, positive_rows):
    meta = jnp.concatenate([owner_rows, block_rows, positive_rows], axis=1).astype(BF16)
    meta = jnp.pad(meta, ((0, META_ROWS - meta.shape[0]), (0, feats.shape[1] - meta.shape[1])))
    return jnp.concatenate([feats, meta], axis=0)


def local(feats, enc_weight, label_weight, owners, blocks, positives):
    n_labels = lax.axis_size("labels")
    n_data = lax.axis_size("dp")
    n_owner = n_labels * n_data
    row_count, width = feats.shape
    pick_count = owners.shape[1]
    cap = max(2, 2 * row_count * pick_count // n_owner)

    if row_count <= n_data * cap:
        own = call(
            own_block_kernel,
            "own_block",
            shaped((row_count + META_ROWS, width)),
            [
                pltpu.VMEM((3, pick_count, row_count), jnp.int32),
                pltpu.SemaphoreType.DMA((4,)),
            ],
            0,
            1,
            feats,
            owners.T,
            blocks.T,
            positives.T,
            space=HBM,
            limit=60,
        )
        labels = [label_weight, partner(label_weight, "dp", 1)]
        labels[0], own_shard = call(
            load_kernel,
            "load",
            [shaped(label_weight.shape), shaped(enc_weight.shape)],
            [],
            0,
            4,
            after(label_weight, labels[1]),
            enc_weight,
        )
        near = gather_labels(own, labels[0])
        far = {0: gather_far(own)}
        shards = gather_near(gather_far(enc_weight))
        shards[0] = own_shard
        works, backs = [], {}
        last_call = list(range(1, n_labels, 2))
        for call_runs in (list(range(0, n_labels, 2)), last_call):
            sources = []
            for run in call_runs:
                if run == n_labels - 1:
                    far[run] = gather_far(after(near[run], *far[run - 1][1:]))
                elif run % 2:
                    sent = [after(x, *shards[1:]) for x in far[run - 1][1:]]
                    far[run] = near[run : run + 1] + [partner(x, "labels", 1) for x in sent]
                elif run:
                    far[run] = gather_far(after(near[run], *far[0][1:], *near[1:3], labels[0]))
                sources += [after(near[run], *([] if run else near[1:3]))] + far[run][1:]
            before, last = works[-1] if works else None, call_runs is last_call
            works.append(pair_work(sources, labels, shards, cap, pick_count, before, last))
            parts = len(sources) // len(call_runs)
            for i, run in enumerate(call_runs):
                backs[run] = works[-1]["back"][i * parts : (i + 1) * parts]
        even, odd = works[-1]["shares"]
        got, share_terms, sent = dp_terms(even, odd)
        near_last, *far_last = backs[n_labels - 1]
        got_last = [partner(x, "labels", 1) for x in (after(near_last, sent), *far_last)]
        keep, first, share = sum_shares(even, got, share_terms, *got_last)
        terms = reduce_runs(backs, got_last, sent, keep, first)
        other = partner(grad_label_work(works, 2, 1, label_weight.shape), "dp", 1)
        grad_label = grad_label_work(works, 2, 0, label_weight.shape, other)
        grad_enc = join_halves(share, grad_label)
        grad_feats = add(after(terms[0], grad_enc), *terms[1:]).astype(BF16)
    else:
        shards = gather_near(gather_far(enc_weight))
        flat = owners.reshape(-1)
        onehot = (flat[:, None] == jnp.arange(n_owner, dtype=jnp.int32)[None, :]).astype(jnp.int32)
        rank = jnp.sum((jnp.cumsum(onehot, axis=0) - onehot) * onehot, axis=1)
        slot = (flat * cap + rank).reshape(row_count, pick_count)
        slot_total = n_owner * cap
        slots = jnp.arange(slot_total, dtype=jnp.int32)
        place = slots[:, None, None] == slot[None]
        pick = jnp.any(place, axis=2).astype(BF16)
        live = jnp.any(place, axis=(1, 2))
        block_of = jnp.sum(jnp.where(place, blocks[None], 0), axis=(1, 2))
        wanted = jnp.sum(jnp.where(place, positives[None], 0), axis=(1, 2))
        owner_of = jnp.where(live, slots // cap, -1)
        out = dot(pick, feats).astype(BF16).reshape(n_labels, n_data, cap, width)
        meta = jnp.stack([owner_of, block_of, wanted], axis=1).reshape(n_labels, n_data, cap, 3)
        tiles = slot_total // TILE
        got = swap(out).reshape(tiles, TILE, width)
        got_meta = swap(meta).reshape(tiles, TILE, 3).transpose(0, 2, 1)
        sources = [
            with_meta(got[i], got_meta[i, 0:1], got_meta[i, 1:2], got_meta[i, 2:3])
            for i in range(tiles)
        ]
        works = []
        for i in range(0, tiles, 4):
            before = works[-1] if works else None
            last = i + 4 >= tiles
            works.append(pair_work(sources[i : i + 4], [label_weight], shards, TILE, 1, before, last))
        back = jnp.concatenate([back for work in works for back in work["back"]], axis=0)
        back = swap(back.reshape(n_labels, n_data, cap, width)).reshape(slot_total, width)
        grad_feats = dot(pick, back, 0, 0).astype(BF16)
        even, odd = works[-1]["shares"]
        got, share_terms, _ = dp_terms(even, odd)
        *_, share = sum_shares(even, got, share_terms)
        grad_label = grad_label_work(works, 1, 0, label_weight.shape)
        grad_enc = join_halves(share, grad_label, grad_feats)

    return (grad_feats, grad_label, grad_enc)


def solution(mesh):
    rows = P(("groups", "labels", "dp"), None)
    return jax.shard_map(
        local,
        mesh=mesh,
        in_specs=(rows, P("dp", None), rows, rows, rows, rows),
        out_specs=(rows, rows, P(("groups", "dp"), None)),
        check_vma=False,
    )
```

```python
import functools

import jax
import jax.numpy as jnp
from jax import lax
from jax.experimental import pallas as pl
from jax.experimental.pallas import tpu as pltpu
from jax.sharding import PartitionSpec as P

BLK = 128
EPSILON = 1e-06
META_ROWS = 8
TILE = 128
F32 = jnp.float32
BF16 = jnp.bfloat16
VMEM = pl.BlockSpec(memory_space=pltpu.VMEM)
HBM = pl.BlockSpec(memory_space=pltpu.HBM)


def dot(a, b, da=1, db=0):
    return lax.dot_general(a, b, (((da,), (db,)), ((), ())), preferred_element_type=F32)


def shard_at(m, shard_rows):
    at = jnp.bitwise_xor(lax.axis_index("dp"), m) * shard_rows
    return pl.ds(pl.multiple_of(at, 16), shard_rows)


def pair_kernel(*refs, cap, pick_count, n_sources, n_sets, n_data, first, last):
    it = iter(refs)
    take = lambda n: [next(it) for _ in range(n)]
    sources, labels = take(n_sources), take(n_sets)
    shards = take(n_data if first else 0)
    enc, total_in = (None, None) if first else take(2)
    backs, grad_scores_ref, block_ref, embedding_ref = take(n_sources), *take(3)
    grad_hidden_ref = next(it) if last else None
    enc = next(it) if first else enc
    shares = take(2 if last else 0)
    total_ref = next(it)

    n_owner_data = lax.axis_size("dp")
    me = lax.axis_index("labels") * n_owner_data + lax.axis_index("dp")
    rows = sources[0].shape[0] - META_ROWS
    shard_rows = enc.shape[0] // n_data
    n_blocks = labels[0].shape[0] // BLK
    part = n_sources * cap
    slots = n_sets * part

    for m, shard in enumerate(shards):
        enc[shard_at(m, shard_rows), :] = shard[...]

    row_id = lax.broadcasted_iota(jnp.int32, (rows, rows), 0)
    col_id = lax.broadcasted_iota(jnp.int32, (rows, rows), 1)
    before = (row_id < col_id).astype(BF16)
    slot_id = lax.broadcasted_iota(jnp.int32, (cap, rows), 0).astype(F32)
    column = lax.broadcasted_iota(jnp.int32, (slots, BLK), 1)

    hits, codes = [], []
    for source in sources:
        meta = source[rows:, 0 : 3 * rows].astype(F32)[:pick_count]
        code = meta[:, rows : 2 * rows] * 256.0 + meta[:, 2 * rows :] + 1.0
        for j in range(n_sets):
            named = meta[:, :rows] == jnp.bitwise_xor(me, j).astype(F32)
            hits.append(jnp.sum(named.astype(F32), axis=0, keepdims=True))
            codes.append(jnp.sum(jnp.where(named, code, 0.0), axis=0, keepdims=True))
    rank = dot(jnp.concatenate(hits, axis=0).astype(BF16), before)

    picks, picked, slot_codes = [], {}, {}
    for s, source in enumerate(sources):
        pick = []
        for j in range(n_sets):
            i = s * n_sets + j
            pick.append(jnp.where((slot_id == rank[i : i + 1]) & (hits[i] > 0.0), 1.0, 0.0))
            slot_codes[j, s] = jnp.sum(pick[j] * codes[i], axis=1, keepdims=True)
        picks.append(jnp.concatenate(pick, axis=0).astype(BF16))
        found = dot(picks[s], source[:rows, :]).astype(BF16)
        for j in range(n_sets):
            picked[j, s] = found[j * cap : (j + 1) * cap]
    order = [(j, s) for j in range(n_sets) for s in range(n_sources)]
    feats = jnp.concatenate([picked[i] for i in order], axis=0)
    code = jnp.concatenate([slot_codes[i] for i in order], axis=0).astype(jnp.int32) - 1

    hidden = dot(feats, enc[...])
    inv_rms = lax.rsqrt(jnp.mean(hidden * hidden, axis=-1, keepdims=True) + EPSILON)
    embedding = (hidden * inv_rms).astype(BF16)
    embedding_ref[...] = embedding

    block = jnp.broadcast_to(code >> 8, (slots, BLK))
    block_ref[...] = block
    wanted = jnp.broadcast_to(code & 255, (slots, BLK))
    target = jnp.where(column == wanted, 1.0, 0.0)
    grad_pairs = []
    for j in range(n_sets):
        at = slice(j * part, (j + 1) * part)
        scores = dot(embedding[at], labels[j][...], 1, 1)
        mine = block[at]
        own_scores = jnp.zeros((part, BLK), F32)
        for b in range(n_blocks):
            own_scores = jnp.where(mine == b, scores[:, b * BLK : (b + 1) * BLK], own_scores)
        grad_scores = jnp.where(mine >= 0, jax.nn.sigmoid(own_scores) - target[at], 0.0)
        grad_scores_ref[at, :] = grad_scores
        spread = jnp.concatenate(
            [jnp.where(mine == b, grad_scores, 0.0).astype(BF16) for b in range(n_blocks)], axis=1
        )
        grad_pairs.append(dot(spread, labels[j][...]))
    grad_pair = jnp.concatenate(grad_pairs, axis=0).astype(BF16).astype(F32)

    projection = jnp.mean(hidden * grad_pair, axis=-1, keepdims=True)
    grad_hidden = (inv_rms * grad_pair - hidden * (inv_rms**3 * projection)).astype(BF16)
    total = dot(feats, grad_hidden, 0, 0)
    total_ref[...] = total if first else total + total_in[...]
    for m in range(n_data if last else 0):
        shares[m % 2][m // 2] = total_ref[shard_at(m, shard_rows), :].astype(BF16)

    if last:
        grad_hidden_ref[...] = grad_hidden
        for pick, ref in zip(picks, backs):
            ref[...] = pick
        return
    for ref, back in zip(backs, back_rows(picks, grad_hidden, enc[...], cap, n_sets)):
        ref[...] = back


def back_rows(picks, grad_hidden, enc, cap, n_sets):
    grad_feats = dot(grad_hidden, enc, 1, 1).astype(BF16)
    for s, pick in enumerate(picks):
        parts = []
        for j in range(n_sets):
            at = (j * len(picks) + s) * cap
            parts.append(grad_feats[at : at + cap])
        yield dot(pick, jnp.concatenate(parts, axis=0), 0, 0).astype(BF16)


def back_kernel(*refs, cap, n_sets):
    sources = (len(refs) - 2) // 2
    picks = [r[...] for r in refs[:sources]]
    grad_hidden, enc = refs[sources][...], refs[sources + 1][...]
    backs = back_rows(picks, grad_hidden, enc, cap, n_sets)
    for ref, back in zip(refs[sources + 2 :], backs):
        ref[...] = back


def grad_label_kernel(*refs, calls, n_sets, j, n_more):
    grad_scores, blocks, embeddings = refs[:calls], refs[calls : 2 * calls], refs[2 * calls : 3 * calls]
    more, rest = refs[3 * calls : 3 * calls + n_more], refs[3 * calls + n_more :]
    out_ref, (result, *sem) = rest[0], rest[-2:] if len(rest) > 1 else rest
    rows_of = [slice(j * r.shape[0] // n_sets, (j + 1) * r.shape[0] // n_sets) for r in blocks]
    grad_scores_t = jnp.concatenate([r[at, :].T for r, at in zip(grad_scores, rows_of)], axis=1)
    block_t = jnp.concatenate([r[at, :].T for r, at in zip(blocks, rows_of)], axis=1)
    embedding = jnp.concatenate([r[at, :] for r, at in zip(embeddings, rows_of)], axis=0)
    copies = []
    for b in range(out_ref.shape[0] // BLK):
        rows = pl.ds(b * BLK, BLK)
        spread_t = jnp.where(block_t == b, grad_scores_t, 0.0).astype(BF16)
        total = dot(spread_t, embedding)
        for ref in more:
            total = total + ref[rows, :].astype(F32)
        result[rows, :] = total.astype(BF16)
        if sem:
            copies.append(pltpu.make_async_copy(result.at[rows], out_ref.at[rows], sem[0].at[b]))
            copies[b].start()
    for copy in copies:
        copy.wait()


def own_block_kernel(feats_ref, owners_ref, blocks_ref, positives_ref, out_ref, ints, sem):
    rows, width = feats_ref.shape
    feats = pltpu.make_async_copy(feats_ref, out_ref.at[pl.ds(0, rows)], sem.at[0])
    feats.start()
    copies = []
    for i, ref in enumerate((owners_ref, blocks_ref, positives_ref)):
        copies.append(pltpu.make_async_copy(ref, ints.at[i], sem.at[i + 1]))
        copies[i].start()
    for copy in copies:
        copy.wait()
    meta = [ints[i].astype(F32) for i in range(3)]
    meta += [jnp.zeros((meta[0].shape[0], width - 3 * rows), F32)]
    meta = jnp.concatenate(meta, axis=1)
    rest = jnp.zeros((META_ROWS - meta.shape[0], width), F32)
    out_ref[rows:, :] = jnp.concatenate([meta, rest], axis=0).astype(BF16)
    feats.wait()


def load_kernel(label_ref, shard_ref, label_out, shard_out):
    label_out[...] = label_ref[...]
    shard_out[...] = shard_ref[...]


def half_at(mine, half):
    odd = jnp.bitwise_and(lax.axis_index("labels"), 1)
    return pl.ds(pl.multiple_of((odd if mine else 1 - odd) * half, 16), half)


def split_kernel(even_ref, got_ref, *refs):
    *more, keep_ref, send_ref, total = refs
    share = even_ref[0].astype(F32) + got_ref[0].astype(F32)
    for ref in more:
        share = share + ref[...].astype(F32)
    total[...] = share
    half = keep_ref.shape[0]
    keep_ref[...] = total[half_at(True, half), :]
    send_ref[...] = total[half_at(False, half), :].astype(BF16)


def merge_kernel(mine_ref, other_ref, out_ref):
    half = mine_ref.shape[0]
    out_ref[half_at(True, half), :] = mine_ref[...].astype(F32)
    out_ref[half_at(False, half), :] = other_ref[...].astype(F32)


def call(kernel, name, out_shape, scratch, flops, megabytes, *args, space=VMEM, out_space=VMEM, limit=24):
    return pl.pallas_call(
        kernel,
        in_specs=[space] * len(args),
        out_specs=jax.tree.map(lambda _: out_space, out_shape),
        out_shape=out_shape,
        scratch_shapes=scratch,
        compiler_params=pltpu.CompilerParams(vmem_limit_bytes=limit << 20),
        cost_estimate=pl.CostEstimate(
            flops=flops, bytes_accessed=megabytes << 20, transcendentals=0
        ),
        name=name,
    )(*args)


def shaped(shape, dtype=BF16):
    return jax.ShapeDtypeStruct(shape, dtype)


def pair_work(sources, labels, shards, cap, pick_count, before, last):
    n_data, n_sets = len(shards), len(labels)
    block_rows, width = sources[0].shape
    rows = block_rows - META_ROWS
    slots = n_sets * len(sources) * cap
    shard_rows = shards[0].shape[0]
    full = (n_data * shard_rows, width)
    backs = len(sources)
    shapes = [shaped((n_sets * cap, rows) if last else (rows, width))] * backs
    shapes += [shaped((slots, BLK), F32), shaped((slots, BLK), jnp.int32), shaped((slots, width))]
    if last:
        shapes += [shaped((slots, width))]
    more = [before["enc"], before["total"]] if before else shards
    scratch = []
    if not before:
        shapes += [shaped(full)]
    if last:
        shapes += [shaped((n_data // 2, shard_rows, width))] * 2
        scratch = [pltpu.VMEM(full, F32)]
    else:
        shapes += [shaped(full, F32)]
    out = call(
        functools.partial(
            pair_kernel,
            cap=cap,
            pick_count=pick_count,
            n_sources=len(sources),
            n_sets=n_sets,
            n_data=n_data,
            first=not before,
            last=last,
        ),
        "pair_work",
        shapes,
        scratch,
        2 * slots * width * (2 * labels[0].shape[0] + 3 * width + 2 * rows),
        8,
        *sources,
        *labels,
        *more,
    )
    result = {"back": list(out[:backs]), "slots": list(out[backs : backs + 3])}
    rest = list(out[backs + 3 :])
    grad_hidden = rest.pop(0) if last else None
    result["enc"] = before["enc"] if before else rest.pop(0)
    result["shares" if last else "total"] = rest if last else rest[0]
    if last:
        result["back"] = call(
            functools.partial(back_kernel, cap=cap, n_sets=n_sets),
            "back_work",
            [shaped((rows, width))] * backs,
            [],
            2 * slots * width * (width + rows),
            3,
            *result["back"],
            grad_hidden,
            result["enc"],
        )
    return result


def grad_label_work(works, n_sets, j, labels_shape, *more):
    slots = list(zip(*(work["slots"] for work in works)))
    scratch = []
    if j == 0:
        sem = pltpu.SemaphoreType.DMA((labels_shape[0] // BLK,))
        scratch = [pltpu.VMEM(labels_shape, BF16), sem]
    return call(
        functools.partial(
            grad_label_kernel, calls=len(works), n_sets=n_sets, j=j, n_more=len(more)
        ),
        "grad_label_work",
        shaped(labels_shape),
        scratch,
        2 * sum(x.shape[0] for x in slots[0]) // n_sets * labels_shape[0] * labels_shape[1],
        4,
        *slots[0],
        *slots[1],
        *slots[2],
        *more,
        out_space=pl.BlockSpec(memory_space=pl.ANY) if scratch else VMEM,
    )


def swap(x):
    x = lax.all_to_all(x, "labels", split_axis=0, concat_axis=0, tiled=True)
    return lax.all_to_all(x, "dp", split_axis=1, concat_axis=1, tiled=True)


def partner(x, axis, mask):
    return lax.ppermute(x, axis, [(i, i ^ mask) for i in range(lax.axis_size(axis))])


def masks(n):
    return [1 << i for i in range(n.bit_length() - 1)]


def after(x, *others):
    return lax.optimization_barrier((x, *others))[0]


def gather_far(x):
    got = {0: x}
    for mask in reversed(masks(lax.axis_size("dp"))[1:]):
        got.update({m | mask: partner(v, "dp", mask) for m, v in list(got.items())})
    return [got[m] for m in sorted(got)]


def gather_near(far, *first):
    near = [partner(after(v, *far[1:], *first), "dp", 1) for v in far]
    return [v for pair in zip(far, near) for v in pair]


def gather_labels(x, first):
    got = {0: x}
    for mask in reversed(masks(lax.axis_size("labels"))):
        for m, v in list(got.items()):
            got[m | mask] = partner(after(v, first) if m else v, "labels", mask)
    return [got[m] for m in range(len(got))]


def add(*terms):
    return sum(t.astype(F32) for t in terms)


def dp_terms(even, odd):
    got = sent = partner(odd, "dp", 1)
    terms = [[even[i], got[i]] for i in range(even.shape[0])]
    for mask in masks(len(terms)):
        for i in range(len(terms)):
            if i & mask == 0 and i % mask == 0:
                sent = add(*terms[i | mask]).astype(BF16)
                terms[i].append(partner(sent, "dp", 2 * mask))
    return got, terms[0], sent


def sum_shares(even, got, terms, *first):
    rows, width = even.shape[1:]
    half = rows // 2
    keep, send = call(
        split_kernel,
        "split_share",
        [shaped((half, width), F32), shaped((half, width))],
        [pltpu.VMEM((rows, width), F32)],
        0,
        1,
        even,
        after(got, *first),
        *terms[2:],
    )
    x = add(keep, partner(send, "labels", 1)).astype(BF16)
    first = x
    for mask in masks(lax.axis_size("labels"))[1:]:
        x = add(x, partner(x, "labels", mask)).astype(BF16)
    return keep, first, x


def join_halves(x, *first):
    other = partner(x, "labels", 1)
    out = shaped((2 * x.shape[0], x.shape[1]), F32)
    return call(merge_kernel, "merge_share", out, [], 0, 1, after(x, *first), other)


def reduce_runs(runs, got_last, ahead, keep, first):
    def over_dp(parts, *hold):
        parts = [list(part) for part in parts]
        for mask in masks(len(parts)):
            for h in range(0, len(parts), 2 * mask):
                sent = after(add(*parts[h + mask]).astype(BF16), *hold)
                parts[h].append(partner(sent, "dp", 2 * mask))
        return parts[0]

    n = len(runs)
    sums, sent_near = {n - 2: over_dp(list(zip(runs[n - 2], got_last)), ahead)}, []
    for i in reversed(range(0, n - 2, 2)):
        near = add(*over_dp([[x] for x in runs[i + 1]], ahead)).astype(BF16)
        sent_near.append(partner(near, "labels", 1))
        sums[i] = over_dp([[x] for x in runs[i]], keep) + sent_near[-1:]
    for mask in masks(n)[1:]:
        for i in range(0, n, 2 * mask):
            sent = after(add(*sums[i + mask]).astype(BF16), first, *sent_near)
            sums[i].append(partner(sent, "labels", mask))
    return sums[0]


def with_meta(feats, owner_rows, block_rows, positive_rows):
    meta = jnp.concatenate([owner_rows, block_rows, positive_rows], axis=1).astype(BF16)
    meta = jnp.pad(meta, ((0, META_ROWS - meta.shape[0]), (0, feats.shape[1] - meta.shape[1])))
    return jnp.concatenate([feats, meta], axis=0)


def local(feats, enc_weight, label_weight, owners, blocks, positives):
    n_labels = lax.axis_size("labels")
    n_data = lax.axis_size("dp")
    n_owner = n_labels * n_data
    row_count, width = feats.shape
    pick_count = owners.shape[1]
    cap = max(2, 2 * row_count * pick_count // n_owner)

    if row_count <= n_data * cap:
        own = call(
            own_block_kernel,
            "own_block",
            shaped((row_count + META_ROWS, width)),
            [
                pltpu.VMEM((3, pick_count, row_count), jnp.int32),
                pltpu.SemaphoreType.DMA((4,)),
            ],
            0,
            1,
            feats,
            owners.T,
            blocks.T,
            positives.T,
            space=HBM,
            limit=60,
        )
        labels = [label_weight, partner(label_weight, "dp", 1)]
        labels[0], own_shard = call(
            load_kernel,
            "load",
            [shaped(label_weight.shape), shaped(enc_weight.shape)],
            [],
            0,
            4,
            after(label_weight, labels[1]),
            enc_weight,
        )
        near = gather_labels(own, labels[0])
        far = {0: gather_far(own)}
        shards = gather_near(gather_far(enc_weight))
        shards[0] = own_shard
        works, backs = [], {}
        last_call = list(range(1, n_labels, 2))
        for call_runs in (list(range(0, n_labels, 2)), last_call):
            sources = []
            for run in call_runs:
                if run == n_labels - 1:
                    far[run] = gather_far(after(near[run], *far[run - 1][1:]))
                elif run % 2:
                    sent = [after(x, *shards[1:]) for x in far[run - 1][1:]]
                    far[run] = near[run : run + 1] + [partner(x, "labels", 1) for x in sent]
                elif run:
                    far[run] = gather_far(after(near[run], *far[0][1:], *near[1:3], labels[0]))
                sources += [after(near[run], *([] if run else near[1:3]))] + far[run][1:]
            before, last = works[-1] if works else None, call_runs is last_call
            works.append(pair_work(sources, labels, shards, cap, pick_count, before, last))
            parts = len(sources) // len(call_runs)
            for i, run in enumerate(call_runs):
                backs[run] = works[-1]["back"][i * parts : (i + 1) * parts]
        even, odd = works[-1]["shares"]
        got, share_terms, sent = dp_terms(even, odd)
        near_last, *far_last = backs[n_labels - 1]
        got_last = [partner(x, "labels", 1) for x in (after(near_last, sent), *far_last)]
        keep, first, share = sum_shares(even, got, share_terms, *got_last)
        terms = reduce_runs(backs, got_last, sent, keep, first)
        other = partner(grad_label_work(works, 2, 1, label_weight.shape), "dp", 1)
        grad_label = grad_label_work(works, 2, 0, label_weight.shape, other)
        grad_enc = join_halves(share, grad_label)
        grad_feats = add(after(terms[0], grad_enc), *terms[1:]).astype(BF16)
    else:
        shards = gather_near(gather_far(enc_weight))
        flat = owners.reshape(-1)
        onehot = (flat[:, None] == jnp.arange(n_owner, dtype=jnp.int32)[None, :]).astype(jnp.int32)
        rank = jnp.sum((jnp.cumsum(onehot, axis=0) - onehot) * onehot, axis=1)
        slot = (flat * cap + rank).reshape(row_count, pick_count)
        slot_total = n_owner * cap
        slots = jnp.arange(slot_total, dtype=jnp.int32)
        place = slots[:, None, None] == slot[None]
        pick = jnp.any(place, axis=2).astype(BF16)
        live = jnp.any(place, axis=(1, 2))
        block_of = jnp.sum(jnp.where(place, blocks[None], 0), axis=(1, 2))
        wanted = jnp.sum(jnp.where(place, positives[None], 0), axis=(1, 2))
        owner_of = jnp.where(live, slots // cap, -1)
        out = dot(pick, feats).astype(BF16).reshape(n_labels, n_data, cap, width)
        meta = jnp.stack([owner_of, block_of, wanted], axis=1).reshape(n_labels, n_data, cap, 3)
        tiles = slot_total // TILE
        got = swap(out).reshape(tiles, TILE, width)
        got_meta = swap(meta).reshape(tiles, TILE, 3).transpose(0, 2, 1)
        sources = [
            with_meta(got[i], got_meta[i, 0:1], got_meta[i, 1:2], got_meta[i, 2:3])
            for i in range(tiles)
        ]
        works = []
        for i in range(0, tiles, 4):
            before = works[-1] if works else None
            last = i + 4 >= tiles
            works.append(pair_work(sources[i : i + 4], [label_weight], shards, TILE, 1, before, last))
        back = jnp.concatenate([back for work in works for back in work["back"]], axis=0)
        back = swap(back.reshape(n_labels, n_data, cap, width)).reshape(slot_total, width)
        grad_feats = dot(pick, back, 0, 0).astype(BF16)
        even, odd = works[-1]["shares"]
        got, share_terms, _ = dp_terms(even, odd)
        *_, share = sum_shares(even, got, share_terms)
        grad_label = grad_label_work(works, 1, 0, label_weight.shape)
        grad_enc = join_halves(share, grad_label, grad_feats)

    return (grad_feats, grad_label, grad_enc)


def solution(mesh):
    rows = P(("groups", "labels", "dp"), None)
    return jax.shard_map(
        local,
        mesh=mesh,
        in_specs=(rows, P("dp", None), rows, rows, rows, rows),
        out_specs=(rows, rows, P(("groups", "dp"), None)),
        check_vma=False,
    )
```

```python
import functools

import jax
import jax.numpy as jnp
from jax import lax
from jax.experimental import pallas as pl
from jax.experimental.pallas import tpu as pltpu
from jax.sharding import PartitionSpec as P

BLK = 128
EPSILON = 1e-06
META_ROWS = 8
TILE = 128
F32 = jnp.float32
BF16 = jnp.bfloat16
VMEM = pl.BlockSpec(memory_space=pltpu.VMEM)
HBM = pl.BlockSpec(memory_space=pltpu.HBM)


def dot(a, b, da=1, db=0):
    return lax.dot_general(a, b, (((da,), (db,)), ((), ())), preferred_element_type=F32)


def shard_at(m, shard_rows):
    at = jnp.bitwise_xor(lax.axis_index("dp"), m) * shard_rows
    return pl.ds(pl.multiple_of(at, 16), shard_rows)


def pair_kernel(*refs, cap, pick_count, n_sources, n_sets, n_data, first, last):
    it = iter(refs)
    take = lambda n: [next(it) for _ in range(n)]
    sources, labels = take(n_sources), take(n_sets)
    shards = take(n_data if first else 0)
    enc, total_in = (None, None) if first else take(2)
    backs, grad_scores_ref, block_ref, embedding_ref = take(n_sources), *take(3)
    enc = next(it) if first else enc
    shares = take(2 if last else 0)
    total_ref = next(it)

    n_owner_data = lax.axis_size("dp")
    me = lax.axis_index("labels") * n_owner_data + lax.axis_index("dp")
    rows = sources[0].shape[0] - META_ROWS
    shard_rows = enc.shape[0] // n_data
    n_blocks = labels[0].shape[0] // BLK
    part = n_sources * cap
    slots = n_sets * part

    for m, shard in enumerate(shards):
        enc[shard_at(m, shard_rows), :] = shard[...]

    row_id = lax.broadcasted_iota(jnp.int32, (rows, rows), 0)
    col_id = lax.broadcasted_iota(jnp.int32, (rows, rows), 1)
    before = (row_id < col_id).astype(BF16)
    slot_id = lax.broadcasted_iota(jnp.int32, (cap, rows), 0).astype(F32)
    column = lax.broadcasted_iota(jnp.int32, (slots, BLK), 1)

    hits, codes = [], []
    for source in sources:
        meta = source[rows:, 0 : 3 * rows].astype(F32)[:pick_count]
        code = meta[:, rows : 2 * rows] * 256.0 + meta[:, 2 * rows :] + 1.0
        for j in range(n_sets):
            named = meta[:, :rows] == jnp.bitwise_xor(me, j).astype(F32)
            hits.append(jnp.sum(named.astype(F32), axis=0, keepdims=True))
            codes.append(jnp.sum(jnp.where(named, code, 0.0), axis=0, keepdims=True))
    rank = dot(jnp.concatenate(hits, axis=0).astype(BF16), before)

    picks, picked, slot_codes = [], {}, {}
    for s, source in enumerate(sources):
        pick = []
        for j in range(n_sets):
            i = s * n_sets + j
            pick.append(jnp.where((slot_id == rank[i : i + 1]) & (hits[i] > 0.0), 1.0, 0.0))
            slot_codes[j, s] = jnp.sum(pick[j] * codes[i], axis=1, keepdims=True)
        picks.append(jnp.concatenate(pick, axis=0).astype(BF16))
        found = dot(picks[s], source[:rows, :]).astype(BF16)
        for j in range(n_sets):
            picked[j, s] = found[j * cap : (j + 1) * cap]
    order = [(j, s) for j in range(n_sets) for s in range(n_sources)]
    feats = jnp.concatenate([picked[i] for i in order], axis=0)
    code = jnp.concatenate([slot_codes[i] for i in order], axis=0).astype(jnp.int32) - 1

    hidden = dot(feats, enc[...])
    inv_rms = lax.rsqrt(jnp.mean(hidden * hidden, axis=-1, keepdims=True) + EPSILON)
    embedding = (hidden * inv_rms).astype(BF16)
    embedding_ref[...] = embedding

    block = jnp.broadcast_to(code >> 8, (slots, BLK))
    block_ref[...] = block
    wanted = jnp.broadcast_to(code & 255, (slots, BLK))
    target = jnp.where(column == wanted, 1.0, 0.0)
    grad_pairs = []
    for j in range(n_sets):
        at = slice(j * part, (j + 1) * part)
        scores = dot(embedding[at], labels[j][...], 1, 1)
        mine = block[at]
        own_scores = jnp.zeros((part, BLK), F32)
        for b in range(n_blocks):
            own_scores = jnp.where(mine == b, scores[:, b * BLK : (b + 1) * BLK], own_scores)
        grad_scores = jnp.where(mine >= 0, jax.nn.sigmoid(own_scores) - target[at], 0.0)
        grad_scores_ref[at, :] = grad_scores
        spread = jnp.concatenate(
            [jnp.where(mine == b, grad_scores, 0.0).astype(BF16) for b in range(n_blocks)], axis=1
        )
        grad_pairs.append(dot(spread, labels[j][...]))
    grad_pair = jnp.concatenate(grad_pairs, axis=0).astype(BF16).astype(F32)

    projection = jnp.mean(hidden * grad_pair, axis=-1, keepdims=True)
    grad_hidden = (inv_rms * grad_pair - hidden * (inv_rms**3 * projection)).astype(BF16)
    total = dot(feats, grad_hidden, 0, 0)
    total_ref[...] = total if first else total + total_in[...]
    for m in range(n_data if last else 0):
        shares[m % 2][m // 2] = total_ref[shard_at(m, shard_rows), :].astype(BF16)

    grad_feats = dot(grad_hidden, enc[...], 1, 1).astype(BF16)
    for s in range(n_sources):
        parts = [
            grad_feats[(j * n_sources + s) * cap : (j * n_sources + s + 1) * cap]
            for j in range(n_sets)
        ]
        backs[s][...] = dot(picks[s], jnp.concatenate(parts, axis=0), 0, 0).astype(BF16)


def grad_label_kernel(*refs, calls, n_sets, j, n_more):
    grad_scores, blocks, embeddings = refs[:calls], refs[calls : 2 * calls], refs[2 * calls : 3 * calls]
    more, rest = refs[3 * calls : 3 * calls + n_more], refs[3 * calls + n_more :]
    out_ref, (result, *sem) = rest[0], rest[-2:] if len(rest) > 1 else rest
    rows_of = [slice(j * r.shape[0] // n_sets, (j + 1) * r.shape[0] // n_sets) for r in blocks]
    grad_scores_t = jnp.concatenate([r[at, :].T for r, at in zip(grad_scores, rows_of)], axis=1)
    block_t = jnp.concatenate([r[at, :].T for r, at in zip(blocks, rows_of)], axis=1)
    embedding = jnp.concatenate([r[at, :] for r, at in zip(embeddings, rows_of)], axis=0)
    copies = []
    for b in range(out_ref.shape[0] // BLK):
        rows = pl.ds(b * BLK, BLK)
        spread_t = jnp.where(block_t == b, grad_scores_t, 0.0).astype(BF16)
        total = dot(spread_t, embedding)
        for ref in more:
            total = total + ref[rows, :].astype(F32)
        result[rows, :] = total.astype(BF16)
        if sem:
            copies.append(pltpu.make_async_copy(result.at[rows], out_ref.at[rows], sem[0].at[b]))
            copies[b].start()
    for copy in copies:
        copy.wait()


def own_block_kernel(feats_ref, owners_ref, blocks_ref, positives_ref, out_ref, ints, sem):
    rows, width = feats_ref.shape
    feats = pltpu.make_async_copy(feats_ref, out_ref.at[pl.ds(0, rows)], sem.at[0])
    feats.start()
    copies = []
    for i, ref in enumerate((owners_ref, blocks_ref, positives_ref)):
        copies.append(pltpu.make_async_copy(ref, ints.at[i], sem.at[i + 1]))
        copies[i].start()
    for copy in copies:
        copy.wait()
    meta = [ints[i].astype(F32) for i in range(3)]
    meta += [jnp.zeros((meta[0].shape[0], width - 3 * rows), F32)]
    meta = jnp.concatenate(meta, axis=1)
    rest = jnp.zeros((META_ROWS - meta.shape[0], width), F32)
    out_ref[rows:, :] = jnp.concatenate([meta, rest], axis=0).astype(BF16)
    feats.wait()


def load_kernel(label_ref, shard_ref, label_out, shard_out):
    label_out[...] = label_ref[...]
    shard_out[...] = shard_ref[...]


def half_at(mine, half):
    odd = jnp.bitwise_and(lax.axis_index("labels"), 1)
    return pl.ds(pl.multiple_of((odd if mine else 1 - odd) * half, 16), half)


def split_kernel(even_ref, got_ref, *refs):
    *more, keep_ref, send_ref, total = refs
    share = even_ref[0].astype(F32) + got_ref[0].astype(F32)
    for ref in more:
        share = share + ref[...].astype(F32)
    total[...] = share
    half = keep_ref.shape[0]
    keep_ref[...] = total[half_at(True, half), :]
    send_ref[...] = total[half_at(False, half), :].astype(BF16)


def merge_kernel(mine_ref, other_ref, out_ref):
    half = mine_ref.shape[0]
    out_ref[half_at(True, half), :] = mine_ref[...].astype(F32)
    out_ref[half_at(False, half), :] = other_ref[...].astype(F32)


def call(kernel, name, out_shape, scratch, flops, megabytes, *args, space=VMEM, out_space=VMEM, limit=24):
    return pl.pallas_call(
        kernel,
        in_specs=[space] * len(args),
        out_specs=jax.tree.map(lambda _: out_space, out_shape),
        out_shape=out_shape,
        scratch_shapes=scratch,
        compiler_params=pltpu.CompilerParams(vmem_limit_bytes=limit << 20),
        cost_estimate=pl.CostEstimate(
            flops=flops, bytes_accessed=megabytes << 20, transcendentals=0
        ),
        name=name,
    )(*args)


def shaped(shape, dtype=BF16):
    return jax.ShapeDtypeStruct(shape, dtype)


def pair_work(sources, labels, shards, cap, pick_count, before, last):
    n_data, n_sets = len(shards), len(labels)
    block_rows, width = sources[0].shape
    rows = block_rows - META_ROWS
    slots = n_sets * len(sources) * cap
    shard_rows = shards[0].shape[0]
    full = (n_data * shard_rows, width)
    backs = len(sources)
    shapes = [shaped((rows, width))] * backs
    shapes += [shaped((slots, BLK), F32), shaped((slots, BLK), jnp.int32), shaped((slots, width))]
    more = [before["enc"], before["total"]] if before else shards
    scratch = []
    if not before:
        shapes += [shaped(full)]
    if last:
        shapes += [shaped((n_data // 2, shard_rows, width))] * 2
        scratch = [pltpu.VMEM(full, F32)]
    else:
        shapes += [shaped(full, F32)]
    out = call(
        functools.partial(
            pair_kernel,
            cap=cap,
            pick_count=pick_count,
            n_sources=len(sources),
            n_sets=n_sets,
            n_data=n_data,
            first=not before,
            last=last,
        ),
        "pair_work",
        shapes,
        scratch,
        2 * slots * width * (2 * labels[0].shape[0] + 3 * width + 2 * rows),
        8,
        *sources,
        *labels,
        *more,
    )
    result = {"back": list(out[:backs]), "slots": list(out[backs : backs + 3])}
    rest = list(out[backs + 3 :])
    result["enc"] = before["enc"] if before else rest.pop(0)
    result["shares" if last else "total"] = rest if last else rest[0]
    return result


def grad_label_work(works, n_sets, j, labels_shape, *more):
    slots = list(zip(*(work["slots"] for work in works)))
    scratch = []
    if j == 0:
        sem = pltpu.SemaphoreType.DMA((labels_shape[0] // BLK,))
        scratch = [pltpu.VMEM(labels_shape, BF16), sem]
    return call(
        functools.partial(
            grad_label_kernel, calls=len(works), n_sets=n_sets, j=j, n_more=len(more)
        ),
        "grad_label_work",
        shaped(labels_shape),
        scratch,
        2 * sum(x.shape[0] for x in slots[0]) // n_sets * labels_shape[0] * labels_shape[1],
        4,
        *slots[0],
        *slots[1],
        *slots[2],
        *more,
        out_space=pl.BlockSpec(memory_space=pl.ANY) if scratch else VMEM,
    )


def swap(x):
    x = lax.all_to_all(x, "labels", split_axis=0, concat_axis=0, tiled=True)
    return lax.all_to_all(x, "dp", split_axis=1, concat_axis=1, tiled=True)


def partner(x, axis, mask):
    return lax.ppermute(x, axis, [(i, i ^ mask) for i in range(lax.axis_size(axis))])


def masks(n):
    return [1 << i for i in range(n.bit_length() - 1)]


def after(x, *others):
    return lax.optimization_barrier((x, *others))[0]


def gather_far(x):
    got = {0: x}
    for mask in reversed(masks(lax.axis_size("dp"))[1:]):
        got.update({m | mask: partner(v, "dp", mask) for m, v in list(got.items())})
    return [got[m] for m in sorted(got)]


def gather_near(far, *first):
    near = [partner(after(v, *far[1:], *first), "dp", 1) for v in far]
    return [v for pair in zip(far, near) for v in pair]


def gather_labels(x, first):
    got = {0: x}
    for mask in reversed(masks(lax.axis_size("labels"))):
        for m, v in list(got.items()):
            got[m | mask] = partner(after(v, first) if m else v, "labels", mask)
    return [got[m] for m in range(len(got))]


def add(*terms):
    return sum(t.astype(F32) for t in terms)


def dp_terms(even, odd):
    got = sent = partner(odd, "dp", 1)
    terms = [[even[i], got[i]] for i in range(even.shape[0])]
    for mask in masks(len(terms)):
        for i in range(len(terms)):
            if i & mask == 0 and i % mask == 0:
                sent = add(*terms[i | mask]).astype(BF16)
                terms[i].append(partner(sent, "dp", 2 * mask))
    return got, terms[0], sent


def sum_shares(even, got, terms, *first):
    rows, width = even.shape[1:]
    half = rows // 2
    keep, send = call(
        split_kernel,
        "split_share",
        [shaped((half, width), F32), shaped((half, width))],
        [pltpu.VMEM((rows, width), F32)],
        0,
        1,
        even,
        after(got, *first),
        *terms[2:],
    )
    x = add(keep, partner(send, "labels", 1)).astype(BF16)
    first = x
    for mask in masks(lax.axis_size("labels"))[1:]:
        x = add(x, partner(x, "labels", mask)).astype(BF16)
    return keep, first, x


def join_halves(x, *first):
    other = partner(x, "labels", 1)
    out = shaped((2 * x.shape[0], x.shape[1]), F32)
    return call(merge_kernel, "merge_share", out, [], 0, 1, after(x, *first), other)


def reduce_runs(runs, got_last, ahead, keep, first):
    def over_dp(parts, *hold):
        parts = [list(part) for part in parts]
        for mask in masks(len(parts)):
            for h in range(0, len(parts), 2 * mask):
                sent = after(add(*parts[h + mask]).astype(BF16), *hold)
                parts[h].append(partner(sent, "dp", 2 * mask))
        return parts[0]

    n = len(runs)
    sums, sent_near = {n - 2: over_dp(list(zip(runs[n - 2], got_last)), ahead)}, []
    for i in reversed(range(0, n - 2, 2)):
        near = add(*over_dp([[x] for x in runs[i + 1]], ahead)).astype(BF16)
        sent_near.append(partner(near, "labels", 1))
        sums[i] = over_dp([[x] for x in runs[i]], keep) + sent_near[-1:]
    for mask in masks(n)[1:]:
        for i in range(0, n, 2 * mask):
            sent = after(add(*sums[i + mask]).astype(BF16), first, *sent_near)
            sums[i].append(partner(sent, "labels", mask))
    return sums[0]


def with_meta(feats, owner_rows, block_rows, positive_rows):
    meta = jnp.concatenate([owner_rows, block_rows, positive_rows], axis=1).astype(BF16)
    meta = jnp.pad(meta, ((0, META_ROWS - meta.shape[0]), (0, feats.shape[1] - meta.shape[1])))
    return jnp.concatenate([feats, meta], axis=0)


def local(feats, enc_weight, label_weight, owners, blocks, positives):
    n_labels = lax.axis_size("labels")
    n_data = lax.axis_size("dp")
    n_owner = n_labels * n_data
    row_count, width = feats.shape
    pick_count = owners.shape[1]
    cap = max(2, 2 * row_count * pick_count // n_owner)

    if row_count <= n_data * cap:
        own = call(
            own_block_kernel,
            "own_block",
            shaped((row_count + META_ROWS, width)),
            [
                pltpu.VMEM((3, pick_count, row_count), jnp.int32),
                pltpu.SemaphoreType.DMA((4,)),
            ],
            0,
            1,
            feats,
            owners.T,
            blocks.T,
            positives.T,
            space=HBM,
            limit=60,
        )
        labels = [label_weight, partner(label_weight, "dp", 1)]
        labels[0], own_shard = call(
            load_kernel,
            "load",
            [shaped(label_weight.shape), shaped(enc_weight.shape)],
            [],
            0,
            4,
            after(label_weight, labels[1]),
            enc_weight,
        )
        near = gather_labels(own, labels[0])
        far = {0: gather_far(own)}
        shards = gather_near(gather_far(enc_weight))
        shards[0] = own_shard
        works, backs = [], {}
        last_call = list(range(1, n_labels, 2))
        for call_runs in (list(range(0, n_labels, 2)), last_call):
            sources = []
            for run in call_runs:
                if run == n_labels - 1:
                    far[run] = gather_far(after(near[run], *far[run - 1][1:]))
                elif run % 2:
                    sent = [after(x, *shards[1:]) for x in far[run - 1][1:]]
                    far[run] = near[run : run + 1] + [partner(x, "labels", 1) for x in sent]
                elif run:
                    far[run] = gather_far(after(near[run], *far[0][1:], *near[1:3], labels[0]))
                sources += [after(near[run], *([] if run else near[1:3]))] + far[run][1:]
            before, last = works[-1] if works else None, call_runs is last_call
            works.append(pair_work(sources, labels, shards, cap, pick_count, before, last))
            parts = len(sources) // len(call_runs)
            for i, run in enumerate(call_runs):
                backs[run] = works[-1]["back"][i * parts : (i + 1) * parts]
        even, odd = works[-1]["shares"]
        got, share_terms, sent = dp_terms(even, odd)
        near_last, *far_last = backs[n_labels - 1]
        got_last = [partner(x, "labels", 1) for x in (after(near_last, sent), *far_last)]
        keep, first, share = sum_shares(even, got, share_terms, *got_last)
        terms = reduce_runs(backs, got_last, sent, keep, first)
        other = partner(grad_label_work(works, 2, 1, label_weight.shape), "dp", 1)
        grad_label = grad_label_work(works, 2, 0, label_weight.shape, other)
        grad_feats = add(after(terms[0], grad_label), *terms[1:]).astype(BF16)
        grad_enc = join_halves(share, grad_feats)
    else:
        shards = gather_near(gather_far(enc_weight))
        flat = owners.reshape(-1)
        onehot = (flat[:, None] == jnp.arange(n_owner, dtype=jnp.int32)[None, :]).astype(jnp.int32)
        rank = jnp.sum((jnp.cumsum(onehot, axis=0) - onehot) * onehot, axis=1)
        slot = (flat * cap + rank).reshape(row_count, pick_count)
        slot_total = n_owner * cap
        slots = jnp.arange(slot_total, dtype=jnp.int32)
        place = slots[:, None, None] == slot[None]
        pick = jnp.any(place, axis=2).astype(BF16)
        live = jnp.any(place, axis=(1, 2))
        block_of = jnp.sum(jnp.where(place, blocks[None], 0), axis=(1, 2))
        wanted = jnp.sum(jnp.where(place, positives[None], 0), axis=(1, 2))
        owner_of = jnp.where(live, slots // cap, -1)
        out = dot(pick, feats).astype(BF16).reshape(n_labels, n_data, cap, width)
        meta = jnp.stack([owner_of, block_of, wanted], axis=1).reshape(n_labels, n_data, cap, 3)
        tiles = slot_total // TILE
        got = swap(out).reshape(tiles, TILE, width)
        got_meta = swap(meta).reshape(tiles, TILE, 3).transpose(0, 2, 1)
        sources = [
            with_meta(got[i], got_meta[i, 0:1], got_meta[i, 1:2], got_meta[i, 2:3])
            for i in range(tiles)
        ]
        works = []
        for i in range(0, tiles, 4):
            before = works[-1] if works else None
            last = i + 4 >= tiles
            works.append(pair_work(sources[i : i + 4], [label_weight], shards, TILE, 1, before, last))
        back = jnp.concatenate([back for work in works for back in work["back"]], axis=0)
        back = swap(back.reshape(n_labels, n_data, cap, width)).reshape(slot_total, width)
        grad_feats = dot(pick, back, 0, 0).astype(BF16)
        even, odd = works[-1]["shares"]
        got, share_terms, _ = dp_terms(even, odd)
        *_, share = sum_shares(even, got, share_terms)
        grad_label = grad_label_work(works, 1, 0, label_weight.shape)
        grad_enc = join_halves(share, grad_label, grad_feats)

    return (grad_feats, grad_label, grad_enc)


def solution(mesh):
    rows = P(("groups", "labels", "dp"), None)
    return jax.shard_map(
        local,
        mesh=mesh,
        in_specs=(rows, P("dp", None), rows, rows, rows, rows),
        out_specs=(rows, rows, P(("groups", "dp"), None)),
        check_vma=False,
    )
```

```python
import functools

import jax
import jax.numpy as jnp
from jax import lax
from jax.experimental import pallas as pl
from jax.experimental.pallas import tpu as pltpu
from jax.sharding import PartitionSpec as P

BLK = 128
EPSILON = 1e-06
META_ROWS = 8
TILE = 128
F32 = jnp.float32
BF16 = jnp.bfloat16
VMEM = pl.BlockSpec(memory_space=pltpu.VMEM)
HBM = pl.BlockSpec(memory_space=pltpu.HBM)


def dot(a, b, da=1, db=0):
    return lax.dot_general(a, b, (((da,), (db,)), ((), ())), preferred_element_type=F32)


def shard_at(m, shard_rows):
    at = jnp.bitwise_xor(lax.axis_index("dp"), m) * shard_rows
    return pl.ds(pl.multiple_of(at, 16), shard_rows)


def pair_kernel(*refs, cap, pick_count, n_sources, n_sets, n_data, first, last):
    it = iter(refs)
    take = lambda n: [next(it) for _ in range(n)]
    sources, labels = take(n_sources), take(n_sets)
    shards = take(n_data if first else 0)
    enc, total_in = (None, None) if first else take(2)
    backs, grad_scores_ref, block_ref, embedding_ref = take(n_sources), *take(3)
    enc = next(it) if first else enc
    shares = take(2 if last else 0)
    total_ref = next(it)

    n_owner_data = lax.axis_size("dp")
    me = lax.axis_index("labels") * n_owner_data + lax.axis_index("dp")
    rows = sources[0].shape[0] - META_ROWS
    shard_rows = enc.shape[0] // n_data
    n_blocks = labels[0].shape[0] // BLK
    part = n_sources * cap
    slots = n_sets * part

    for m, shard in enumerate(shards):
        enc[shard_at(m, shard_rows), :] = shard[...]

    row_id = lax.broadcasted_iota(jnp.int32, (rows, rows), 0)
    col_id = lax.broadcasted_iota(jnp.int32, (rows, rows), 1)
    before = (row_id < col_id).astype(BF16)
    slot_id = lax.broadcasted_iota(jnp.int32, (cap, rows), 0).astype(F32)
    column = lax.broadcasted_iota(jnp.int32, (slots, BLK), 1)

    hits, codes = [], []
    for source in sources:
        meta = source[rows:, 0 : 3 * rows].astype(F32)[:pick_count]
        code = meta[:, rows : 2 * rows] * 256.0 + meta[:, 2 * rows :] + 1.0
        for j in range(n_sets):
            named = meta[:, :rows] == jnp.bitwise_xor(me, j).astype(F32)
            hits.append(jnp.sum(named.astype(F32), axis=0, keepdims=True))
            codes.append(jnp.sum(jnp.where(named, code, 0.0), axis=0, keepdims=True))
    rank = dot(jnp.concatenate(hits, axis=0).astype(BF16), before)

    picks, picked, slot_codes = [], {}, {}
    for s, source in enumerate(sources):
        pick = []
        for j in range(n_sets):
            i = s * n_sets + j
            pick.append(jnp.where((slot_id == rank[i : i + 1]) & (hits[i] > 0.0), 1.0, 0.0))
            slot_codes[j, s] = jnp.sum(pick[j] * codes[i], axis=1, keepdims=True)
        picks.append(jnp.concatenate(pick, axis=0).astype(BF16))
        found = dot(picks[s], source[:rows, :]).astype(BF16)
        for j in range(n_sets):
            picked[j, s] = found[j * cap : (j + 1) * cap]
    order = [(j, s) for j in range(n_sets) for s in range(n_sources)]
    feats = jnp.concatenate([picked[i] for i in order], axis=0)
    code = jnp.concatenate([slot_codes[i] for i in order], axis=0).astype(jnp.int32) - 1

    hidden = dot(feats, enc[...])
    inv_rms = lax.rsqrt(jnp.mean(hidden * hidden, axis=-1, keepdims=True) + EPSILON)
    embedding = (hidden * inv_rms).astype(BF16)
    embedding_ref[...] = embedding

    block = jnp.broadcast_to(code >> 8, (slots, BLK))
    block_ref[...] = block
    wanted = jnp.broadcast_to(code & 255, (slots, BLK))
    target = jnp.where(column == wanted, 1.0, 0.0)
    grad_pairs = []
    for j in range(n_sets):
        at = slice(j * part, (j + 1) * part)
        scores = dot(embedding[at], labels[j][...], 1, 1)
        mine = block[at]
        own_scores = jnp.zeros((part, BLK), F32)
        for b in range(n_blocks):
            own_scores = jnp.where(mine == b, scores[:, b * BLK : (b + 1) * BLK], own_scores)
        grad_scores = jnp.where(mine >= 0, jax.nn.sigmoid(own_scores) - target[at], 0.0)
        grad_scores_ref[at, :] = grad_scores
        spread = jnp.concatenate(
            [jnp.where(mine == b, grad_scores, 0.0).astype(BF16) for b in range(n_blocks)], axis=1
        )
        grad_pairs.append(dot(spread, labels[j][...]))
    grad_pair = jnp.concatenate(grad_pairs, axis=0).astype(BF16).astype(F32)

    projection = jnp.mean(hidden * grad_pair, axis=-1, keepdims=True)
    grad_hidden = (inv_rms * grad_pair - hidden * (inv_rms**3 * projection)).astype(BF16)
    total = dot(feats, grad_hidden, 0, 0)
    total_ref[...] = total if first else total + total_in[...]
    for m in range(n_data if last else 0):
        shares[m % 2][m // 2] = total_ref[shard_at(m, shard_rows), :].astype(BF16)

    grad_feats = dot(grad_hidden, enc[...], 1, 1).astype(BF16)
    for s in range(n_sources):
        parts = [
            grad_feats[(j * n_sources + s) * cap : (j * n_sources + s + 1) * cap]
            for j in range(n_sets)
        ]
        backs[s][...] = dot(picks[s], jnp.concatenate(parts, axis=0), 0, 0).astype(BF16)


def grad_label_kernel(*refs, calls, n_sets, j, n_more):
    grad_scores, blocks, embeddings = refs[:calls], refs[calls : 2 * calls], refs[2 * calls : 3 * calls]
    more, rest = refs[3 * calls : 3 * calls + n_more], refs[3 * calls + n_more :]
    out_ref, (result, *sem) = rest[0], rest[-2:] if len(rest) > 1 else rest
    rows_of = [slice(j * r.shape[0] // n_sets, (j + 1) * r.shape[0] // n_sets) for r in blocks]
    grad_scores_t = jnp.concatenate([r[at, :].T for r, at in zip(grad_scores, rows_of)], axis=1)
    block_t = jnp.concatenate([r[at, :].T for r, at in zip(blocks, rows_of)], axis=1)
    embedding = jnp.concatenate([r[at, :] for r, at in zip(embeddings, rows_of)], axis=0)
    copies = []
    for b in range(out_ref.shape[0] // BLK):
        rows = pl.ds(b * BLK, BLK)
        spread_t = jnp.where(block_t == b, grad_scores_t, 0.0).astype(BF16)
        total = dot(spread_t, embedding)
        for ref in more:
            total = total + ref[rows, :].astype(F32)
        result[rows, :] = total.astype(BF16)
        if sem:
            copies.append(pltpu.make_async_copy(result.at[rows], out_ref.at[rows], sem[0].at[b]))
            copies[b].start()
    for copy in copies:
        copy.wait()


def own_block_kernel(feats_ref, owners_ref, blocks_ref, positives_ref, out_ref, ints, sem):
    rows, width = feats_ref.shape
    feats = pltpu.make_async_copy(feats_ref, out_ref.at[pl.ds(0, rows)], sem.at[0])
    feats.start()
    copies = []
    for i, ref in enumerate((owners_ref, blocks_ref, positives_ref)):
        copies.append(pltpu.make_async_copy(ref, ints.at[i], sem.at[i + 1]))
        copies[i].start()
    for copy in copies:
        copy.wait()
    meta = [ints[i].astype(F32) for i in range(3)]
    meta += [jnp.zeros((meta[0].shape[0], width - 3 * rows), F32)]
    meta = jnp.concatenate(meta, axis=1)
    rest = jnp.zeros((META_ROWS - meta.shape[0], width), F32)
    out_ref[rows:, :] = jnp.concatenate([meta, rest], axis=0).astype(BF16)
    feats.wait()


def load_kernel(label_ref, shard_ref, label_out, shard_out):
    label_out[...] = label_ref[...]
    shard_out[...] = shard_ref[...]


def half_at(mine, half):
    odd = jnp.bitwise_and(lax.axis_index("labels"), 1)
    return pl.ds(pl.multiple_of((odd if mine else 1 - odd) * half, 16), half)


def split_kernel(even_ref, got_ref, *refs):
    *more, keep_ref, send_ref, total = refs
    share = even_ref[0].astype(F32) + got_ref[0].astype(F32)
    for ref in more:
        share = share + ref[...].astype(F32)
    total[...] = share
    half = keep_ref.shape[0]
    keep_ref[...] = total[half_at(True, half), :]
    send_ref[...] = total[half_at(False, half), :].astype(BF16)


def merge_kernel(mine_ref, other_ref, out_ref):
    half = mine_ref.shape[0]
    out_ref[half_at(True, half), :] = mine_ref[...].astype(F32)
    out_ref[half_at(False, half), :] = other_ref[...].astype(F32)


def call(kernel, name, out_shape, scratch, flops, megabytes, *args, space=VMEM, out_space=VMEM, limit=24):
    return pl.pallas_call(
        kernel,
        in_specs=[space] * len(args),
        out_specs=jax.tree.map(lambda _: out_space, out_shape),
        out_shape=out_shape,
        scratch_shapes=scratch,
        compiler_params=pltpu.CompilerParams(vmem_limit_bytes=limit << 20),
        cost_estimate=pl.CostEstimate(
            flops=flops, bytes_accessed=megabytes << 20, transcendentals=0
        ),
        name=name,
    )(*args)


def shaped(shape, dtype=BF16):
    return jax.ShapeDtypeStruct(shape, dtype)


def pair_work(sources, labels, shards, cap, pick_count, before, last):
    n_data, n_sets = len(shards), len(labels)
    block_rows, width = sources[0].shape
    rows = block_rows - META_ROWS
    slots = n_sets * len(sources) * cap
    shard_rows = shards[0].shape[0]
    full = (n_data * shard_rows, width)
    backs = len(sources)
    shapes = [shaped((rows, width))] * backs
    shapes += [shaped((slots, BLK), F32), shaped((slots, BLK), jnp.int32), shaped((slots, width))]
    more = [before["enc"], before["total"]] if before else shards
    scratch = []
    if not before:
        shapes += [shaped(full)]
    if last:
        shapes += [shaped((n_data // 2, shard_rows, width))] * 2
        scratch = [pltpu.VMEM(full, F32)]
    else:
        shapes += [shaped(full, F32)]
    out = call(
        functools.partial(
            pair_kernel,
            cap=cap,
            pick_count=pick_count,
            n_sources=len(sources),
            n_sets=n_sets,
            n_data=n_data,
            first=not before,
            last=last,
        ),
        "pair_work",
        shapes,
        scratch,
        2 * slots * width * (2 * labels[0].shape[0] + 3 * width + 2 * rows),
        8,
        *sources,
        *labels,
        *more,
    )
    result = {"back": list(out[:backs]), "slots": list(out[backs : backs + 3])}
    rest = list(out[backs + 3 :])
    result["enc"] = before["enc"] if before else rest.pop(0)
    result["shares" if last else "total"] = rest if last else rest[0]
    return result


def grad_label_work(works, n_sets, j, labels_shape, *more):
    slots = list(zip(*(work["slots"] for work in works)))
    scratch = []
    if j == 0:
        sem = pltpu.SemaphoreType.DMA((labels_shape[0] // BLK,))
        scratch = [pltpu.VMEM(labels_shape, BF16), sem]
    return call(
        functools.partial(
            grad_label_kernel, calls=len(works), n_sets=n_sets, j=j, n_more=len(more)
        ),
        "grad_label_work",
        shaped(labels_shape),
        scratch,
        2 * sum(x.shape[0] for x in slots[0]) // n_sets * labels_shape[0] * labels_shape[1],
        4,
        *slots[0],
        *slots[1],
        *slots[2],
        *more,
        out_space=pl.BlockSpec(memory_space=pl.ANY) if scratch else VMEM,
    )


def swap(x):
    x = lax.all_to_all(x, "labels", split_axis=0, concat_axis=0, tiled=True)
    return lax.all_to_all(x, "dp", split_axis=1, concat_axis=1, tiled=True)


def partner(x, axis, mask):
    return lax.ppermute(x, axis, [(i, i ^ mask) for i in range(lax.axis_size(axis))])


def masks(n):
    return [1 << i for i in range(n.bit_length() - 1)]


def after(x, *others):
    return lax.optimization_barrier((x, *others))[0]


def gather_far(x):
    got = {0: x}
    for mask in reversed(masks(lax.axis_size("dp"))[1:]):
        got.update({m | mask: partner(v, "dp", mask) for m, v in list(got.items())})
    return [got[m] for m in sorted(got)]


def gather_near(far, *first):
    near = [partner(after(v, *far[1:], *first), "dp", 1) for v in far]
    return [v for pair in zip(far, near) for v in pair]


def gather_labels(x, first):
    got = {0: x}
    for mask in reversed(masks(lax.axis_size("labels"))):
        for m, v in list(got.items()):
            got[m | mask] = partner(after(v, first) if m else v, "labels", mask)
    return [got[m] for m in range(len(got))]


def add(*terms):
    return sum(t.astype(F32) for t in terms)


def dp_terms(even, odd):
    got = sent = partner(odd, "dp", 1)
    terms = [[even[i], got[i]] for i in range(even.shape[0])]
    for mask in masks(len(terms)):
        for i in range(len(terms)):
            if i & mask == 0 and i % mask == 0:
                sent = add(*terms[i | mask]).astype(BF16)
                terms[i].append(partner(sent, "dp", 2 * mask))
    return got, terms[0], sent


def sum_shares(even, got, terms, *first):
    rows, width = even.shape[1:]
    half = rows // 2
    keep, send = call(
        split_kernel,
        "split_share",
        [shaped((half, width), F32), shaped((half, width))],
        [pltpu.VMEM((rows, width), F32)],
        0,
        1,
        even,
        after(got, *first),
        *terms[2:],
    )
    x = add(keep, partner(send, "labels", 1)).astype(BF16)
    first = x
    for mask in masks(lax.axis_size("labels"))[1:]:
        x = add(x, partner(x, "labels", mask)).astype(BF16)
    return keep, first, x


def join_halves(x, *first):
    other = partner(x, "labels", 1)
    out = shaped((2 * x.shape[0], x.shape[1]), F32)
    return call(merge_kernel, "merge_share", out, [], 0, 1, after(x, *first), other)


def reduce_runs(runs, got_last, ahead, keep, first):
    def over_dp(parts, *hold):
        parts = [list(part) for part in parts]
        for mask in masks(len(parts)):
            for h in range(0, len(parts), 2 * mask):
                sent = after(add(*parts[h + mask]).astype(BF16), *hold)
                parts[h].append(partner(sent, "dp", 2 * mask))
        return parts[0]

    n = len(runs)
    sums, sent_near = {n - 2: over_dp(list(zip(runs[n - 2], got_last)), ahead)}, []
    for i in reversed(range(0, n - 2, 2)):
        near = add(*over_dp([[x] for x in runs[i + 1]], ahead)).astype(BF16)
        sent_near.append(partner(near, "labels", 1))
        sums[i] = over_dp([[x] for x in runs[i]], keep) + sent_near[-1:]
    for mask in masks(n)[1:]:
        for i in range(0, n, 2 * mask):
            sent = after(add(*sums[i + mask]).astype(BF16), first)
            sums[i].append(partner(sent, "labels", mask))
    return sums[0]


def with_meta(feats, owner_rows, block_rows, positive_rows):
    meta = jnp.concatenate([owner_rows, block_rows, positive_rows], axis=1).astype(BF16)
    meta = jnp.pad(meta, ((0, META_ROWS - meta.shape[0]), (0, feats.shape[1] - meta.shape[1])))
    return jnp.concatenate([feats, meta], axis=0)


def local(feats, enc_weight, label_weight, owners, blocks, positives):
    n_labels = lax.axis_size("labels")
    n_data = lax.axis_size("dp")
    n_owner = n_labels * n_data
    row_count, width = feats.shape
    pick_count = owners.shape[1]
    cap = max(2, 2 * row_count * pick_count // n_owner)

    if row_count <= n_data * cap:
        own = call(
            own_block_kernel,
            "own_block",
            shaped((row_count + META_ROWS, width)),
            [
                pltpu.VMEM((3, pick_count, row_count), jnp.int32),
                pltpu.SemaphoreType.DMA((4,)),
            ],
            0,
            1,
            feats,
            owners.T,
            blocks.T,
            positives.T,
            space=HBM,
            limit=60,
        )
        labels = [label_weight, partner(label_weight, "dp", 1)]
        labels[0], own_shard = call(
            load_kernel,
            "load",
            [shaped(label_weight.shape), shaped(enc_weight.shape)],
            [],
            0,
            4,
            after(label_weight, labels[1]),
            enc_weight,
        )
        near = gather_labels(own, labels[0])
        far = {0: gather_far(own)}
        shards = gather_near(gather_far(enc_weight))
        shards[0] = own_shard
        works, backs = [], {}
        last_call = list(range(1, n_labels, 2))
        for call_runs in (list(range(0, n_labels, 2)), last_call):
            sources = []
            for run in call_runs:
                if run == n_labels - 1:
                    far[run] = gather_far(after(near[run], *far[run - 1][1:]))
                elif run % 2:
                    sent = [after(x, *shards[1:]) for x in far[run - 1][1:]]
                    far[run] = near[run : run + 1] + [partner(x, "labels", 1) for x in sent]
                elif run:
                    far[run] = gather_far(after(near[run], *far[0][1:], *near[1:3], labels[0]))
                sources += [after(near[run], *([] if run else near[1:3]))] + far[run][1:]
            before, last = works[-1] if works else None, call_runs is last_call
            works.append(pair_work(sources, labels, shards, cap, pick_count, before, last))
            parts = len(sources) // len(call_runs)
            for i, run in enumerate(call_runs):
                backs[run] = works[-1]["back"][i * parts : (i + 1) * parts]
        even, odd = works[-1]["shares"]
        got, share_terms, sent = dp_terms(even, odd)
        near_last, *far_last = backs[n_labels - 1]
        got_last = [partner(x, "labels", 1) for x in (after(near_last, sent), *far_last)]
        keep, first, share = sum_shares(even, got, share_terms, *got_last)
        terms = reduce_runs(backs, got_last, sent, keep, first)
        other = partner(grad_label_work(works, 2, 1, label_weight.shape), "dp", 1)
        grad_label = grad_label_work(works, 2, 0, label_weight.shape, other)
        grad_feats = add(after(terms[0], grad_label), *terms[1:]).astype(BF16)
        grad_enc = join_halves(share, grad_feats)
    else:
        shards = gather_near(gather_far(enc_weight))
        flat = owners.reshape(-1)
        onehot = (flat[:, None] == jnp.arange(n_owner, dtype=jnp.int32)[None, :]).astype(jnp.int32)
        rank = jnp.sum((jnp.cumsum(onehot, axis=0) - onehot) * onehot, axis=1)
        slot = (flat * cap + rank).reshape(row_count, pick_count)
        slot_total = n_owner * cap
        slots = jnp.arange(slot_total, dtype=jnp.int32)
        place = slots[:, None, None] == slot[None]
        pick = jnp.any(place, axis=2).astype(BF16)
        live = jnp.any(place, axis=(1, 2))
        block_of = jnp.sum(jnp.where(place, blocks[None], 0), axis=(1, 2))
        wanted = jnp.sum(jnp.where(place, positives[None], 0), axis=(1, 2))
        owner_of = jnp.where(live, slots // cap, -1)
        out = dot(pick, feats).astype(BF16).reshape(n_labels, n_data, cap, width)
        meta = jnp.stack([owner_of, block_of, wanted], axis=1).reshape(n_labels, n_data, cap, 3)
        tiles = slot_total // TILE
        got = swap(out).reshape(tiles, TILE, width)
        got_meta = swap(meta).reshape(tiles, TILE, 3).transpose(0, 2, 1)
        sources = [
            with_meta(got[i], got_meta[i, 0:1], got_meta[i, 1:2], got_meta[i, 2:3])
            for i in range(tiles)
        ]
        works = []
        for i in range(0, tiles, 4):
            before = works[-1] if works else None
            last = i + 4 >= tiles
            works.append(pair_work(sources[i : i + 4], [label_weight], shards, TILE, 1, before, last))
        back = jnp.concatenate([back for work in works for back in work["back"]], axis=0)
        back = swap(back.reshape(n_labels, n_data, cap, width)).reshape(slot_total, width)
        grad_feats = dot(pick, back, 0, 0).astype(BF16)
        even, odd = works[-1]["shares"]
        got, share_terms, _ = dp_terms(even, odd)
        *_, share = sum_shares(even, got, share_terms)
        grad_label = grad_label_work(works, 1, 0, label_weight.shape)
        grad_enc = join_halves(share, grad_label, grad_feats)

    return (grad_feats, grad_label, grad_enc)


def solution(mesh):
    rows = P(("groups", "labels", "dp"), None)
    return jax.shard_map(
        local,
        mesh=mesh,
        in_specs=(rows, P("dp", None), rows, rows, rows, rows),
        out_specs=(rows, rows, P(("groups", "dp"), None)),
        check_vma=False,
    )
```

```python
import functools

import jax
import jax.numpy as jnp
from jax import lax
from jax.experimental import pallas as pl
from jax.experimental.pallas import tpu as pltpu
from jax.sharding import PartitionSpec as P

BLK = 128
EPSILON = 1e-06
META_ROWS = 8
TILE = 128
F32 = jnp.float32
BF16 = jnp.bfloat16
VMEM = pl.BlockSpec(memory_space=pltpu.VMEM)
HBM = pl.BlockSpec(memory_space=pltpu.HBM)


def dot(a, b, da=1, db=0):
    return lax.dot_general(a, b, (((da,), (db,)), ((), ())), preferred_element_type=F32)


def shard_at(m, shard_rows):
    at = jnp.bitwise_xor(lax.axis_index("dp"), m) * shard_rows
    return pl.ds(pl.multiple_of(at, 16), shard_rows)


def pair_kernel(*refs, cap, pick_count, n_sources, n_sets, n_data, first, last):
    it = iter(refs)
    take = lambda n: [next(it) for _ in range(n)]
    sources, labels = take(n_sources), take(n_sets)
    shards = take(n_data if first else 0)
    enc, total_in = (None, None) if first else take(2)
    backs, grad_scores_ref, block_ref, embedding_ref = take(n_sources), *take(3)
    enc = next(it) if first else enc
    shares = take(2 if last else 0)
    total_ref = next(it)

    n_owner_data = lax.axis_size("dp")
    me = lax.axis_index("labels") * n_owner_data + lax.axis_index("dp")
    rows = sources[0].shape[0] - META_ROWS
    shard_rows = enc.shape[0] // n_data
    n_blocks = labels[0].shape[0] // BLK
    part = n_sources * cap
    slots = n_sets * part

    for m, shard in enumerate(shards):
        enc[shard_at(m, shard_rows), :] = shard[...]

    row_id = lax.broadcasted_iota(jnp.int32, (rows, rows), 0)
    col_id = lax.broadcasted_iota(jnp.int32, (rows, rows), 1)
    before = (row_id < col_id).astype(BF16)
    slot_id = lax.broadcasted_iota(jnp.int32, (cap, rows), 0).astype(F32)
    column = lax.broadcasted_iota(jnp.int32, (slots, BLK), 1)

    hits, codes = [], []
    for source in sources:
        meta = source[rows:, 0 : 3 * rows].astype(F32)[:pick_count]
        code = meta[:, rows : 2 * rows] * 256.0 + meta[:, 2 * rows :] + 1.0
        for j in range(n_sets):
            named = meta[:, :rows] == jnp.bitwise_xor(me, j).astype(F32)
            hits.append(jnp.sum(named.astype(F32), axis=0, keepdims=True))
            codes.append(jnp.sum(jnp.where(named, code, 0.0), axis=0, keepdims=True))
    rank = dot(jnp.concatenate(hits, axis=0).astype(BF16), before)

    picks, picked, slot_codes = [], {}, {}
    for s, source in enumerate(sources):
        pick = []
        for j in range(n_sets):
            i = s * n_sets + j
            pick.append(jnp.where((slot_id == rank[i : i + 1]) & (hits[i] > 0.0), 1.0, 0.0))
            slot_codes[j, s] = jnp.sum(pick[j] * codes[i], axis=1, keepdims=True)
        picks.append(jnp.concatenate(pick, axis=0).astype(BF16))
        found = dot(picks[s], source[:rows, :]).astype(BF16)
        for j in range(n_sets):
            picked[j, s] = found[j * cap : (j + 1) * cap]
    order = [(j, s) for j in range(n_sets) for s in range(n_sources)]
    feats = jnp.concatenate([picked[i] for i in order], axis=0)
    code = jnp.concatenate([slot_codes[i] for i in order], axis=0).astype(jnp.int32) - 1

    hidden = dot(feats, enc[...])
    inv_rms = lax.rsqrt(jnp.mean(hidden * hidden, axis=-1, keepdims=True) + EPSILON)
    embedding = (hidden * inv_rms).astype(BF16)
    embedding_ref[...] = embedding

    block = jnp.broadcast_to(code >> 8, (slots, BLK))
    block_ref[...] = block
    wanted = jnp.broadcast_to(code & 255, (slots, BLK))
    target = jnp.where(column == wanted, 1.0, 0.0)
    grad_pairs = []
    for j in range(n_sets):
        at = slice(j * part, (j + 1) * part)
        scores = dot(embedding[at], labels[j][...], 1, 1)
        mine = block[at]
        own_scores = jnp.zeros((part, BLK), F32)
        for b in range(n_blocks):
            own_scores = jnp.where(mine == b, scores[:, b * BLK : (b + 1) * BLK], own_scores)
        grad_scores = jnp.where(mine >= 0, jax.nn.sigmoid(own_scores) - target[at], 0.0)
        grad_scores_ref[at, :] = grad_scores
        spread = jnp.concatenate(
            [jnp.where(mine == b, grad_scores, 0.0).astype(BF16) for b in range(n_blocks)], axis=1
        )
        grad_pairs.append(dot(spread, labels[j][...]))
    grad_pair = jnp.concatenate(grad_pairs, axis=0).astype(BF16).astype(F32)

    projection = jnp.mean(hidden * grad_pair, axis=-1, keepdims=True)
    grad_hidden = (inv_rms * grad_pair - hidden * (inv_rms**3 * projection)).astype(BF16)
    total = dot(feats, grad_hidden, 0, 0)
    total_ref[...] = total if first else total + total_in[...]
    for m in range(n_data if last else 0):
        shares[m % 2][m // 2] = total_ref[shard_at(m, shard_rows), :].astype(BF16)

    grad_feats = dot(grad_hidden, enc[...], 1, 1).astype(BF16)
    for s in range(n_sources):
        parts = [
            grad_feats[(j * n_sources + s) * cap : (j * n_sources + s + 1) * cap]
            for j in range(n_sets)
        ]
        backs[s][...] = dot(picks[s], jnp.concatenate(parts, axis=0), 0, 0).astype(BF16)


def grad_label_kernel(*refs, calls, n_sets, j, n_more):
    grad_scores, blocks, embeddings = refs[:calls], refs[calls : 2 * calls], refs[2 * calls : 3 * calls]
    more, rest = refs[3 * calls : 3 * calls + n_more], refs[3 * calls + n_more :]
    out_ref, (result, *sem) = rest[0], rest[-2:] if len(rest) > 1 else rest
    rows_of = [slice(j * r.shape[0] // n_sets, (j + 1) * r.shape[0] // n_sets) for r in blocks]
    grad_scores_t = jnp.concatenate([r[at, :].T for r, at in zip(grad_scores, rows_of)], axis=1)
    block_t = jnp.concatenate([r[at, :].T for r, at in zip(blocks, rows_of)], axis=1)
    embedding = jnp.concatenate([r[at, :] for r, at in zip(embeddings, rows_of)], axis=0)
    copies = []
    for b in range(out_ref.shape[0] // BLK):
        rows = pl.ds(b * BLK, BLK)
        spread_t = jnp.where(block_t == b, grad_scores_t, 0.0).astype(BF16)
        total = dot(spread_t, embedding)
        for ref in more:
            total = total + ref[rows, :].astype(F32)
        result[rows, :] = total.astype(BF16)
        if sem:
            copies.append(pltpu.make_async_copy(result.at[rows], out_ref.at[rows], sem[0].at[b]))
            copies[b].start()
    for copy in copies:
        copy.wait()


def own_block_kernel(feats_ref, owners_ref, blocks_ref, positives_ref, out_ref, ints, sem):
    rows, width = feats_ref.shape
    feats = pltpu.make_async_copy(feats_ref, out_ref.at[pl.ds(0, rows)], sem.at[0])
    feats.start()
    copies = []
    for i, ref in enumerate((owners_ref, blocks_ref, positives_ref)):
        copies.append(pltpu.make_async_copy(ref, ints.at[i], sem.at[i + 1]))
        copies[i].start()
    for copy in copies:
        copy.wait()
    meta = [ints[i].astype(F32) for i in range(3)]
    meta += [jnp.zeros((meta[0].shape[0], width - 3 * rows), F32)]
    meta = jnp.concatenate(meta, axis=1)
    rest = jnp.zeros((META_ROWS - meta.shape[0], width), F32)
    out_ref[rows:, :] = jnp.concatenate([meta, rest], axis=0).astype(BF16)
    feats.wait()


def load_kernel(label_ref, shard_ref, label_out, shard_out):
    label_out[...] = label_ref[...]
    shard_out[...] = shard_ref[...]


def half_at(mine, half):
    odd = jnp.bitwise_and(lax.axis_index("labels"), 1)
    return pl.ds(pl.multiple_of((odd if mine else 1 - odd) * half, 16), half)


def split_kernel(even_ref, got_ref, *refs):
    *more, keep_ref, send_ref, total = refs
    share = even_ref[0].astype(F32) + got_ref[0].astype(F32)
    for ref in more:
        share = share + ref[...].astype(F32)
    total[...] = share
    half = keep_ref.shape[0]
    keep_ref[...] = total[half_at(True, half), :]
    send_ref[...] = total[half_at(False, half), :].astype(BF16)


def merge_kernel(mine_ref, other_ref, out_ref):
    half = mine_ref.shape[0]
    out_ref[half_at(True, half), :] = mine_ref[...].astype(F32)
    out_ref[half_at(False, half), :] = other_ref[...].astype(F32)


def call(kernel, name, out_shape, scratch, flops, megabytes, *args, space=VMEM, out_space=VMEM, limit=24):
    return pl.pallas_call(
        kernel,
        in_specs=[space] * len(args),
        out_specs=jax.tree.map(lambda _: out_space, out_shape),
        out_shape=out_shape,
        scratch_shapes=scratch,
        compiler_params=pltpu.CompilerParams(vmem_limit_bytes=limit << 20),
        cost_estimate=pl.CostEstimate(
            flops=flops, bytes_accessed=megabytes << 20, transcendentals=0
        ),
        name=name,
    )(*args)


def shaped(shape, dtype=BF16):
    return jax.ShapeDtypeStruct(shape, dtype)


def pair_work(sources, labels, shards, cap, pick_count, before, last):
    n_data, n_sets = len(shards), len(labels)
    block_rows, width = sources[0].shape
    rows = block_rows - META_ROWS
    slots = n_sets * len(sources) * cap
    shard_rows = shards[0].shape[0]
    full = (n_data * shard_rows, width)
    backs = len(sources)
    shapes = [shaped((rows, width))] * backs
    shapes += [shaped((slots, BLK), F32), shaped((slots, BLK), jnp.int32), shaped((slots, width))]
    more = [before["enc"], before["total"]] if before else shards
    scratch = []
    if not before:
        shapes += [shaped(full)]
    if last:
        shapes += [shaped((n_data // 2, shard_rows, width))] * 2
        scratch = [pltpu.VMEM(full, F32)]
    else:
        shapes += [shaped(full, F32)]
    out = call(
        functools.partial(
            pair_kernel,
            cap=cap,
            pick_count=pick_count,
            n_sources=len(sources),
            n_sets=n_sets,
            n_data=n_data,
            first=not before,
            last=last,
        ),
        "pair_work",
        shapes,
        scratch,
        2 * slots * width * (2 * labels[0].shape[0] + 3 * width + 2 * rows),
        8,
        *sources,
        *labels,
        *more,
    )
    result = {"back": list(out[:backs]), "slots": list(out[backs : backs + 3])}
    rest = list(out[backs + 3 :])
    result["enc"] = before["enc"] if before else rest.pop(0)
    result["shares" if last else "total"] = rest if last else rest[0]
    return result


def grad_label_work(works, n_sets, j, labels_shape, *more):
    slots = list(zip(*(work["slots"] for work in works)))
    scratch = []
    if j == 0:
        sem = pltpu.SemaphoreType.DMA((labels_shape[0] // BLK,))
        scratch = [pltpu.VMEM(labels_shape, BF16), sem]
    return call(
        functools.partial(
            grad_label_kernel, calls=len(works), n_sets=n_sets, j=j, n_more=len(more)
        ),
        "grad_label_work",
        shaped(labels_shape),
        scratch,
        2 * sum(x.shape[0] for x in slots[0]) // n_sets * labels_shape[0] * labels_shape[1],
        4,
        *slots[0],
        *slots[1],
        *slots[2],
        *more,
        out_space=pl.BlockSpec(memory_space=pl.ANY) if scratch else VMEM,
    )


def swap(x):
    x = lax.all_to_all(x, "labels", split_axis=0, concat_axis=0, tiled=True)
    return lax.all_to_all(x, "dp", split_axis=1, concat_axis=1, tiled=True)


def partner(x, axis, mask):
    return lax.ppermute(x, axis, [(i, i ^ mask) for i in range(lax.axis_size(axis))])


def masks(n):
    return [1 << i for i in range(n.bit_length() - 1)]


def after(x, *others):
    return lax.optimization_barrier((x, *others))[0]


def gather_far(x):
    got = {0: x}
    for mask in reversed(masks(lax.axis_size("dp"))[1:]):
        got.update({m | mask: partner(v, "dp", mask) for m, v in list(got.items())})
    return [got[m] for m in sorted(got)]


def gather_near(far, *first):
    near = [partner(after(v, *far[1:], *first), "dp", 1) for v in far]
    return [v for pair in zip(far, near) for v in pair]


def gather_labels(x, first):
    got = {0: x}
    for mask in reversed(masks(lax.axis_size("labels"))):
        for m, v in list(got.items()):
            got[m | mask] = partner(after(v, first) if m else v, "labels", mask)
    return [got[m] for m in range(len(got))]


def add(*terms):
    return sum(t.astype(F32) for t in terms)


def dp_terms(even, odd):
    got = sent = partner(odd, "dp", 1)
    terms = [[even[i], got[i]] for i in range(even.shape[0])]
    for mask in masks(len(terms)):
        for i in range(len(terms)):
            if i & mask == 0 and i % mask == 0:
                sent = add(*terms[i | mask]).astype(BF16)
                terms[i].append(partner(sent, "dp", 2 * mask))
    return got, terms[0], sent


def sum_shares(even, got, terms, *first):
    rows, width = even.shape[1:]
    half = rows // 2
    keep, send = call(
        split_kernel,
        "split_share",
        [shaped((half, width), F32), shaped((half, width))],
        [pltpu.VMEM((rows, width), F32)],
        0,
        1,
        even,
        after(got, *first),
        *terms[2:],
    )
    x = add(keep, partner(send, "labels", 1)).astype(BF16)
    first = x
    for mask in masks(lax.axis_size("labels"))[1:]:
        x = add(x, partner(x, "labels", mask)).astype(BF16)
    return keep, first, x


def join_halves(x, *first):
    other = partner(x, "labels", 1)
    out = shaped((2 * x.shape[0], x.shape[1]), F32)
    return call(merge_kernel, "merge_share", out, [], 0, 1, after(x, *first), other)


def reduce_runs(runs, got_last, ahead, keep, first):
    def over_dp(parts, *hold):
        parts = [list(part) for part in parts]
        for mask in masks(len(parts)):
            for h in range(0, len(parts), 2 * mask):
                sent = after(add(*parts[h + mask]).astype(BF16), *hold)
                parts[h].append(partner(sent, "dp", 2 * mask))
        return parts[0]

    n = len(runs)
    sums, sent_near = {n - 2: over_dp(list(zip(runs[n - 2], got_last)), ahead)}, []
    for i in reversed(range(0, n - 2, 2)):
        near = add(*over_dp([[x] for x in runs[i + 1]], ahead)).astype(BF16)
        sent_near.append(partner(near, "labels", 1))
        sums[i] = over_dp([[x] for x in runs[i]], keep) + sent_near[-1:]
    for mask in masks(n)[1:]:
        for i in range(0, n, 2 * mask):
            sent = after(add(*sums[i + mask]).astype(BF16), first)
            sums[i].append(partner(sent, "labels", mask))
    return sums[0]


def with_meta(feats, owner_rows, block_rows, positive_rows):
    meta = jnp.concatenate([owner_rows, block_rows, positive_rows], axis=1).astype(BF16)
    meta = jnp.pad(meta, ((0, META_ROWS - meta.shape[0]), (0, feats.shape[1] - meta.shape[1])))
    return jnp.concatenate([feats, meta], axis=0)


def local(feats, enc_weight, label_weight, owners, blocks, positives):
    n_labels = lax.axis_size("labels")
    n_data = lax.axis_size("dp")
    n_owner = n_labels * n_data
    row_count, width = feats.shape
    pick_count = owners.shape[1]
    cap = max(2, 2 * row_count * pick_count // n_owner)

    if row_count <= n_data * cap:
        own = call(
            own_block_kernel,
            "own_block",
            shaped((row_count + META_ROWS, width)),
            [
                pltpu.VMEM((3, pick_count, row_count), jnp.int32),
                pltpu.SemaphoreType.DMA((4,)),
            ],
            0,
            1,
            feats,
            owners.T,
            blocks.T,
            positives.T,
            space=HBM,
            limit=60,
        )
        labels = [label_weight, partner(label_weight, "dp", 1)]
        labels[0], own_shard = call(
            load_kernel,
            "load",
            [shaped(label_weight.shape), shaped(enc_weight.shape)],
            [],
            0,
            4,
            after(label_weight, labels[1]),
            enc_weight,
        )
        near = gather_labels(own, labels[0])
        far = {0: gather_far(own)}
        shards = gather_near(gather_far(enc_weight))
        shards[0] = own_shard
        works, backs = [], {}
        last_call = list(range(1, n_labels, 2))
        for call_runs in (list(range(0, n_labels, 2)), last_call):
            sources = []
            for run in call_runs:
                if run == n_labels - 1:
                    far[run] = gather_far(after(near[run], *far[run - 1][1:]))
                elif run % 2:
                    sent = [after(x, *shards[1:]) for x in far[run - 1][1:]]
                    far[run] = near[run : run + 1] + [partner(x, "labels", 1) for x in sent]
                elif run:
                    far[run] = gather_far(after(near[run], *far[0][1:], *near[1:3], labels[0]))
                sources += [after(near[run], *([] if run else near[1:3]))] + far[run][1:]
            before, last = works[-1] if works else None, call_runs is last_call
            works.append(pair_work(sources, labels, shards, cap, pick_count, before, last))
            parts = len(sources) // len(call_runs)
            for i, run in enumerate(call_runs):
                backs[run] = works[-1]["back"][i * parts : (i + 1) * parts]
        even, odd = works[-1]["shares"]
        got, share_terms, sent = dp_terms(even, odd)
        near_last, *far_last = backs[n_labels - 1]
        got_last = [partner(after(x, sent), "labels", 1) for x in (near_last, *far_last)]
        keep, first, share = sum_shares(even, got, share_terms, *got_last)
        terms = reduce_runs(backs, got_last, sent, keep, first)
        other = partner(grad_label_work(works, 2, 1, label_weight.shape), "dp", 1)
        grad_label = grad_label_work(works, 2, 0, label_weight.shape, other)
        grad_feats = add(after(terms[0], grad_label), *terms[1:]).astype(BF16)
        grad_enc = join_halves(share, grad_feats)
    else:
        shards = gather_near(gather_far(enc_weight))
        flat = owners.reshape(-1)
        onehot = (flat[:, None] == jnp.arange(n_owner, dtype=jnp.int32)[None, :]).astype(jnp.int32)
        rank = jnp.sum((jnp.cumsum(onehot, axis=0) - onehot) * onehot, axis=1)
        slot = (flat * cap + rank).reshape(row_count, pick_count)
        slot_total = n_owner * cap
        slots = jnp.arange(slot_total, dtype=jnp.int32)
        place = slots[:, None, None] == slot[None]
        pick = jnp.any(place, axis=2).astype(BF16)
        live = jnp.any(place, axis=(1, 2))
        block_of = jnp.sum(jnp.where(place, blocks[None], 0), axis=(1, 2))
        wanted = jnp.sum(jnp.where(place, positives[None], 0), axis=(1, 2))
        owner_of = jnp.where(live, slots // cap, -1)
        out = dot(pick, feats).astype(BF16).reshape(n_labels, n_data, cap, width)
        meta = jnp.stack([owner_of, block_of, wanted], axis=1).reshape(n_labels, n_data, cap, 3)
        tiles = slot_total // TILE
        got = swap(out).reshape(tiles, TILE, width)
        got_meta = swap(meta).reshape(tiles, TILE, 3).transpose(0, 2, 1)
        sources = [
            with_meta(got[i], got_meta[i, 0:1], got_meta[i, 1:2], got_meta[i, 2:3])
            for i in range(tiles)
        ]
        works = []
        for i in range(0, tiles, 4):
            before = works[-1] if works else None
            last = i + 4 >= tiles
            works.append(pair_work(sources[i : i + 4], [label_weight], shards, TILE, 1, before, last))
        back = jnp.concatenate([back for work in works for back in work["back"]], axis=0)
        back = swap(back.reshape(n_labels, n_data, cap, width)).reshape(slot_total, width)
        grad_feats = dot(pick, back, 0, 0).astype(BF16)
        even, odd = works[-1]["shares"]
        got, share_terms, _ = dp_terms(even, odd)
        *_, share = sum_shares(even, got, share_terms)
        grad_label = grad_label_work(works, 1, 0, label_weight.shape)
        grad_enc = join_halves(share, grad_label, grad_feats)

    return (grad_feats, grad_label, grad_enc)


def solution(mesh):
    rows = P(("groups", "labels", "dp"), None)
    return jax.shard_map(
        local,
        mesh=mesh,
        in_specs=(rows, P("dp", None), rows, rows, rows, rows),
        out_specs=(rows, rows, P(("groups", "dp"), None)),
        check_vma=False,
    )
```

```python
import functools

import jax
import jax.numpy as jnp
from jax import lax
from jax.experimental import pallas as pl
from jax.experimental.pallas import tpu as pltpu
from jax.sharding import PartitionSpec as P

BLK = 128
EPSILON = 1e-06
META_ROWS = 8
TILE = 128
F32 = jnp.float32
BF16 = jnp.bfloat16
VMEM = pl.BlockSpec(memory_space=pltpu.VMEM)
HBM = pl.BlockSpec(memory_space=pltpu.HBM)


def dot(a, b, da=1, db=0):
    return lax.dot_general(a, b, (((da,), (db,)), ((), ())), preferred_element_type=F32)


def shard_at(m, shard_rows):
    at = jnp.bitwise_xor(lax.axis_index("dp"), m) * shard_rows
    return pl.ds(pl.multiple_of(at, 16), shard_rows)


def pair_kernel(*refs, cap, pick_count, n_sources, n_sets, n_data, first, last):
    it = iter(refs)
    take = lambda n: [next(it) for _ in range(n)]
    sources, labels = take(n_sources), take(n_sets)
    shards = take(n_data if first else 0)
    enc, total_in = (None, None) if first else take(2)
    backs, grad_scores_ref, block_ref, embedding_ref = take(n_sources), *take(3)
    enc = next(it) if first else enc
    shares = take(2 if last else 0)
    total_ref = next(it)

    n_owner_data = lax.axis_size("dp")
    me = lax.axis_index("labels") * n_owner_data + lax.axis_index("dp")
    rows = sources[0].shape[0] - META_ROWS
    shard_rows = enc.shape[0] // n_data
    n_blocks = labels[0].shape[0] // BLK
    part = n_sources * cap
    slots = n_sets * part

    for m, shard in enumerate(shards):
        enc[shard_at(m, shard_rows), :] = shard[...]

    row_id = lax.broadcasted_iota(jnp.int32, (rows, rows), 0)
    col_id = lax.broadcasted_iota(jnp.int32, (rows, rows), 1)
    before = (row_id < col_id).astype(BF16)
    slot_id = lax.broadcasted_iota(jnp.int32, (cap, rows), 0).astype(F32)
    column = lax.broadcasted_iota(jnp.int32, (slots, BLK), 1)

    hits, codes = [], []
    for source in sources:
        meta = source[rows:, 0 : 3 * rows].astype(F32)[:pick_count]
        code = meta[:, rows : 2 * rows] * 256.0 + meta[:, 2 * rows :] + 1.0
        for j in range(n_sets):
            named = meta[:, :rows] == jnp.bitwise_xor(me, j).astype(F32)
            hits.append(jnp.sum(named.astype(F32), axis=0, keepdims=True))
            codes.append(jnp.sum(jnp.where(named, code, 0.0), axis=0, keepdims=True))
    rank = dot(jnp.concatenate(hits, axis=0).astype(BF16), before)

    picks, picked, slot_codes = [], {}, {}
    for s, source in enumerate(sources):
        pick = []
        for j in range(n_sets):
            i = s * n_sets + j
            pick.append(jnp.where((slot_id == rank[i : i + 1]) & (hits[i] > 0.0), 1.0, 0.0))
            slot_codes[j, s] = jnp.sum(pick[j] * codes[i], axis=1, keepdims=True)
        picks.append(jnp.concatenate(pick, axis=0).astype(BF16))
        found = dot(picks[s], source[:rows, :]).astype(BF16)
        for j in range(n_sets):
            picked[j, s] = found[j * cap : (j + 1) * cap]
    order = [(j, s) for j in range(n_sets) for s in range(n_sources)]
    feats = jnp.concatenate([picked[i] for i in order], axis=0)
    code = jnp.concatenate([slot_codes[i] for i in order], axis=0).astype(jnp.int32) - 1

    hidden = dot(feats, enc[...])
    inv_rms = lax.rsqrt(jnp.mean(hidden * hidden, axis=-1, keepdims=True) + EPSILON)
    embedding = (hidden * inv_rms).astype(BF16)
    embedding_ref[...] = embedding

    block = jnp.broadcast_to(code >> 8, (slots, BLK))
    block_ref[...] = block
    wanted = jnp.broadcast_to(code & 255, (slots, BLK))
    target = jnp.where(column == wanted, 1.0, 0.0)
    grad_pairs = []
    for j in range(n_sets):
        at = slice(j * part, (j + 1) * part)
        scores = dot(embedding[at], labels[j][...], 1, 1)
        mine = block[at]
        own_scores = jnp.zeros((part, BLK), F32)
        for b in range(n_blocks):
            own_scores = jnp.where(mine == b, scores[:, b * BLK : (b + 1) * BLK], own_scores)
        grad_scores = jnp.where(mine >= 0, jax.nn.sigmoid(own_scores) - target[at], 0.0)
        grad_scores_ref[at, :] = grad_scores
        spread = jnp.concatenate(
            [jnp.where(mine == b, grad_scores, 0.0).astype(BF16) for b in range(n_blocks)], axis=1
        )
        grad_pairs.append(dot(spread, labels[j][...]))
    grad_pair = jnp.concatenate(grad_pairs, axis=0).astype(BF16).astype(F32)

    projection = jnp.mean(hidden * grad_pair, axis=-1, keepdims=True)
    grad_hidden = (inv_rms * grad_pair - hidden * (inv_rms**3 * projection)).astype(BF16)
    total = dot(feats, grad_hidden, 0, 0)
    total_ref[...] = total if first else total + total_in[...]
    for m in range(n_data if last else 0):
        shares[m % 2][m // 2] = total_ref[shard_at(m, shard_rows), :].astype(BF16)

    grad_feats = dot(grad_hidden, enc[...], 1, 1).astype(BF16)
    for s in range(n_sources):
        parts = [
            grad_feats[(j * n_sources + s) * cap : (j * n_sources + s + 1) * cap]
            for j in range(n_sets)
        ]
        backs[s][...] = dot(picks[s], jnp.concatenate(parts, axis=0), 0, 0).astype(BF16)


def grad_label_kernel(*refs, calls, n_sets, j, n_more):
    grad_scores, blocks, embeddings = refs[:calls], refs[calls : 2 * calls], refs[2 * calls : 3 * calls]
    more, rest = refs[3 * calls : 3 * calls + n_more], refs[3 * calls + n_more :]
    out_ref, (result, *sem) = rest[0], rest[-2:] if len(rest) > 1 else rest
    rows_of = [slice(j * r.shape[0] // n_sets, (j + 1) * r.shape[0] // n_sets) for r in blocks]
    grad_scores_t = jnp.concatenate([r[at, :].T for r, at in zip(grad_scores, rows_of)], axis=1)
    block_t = jnp.concatenate([r[at, :].T for r, at in zip(blocks, rows_of)], axis=1)
    embedding = jnp.concatenate([r[at, :] for r, at in zip(embeddings, rows_of)], axis=0)
    copies = []
    for b in range(out_ref.shape[0] // BLK):
        rows = pl.ds(b * BLK, BLK)
        spread_t = jnp.where(block_t == b, grad_scores_t, 0.0).astype(BF16)
        total = dot(spread_t, embedding)
        for ref in more:
            total = total + ref[rows, :].astype(F32)
        result[rows, :] = total.astype(BF16)
        if sem:
            copies.append(pltpu.make_async_copy(result.at[rows], out_ref.at[rows], sem[0].at[b]))
            copies[b].start()
    for copy in copies:
        copy.wait()


def own_block_kernel(feats_ref, owners_ref, blocks_ref, positives_ref, out_ref, ints, sem):
    rows, width = feats_ref.shape
    feats = pltpu.make_async_copy(feats_ref, out_ref.at[pl.ds(0, rows)], sem.at[0])
    feats.start()
    copies = []
    for i, ref in enumerate((owners_ref, blocks_ref, positives_ref)):
        copies.append(pltpu.make_async_copy(ref, ints.at[i], sem.at[i + 1]))
        copies[i].start()
    for copy in copies:
        copy.wait()
    meta = [ints[i].astype(F32) for i in range(3)]
    meta += [jnp.zeros((meta[0].shape[0], width - 3 * rows), F32)]
    meta = jnp.concatenate(meta, axis=1)
    rest = jnp.zeros((META_ROWS - meta.shape[0], width), F32)
    out_ref[rows:, :] = jnp.concatenate([meta, rest], axis=0).astype(BF16)
    feats.wait()


def load_kernel(label_ref, shard_ref, label_out, shard_out):
    label_out[...] = label_ref[...]
    shard_out[...] = shard_ref[...]


def half_at(mine, half):
    odd = jnp.bitwise_and(lax.axis_index("labels"), 1)
    return pl.ds(pl.multiple_of((odd if mine else 1 - odd) * half, 16), half)


def split_kernel(even_ref, got_ref, *refs):
    *more, keep_ref, send_ref, total = refs
    share = even_ref[0].astype(F32) + got_ref[0].astype(F32)
    for ref in more:
        share = share + ref[...].astype(F32)
    total[...] = share
    half = keep_ref.shape[0]
    keep_ref[...] = total[half_at(True, half), :]
    send_ref[...] = total[half_at(False, half), :].astype(BF16)


def merge_kernel(mine_ref, other_ref, out_ref):
    half = mine_ref.shape[0]
    out_ref[half_at(True, half), :] = mine_ref[...].astype(F32)
    out_ref[half_at(False, half), :] = other_ref[...].astype(F32)


def call(kernel, name, out_shape, scratch, flops, megabytes, *args, space=VMEM, out_space=VMEM, limit=24):
    return pl.pallas_call(
        kernel,
        in_specs=[space] * len(args),
        out_specs=jax.tree.map(lambda _: out_space, out_shape),
        out_shape=out_shape,
        scratch_shapes=scratch,
        compiler_params=pltpu.CompilerParams(vmem_limit_bytes=limit << 20),
        cost_estimate=pl.CostEstimate(
            flops=flops, bytes_accessed=megabytes << 20, transcendentals=0
        ),
        name=name,
    )(*args)


def shaped(shape, dtype=BF16):
    return jax.ShapeDtypeStruct(shape, dtype)


def pair_work(sources, labels, shards, cap, pick_count, before, last):
    n_data, n_sets = len(shards), len(labels)
    block_rows, width = sources[0].shape
    rows = block_rows - META_ROWS
    slots = n_sets * len(sources) * cap
    shard_rows = shards[0].shape[0]
    full = (n_data * shard_rows, width)
    backs = len(sources)
    shapes = [shaped((rows, width))] * backs
    shapes += [shaped((slots, BLK), F32), shaped((slots, BLK), jnp.int32), shaped((slots, width))]
    more = [before["enc"], before["total"]] if before else shards
    scratch = []
    if not before:
        shapes += [shaped(full)]
    if last:
        shapes += [shaped((n_data // 2, shard_rows, width))] * 2
        scratch = [pltpu.VMEM(full, F32)]
    else:
        shapes += [shaped(full, F32)]
    out = call(
        functools.partial(
            pair_kernel,
            cap=cap,
            pick_count=pick_count,
            n_sources=len(sources),
            n_sets=n_sets,
            n_data=n_data,
            first=not before,
            last=last,
        ),
        "pair_work",
        shapes,
        scratch,
        2 * slots * width * (2 * labels[0].shape[0] + 3 * width + 2 * rows),
        8,
        *sources,
        *labels,
        *more,
    )
    result = {"back": list(out[:backs]), "slots": list(out[backs : backs + 3])}
    rest = list(out[backs + 3 :])
    result["enc"] = before["enc"] if before else rest.pop(0)
    result["shares" if last else "total"] = rest if last else rest[0]
    return result


def grad_label_work(works, n_sets, j, labels_shape, *more):
    slots = list(zip(*(work["slots"] for work in works)))
    scratch = []
    if j == 0:
        sem = pltpu.SemaphoreType.DMA((labels_shape[0] // BLK,))
        scratch = [pltpu.VMEM(labels_shape, BF16), sem]
    return call(
        functools.partial(
            grad_label_kernel, calls=len(works), n_sets=n_sets, j=j, n_more=len(more)
        ),
        "grad_label_work",
        shaped(labels_shape),
        scratch,
        2 * sum(x.shape[0] for x in slots[0]) // n_sets * labels_shape[0] * labels_shape[1],
        4,
        *slots[0],
        *slots[1],
        *slots[2],
        *more,
        out_space=pl.BlockSpec(memory_space=pl.ANY) if scratch else VMEM,
    )


def swap(x):
    x = lax.all_to_all(x, "labels", split_axis=0, concat_axis=0, tiled=True)
    return lax.all_to_all(x, "dp", split_axis=1, concat_axis=1, tiled=True)


def partner(x, axis, mask):
    return lax.ppermute(x, axis, [(i, i ^ mask) for i in range(lax.axis_size(axis))])


def masks(n):
    return [1 << i for i in range(n.bit_length() - 1)]


def after(x, *others):
    return lax.optimization_barrier((x, *others))[0]


def gather_far(x):
    got = {0: x}
    for mask in reversed(masks(lax.axis_size("dp"))[1:]):
        got.update({m | mask: partner(v, "dp", mask) for m, v in list(got.items())})
    return [got[m] for m in sorted(got)]


def gather_near(far, *first):
    near = [partner(after(v, *far[1:], *first), "dp", 1) for v in far]
    return [v for pair in zip(far, near) for v in pair]


def gather_labels(x, first):
    got = {0: x}
    for mask in reversed(masks(lax.axis_size("labels"))):
        for m, v in list(got.items()):
            got[m | mask] = partner(after(v, first) if m else v, "labels", mask)
    return [got[m] for m in range(len(got))]


def add(*terms):
    return sum(t.astype(F32) for t in terms)


def dp_terms(even, odd):
    got = sent = partner(odd, "dp", 1)
    terms = [[even[i], got[i]] for i in range(even.shape[0])]
    for mask in masks(len(terms)):
        for i in range(len(terms)):
            if i & mask == 0 and i % mask == 0:
                sent = add(*terms[i | mask]).astype(BF16)
                terms[i].append(partner(sent, "dp", 2 * mask))
    return got, terms[0], sent


def sum_shares(even, got, terms, *first):
    rows, width = even.shape[1:]
    half = rows // 2
    keep, send = call(
        split_kernel,
        "split_share",
        [shaped((half, width), F32), shaped((half, width))],
        [pltpu.VMEM((rows, width), F32)],
        0,
        1,
        even,
        after(got, *first),
        *terms[2:],
    )
    x = add(keep, partner(send, "labels", 1)).astype(BF16)
    first = x
    for mask in masks(lax.axis_size("labels"))[1:]:
        x = add(x, partner(x, "labels", mask)).astype(BF16)
    return keep, first, x


def join_halves(x, *first):
    other = partner(x, "labels", 1)
    out = shaped((2 * x.shape[0], x.shape[1]), F32)
    return call(merge_kernel, "merge_share", out, [], 0, 1, after(x, *first), other)


def reduce_runs(runs, got_last, ahead, keep, first):
    def over_dp(parts, *hold):
        parts = [list(part) for part in parts]
        for mask in masks(len(parts)):
            for h in range(0, len(parts), 2 * mask):
                sent = after(add(*parts[h + mask]).astype(BF16), *hold)
                parts[h].append(partner(sent, "dp", 2 * mask))
        return parts[0]

    n = len(runs)
    sums, sent_near = {n - 2: over_dp(list(zip(runs[n - 2], got_last)), ahead)}, []
    for i in reversed(range(0, n - 2, 2)):
        near = add(*over_dp([[x] for x in runs[i + 1]], ahead)).astype(BF16)
        sent_near.append(partner(near, "labels", 1))
        sums[i] = over_dp([[x] for x in runs[i]], sent_near[-1]) + sent_near[-1:]
    for mask in masks(n)[1:]:
        for i in range(0, n, 2 * mask):
            sent = after(add(*sums[i + mask]).astype(BF16), first)
            sums[i].append(partner(sent, "labels", mask))
    return sums[0]


def with_meta(feats, owner_rows, block_rows, positive_rows):
    meta = jnp.concatenate([owner_rows, block_rows, positive_rows], axis=1).astype(BF16)
    meta = jnp.pad(meta, ((0, META_ROWS - meta.shape[0]), (0, feats.shape[1] - meta.shape[1])))
    return jnp.concatenate([feats, meta], axis=0)


def local(feats, enc_weight, label_weight, owners, blocks, positives):
    n_labels = lax.axis_size("labels")
    n_data = lax.axis_size("dp")
    n_owner = n_labels * n_data
    row_count, width = feats.shape
    pick_count = owners.shape[1]
    cap = max(2, 2 * row_count * pick_count // n_owner)

    if row_count <= n_data * cap:
        own = call(
            own_block_kernel,
            "own_block",
            shaped((row_count + META_ROWS, width)),
            [
                pltpu.VMEM((3, pick_count, row_count), jnp.int32),
                pltpu.SemaphoreType.DMA((4,)),
            ],
            0,
            1,
            feats,
            owners.T,
            blocks.T,
            positives.T,
            space=HBM,
            limit=60,
        )
        labels = [label_weight, partner(label_weight, "dp", 1)]
        labels[0], own_shard = call(
            load_kernel,
            "load",
            [shaped(label_weight.shape), shaped(enc_weight.shape)],
            [],
            0,
            4,
            after(label_weight, labels[1]),
            enc_weight,
        )
        near = gather_labels(own, labels[0])
        far = {0: gather_far(own)}
        shards = gather_near(gather_far(enc_weight))
        shards[0] = own_shard
        works, backs = [], {}
        last_call = list(range(1, n_labels, 2))
        for call_runs in (list(range(0, n_labels, 2)), last_call):
            sources = []
            for run in call_runs:
                if run == n_labels - 1:
                    far[run] = gather_far(after(near[run], *far[run - 1][1:]))
                elif run % 2:
                    sent = [after(x, *shards[1:]) for x in far[run - 1][1:]]
                    far[run] = near[run : run + 1] + [partner(x, "labels", 1) for x in sent]
                elif run:
                    far[run] = gather_far(after(near[run], *far[0][1:], *near[1:3], labels[0]))
                sources += [after(near[run], *([] if run else near[1:3]))] + far[run][1:]
            before, last = works[-1] if works else None, call_runs is last_call
            works.append(pair_work(sources, labels, shards, cap, pick_count, before, last))
            parts = len(sources) // len(call_runs)
            for i, run in enumerate(call_runs):
                backs[run] = works[-1]["back"][i * parts : (i + 1) * parts]
        even, odd = works[-1]["shares"]
        got, share_terms, sent = dp_terms(even, odd)
        near_last, *far_last = backs[n_labels - 1]
        got_last = [partner(x, "labels", 1) for x in (after(near_last, sent), *far_last)]
        keep, first, share = sum_shares(even, got, share_terms, *got_last)
        terms = reduce_runs(backs, got_last, sent, keep, first)
        other = partner(grad_label_work(works, 2, 1, label_weight.shape), "dp", 1)
        grad_label = grad_label_work(works, 2, 0, label_weight.shape, other)
        grad_feats = add(after(terms[0], grad_label), *terms[1:]).astype(BF16)
        grad_enc = join_halves(share, grad_feats)
    else:
        shards = gather_near(gather_far(enc_weight))
        flat = owners.reshape(-1)
        onehot = (flat[:, None] == jnp.arange(n_owner, dtype=jnp.int32)[None, :]).astype(jnp.int32)
        rank = jnp.sum((jnp.cumsum(onehot, axis=0) - onehot) * onehot, axis=1)
        slot = (flat * cap + rank).reshape(row_count, pick_count)
        slot_total = n_owner * cap
        slots = jnp.arange(slot_total, dtype=jnp.int32)
        place = slots[:, None, None] == slot[None]
        pick = jnp.any(place, axis=2).astype(BF16)
        live = jnp.any(place, axis=(1, 2))
        block_of = jnp.sum(jnp.where(place, blocks[None], 0), axis=(1, 2))
        wanted = jnp.sum(jnp.where(place, positives[None], 0), axis=(1, 2))
        owner_of = jnp.where(live, slots // cap, -1)
        out = dot(pick, feats).astype(BF16).reshape(n_labels, n_data, cap, width)
        meta = jnp.stack([owner_of, block_of, wanted], axis=1).reshape(n_labels, n_data, cap, 3)
        tiles = slot_total // TILE
        got = swap(out).reshape(tiles, TILE, width)
        got_meta = swap(meta).reshape(tiles, TILE, 3).transpose(0, 2, 1)
        sources = [
            with_meta(got[i], got_meta[i, 0:1], got_meta[i, 1:2], got_meta[i, 2:3])
            for i in range(tiles)
        ]
        works = []
        for i in range(0, tiles, 4):
            before = works[-1] if works else None
            last = i + 4 >= tiles
            works.append(pair_work(sources[i : i + 4], [label_weight], shards, TILE, 1, before, last))
        back = jnp.concatenate([back for work in works for back in work["back"]], axis=0)
        back = swap(back.reshape(n_labels, n_data, cap, width)).reshape(slot_total, width)
        grad_feats = dot(pick, back, 0, 0).astype(BF16)
        even, odd = works[-1]["shares"]
        got, share_terms, _ = dp_terms(even, odd)
        *_, share = sum_shares(even, got, share_terms)
        grad_label = grad_label_work(works, 1, 0, label_weight.shape)
        grad_enc = join_halves(share, grad_label, grad_feats)

    return (grad_feats, grad_label, grad_enc)


def solution(mesh):
    rows = P(("groups", "labels", "dp"), None)
    return jax.shard_map(
        local,
        mesh=mesh,
        in_specs=(rows, P("dp", None), rows, rows, rows, rows),
        out_specs=(rows, rows, P(("groups", "dp"), None)),
        check_vma=False,
    )
```
